32 devices in a mesh: mode: 8 (over z, x), space: 4 (over y, core).
Axes of the slice: x: 2, y: 2, z: 4, core: 2. Of those that a mesh axis runs over, the one named last changes fastest.
Arguments:
- right_side: float32 [288, 3, 12, 8, 128], P('mode', None, 'space'), as said below
- mean_stiffness: float32 [12, 8, 128], P('space'), may hold values from 1 to 4
- ply_stiffness: float32 [10], replicated, may hold values from 0.1 to 0.4
- fibre_weights: float32 [3, 3], replicated, may hold values from 0.5 to 2
- ply_map: int32 [12, 8, 128], P('space'), may hold values from 0 to 9
- coupling_table: int32 [660, 4], replicated, may hold values from 0 to 285, as said below
Outputs:
- solution_field: float32 [288, 3, 12, 8, 128], P('mode', None, 'space')
- residual: float32 [288, 3, 12, 8, 128], P('mode', None, 'space')
The draws below stay inside these ranges and needn't reach their ends.
Inputs may be any that keep to these rules, and one draw needn't show every extreme that they name: `coupling_table`: the modes below 286 number the multi-indices of total degree at most 3 in 10 variables in some order; for every multi-index alpha of degree at most 2 and every variable k there is one row (mode of alpha, mode of alpha + e_k, k, alpha_k + 1), in some order of rows, and no other rows. `right_side`: mode slots 286 and above are zero.
All inputs are finite; a program needn't handle non-finite values.
Results may differ from the reference program's by a relative error of at most 0.015.
Values sent between devices are 32-bit elements; how exact they have to be, the bound alone decides.
No kernel may reach another device: no remote copies, remote signals or barrier semaphores. Data moves between devices by JAX's collectives and lax.ppermute only.
A program may use at most 192 MiB of HBM per device.

```python
import math
import jax
import jax.numpy as jnp
import numpy as np
from jax import lax

VARS = 10
CHAOS = 286
NY = 8
NZ = 128
ITERS = 2
SLOTS = 288
NX = 12
NNZ = 660


def draw_right_side(key, part):
    key = jax.random.fold_in(key, 11)
    shape = (SLOTS, 3, NX, NY, NZ)
    modes = jnp.arange(SLOTS, dtype=jnp.int32).reshape(SLOTS, 1, 1, 1, 1)
    rising = 3.0 ** (modes.astype(jnp.float32) / SLOTS)
    living = (modes < CHAOS).astype(jnp.float32)
    values = jax.random.normal(key, shape, jnp.float32)
    return (values * rising * living).astype(jnp.float32)


def multi_indices(count, degree):
    if count == 0:
        return [()]
    listed = []
    for first in range(degree + 1):
        for tail in multi_indices(count - 1, degree - first):
            listed.append((first,) + tail)
    return listed


def ladder_rows():
    every_index = multi_indices(VARS, 3)
    every_index.sort(key=sum)
    lookup = {}
    for position, alpha in enumerate(every_index):
        lookup[alpha] = position
    listed = []
    for alpha in every_index:
        if sum(alpha) <= 2:
            for which in range(VARS):
                raised = tuple((alpha[place] + (1 if place == which else 0) for place in range(VARS)))
                listed.append((lookup[alpha], lookup[raised], which, alpha[which] + 1))
    return np.array(listed, dtype=np.int32)


def draw_coupling_table(key, part):
    key = jax.random.fold_in(key, 7)
    order_key, row_key = jax.random.split(key)
    table = jnp.asarray(ladder_rows())
    relabel = jax.random.permutation(order_key, CHAOS).astype(jnp.int32)
    first_mode = relabel[table[:, 0]]
    second_mode = relabel[table[:, 1]]
    stacked = jnp.stack([first_mode, second_mode, table[:, 2], table[:, 3]], axis=1).astype(jnp.int32)
    row_order = jax.random.permutation(row_key, NNZ).astype(jnp.int32)
    return stacked[row_order]


def place_ends(drawn, rng, low, top_value):
    extent = drawn.shape
    spot = [jax.random.randint(jax.random.fold_in(rng, axis), (), 0, extent[axis]) for axis in range(len(extent))]
    drawn = drawn.at[tuple(spot)].set(low)
    longest = extent.index(max(extent))
    spot[longest] = (spot[longest] + 1) % extent[longest]
    return drawn.at[tuple(spot)].set(top_value)


def levels(stream_key, shape, cuts, least, top_value):
    gain = 1.0
    for dim, parts in cuts:
        steps = jax.random.uniform(jax.random.fold_in(jax.random.fold_in(stream_key, 6), dim), (parts,), jnp.float32, least / len(cuts), top_value / len(cuts))
        gain = gain * jnp.repeat(jnp.exp(steps), shape[dim] // parts).reshape((-1,) + (1,) * (len(shape) - 1 - dim))
    return gain


def setup_inputs(seed: int = 0) -> dict:
    streams_of = jax.random.split(jax.random.key(seed), 7)
    right_side = draw_right_side(jax.random.fold_in(streams_of[6], 71), 0)
    mean_stiffness = jnp.clip(jnp.exp(math.log(4.0) - 1.3862944 * jax.random.uniform(streams_of[1], (NX, NY, NZ), jnp.float32) ** levels(streams_of[1], (NX, NY, NZ), ((0, 4),), -0.2, 0.2)), 1.0, 4.0)
    ply_stiffness = jnp.clip(jnp.exp(jax.random.uniform(streams_of[2], (VARS,), jnp.float32, math.log(0.1), math.log(0.4))), 0.1, 0.4)
    fibre_weights = jnp.clip(jnp.exp(jax.random.uniform(streams_of[3], (3, 3), jnp.float32, math.log(0.5), math.log(2.0))), 0.5, 2.0)
    ply_map = place_ends(jax.random.randint(streams_of[4], (NX, NY, NZ), 0, VARS), jax.random.fold_in(streams_of[4], 1), 0, VARS - 1).astype(jnp.int32)
    coupling_table = draw_coupling_table(jax.random.fold_in(streams_of[6], 71), 0)
    return {"right_side": right_side, "mean_stiffness": mean_stiffness, "ply_stiffness": ply_stiffness, "fibre_weights": fibre_weights, "ply_map": ply_map, "coupling_table": coupling_table}


def window(array_in, dim_index, offset):
    slicers = [slice(None)] * (array_in.ndim - 3)
    for which in range(3):
        shift_by = offset if which == dim_index else 0
        length_here = array_in.shape[array_in.ndim - 3 + which] - 2
        slicers.append(slice(1 + shift_by, 1 + shift_by + length_here))
    return array_in[tuple(slicers)]

def diffuse(vector, stiffness, fibre_weights):
    vector_pads = [(0, 0)] * (vector.ndim - 2) + [(1, 1), (1, 1)]
    stiff_pads = [(0, 0)] * (stiffness.ndim - 2) + [(1, 1), (1, 1)]
    padded_v = jnp.pad(vector, vector_pads)
    padded_c = jnp.pad(stiffness, stiff_pads)
    centre = window(padded_v, 0, 0)
    middle = window(padded_c, 0, 0)
    result = None
    for dim_index in range(3):
        upper = 0.5 * (middle + window(padded_c, dim_index, 1)) * (centre - window(padded_v, dim_index, 1))
        lower = 0.5 * (middle + window(padded_c, dim_index, -1)) * (centre - window(padded_v, dim_index, -1))
        column = fibre_weights[:, dim_index].reshape(3, 1, 1, 1)
        term = column * (upper + lower)
        result = term if result is None else result + term
    return result

def pad_slabs(array_in, dim_index):
    padding = [(0, 0)] * array_in.ndim
    padding[dim_index] = (1, 1)
    return jnp.pad(array_in, padding)

def reference(right_side, mean_stiffness, ply_stiffness, fibre_weights, ply_map, coupling_table):
    first_mode = coupling_table[:, 0]
    second_mode = coupling_table[:, 1]
    variable = coupling_table[:, 2]
    entry_weight = jnp.sqrt(coupling_table[:, 3].astype(jnp.float32))
    coupling = jnp.zeros((VARS, SLOTS, SLOTS), jnp.float32)
    coupling = coupling.at[variable, first_mode, second_mode].add(entry_weight)
    coupling = coupling.at[variable, second_mode, first_mode].add(entry_weight)
    plies = jnp.arange(VARS, dtype=jnp.int32).reshape(VARS, 1, 1, 1)
    ply_fields = (ply_map[None] == plies).astype(jnp.float32) * ply_stiffness.reshape(VARS, 1, 1, 1)
    mean_rim = pad_slabs(mean_stiffness, 0)[None]
    ply_rims = pad_slabs(ply_fields, 1)

    def operate(vector):
        flat = vector.reshape(SLOTS, -1)
        result = vector + diffuse(pad_slabs(vector, 2), mean_rim, fibre_weights)
        for which in range(VARS):
            mixed = jnp.dot(coupling[which], flat, precision=lax.Precision.HIGHEST, preferred_element_type=jnp.float32).reshape(vector.shape)
            result = result + diffuse(pad_slabs(mixed, 2), ply_rims[which][None], fibre_weights)
        return result
    solution_field = jnp.zeros_like(right_side)
    residual = right_side
    direction = right_side
    norm_now = jnp.sum(residual * residual)
    for iteration in range(ITERS):
        image = operate(direction)
        step_size = norm_now / jnp.sum(direction * image)
        solution_field = solution_field + step_size * direction
        residual = residual - step_size * image
        norm_next = jnp.sum(residual * residual)
        direction = residual + norm_next / norm_now * direction
        norm_now = norm_next
    return (solution_field, residual)
```

```python
import functools

import jax
import jax.numpy as jnp
from jax import lax
from jax.experimental import pallas as pl
from jax.experimental.pallas import tpu as pltpu
from jax.sharding import PartitionSpec as P

VARS = 10
ITERS = 2


def extended(array, sides, width):
    for axis, dim in sides:
        devices, length = (lax.axis_size(axis), array.shape[dim])
        up = [(i, (i + 1) % devices) for i in range(devices - 1)]
        down = [(j, i) for i, j in up]
        last = lax.slice_in_dim(array, length - width, length, axis=dim)
        leading = lax.slice_in_dim(array, 0, width, axis=dim)
        before = lax.ppermute(last, axis, up)
        after = lax.ppermute(leading, axis, down)
        array = jnp.concatenate([before, array, after], axis=dim)
    return array


def window(array_in, dim_index, offset):
    slicers = [slice(None)] * (array_in.ndim - 3)
    for which in range(3):
        shift_by = offset if which == dim_index else 0
        length_here = array_in.shape[array_in.ndim - 3 + which] - 2
        slicers.append(slice(1 + shift_by, 1 + shift_by + length_here))
    return array_in[tuple(slicers)]


def diffuse(vector, stiffness, fibre_weights):
    vector_pads = [(0, 0)] * (vector.ndim - 2) + [(1, 1), (1, 1)]
    stiff_pads = [(0, 0)] * (stiffness.ndim - 2) + [(1, 1), (1, 1)]
    padded_v = jnp.pad(vector, vector_pads)
    padded_c = jnp.pad(stiffness, stiff_pads)
    centre = window(padded_v, 0, 0)
    middle = window(padded_c, 0, 0)
    result = None
    for dim_index in range(3):
        upper = (
            0.5
            * (middle + window(padded_c, dim_index, 1))
            * (centre - window(padded_v, dim_index, 1))
        )
        lower = (
            0.5
            * (middle + window(padded_c, dim_index, -1))
            * (centre - window(padded_v, dim_index, -1))
        )
        column = fibre_weights[:, dim_index].reshape(3, 1, 1, 1)
        term = column * (upper + lower)
        result = term if result is None else result + term
    return result


def squares(vector):
    return lax.psum(jnp.sum(vector * vector), ("mode", "space"))


def row_table(both_rows, both_cols, both_vars, both_weights, base, mode_dev, slots):
    local_rows = both_rows - base
    valid_rows = (local_rows >= 0) & (local_rows < mode_dev)
    local_rows = jnp.where(valid_rows, local_rows, mode_dev)
    row_coupling = jnp.zeros((VARS, mode_dev, slots), jnp.float32)
    row_coupling = row_coupling.at[both_vars, local_rows, both_cols].add(both_weights, mode="drop")
    return row_coupling.reshape(VARS * mode_dev, slots)


def plain(right_side, mean_stiffness, ply_stiffness, fibre_weights, ply_map, coupling_table):
    mode_dev = right_side.shape[0]
    slots = mode_dev * lax.axis_size("mode")
    base = lax.axis_index("mode") * mode_dev
    first_mode = coupling_table[:, 0]
    second_mode = coupling_table[:, 1]
    variable = coupling_table[:, 2]
    entry_weight = jnp.sqrt(coupling_table[:, 3].astype(jnp.float32))
    both_rows = jnp.concatenate([first_mode, second_mode])
    both_cols = jnp.concatenate([second_mode, first_mode])
    both_vars = jnp.concatenate([variable, variable])
    both_weights = jnp.concatenate([entry_weight, entry_weight])
    plies = jnp.arange(VARS, dtype=jnp.int32).reshape(VARS, 1, 1, 1)
    ply_fields = (ply_map[None] == plies).astype(jnp.float32) * ply_stiffness.reshape(VARS, 1, 1, 1)
    stiff_stack = jnp.concatenate([mean_stiffness[None], ply_fields], axis=0)
    stiff_rims = extended(stiff_stack, (("space", 1),), 1)
    stiff_rims = stiff_rims[:, None]
    row_coupling = row_table(both_rows, both_cols, both_vars, both_weights, base, mode_dev, slots)
    solution_field = jnp.zeros_like(right_side)
    residual = right_side
    direction = right_side
    norm_now = squares(residual)
    for iteration in range(ITERS):
        shard_piece = lax.all_gather(direction, "mode", axis=0, tiled=True)
        mixed = jnp.dot(
            row_coupling,
            shard_piece.reshape(shard_piece.shape[0], -1),
            precision=lax.Precision.HIGHEST,
            preferred_element_type=jnp.float32,
        )
        stacked = jnp.concatenate(
            [direction[None], mixed.reshape((VARS,) + direction.shape)], axis=0
        )
        padded = extended(stacked, (("space", 3),), 1)
        terms = diffuse(padded, stiff_rims[:, None], fibre_weights)
        image = direction + jnp.sum(terms, axis=0)
        step_size = norm_now / lax.psum(jnp.sum(direction * image), ("mode", "space"))
        solution_field = solution_field + step_size * direction
        residual = residual - step_size * image
        norm_next = squares(residual)
        direction = residual + norm_next / norm_now * direction
        norm_now = norm_next
    return (solution_field, residual)


COMPS = 3
SLAB = 3
PARTS = 8
WIDE = 16
ROWS = 4
EVEN = 1 + VARS * (VARS + 1) // 2
SPAN = VARS * EVEN
FULL = 624
INNER = 6
TILES = 8
LANES = 128
VMEM = 56 * 1024 * 1024


def lane_id():
    return lax.broadcasted_iota(jnp.int32, (8, LANES), 1)


def block_swap(tile):
    row = lax.broadcasted_iota(jnp.int32, (8, LANES), 0)
    block = lane_id() // WIDE
    for bit in (4, 2, 1):
        low = (row & bit) == 0
        same = low == ((block & bit) == 0)
        up = pltpu.roll(pltpu.roll(tile, 8 - bit, 0), WIDE * bit, 1)
        if bit == 4:
            moved = up
        else:
            down = pltpu.roll(pltpu.roll(tile, bit, 0), LANES - WIDE * bit, 1)
            moved = jnp.where(low, up, down)
        tile = jnp.where(same, tile, moved)
    return tile


def pack_kernel(field, *outs):
    modes = field.shape[0]
    lane = lane_id()
    slot = lane % WIDE

    def body(mode, carry):
        for comp in range(COMPS):
            planes = [field[mode, comp, x] for x in range(SLAB)]
            halo = jnp.zeros((8, LANES), jnp.float32)
            for x in range(SLAB):
                for offset, place in ((-1, x + 1), (16, x + 6), (-2, x + 10), (17, x + 13)):
                    inside = (lane >= WIDE) if offset < 0 else (lane < LANES - WIDE)
                    moved = pltpu.roll(planes[x], (place - offset) % LANES, 1)
                    halo = jnp.where((slot == place) & inside, moved, halo)
            for p, tile in enumerate(planes + [halo]):
                outs[comp][pl.ds(mode * ROWS + p, PARTS, stride=ROWS * modes), :] = block_swap(tile)
        return carry

    lax.fori_loop(0, modes, body, 0)


def pack(field):
    modes = field.shape[0]
    shape = jax.ShapeDtypeStruct((PARTS * modes * ROWS, LANES), jnp.float32)
    return pl.pallas_call(
        pack_kernel,
        out_shape=[shape] * COMPS,
        compiler_params=pltpu.CompilerParams(vmem_limit_bytes=VMEM),
        name="pack",
    )(field)


def laplace(tiles, weights, which):
    lane = lax.broadcasted_iota(jnp.int32, tiles[0].shape, 1)
    slot = lane % WIDE
    halo = tiles[5]
    roll = lambda t, s: pltpu.roll(t, s % LANES, 1)

    def along_y(t):
        return jnp.where(lane >= WIDE, roll(t, WIDE), 0.0) + jnp.where(
            lane < LANES - WIDE, roll(t, -WIDE), 0.0
        )

    at = {0: 0, 1: 1, 2: 2, -1: 3, 3: 4, -2: 6, 4: 7}
    place = {index: x for x, index in at.items()}
    sums = {}
    for index in which:
        t = tiles[index]
        if index == 5:
            along_x = roll(t, 1) + roll(t, -1)
            outer = jnp.where(slot < 5, roll(t, -9), roll(t, -7))
            inner = roll(tiles[2], -7)
            for x, index_in in ((0, 0), (1, 1), (2, 2)):
                inner = jnp.where(slot == x + 1, roll(tiles[index_in], x + 1), inner)
                if x < 2:
                    inner = jnp.where(slot == x + 6, roll(tiles[index_in], x - 9), inner)
            along_z = outer + inner
        else:
            x = place[index]
            along_x = tiles[at[x - 1]] + tiles[at[x + 1]]
            along_z = jnp.where(slot == 0, roll(halo, -(x + 1)), roll(t, 1)) + jnp.where(
                slot == WIDE - 1, roll(halo, 9 - x), roll(t, -1)
            )
        sums[index] = weights[0] * along_x + weights[1] * along_y(t) + weights[2] * along_z
    return sums


def split(array):
    high = array.astype(jnp.bfloat16)
    low = (array - high.astype(jnp.float32)).astype(jnp.bfloat16)
    return jnp.concatenate([high, low], axis=0)


STEP = 16


def apply_operator(src, dst, ell, acc, zhat, coeffs, to_even, to_all, weights, inner, outer):
    slots = src.shape[0]
    twice = 2.0 * (weights[0] + weights[1] + weights[2])

    def first(step, carry):
        rows = pl.ds(pl.multiple_of(step * STEP, STEP), STEP)
        tiles = [src[rows, LANES * t : LANES * (t + 1)] for t in range(inner)]
        sums = laplace(tiles, weights, range(outer))
        for t in range(outer):
            ell[rows, LANES * t : LANES * (t + 1)] = twice * tiles[t] - sums[t]
        return carry

    lax.fori_loop(0, slots // STEP, first, 0)

    def mix(array):
        return jnp.dot(to_even[...], split(array), preferred_element_type=jnp.float32)

    def spread(scaled, even):
        pad = jnp.zeros((FULL - SPAN - EVEN, even.shape[1]), jnp.float32)
        stacked = split(jnp.concatenate(scaled + [even, pad], axis=0))
        return jnp.dot(to_all[...], stacked, preferred_element_type=jnp.float32)

    def group(array, k):
        return array[k * EVEN : (k + 1) * EVEN]

    chunk = 2 * LANES
    for start in range(0, inner * LANES, chunk):
        cols = slice(start, start + chunk)
        value = src[:, cols]
        mixed = mix(value)
        even = group(mixed, VARS)
        own = [coeffs[k : k + 1, cols] for k in range(VARS)]
        total = own[0] * group(mixed, 0)
        for k in range(1, VARS):
            total = total + own[k] * group(mixed, k)
        coupled = spread([own[k] * even for k in range(VARS)], total)
        zhat[:, cols] = coupled + coeffs[2 * VARS : 2 * VARS + 1, cols] * value
        if start < outer * LANES:
            lap = ell[:, cols]
            mixed_lap = mix(lap)
            even_lap = group(mixed_lap, VARS)
            beside = [coeffs[VARS + k : VARS + k + 1, cols] for k in range(VARS)]
            total = beside[0] * group(mixed, 0) + 0.5 * own[0] * group(mixed_lap, 0)
            for k in range(1, VARS):
                total = total + beside[k] * group(mixed, k) + 0.5 * own[k] * group(mixed_lap, k)
            scaled = [beside[k] * even + 0.5 * own[k] * even_lap for k in range(VARS)]
            half_mean = 0.5 * coeffs[2 * VARS : 2 * VARS + 1, cols]
            centre = coeffs[2 * VARS + 1 : 2 * VARS + 2, cols]
            acc[:, cols] = spread(scaled, total) + centre * value + half_mean * lap

    def last(step, carry):
        rows = pl.ds(pl.multiple_of(step * STEP, STEP), STEP)
        tiles = [zhat[rows, LANES * t : LANES * (t + 1)] for t in range(inner)]
        sums = laplace(tiles, weights, range(outer))
        for t in range(outer):
            cols = slice(LANES * t, LANES * (t + 1))
            result = acc[rows, cols] - 0.5 * sums[t]
            if t >= SLAB:
                result = coeffs[2 * VARS + 2 : 2 * VARS + 3, cols] * result
            dst[rows, cols] = result
        return carry

    lax.fori_loop(0, slots // STEP, last, 0)


def apply_kernel(
    own, before, after, scale, unscale, to_even, to_all, coeffs, fibre, so_far,
    out, partial, field, first, second, ell, acc, zhat, *, comp,
):
    slots = scale.shape[0]
    weights = [fibre[comp, d] for d in range(3)]
    lane = lax.broadcasted_iota(jnp.int32, (slots, LANES), 1)
    slot = lane % WIDE
    load = lambda ref, p: ref[pl.ds(p, slots, stride=ROWS), :]
    left = pltpu.roll(load(before, 3), LANES - 3, 1)
    right = pltpu.roll(load(after, 3), 3, 1)
    halo = jnp.where((slot == 0) | (slot == 5), left, load(own, 3))
    halo = jnp.where((slot == 4) | (slot == 9), right, halo)
    ordered = [
        load(own, 0), load(own, 1), load(own, 2), load(before, 2), load(after, 0), halo,
        load(before, 1), load(after, 1),
    ]
    for t, tile in enumerate(ordered):
        field[:, LANES * t : LANES * (t + 1)] = tile * scale[...]
    consts = (coeffs, to_even, to_all, weights)
    apply_operator(field, first, ell, acc, zhat, *consts, TILES, INNER)
    apply_operator(first, second, ell, acc, zhat, *consts, INNER, SLAB)
    sums = [jnp.zeros((1, LANES), jnp.float32)] * 5
    for p in range(SLAB):
        cols = slice(LANES * p, LANES * (p + 1))
        b = load(own, p)
        q = first[:, cols] * unscale[...]
        w = second[:, cols] * unscale[...]
        out[pl.ds(p, slots, stride=2 * SLAB), :] = q
        out[pl.ds(p + SLAB, slots, stride=2 * SLAB), :] = w
        for n, (one, two) in enumerate(((b, b), (b, q), (q, q), (b, w), (q, w))):
            sums[n] = sums[n] + jnp.sum(one * two, axis=0, keepdims=True)
    partial[...] = so_far[...] + jnp.concatenate(sums + [jnp.zeros((3, LANES), jnp.float32)], axis=0)


def apply_twice(comp, own, before, after, tables, coeffs, fibre, so_far):
    scale, unscale, to_even, to_all = tables
    slots = scale.shape[0]
    vmem = pl.BlockSpec(memory_space=pltpu.VMEM)
    f32 = lambda *shape: pltpu.VMEM(shape, jnp.float32)
    return pl.pallas_call(
        functools.partial(apply_kernel, comp=comp),
        out_shape=[
            jax.ShapeDtypeStruct((slots * 2 * SLAB, LANES), jnp.float32),
            jax.ShapeDtypeStruct((8, LANES), jnp.float32),
        ],
        in_specs=[vmem] * 8 + [pl.BlockSpec(memory_space=pltpu.SMEM), vmem],
        out_specs=[vmem, vmem],
        scratch_shapes=[
            f32(slots, TILES * LANES),
            f32(slots, INNER * LANES),
            f32(slots, 4 * LANES),
            f32(slots, INNER * LANES),
            f32(slots, INNER * LANES),
            f32(slots, TILES * LANES),
        ],
        compiler_params=pltpu.CompilerParams(vmem_limit_bytes=VMEM),
        name="apply_twice",
    )(own, before, after, scale, unscale, to_even, to_all, coeffs, fibre, so_far)


def finish(field, images, coefs):
    modes = field.shape[0]
    per_part = modes * 2 * SLAB
    steps = 4

    def kernel(field, *refs):
        images, coefs, solution_field, residual = refs[:COMPS], refs[COMPS], refs[-2], refs[-1]
        first = pl.program_id(0) * (modes // steps)

        def body(mode, carry):
            base = (first + mode) * 2 * SLAB
            for comp in range(COMPS):
                for p in range(SLAB):
                    b = field[mode, comp, p]
                    q = block_swap(images[comp][pl.ds(base + p, PARTS, stride=per_part), :])
                    w = block_swap(images[comp][pl.ds(base + p + SLAB, PARTS, stride=per_part), :])
                    solution_field[mode, comp, p] = coefs[0] * b + coefs[1] * q
                    residual[mode, comp, p] = b + coefs[2] * q + coefs[3] * w
            return carry

        lax.fori_loop(0, modes // steps, body, 0)

    block = pl.BlockSpec((modes // steps,) + field.shape[1:], lambda i: (i, 0, 0, 0, 0))
    whole = pl.BlockSpec(memory_space=pltpu.VMEM)
    return pl.pallas_call(
        kernel,
        grid=(steps,),
        out_shape=[jax.ShapeDtypeStruct(field.shape, jnp.float32)] * 2,
        in_specs=[block] + [whole] * COMPS + [pl.BlockSpec(memory_space=pltpu.SMEM)],
        out_specs=[block, block],
        compiler_params=pltpu.CompilerParams(vmem_limit_bytes=VMEM),
        name="finish",
    )(field, *images, coefs)


def mode_tables(coupling_table, slots):
    lower, upper, variable, code = (coupling_table[:, n] for n in range(4))
    slot = jnp.arange(slots, dtype=jnp.int32)
    is_lower = lower[:, None] == slot
    is_upper = upper[:, None] == slot
    degree = jnp.sum(jnp.where(is_upper, code[:, None], 0), axis=0)
    factor = jnp.where(code == 3, 6, code).astype(jnp.float32)[:, None]
    factorial = jnp.prod(jnp.where(is_upper, factor, 1.0), axis=0)
    root = (degree == 0) & jnp.any(is_lower, axis=0)
    even = (degree == 2) | root
    rank = jnp.sum(jnp.where(even[:, None] & (slot[:, None] < slot), 1, 0), axis=0)
    lower_even = jnp.any(is_lower & even, axis=1)
    is_even_end = jnp.where(lower_even[:, None], is_lower, is_upper)
    is_odd_end = jnp.where(lower_even[:, None], is_upper, is_lower)
    column = variable * EVEN + jnp.sum(jnp.where(is_even_end, rank, 0), axis=1)
    at_column = column[:, None] == jnp.arange(FULL, dtype=jnp.int32)
    down = code.astype(jnp.float32)[:, None]
    first = jnp.where(lower_even[:, None], 1.0, down)
    second = jnp.where(lower_even[:, None], down, 1.0)
    odd_ends = is_odd_end.astype(jnp.float32)
    columns = at_column.astype(jnp.float32)
    half = jnp.bfloat16
    to_even = jnp.dot(
        columns.astype(half).T, (odd_ends * first).astype(half), preferred_element_type=jnp.float32
    )
    to_odd = jnp.dot(
        odd_ends.astype(half).T, (columns * second).astype(half), preferred_element_type=jnp.float32
    )
    pick = (jnp.arange(FULL, dtype=jnp.int32)[:, None] - SPAN == rank) & even
    pick = pick.astype(jnp.float32)
    to_even = (to_even + pick).astype(half)
    to_all = (to_odd + pick.T).astype(half)
    scale = jnp.sqrt(factorial)
    wide = lambda v: jnp.broadcast_to(v[:, None], (slots, LANES))
    twice = lambda v: jnp.concatenate([v, v], axis=1)
    return wide(scale), wide(1.0 / scale), twice(to_even), twice(to_all)


def as_tiles(fields):
    flat = lambda f: f.reshape(f.shape[:-2] + (LANES,))
    plane = lambda x: flat(fields[..., x + 2, :, 2:18])
    column = lambda low, high, z: jnp.moveaxis(fields[..., low + 2 : high + 2, :, z + 2], -2, -1)
    halo = jnp.concatenate(
        [column(-1, 4, -1), column(-1, 4, 16), column(0, 3, -2), column(0, 3, 17)], axis=-1
    )
    return jnp.concatenate(
        [plane(0), plane(1), plane(2), plane(-1), plane(3), flat(halo), plane(-2), plane(4)], axis=-1
    )


def coefficient_rows(mean_stiffness, ply_stiffness, fibre_weights, ply_map, up, down):
    both = jnp.stack([mean_stiffness, (ply_map + 1).astype(jnp.float32)])
    before = lax.ppermute(both, "space", up)
    after = lax.ppermute(both, "space", down)
    both = jnp.concatenate([before[:, 1:], both, after[:, :2]], axis=1)
    both = jnp.pad(both, ((0, 0), (0, 0), (0, 0), (2, 2)))
    both = lax.dynamic_slice_in_dim(both, lax.axis_index("mode") * WIDE, WIDE + 4, axis=3)
    mean, ply = both[0], both[1]
    plies = jnp.arange(1, VARS + 1, dtype=jnp.float32).reshape(VARS, 1, 1, 1)
    own = jnp.where(ply[None] == plies, ply_stiffness.reshape(VARS, 1, 1, 1), 0.0)
    fields = jnp.concatenate([own, mean[None]], axis=0)
    rim = jnp.pad(fields, ((0, 0), (1, 1), (1, 1), (1, 1)))
    sums = [
        rim[:, 2:, 1:-1, 1:-1] + rim[:, :-2, 1:-1, 1:-1],
        rim[:, 1:-1, 2:, 1:-1] + rim[:, 1:-1, :-2, 1:-1],
        rim[:, 1:-1, 1:-1, 2:] + rim[:, 1:-1, 1:-1, :-2],
    ]
    inside = (ply > 0).astype(jnp.float32)[None]
    slot = jnp.arange(LANES, dtype=jnp.int32) % WIDE
    used = ((slot >= 1) & (slot <= 3)) | ((slot >= 6) & (slot <= 8))
    live = jnp.ones((TILES, LANES), jnp.float32).at[5].set(used.astype(jnp.float32)).reshape(-1)
    rows = []
    for comp in range(COMPS):
        beside = 0.5 * sum(fibre_weights[comp, d] * sums[d] for d in range(3))
        stacked = jnp.concatenate(
            [own, beside[:VARS], mean[None], 1.0 + beside[VARS:], inside, inside], axis=0
        )
        tiles = as_tiles(stacked)
        rows.append(tiles.at[2 * VARS + 2].multiply(live))
    return rows


def all_sum(value):
    for axis in ("space", "mode"):
        devices = lax.axis_size(axis)
        bit = 1
        while bit < devices:
            value = value + lax.ppermute(value, axis, [(i, i ^ bit) for i in range(devices)])
            bit *= 2
    return value


def transposed(right_side, mean_stiffness, ply_stiffness, fibre_weights, ply_map, coupling_table):
    slots = right_side.shape[0] * PARTS
    devices = lax.axis_size("space")
    up = [(i, i + 1) for i in range(devices - 1)]
    down = [(j, i) for i, j in up]
    swap = lambda v: lax.all_to_all(v, "mode", 0, 0, tiled=True)
    packed = pack(right_side)
    own = [swap(p) for p in packed]
    before = [lax.ppermute(p, "space", up) for p in own]
    after = [lax.ppermute(p, "space", down) for p in own]
    tables = mode_tables(coupling_table, slots)
    rows = coefficient_rows(mean_stiffness, ply_stiffness, fibre_weights, ply_map, up, down)
    partial = jnp.zeros((8, LANES), jnp.float32)
    images = []
    for comp in range(COMPS):
        out, partial = apply_twice(
            comp, own[comp], before[comp], after[comp], tables, rows[comp], fibre_weights, partial
        )
        images.append(swap(out))
    bb, bq, qq, bw, qw = (jnp.sum(all_sum(partial)[n]) for n in range(5))
    step_one = bb / bq
    norm = bb - 2.0 * step_one * bq + step_one * step_one * qq
    beta = norm / bb
    grown = 1.0 + beta
    curve = grown * grown * bq - step_one * grown * (bw + qq) + step_one * step_one * qw
    step_two = norm / curve
    coefs = jnp.stack(
        [
            step_one + step_two * grown,
            -step_one * step_two,
            -step_one - step_two * grown,
            step_one * step_two,
        ]
    )
    return tuple(finish(right_side, images, coefs))


def on_device(right_side, mean_stiffness, ply_stiffness, fibre_weights, ply_map, coupling_table):
    args = (right_side, mean_stiffness, ply_stiffness, fibre_weights, ply_map, coupling_table)
    fits = right_side.shape[1:] == (COMPS, SLAB, 8, 128) and lax.axis_size("mode") == PARTS
    return transposed(*args) if fits else plain(*args)


def solution(mesh):
    return jax.shard_map(
        on_device,
        mesh=mesh,
        in_specs=(
            P("mode", None, "space", None, None),
            P("space", None, None),
            P(),
            P(),
            P("space", None, None),
            P(),
        ),
        out_specs=(P("mode", None, "space", None, None), P("mode", None, "space", None, None)),
        check_vma=False,
    )
```

```python
import functools

import jax
import jax.numpy as jnp
from jax import lax
from jax.experimental import pallas as pl
from jax.experimental.pallas import tpu as pltpu
from jax.sharding import PartitionSpec as P

VARS = 10
ITERS = 2


def extended(array, sides, width):
    for axis, dim in sides:
        devices, length = (lax.axis_size(axis), array.shape[dim])
        up = [(i, (i + 1) % devices) for i in range(devices - 1)]
        down = [(j, i) for i, j in up]
        last = lax.slice_in_dim(array, length - width, length, axis=dim)
        leading = lax.slice_in_dim(array, 0, width, axis=dim)
        before = lax.ppermute(last, axis, up)
        after = lax.ppermute(leading, axis, down)
        array = jnp.concatenate([before, array, after], axis=dim)
    return array


def window(array_in, dim_index, offset):
    slicers = [slice(None)] * (array_in.ndim - 3)
    for which in range(3):
        shift_by = offset if which == dim_index else 0
        length_here = array_in.shape[array_in.ndim - 3 + which] - 2
        slicers.append(slice(1 + shift_by, 1 + shift_by + length_here))
    return array_in[tuple(slicers)]


def diffuse(vector, stiffness, fibre_weights):
    vector_pads = [(0, 0)] * (vector.ndim - 2) + [(1, 1), (1, 1)]
    stiff_pads = [(0, 0)] * (stiffness.ndim - 2) + [(1, 1), (1, 1)]
    padded_v = jnp.pad(vector, vector_pads)
    padded_c = jnp.pad(stiffness, stiff_pads)
    centre = window(padded_v, 0, 0)
    middle = window(padded_c, 0, 0)
    result = None
    for dim_index in range(3):
        upper = (
            0.5
            * (middle + window(padded_c, dim_index, 1))
            * (centre - window(padded_v, dim_index, 1))
        )
        lower = (
            0.5
            * (middle + window(padded_c, dim_index, -1))
            * (centre - window(padded_v, dim_index, -1))
        )
        column = fibre_weights[:, dim_index].reshape(3, 1, 1, 1)
        term = column * (upper + lower)
        result = term if result is None else result + term
    return result


def squares(vector):
    return lax.psum(jnp.sum(vector * vector), ("mode", "space"))


def row_table(both_rows, both_cols, both_vars, both_weights, base, mode_dev, slots):
    local_rows = both_rows - base
    valid_rows = (local_rows >= 0) & (local_rows < mode_dev)
    local_rows = jnp.where(valid_rows, local_rows, mode_dev)
    row_coupling = jnp.zeros((VARS, mode_dev, slots), jnp.float32)
    row_coupling = row_coupling.at[both_vars, local_rows, both_cols].add(both_weights, mode="drop")
    return row_coupling.reshape(VARS * mode_dev, slots)


def plain(right_side, mean_stiffness, ply_stiffness, fibre_weights, ply_map, coupling_table):
    mode_dev = right_side.shape[0]
    slots = mode_dev * lax.axis_size("mode")
    base = lax.axis_index("mode") * mode_dev
    first_mode = coupling_table[:, 0]
    second_mode = coupling_table[:, 1]
    variable = coupling_table[:, 2]
    entry_weight = jnp.sqrt(coupling_table[:, 3].astype(jnp.float32))
    both_rows = jnp.concatenate([first_mode, second_mode])
    both_cols = jnp.concatenate([second_mode, first_mode])
    both_vars = jnp.concatenate([variable, variable])
    both_weights = jnp.concatenate([entry_weight, entry_weight])
    plies = jnp.arange(VARS, dtype=jnp.int32).reshape(VARS, 1, 1, 1)
    ply_fields = (ply_map[None] == plies).astype(jnp.float32) * ply_stiffness.reshape(VARS, 1, 1, 1)
    stiff_stack = jnp.concatenate([mean_stiffness[None], ply_fields], axis=0)
    stiff_rims = extended(stiff_stack, (("space", 1),), 1)
    stiff_rims = stiff_rims[:, None]
    row_coupling = row_table(both_rows, both_cols, both_vars, both_weights, base, mode_dev, slots)
    solution_field = jnp.zeros_like(right_side)
    residual = right_side
    direction = right_side
    norm_now = squares(residual)
    for iteration in range(ITERS):
        shard_piece = lax.all_gather(direction, "mode", axis=0, tiled=True)
        mixed = jnp.dot(
            row_coupling,
            shard_piece.reshape(shard_piece.shape[0], -1),
            precision=lax.Precision.HIGHEST,
            preferred_element_type=jnp.float32,
        )
        stacked = jnp.concatenate(
            [direction[None], mixed.reshape((VARS,) + direction.shape)], axis=0
        )
        padded = extended(stacked, (("space", 3),), 1)
        terms = diffuse(padded, stiff_rims[:, None], fibre_weights)
        image = direction + jnp.sum(terms, axis=0)
        step_size = norm_now / lax.psum(jnp.sum(direction * image), ("mode", "space"))
        solution_field = solution_field + step_size * direction
        residual = residual - step_size * image
        norm_next = squares(residual)
        direction = residual + norm_next / norm_now * direction
        norm_now = norm_next
    return (solution_field, residual)


COMPS = 3
SLAB = 3
PARTS = 8
WIDE = 16
ROWS = 4
EVEN = 1 + VARS * (VARS + 1) // 2
SPAN = VARS * EVEN
FULL = 624
INNER = 6
TILES = 8
LANES = 128
VMEM = 56 * 1024 * 1024


def lane_id():
    return lax.broadcasted_iota(jnp.int32, (8, LANES), 1)


def swap_out(tile):
    block = lane_id() // WIDE
    tile = pltpu.roll(tile, 0, 1, stride=WIDE, stride_axis=0)
    for bit in (1, 2, 4):
        tile = jnp.where((block & bit) != 0, pltpu.roll(tile, 8 - bit, 0), tile)
    return tile


def swap_back(tile):
    block = lane_id() // WIDE
    row = lax.broadcasted_iota(jnp.int32, (8, LANES), 0)
    for bit in (1, 2, 4):
        tile = jnp.where((block & bit) != 0, pltpu.roll(tile, bit, 0), tile)
    for bit in (1, 2, 4):
        tile = jnp.where((row & bit) != 0, pltpu.roll(tile, LANES - WIDE * bit, 1), tile)
    return tile


def halo_row(planes):
    lane = lane_id()
    slot = lane % WIDE
    halo = jnp.zeros((8, LANES), jnp.float32)
    for x, plane in planes.items():
        places = [(-1, x + 1), (WIDE, x + 6)]
        if 0 <= x < SLAB:
            places += [(-2, x + 10), (WIDE + 1, x + 13)]
        for offset, place in places:
            inside = (lane >= WIDE) if offset < 0 else (lane < LANES - WIDE)
            moved = pltpu.roll(plane, (place - offset) % LANES, 1)
            halo = jnp.where((slot == place) & inside, moved, halo)
    return halo


UNROLL = 3


def pack_kernel(field, mean, ply, *outs):
    modes = field.shape[0]
    both = outs[-1]
    for x in range(SLAB):
        both[0, x] = mean[x]
        both[1, x] = (ply[x] + 1).astype(jnp.float32)

    def body(step, carry):
        for inner in range(UNROLL):
            mode = step * UNROLL + inner
            for comp in range(COMPS):
                planes = [field[mode, comp, x] for x in range(SLAB)]
                halo = halo_row(dict(enumerate(planes)))
                for p, tile in enumerate(planes + [halo]):
                    place = pl.ds(mode * ROWS + p, PARTS, stride=ROWS * modes)
                    outs[comp][place, :] = swap_out(tile)
        return carry

    lax.fori_loop(0, modes // UNROLL, body, 0)


def estimate(micros):
    return pl.CostEstimate(flops=int(micros * 1e9), bytes_accessed=int(micros * 3e6), transcendentals=0)


def pack(field, mean, ply):
    modes = field.shape[0]
    shape = jax.ShapeDtypeStruct((PARTS * modes * ROWS, LANES), jnp.float32)
    return pl.pallas_call(
        pack_kernel,
        out_shape=[shape] * COMPS + [jax.ShapeDtypeStruct((2,) + mean.shape, jnp.float32)],
        compiler_params=pltpu.CompilerParams(vmem_limit_bytes=VMEM),
        cost_estimate=estimate(5),
        name="pack",
    )(field, mean, ply)


def stiffness_kernel(place, before, both, after, ply_stiffness, fields, wide):
    rows = []
    for kind in range(2):
        planes = {-2: before[kind, 1], -1: before[kind, 2], 3: after[kind, 0], 4: after[kind, 1]}
        planes.update({x: both[kind, x] for x in range(SLAB)})
        halo = halo_row({x: planes[x] for x in range(-1, 4)})
        ordered = [planes[0], planes[1], planes[2], planes[-1], planes[3], halo, planes[-2], planes[4]]
        for t, tile in enumerate(ordered):
            wide[...] = swap_out(tile)
            rows.append(wide[pl.ds(place[0], 1), :])
    for t in range(TILES):
        mean, ply = rows[t], rows[TILES + t]
        cols = slice(LANES * t, LANES * (t + 1))
        for k in range(VARS):
            fields[k : k + 1, cols] = jnp.where(ply == k + 1.0, ply_stiffness[k], 0.0)
        fields[VARS : VARS + 1, cols] = mean
        fields[VARS + 1 : VARS + 2, cols] = jnp.where(ply > 0.0, 1.0, 0.0)
        fields[VARS + 2 : 16, cols] = jnp.zeros((4, LANES), jnp.float32)


def stiffness_fields(place, before, both, after, ply_stiffness):
    vmem = pl.BlockSpec(memory_space=pltpu.VMEM)
    smem = pl.BlockSpec(memory_space=pltpu.SMEM)
    return pl.pallas_call(
        stiffness_kernel,
        out_shape=jax.ShapeDtypeStruct((16, TILES * LANES), jnp.float32),
        in_specs=[smem, vmem, vmem, vmem, smem],
        out_specs=vmem,
        scratch_shapes=[pltpu.VMEM((8, LANES), jnp.float32)],
        cost_estimate=estimate(2),
        name="stiffness_fields",
    )(place, before, both, after, ply_stiffness)


AT = {0: 0, 1: 1, 2: 2, -1: 3, 3: 4, -2: 6, 4: 7}
PLACE = {index: x for x, index in AT.items()}
HALO = 5


def neighbour(tiles, index, side, place, full=False):
    t = tiles[index]
    lane = lax.broadcasted_iota(jnp.int32, t.shape, 1)
    slot = lane % WIDE
    roll = lambda v, s: pltpu.roll(v, s % LANES, 1)
    if side in (2, 3):
        y = (place + lane // WIDE) & 7
        if side == 2:
            return jnp.where(y > 0, roll(t, WIDE), 0.0)
        return jnp.where(y < 7, roll(t, -WIDE), 0.0)
    if index == HALO:
        if side < 2:
            return roll(t, 1 if side == 0 else -1)
        result = roll(t, -9) if side == 4 else roll(t, -7)
        for x in range(-1, 4) if full else range(SLAB):
            goal, by = (x + 6, x - 9) if side == 4 else (x + 1, x + 1)
            result = jnp.where(slot == goal, roll(tiles[AT[x]], by), result)
        if full:
            result = jnp.where(slot >= 13, roll(t, 7), result) if side == 4 else jnp.where(
                (slot >= 10) & (slot < 13), roll(t, 9), result
            )
        return result
    x = PLACE[index]
    if side < 2:
        return tiles[AT[x - 1 if side == 0 else x + 1]]
    if side == 4:
        return jnp.where(slot == 0, roll(tiles[HALO], -(x + 1)), roll(t, 1))
    return jnp.where(slot == WIDE - 1, roll(tiles[HALO], 9 - x), roll(t, -1))


def sides_of(index, outer):
    if index < outer:
        return range(6)
    return {3: (1,), 4: (0,), HALO: (4, 5), 6: (1,), 7: (0,)}[index]


def split(array):
    high = array.astype(jnp.bfloat16)
    low = (array - high.astype(jnp.float32)).astype(jnp.bfloat16)
    return jnp.concatenate([high, low], axis=0)


STEP = 32
FACE = 16
EVEN_BLOCKS = ((0, 32), (32, EVEN))


def tile_cols(t):
    return slice(LANES * t, LANES * (t + 1))


def face_stiffness(fields, faces, weights, place):
    tiles = [fields[:, tile_cols(t)] for t in range(TILES)]
    for t in range(TILES):
        for side in sides_of(t, INNER):
            value = (0.5 * weights[side // 2]) * (tiles[t] + neighbour(tiles, t, side, place, True))
            faces[side * FACE : (side + 1) * FACE, tile_cols(t)] = value


def apply_operator(src, dst, mixed, flux, scaled, acc, faces, inside, to_even, to_all, place, inner, outer):
    slots = src.shape[0]
    for start in range(0, inner * LANES, 512):
        cols = slice(start, min(start + 512, inner * LANES))
        mixed[:, cols] = jnp.dot(to_even[...], split(src[:, cols]), preferred_element_type=jnp.float32)

    def face(side, k, t):
        return faces[side * FACE + k : side * FACE + k + 1, tile_cols(t)]

    for low, high in EVEN_BLOCKS:
        flows = {}
        for t in range(inner):
            sides = sides_of(t, outer)
            total = {}
            for k in range(VARS):
                value = mixed[k * EVEN + low : k * EVEN + high, tile_cols(t)]
                for side in sides:
                    term = face(side, k, t) * value
                    total[side] = term if k == 0 else total[side] + term
            for side in sides:
                flux[side, low:high, tile_cols(t)] = total[side]
        even = [mixed[SPAN + low : SPAN + high, tile_cols(t)] for t in range(inner)]
        for t in range(outer):
            steps = [even[t] - neighbour(even, t, side, place) for side in range(6)]
            for k in range(VARS):
                total = face(0, k, t) * steps[0]
                for side in range(1, 6):
                    total = total + face(side, k, t) * steps[side]
                scaled[k * EVEN + low : k * EVEN + high, tile_cols(t)] = total
        for t in range(outer):
            total = None
            for side in range(6):
                opposite = FluxTiles(flux, side ^ 1, low, high)
                term = flux[side, low:high, tile_cols(t)] - neighbour(opposite, t, side, place)
                total = term if total is None else total + term
            scaled[SPAN + low : SPAN + high, tile_cols(t)] = total
    scaled[SPAN + EVEN : FULL, : outer * LANES] = jnp.zeros((FULL - SPAN - EVEN, outer * LANES), jnp.float32)
    for start in range(0, outer * LANES, 512):
        cols = slice(start, min(start + 512, outer * LANES))
        acc[:, cols] = jnp.dot(to_all[...], split(scaled[:, cols]), preferred_element_type=jnp.float32)

    def last(step, carry):
        rows = pl.ds(pl.multiple_of(step * STEP, STEP), STEP)
        tiles = [src[rows, tile_cols(t)] for t in range(inner)]
        for t in range(outer):
            result = tiles[t] + acc[rows, tile_cols(t)]
            for side in range(6):
                result = result + face(side, VARS, t) * (tiles[t] - neighbour(tiles, t, side, place))
            if t >= SLAB:
                result = inside[t] * result
            dst[rows, tile_cols(t)] = result
        return carry

    lax.fori_loop(0, slots // STEP, last, 0)


class FluxTiles:
    def __init__(self, flux, side, low, high):
        self.flux, self.side, self.low, self.high = flux, side, low, high

    def __getitem__(self, t):
        return self.flux[self.side, self.low : self.high, tile_cols(t)]


def apply_kernel(
    place, own, before, after, scale, unscale, to_even, to_all, fields, fibre, so_far,
    out, partial, field, first, second, mixed, flux, scaled, acc, faces, *, comp,
):
    slots = scale.shape[0]
    here = place[0]
    face_stiffness(fields, faces, [fibre[comp, d] for d in range(3)], here)
    lane = lax.broadcasted_iota(jnp.int32, (slots, LANES), 1)
    slot = lane % WIDE
    load = lambda ref, p: ref[pl.ds(p, slots, stride=ROWS), :]
    left = pltpu.roll(load(before, 3), LANES - 3, 1)
    right = pltpu.roll(load(after, 3), 3, 1)
    halo = jnp.where((slot == 0) | (slot == 5), left, load(own, 3))
    halo = jnp.where((slot == 4) | (slot == 9), right, halo)
    ordered = [
        load(own, 0), load(own, 1), load(own, 2), load(before, 2), load(after, 0), halo,
        load(before, 1), load(after, 1),
    ]
    for t, tile in enumerate(ordered):
        field[:, tile_cols(t)] = tile * scale[...]
    inside = {t: fields[VARS + 1 : VARS + 2, tile_cols(t)] for t in range(SLAB, INNER)}
    slot = lax.broadcasted_iota(jnp.int32, (1, LANES), 1) % WIDE
    used = ((slot >= 1) & (slot <= 3)) | ((slot >= 6) & (slot <= 8))
    inside[HALO] = jnp.where(used, inside[HALO], 0.0)
    scratch = (mixed, flux, scaled, acc, faces, inside, to_even, to_all, here)
    apply_operator(field, first, *scratch, TILES, INNER)
    apply_operator(first, second, *scratch, INNER, SLAB)
    sums = [jnp.zeros((1, LANES), jnp.float32)] * 5
    for p in range(SLAB):
        b = load(own, p)
        q = first[:, tile_cols(p)] * unscale[...]
        w = second[:, tile_cols(p)] * unscale[...]
        out[pl.ds(p, slots, stride=2 * SLAB), :] = q
        out[pl.ds(p + SLAB, slots, stride=2 * SLAB), :] = w
        for n, (one, two) in enumerate(((b, b), (b, q), (q, q), (b, w), (q, w))):
            sums[n] = sums[n] + jnp.sum(one * two, axis=0, keepdims=True)
    partial[...] = so_far[...] + jnp.concatenate(sums + [jnp.zeros((3, LANES), jnp.float32)], axis=0)


def apply_twice(comp, place, own, before, after, tables, fields, fibre, so_far):
    scale, unscale, to_even, to_all = tables
    slots = scale.shape[0]
    vmem = pl.BlockSpec(memory_space=pltpu.VMEM)
    smem = pl.BlockSpec(memory_space=pltpu.SMEM)
    f32 = lambda *shape: pltpu.VMEM(shape, jnp.float32)
    return pl.pallas_call(
        functools.partial(apply_kernel, comp=comp),
        out_shape=[
            jax.ShapeDtypeStruct((slots * 2 * SLAB, LANES), jnp.float32),
            jax.ShapeDtypeStruct((8, LANES), jnp.float32),
        ],
        in_specs=[smem] + [vmem] * 8 + [smem, vmem],
        out_specs=[vmem, vmem],
        scratch_shapes=[
            f32(slots, TILES * LANES),
            f32(slots, INNER * LANES),
            f32(slots, SLAB * LANES),
            f32(FULL, TILES * LANES),
            f32(6, EVEN, TILES * LANES),
            f32(FULL, INNER * LANES),
            f32(slots, INNER * LANES),
            f32(6 * FACE, TILES * LANES),
        ],
        compiler_params=pltpu.CompilerParams(vmem_limit_bytes=VMEM),
        cost_estimate=estimate(15),
        name="apply_twice",
    )(place, own, before, after, scale, unscale, to_even, to_all, fields, fibre, so_far)


def finish(field, images, coefs):
    modes = field.shape[0]
    per_part = modes * 2 * SLAB
    steps = 4

    def kernel(field, *refs):
        images, coefs, solution_field, residual = refs[:COMPS], refs[COMPS], refs[-2], refs[-1]
        first = pl.program_id(0) * (modes // steps)

        def body(step, carry):
            for inner in range(UNROLL):
                mode = step * UNROLL + inner
                base = (first + mode) * 2 * SLAB
                for comp in range(COMPS):
                    for p in range(SLAB):
                        b = field[mode, comp, p]
                        q = swap_back(images[comp][pl.ds(base + p, PARTS, stride=per_part), :])
                        w = swap_back(images[comp][pl.ds(base + p + SLAB, PARTS, stride=per_part), :])
                        solution_field[mode, comp, p] = coefs[0] * b + coefs[1] * q
                        residual[mode, comp, p] = b + coefs[2] * q + coefs[3] * w
            return carry

        lax.fori_loop(0, modes // steps // UNROLL, body, 0)

    block = pl.BlockSpec((modes // steps,) + field.shape[1:], lambda i: (i, 0, 0, 0, 0))
    whole = pl.BlockSpec(memory_space=pltpu.VMEM)
    return pl.pallas_call(
        kernel,
        grid=(steps,),
        out_shape=[jax.ShapeDtypeStruct(field.shape, jnp.float32)] * 2,
        in_specs=[block] + [whole] * COMPS + [pl.BlockSpec(memory_space=pltpu.SMEM)],
        out_specs=[block, block],
        compiler_params=pltpu.CompilerParams(vmem_limit_bytes=VMEM),
        cost_estimate=estimate(6),
        name="finish",
    )(field, *images, coefs)


def mode_tables(coupling_table, slots):
    lower, upper, variable, code = (coupling_table[:, n] for n in range(4))
    slot = jnp.arange(slots, dtype=jnp.int32)
    is_lower = lower[:, None] == slot
    is_upper = upper[:, None] == slot
    degree = jnp.sum(jnp.where(is_upper, code[:, None], 0), axis=0)
    factor = jnp.where(code == 3, 6, code).astype(jnp.float32)[:, None]
    factorial = jnp.prod(jnp.where(is_upper, factor, 1.0), axis=0)
    root = (degree == 0) & jnp.any(is_lower, axis=0)
    even = (degree == 2) | root
    rank = jnp.sum(jnp.where(even[:, None] & (slot[:, None] < slot), 1, 0), axis=0)
    lower_even = jnp.any(is_lower & even, axis=1)
    is_even_end = jnp.where(lower_even[:, None], is_lower, is_upper)
    is_odd_end = jnp.where(lower_even[:, None], is_upper, is_lower)
    column = variable * EVEN + jnp.sum(jnp.where(is_even_end, rank, 0), axis=1)
    at_column = column[:, None] == jnp.arange(FULL, dtype=jnp.int32)
    down = code.astype(jnp.float32)[:, None]
    first = jnp.where(lower_even[:, None], 1.0, down)
    second = jnp.where(lower_even[:, None], down, 1.0)
    odd_ends = is_odd_end.astype(jnp.float32)
    columns = at_column.astype(jnp.float32)
    half = jnp.bfloat16
    to_even = jnp.dot(
        columns.astype(half).T, (odd_ends * first).astype(half), preferred_element_type=jnp.float32
    )
    to_odd = jnp.dot(
        odd_ends.astype(half).T, (columns * second).astype(half), preferred_element_type=jnp.float32
    )
    pick = (jnp.arange(FULL, dtype=jnp.int32)[:, None] - SPAN == rank) & even
    pick = pick.astype(jnp.float32)
    to_even = (to_even + pick).astype(half)
    to_all = (to_odd + pick.T).astype(half)
    scale = jnp.sqrt(factorial)
    wide = lambda v: jnp.broadcast_to(v[:, None], (slots, LANES))
    twice = lambda v: jnp.concatenate([v, v], axis=1)
    return wide(scale), wide(1.0 / scale), twice(to_even), twice(to_all)


def all_sum(value):
    for axis in ("space", "mode"):
        devices = lax.axis_size(axis)
        bit = 1
        while bit < devices:
            value = value + lax.ppermute(value, axis, [(i, i ^ bit) for i in range(devices)])
            bit *= 2
    return value


def transposed(right_side, mean_stiffness, ply_stiffness, fibre_weights, ply_map, coupling_table):
    slots = right_side.shape[0] * PARTS
    devices = lax.axis_size("space")
    up = [(i, i + 1) for i in range(devices - 1)]
    down = [(j, i) for i, j in up]
    swap = lambda v: lax.all_to_all(v, "mode", 0, 0, tiled=True)
    *packed, both = pack(right_side, mean_stiffness, ply_map)
    own = [swap(p) for p in packed]
    before = [lax.ppermute(p, "space", up) for p in own]
    after = [lax.ppermute(p, "space", down) for p in own]
    tables = mode_tables(coupling_table, slots)
    place = lax.axis_index("mode").astype(jnp.int32).reshape(1)
    both_before = lax.ppermute(both, "space", up)
    both_after = lax.ppermute(both, "space", down)
    fields = stiffness_fields(place, both_before, both, both_after, ply_stiffness)
    partial = jnp.zeros((8, LANES), jnp.float32)
    images = []
    for comp in range(COMPS):
        out, partial = apply_twice(
            comp, place, own[comp], before[comp], after[comp], tables, fields, fibre_weights, partial
        )
        images.append(swap(out))
    bb, bq, qq, bw, qw = (jnp.sum(all_sum(partial)[n]) for n in range(5))
    step_one = bb / bq
    norm = bb - 2.0 * step_one * bq + step_one * step_one * qq
    beta = norm / bb
    grown = 1.0 + beta
    curve = grown * grown * bq - step_one * grown * (bw + qq) + step_one * step_one * qw
    step_two = norm / curve
    coefs = jnp.stack(
        [
            step_one + step_two * grown,
            -step_one * step_two,
            -step_one - step_two * grown,
            step_one * step_two,
        ]
    )
    return tuple(finish(right_side, images, coefs))


def on_device(right_side, mean_stiffness, ply_stiffness, fibre_weights, ply_map, coupling_table):
    args = (right_side, mean_stiffness, ply_stiffness, fibre_weights, ply_map, coupling_table)
    fits = right_side.shape[1:] == (COMPS, SLAB, 8, 128) and lax.axis_size("mode") == PARTS
    return transposed(*args) if fits else plain(*args)


def solution(mesh):
    return jax.shard_map(
        on_device,
        mesh=mesh,
        in_specs=(
            P("mode", None, "space", None, None),
            P("space", None, None),
            P(),
            P(),
            P("space", None, None),
            P(),
        ),
        out_specs=(P("mode", None, "space", None, None), P("mode", None, "space", None, None)),
        check_vma=False,
    )
```

```python
import functools

import jax
import jax.numpy as jnp
from jax import lax
from jax.experimental import pallas as pl
from jax.experimental.pallas import tpu as pltpu
from jax.sharding import PartitionSpec as P

VARS = 10
ITERS = 2


def extended(array, sides, width):
    for axis, dim in sides:
        devices, length = (lax.axis_size(axis), array.shape[dim])
        up = [(i, (i + 1) % devices) for i in range(devices - 1)]
        down = [(j, i) for i, j in up]
        last = lax.slice_in_dim(array, length - width, length, axis=dim)
        leading = lax.slice_in_dim(array, 0, width, axis=dim)
        before = lax.ppermute(last, axis, up)
        after = lax.ppermute(leading, axis, down)
        array = jnp.concatenate([before, array, after], axis=dim)
    return array


def window(array_in, dim_index, offset):
    slicers = [slice(None)] * (array_in.ndim - 3)
    for which in range(3):
        shift_by = offset if which == dim_index else 0
        length_here = array_in.shape[array_in.ndim - 3 + which] - 2
        slicers.append(slice(1 + shift_by, 1 + shift_by + length_here))
    return array_in[tuple(slicers)]


def diffuse(vector, stiffness, fibre_weights):
    vector_pads = [(0, 0)] * (vector.ndim - 2) + [(1, 1), (1, 1)]
    stiff_pads = [(0, 0)] * (stiffness.ndim - 2) + [(1, 1), (1, 1)]
    padded_v = jnp.pad(vector, vector_pads)
    padded_c = jnp.pad(stiffness, stiff_pads)
    centre = window(padded_v, 0, 0)
    middle = window(padded_c, 0, 0)
    result = None
    for dim_index in range(3):
        upper = (
            0.5
            * (middle + window(padded_c, dim_index, 1))
            * (centre - window(padded_v, dim_index, 1))
        )
        lower = (
            0.5
            * (middle + window(padded_c, dim_index, -1))
            * (centre - window(padded_v, dim_index, -1))
        )
        column = fibre_weights[:, dim_index].reshape(3, 1, 1, 1)
        term = column * (upper + lower)
        result = term if result is None else result + term
    return result


def squares(vector):
    return lax.psum(jnp.sum(vector * vector), ("mode", "space"))


def row_table(both_rows, both_cols, both_vars, both_weights, base, mode_dev, slots):
    local_rows = both_rows - base
    valid_rows = (local_rows >= 0) & (local_rows < mode_dev)
    local_rows = jnp.where(valid_rows, local_rows, mode_dev)
    row_coupling = jnp.zeros((VARS, mode_dev, slots), jnp.float32)
    row_coupling = row_coupling.at[both_vars, local_rows, both_cols].add(both_weights, mode="drop")
    return row_coupling.reshape(VARS * mode_dev, slots)


def plain(right_side, mean_stiffness, ply_stiffness, fibre_weights, ply_map, coupling_table):
    mode_dev = right_side.shape[0]
    slots = mode_dev * lax.axis_size("mode")
    base = lax.axis_index("mode") * mode_dev
    first_mode = coupling_table[:, 0]
    second_mode = coupling_table[:, 1]
    variable = coupling_table[:, 2]
    entry_weight = jnp.sqrt(coupling_table[:, 3].astype(jnp.float32))
    both_rows = jnp.concatenate([first_mode, second_mode])
    both_cols = jnp.concatenate([second_mode, first_mode])
    both_vars = jnp.concatenate([variable, variable])
    both_weights = jnp.concatenate([entry_weight, entry_weight])
    plies = jnp.arange(VARS, dtype=jnp.int32).reshape(VARS, 1, 1, 1)
    ply_fields = (ply_map[None] == plies).astype(jnp.float32) * ply_stiffness.reshape(VARS, 1, 1, 1)
    stiff_stack = jnp.concatenate([mean_stiffness[None], ply_fields], axis=0)
    stiff_rims = extended(stiff_stack, (("space", 1),), 1)
    stiff_rims = stiff_rims[:, None]
    row_coupling = row_table(both_rows, both_cols, both_vars, both_weights, base, mode_dev, slots)
    solution_field = jnp.zeros_like(right_side)
    residual = right_side
    direction = right_side
    norm_now = squares(residual)
    for iteration in range(ITERS):
        shard_piece = lax.all_gather(direction, "mode", axis=0, tiled=True)
        mixed = jnp.dot(
            row_coupling,
            shard_piece.reshape(shard_piece.shape[0], -1),
            precision=lax.Precision.HIGHEST,
            preferred_element_type=jnp.float32,
        )
        stacked = jnp.concatenate(
            [direction[None], mixed.reshape((VARS,) + direction.shape)], axis=0
        )
        padded = extended(stacked, (("space", 3),), 1)
        terms = diffuse(padded, stiff_rims[:, None], fibre_weights)
        image = direction + jnp.sum(terms, axis=0)
        step_size = norm_now / lax.psum(jnp.sum(direction * image), ("mode", "space"))
        solution_field = solution_field + step_size * direction
        residual = residual - step_size * image
        norm_next = squares(residual)
        direction = residual + norm_next / norm_now * direction
        norm_now = norm_next
    return (solution_field, residual)


COMPS = 3
SLAB = 3
PARTS = 8
WIDE = 16
ROWS = 4
EVEN = 1 + VARS * (VARS + 1) // 2
SPAN = VARS * EVEN
FULL = 624
INNER = 6
TILES = 8
LANES = 128
VMEM = 56 * 1024 * 1024


def lane_id():
    return lax.broadcasted_iota(jnp.int32, (8, LANES), 1)


def swap_out(tile):
    block = lane_id() // WIDE
    tile = pltpu.roll(tile, 0, 1, stride=WIDE, stride_axis=0)
    for bit in (1, 2, 4):
        tile = jnp.where((block & bit) != 0, pltpu.roll(tile, 8 - bit, 0), tile)
    return tile


def swap_back(tile):
    block = lane_id() // WIDE
    row = lax.broadcasted_iota(jnp.int32, (8, LANES), 0)
    for bit in (1, 2, 4):
        tile = jnp.where((block & bit) != 0, pltpu.roll(tile, bit, 0), tile)
    for bit in (1, 2, 4):
        tile = jnp.where((row & bit) != 0, pltpu.roll(tile, LANES - WIDE * bit, 1), tile)
    return tile


def halo_row(planes):
    lane = lane_id()
    slot = lane % WIDE
    halo = jnp.zeros((8, LANES), jnp.float32)
    for x, plane in planes.items():
        places = [(-1, x + 1), (WIDE, x + 6)]
        if 0 <= x < SLAB:
            places += [(-2, x + 10), (WIDE + 1, x + 13)]
        for offset, place in places:
            inside = (lane >= WIDE) if offset < 0 else (lane < LANES - WIDE)
            moved = pltpu.roll(plane, (place - offset) % LANES, 1)
            halo = jnp.where((slot == place) & inside, moved, halo)
    return halo


UNROLL = 3


def pack_kernel(field, *refs):
    modes = field.shape[0]
    out = refs[-1]
    if len(refs) > 1:
        mean, ply, both, out = refs
        for x in range(SLAB):
            both[0, x] = mean[x]
            both[1, x] = (ply[x] + 1).astype(jnp.float32)

    def body(step, carry):
        for inner in range(UNROLL):
            mode = step * UNROLL + inner
            planes = [field[mode, 0, x] for x in range(SLAB)]
            halo = halo_row(dict(enumerate(planes)))
            for p, tile in enumerate(planes + [halo]):
                out[pl.ds(mode * ROWS + p, PARTS, stride=ROWS * modes), :] = swap_out(tile)
        return carry

    lax.fori_loop(0, modes // UNROLL, body, 0)


def estimate(micros):
    return pl.CostEstimate(flops=int(micros * 1e9), bytes_accessed=int(micros * 3e6), transcendentals=0)


def pack(field, comp, *stiffness):
    modes = field.shape[0]
    block = (modes, 1) + field.shape[2:]
    vmem = pl.BlockSpec(memory_space=pltpu.VMEM)
    shapes = [jax.ShapeDtypeStruct((2,) + s.shape, jnp.float32) for s in stiffness[:1]]
    shapes.append(jax.ShapeDtypeStruct((PARTS * modes * ROWS, LANES), jnp.float32))
    return pl.pallas_call(
        pack_kernel,
        grid=(1,),
        out_shape=shapes,
        in_specs=[pl.BlockSpec(block, lambda i: (0, comp, 0, 0, 0))] + [vmem] * len(stiffness),
        out_specs=[vmem] * len(shapes),
        compiler_params=pltpu.CompilerParams(vmem_limit_bytes=VMEM),
        cost_estimate=estimate(2.5),
        name="pack",
    )(field, *stiffness)


def stiffness_kernel(place, before, both, after, ply_stiffness, fields, wide):
    rows = []
    for kind in range(2):
        planes = {-2: before[kind, 1], -1: before[kind, 2], 3: after[kind, 0], 4: after[kind, 1]}
        planes.update({x: both[kind, x] for x in range(SLAB)})
        halo = halo_row({x: planes[x] for x in range(-1, 4)})
        ordered = [planes[0], planes[1], planes[2], planes[-1], planes[3], halo, planes[-2], planes[4]]
        for t, tile in enumerate(ordered):
            wide[...] = swap_out(tile)
            rows.append(wide[pl.ds(place[0], 1), :])
    for t in range(TILES):
        mean, ply = rows[t], rows[TILES + t]
        cols = slice(LANES * t, LANES * (t + 1))
        for k in range(VARS):
            fields[k : k + 1, cols] = jnp.where(ply == k + 1.0, ply_stiffness[k], 0.0)
        fields[VARS : VARS + 1, cols] = mean
        fields[VARS + 1 : VARS + 2, cols] = jnp.where(ply > 0.0, 1.0, 0.0)
        fields[VARS + 2 : 16, cols] = jnp.zeros((4, LANES), jnp.float32)


def stiffness_fields(place, before, both, after, ply_stiffness):
    vmem = pl.BlockSpec(memory_space=pltpu.VMEM)
    smem = pl.BlockSpec(memory_space=pltpu.SMEM)
    return pl.pallas_call(
        stiffness_kernel,
        out_shape=jax.ShapeDtypeStruct((16, TILES * LANES), jnp.float32),
        in_specs=[smem, vmem, vmem, vmem, smem],
        out_specs=vmem,
        scratch_shapes=[pltpu.VMEM((8, LANES), jnp.float32)],
        cost_estimate=estimate(2),
        name="stiffness_fields",
    )(place, before, both, after, ply_stiffness)


AT = {0: 0, 1: 1, 2: 2, -1: 3, 3: 4, -2: 6, 4: 7}
PLACE = {index: x for x, index in AT.items()}
HALO = 5


def neighbour(tiles, index, side, place, full=False):
    t = tiles[index]
    lane = lax.broadcasted_iota(jnp.int32, t.shape, 1)
    slot = lane % WIDE
    roll = lambda v, s: pltpu.roll(v, s % LANES, 1)
    if side in (2, 3):
        y = (place + lane // WIDE) & 7
        if side == 2:
            return jnp.where(y > 0, roll(t, WIDE), 0.0)
        return jnp.where(y < 7, roll(t, -WIDE), 0.0)
    if index == HALO:
        if side < 2:
            return roll(t, 1 if side == 0 else -1)
        result = roll(t, -9) if side == 4 else roll(t, -7)
        for x in range(-1, 4) if full else range(SLAB):
            goal, by = (x + 6, x - 9) if side == 4 else (x + 1, x + 1)
            result = jnp.where(slot == goal, roll(tiles[AT[x]], by), result)
        if full:
            result = jnp.where(slot >= 13, roll(t, 7), result) if side == 4 else jnp.where(
                (slot >= 10) & (slot < 13), roll(t, 9), result
            )
        return result
    x = PLACE[index]
    if side < 2:
        return tiles[AT[x - 1 if side == 0 else x + 1]]
    if side == 4:
        return jnp.where(slot == 0, roll(tiles[HALO], -(x + 1)), roll(t, 1))
    return jnp.where(slot == WIDE - 1, roll(tiles[HALO], 9 - x), roll(t, -1))


def sides_of(index, outer):
    if index < outer:
        return range(6)
    return {3: (1,), 4: (0,), HALO: (4, 5), 6: (1,), 7: (0,)}[index]


def split(array):
    high = array.astype(jnp.bfloat16)
    low = (array - high.astype(jnp.float32)).astype(jnp.bfloat16)
    return jnp.concatenate([high, low], axis=0)


STEP = 32
FACE = 16
EVEN_BLOCKS = ((0, 32), (32, EVEN))


def tile_cols(t):
    return slice(LANES * t, LANES * (t + 1))


def face_stiffness(fields, faces, weights, place):
    tiles = [fields[:, tile_cols(t)] for t in range(TILES)]
    for t in range(TILES):
        for side in sides_of(t, INNER):
            value = (0.5 * weights[side // 2]) * (tiles[t] + neighbour(tiles, t, side, place, True))
            faces[side * FACE : (side + 1) * FACE, tile_cols(t)] = value


def apply_operator(src, dst, mixed, flux, scaled, acc, faces, inside, to_even, to_all, place, inner, outer):
    slots = src.shape[0]
    for start in range(0, inner * LANES, 512):
        cols = slice(start, min(start + 512, inner * LANES))
        mixed[:, cols] = jnp.dot(to_even[...], split(src[:, cols]), preferred_element_type=jnp.float32)

    def face(side, k, t):
        return faces[side * FACE + k : side * FACE + k + 1, tile_cols(t)]

    for low, high in EVEN_BLOCKS:
        flows = {}
        for t in range(inner):
            sides = sides_of(t, outer)
            total = {}
            for k in range(VARS):
                value = mixed[k * EVEN + low : k * EVEN + high, tile_cols(t)]
                for side in sides:
                    term = face(side, k, t) * value
                    total[side] = term if k == 0 else total[side] + term
            for side in sides:
                flux[side, low:high, tile_cols(t)] = total[side]
        even = [mixed[SPAN + low : SPAN + high, tile_cols(t)] for t in range(inner)]
        for t in range(outer):
            steps = [even[t] - neighbour(even, t, side, place) for side in range(6)]
            for k in range(VARS):
                total = face(0, k, t) * steps[0]
                for side in range(1, 6):
                    total = total + face(side, k, t) * steps[side]
                scaled[k * EVEN + low : k * EVEN + high, tile_cols(t)] = total
        for t in range(outer):
            total = None
            for side in range(6):
                opposite = FluxTiles(flux, side ^ 1, low, high)
                term = flux[side, low:high, tile_cols(t)] - neighbour(opposite, t, side, place)
                total = term if total is None else total + term
            scaled[SPAN + low : SPAN + high, tile_cols(t)] = total
    scaled[SPAN + EVEN : FULL, : outer * LANES] = jnp.zeros((FULL - SPAN - EVEN, outer * LANES), jnp.float32)
    for start in range(0, outer * LANES, 512):
        cols = slice(start, min(start + 512, outer * LANES))
        acc[:, cols] = jnp.dot(to_all[...], split(scaled[:, cols]), preferred_element_type=jnp.float32)

    def last(step, carry):
        rows = pl.ds(pl.multiple_of(step * STEP, STEP), STEP)
        tiles = [src[rows, tile_cols(t)] for t in range(inner)]
        for t in range(outer):
            result = tiles[t] + acc[rows, tile_cols(t)]
            for side in range(6):
                result = result + face(side, VARS, t) * (tiles[t] - neighbour(tiles, t, side, place))
            if t >= SLAB:
                result = inside[t] * result
            dst[rows, tile_cols(t)] = result
        return carry

    lax.fori_loop(0, slots // STEP, last, 0)


class FluxTiles:
    def __init__(self, flux, side, low, high):
        self.flux, self.side, self.low, self.high = flux, side, low, high

    def __getitem__(self, t):
        return self.flux[self.side, self.low : self.high, tile_cols(t)]


def apply_kernel(
    place, own, before, after, scale, unscale, to_even, to_all, fields, fibre, so_far,
    out, partial, field, first, second, mixed, flux, scaled, acc, faces, *, comp,
):
    slots = scale.shape[0]
    here = place[0]
    face_stiffness(fields, faces, [fibre[comp, d] for d in range(3)], here)
    lane = lax.broadcasted_iota(jnp.int32, (slots, LANES), 1)
    slot = lane % WIDE
    load = lambda ref, p: ref[pl.ds(p, slots, stride=ROWS), :]
    left = pltpu.roll(load(before, 3), LANES - 3, 1)
    right = pltpu.roll(load(after, 3), 3, 1)
    halo = jnp.where((slot == 0) | (slot == 5), left, load(own, 3))
    halo = jnp.where((slot == 4) | (slot == 9), right, halo)
    ordered = [
        load(own, 0), load(own, 1), load(own, 2), load(before, 2), load(after, 0), halo,
        load(before, 1), load(after, 1),
    ]
    for t, tile in enumerate(ordered):
        field[:, tile_cols(t)] = tile * scale[...]
    inside = {t: fields[VARS + 1 : VARS + 2, tile_cols(t)] for t in range(SLAB, INNER)}
    slot = lax.broadcasted_iota(jnp.int32, (1, LANES), 1) % WIDE
    used = ((slot >= 1) & (slot <= 3)) | ((slot >= 6) & (slot <= 8))
    inside[HALO] = jnp.where(used, inside[HALO], 0.0)
    scratch = (mixed, flux, scaled, acc, faces, inside, to_even, to_all, here)
    apply_operator(field, first, *scratch, TILES, INNER)
    apply_operator(first, second, *scratch, INNER, SLAB)
    sums = [jnp.zeros((1, LANES), jnp.float32)] * 5
    for p in range(SLAB):
        b = load(own, p)
        q = first[:, tile_cols(p)] * unscale[...]
        w = second[:, tile_cols(p)] * unscale[...]
        out[pl.ds(p, slots, stride=2 * SLAB), :] = q
        out[pl.ds(p + SLAB, slots, stride=2 * SLAB), :] = w
        for n, (one, two) in enumerate(((b, b), (b, q), (q, q), (b, w), (q, w))):
            sums[n] = sums[n] + jnp.sum(one * two, axis=0, keepdims=True)
    partial[...] = so_far[...] + jnp.concatenate(sums + [jnp.zeros((3, LANES), jnp.float32)], axis=0)


def apply_twice(comp, place, own, before, after, tables, fields, fibre, so_far):
    scale, unscale, to_even, to_all = tables
    slots = scale.shape[0]
    vmem = pl.BlockSpec(memory_space=pltpu.VMEM)
    smem = pl.BlockSpec(memory_space=pltpu.SMEM)
    f32 = lambda *shape: pltpu.VMEM(shape, jnp.float32)
    return pl.pallas_call(
        functools.partial(apply_kernel, comp=comp),
        out_shape=[
            jax.ShapeDtypeStruct((slots * 2 * SLAB, LANES), jnp.float32),
            jax.ShapeDtypeStruct((8, LANES), jnp.float32),
        ],
        in_specs=[smem] + [vmem] * 8 + [smem, vmem],
        out_specs=[vmem, vmem],
        scratch_shapes=[
            f32(slots, TILES * LANES),
            f32(slots, INNER * LANES),
            f32(slots, SLAB * LANES),
            f32(FULL, TILES * LANES),
            f32(6, EVEN, TILES * LANES),
            f32(FULL, INNER * LANES),
            f32(slots, INNER * LANES),
            f32(6 * FACE, TILES * LANES),
        ],
        compiler_params=pltpu.CompilerParams(vmem_limit_bytes=VMEM),
        cost_estimate=estimate(15),
        name="apply_twice",
    )(place, own, before, after, scale, unscale, to_even, to_all, fields, fibre, so_far)


def finish(field, images, coefs):
    modes = field.shape[0]
    per_part = modes * 2 * SLAB
    steps = 4

    def kernel(field, first_images, other_images, coefs, solution_field, residual):
        first = pl.program_id(0) * (modes // steps)

        def body(step, carry):
            for inner in range(UNROLL):
                mode = step * UNROLL + inner
                base = (first + mode) * 2 * SLAB
                for comp in range(COMPS):
                    source, stride, start = first_images, per_part, base
                    if comp > 0:
                        source, stride, start = other_images, 2 * per_part, base + (comp - 1) * per_part
                    for p in range(SLAB):
                        b = field[mode, comp, p]
                        q = swap_back(source[pl.ds(start + p, PARTS, stride=stride), :])
                        w = swap_back(source[pl.ds(start + p + SLAB, PARTS, stride=stride), :])
                        solution_field[mode, comp, p] = coefs[0] * b + coefs[1] * q
                        residual[mode, comp, p] = b + coefs[2] * q + coefs[3] * w
            return carry

        lax.fori_loop(0, modes // steps // UNROLL, body, 0)

    block = pl.BlockSpec((modes // steps,) + field.shape[1:], lambda i: (i, 0, 0, 0, 0))
    whole = pl.BlockSpec(memory_space=pltpu.VMEM)
    return pl.pallas_call(
        kernel,
        grid=(steps,),
        out_shape=[jax.ShapeDtypeStruct(field.shape, jnp.float32)] * 2,
        in_specs=[block, whole, whole, pl.BlockSpec(memory_space=pltpu.SMEM)],
        out_specs=[block, block],
        compiler_params=pltpu.CompilerParams(vmem_limit_bytes=VMEM),
        cost_estimate=estimate(6),
        name="finish",
    )(field, *images, coefs)


def mode_tables(coupling_table, slots):
    lower, upper, variable, code = (coupling_table[:, n] for n in range(4))
    slot = jnp.arange(slots, dtype=jnp.int32)
    is_lower = lower[:, None] == slot
    is_upper = upper[:, None] == slot
    degree = jnp.sum(jnp.where(is_upper, code[:, None], 0), axis=0)
    factor = jnp.where(code == 3, 6, code).astype(jnp.float32)[:, None]
    factorial = jnp.prod(jnp.where(is_upper, factor, 1.0), axis=0)
    root = (degree == 0) & jnp.any(is_lower, axis=0)
    even = (degree == 2) | root
    rank = jnp.sum(jnp.where(even[:, None] & (slot[:, None] < slot), 1, 0), axis=0)
    lower_even = jnp.any(is_lower & even, axis=1)
    is_even_end = jnp.where(lower_even[:, None], is_lower, is_upper)
    is_odd_end = jnp.where(lower_even[:, None], is_upper, is_lower)
    column = variable * EVEN + jnp.sum(jnp.where(is_even_end, rank, 0), axis=1)
    at_column = column[:, None] == jnp.arange(FULL, dtype=jnp.int32)
    down = code.astype(jnp.float32)[:, None]
    first = jnp.where(lower_even[:, None], 1.0, down)
    second = jnp.where(lower_even[:, None], down, 1.0)
    odd_ends = is_odd_end.astype(jnp.float32)
    columns = at_column.astype(jnp.float32)
    half = jnp.bfloat16
    to_even = jnp.dot(
        columns.astype(half).T, (odd_ends * first).astype(half), preferred_element_type=jnp.float32
    )
    to_odd = jnp.dot(
        odd_ends.astype(half).T, (columns * second).astype(half), preferred_element_type=jnp.float32
    )
    pick = (jnp.arange(FULL, dtype=jnp.int32)[:, None] - SPAN == rank) & even
    pick = pick.astype(jnp.float32)
    to_even = (to_even + pick).astype(half)
    to_all = (to_odd + pick.T).astype(half)
    scale = jnp.sqrt(factorial)
    wide = lambda v: jnp.broadcast_to(v[:, None], (slots, LANES))
    twice = lambda v: jnp.concatenate([v, v], axis=1)
    return wide(scale), wide(1.0 / scale), twice(to_even), twice(to_all)


def all_sum(value):
    for axis in ("space", "mode"):
        devices = lax.axis_size(axis)
        bit = 1
        while bit < devices:
            value = value + lax.ppermute(value, axis, [(i, i ^ bit) for i in range(devices)])
            bit *= 2
    return value


def transposed(right_side, mean_stiffness, ply_stiffness, fibre_weights, ply_map, coupling_table):
    slots = right_side.shape[0] * PARTS
    devices = lax.axis_size("space")
    up = [(i, i + 1) for i in range(devices - 1)]
    down = [(j, i) for i, j in up]
    swap = lambda v: lax.all_to_all(v, "mode", 0, 0, tiled=True)
    (first,) = pack(right_side, 0)
    both, second = pack(right_side, 1, mean_stiffness, ply_map)
    (third,) = pack(right_side, 2)
    own = [swap(p) for p in (first, second, third)]
    before = [lax.ppermute(p, "space", up) for p in own]
    after = [lax.ppermute(p, "space", down) for p in own]
    tables = mode_tables(coupling_table, slots)
    place = lax.axis_index("mode").astype(jnp.int32).reshape(1)
    both_before = lax.ppermute(both, "space", up)
    both_after = lax.ppermute(both, "space", down)
    fields = stiffness_fields(place, both_before, both, both_after, ply_stiffness)
    partial = jnp.zeros((8, LANES), jnp.float32)
    outs = []
    for comp in range(COMPS):
        out, partial = apply_twice(
            comp, place, own[comp], before[comp], after[comp], tables, fields, fibre_weights, partial
        )
        outs.append(out)
    halves = [o.reshape(PARTS, -1, LANES) for o in outs[1:]]
    images = [swap(outs[0]), swap(jnp.concatenate(halves, axis=1).reshape(-1, LANES))]
    bb, bq, qq, bw, qw = (jnp.sum(all_sum(partial)[n]) for n in range(5))
    step_one = bb / bq
    norm = bb - 2.0 * step_one * bq + step_one * step_one * qq
    beta = norm / bb
    grown = 1.0 + beta
    curve = grown * grown * bq - step_one * grown * (bw + qq) + step_one * step_one * qw
    step_two = norm / curve
    coefs = jnp.stack(
        [
            step_one + step_two * grown,
            -step_one * step_two,
            -step_one - step_two * grown,
            step_one * step_two,
        ]
    )
    return tuple(finish(right_side, images, coefs))


def on_device(right_side, mean_stiffness, ply_stiffness, fibre_weights, ply_map, coupling_table):
    args = (right_side, mean_stiffness, ply_stiffness, fibre_weights, ply_map, coupling_table)
    fits = right_side.shape[1:] == (COMPS, SLAB, 8, 128) and lax.axis_size("mode") == PARTS
    return transposed(*args) if fits else plain(*args)


def solution(mesh):
    return jax.shard_map(
        on_device,
        mesh=mesh,
        in_specs=(
            P("mode", None, "space", None, None),
            P("space", None, None),
            P(),
            P(),
            P("space", None, None),
            P(),
        ),
        out_specs=(P("mode", None, "space", None, None), P("mode", None, "space", None, None)),
        check_vma=False,
    )
```

```python
import functools

import jax
import jax.numpy as jnp
from jax import lax
from jax.experimental import pallas as pl
from jax.experimental.pallas import tpu as pltpu
from jax.sharding import PartitionSpec as P

VARS = 10
ITERS = 2


def extended(array, sides, width):
    for axis, dim in sides:
        devices, length = (lax.axis_size(axis), array.shape[dim])
        up = [(i, (i + 1) % devices) for i in range(devices - 1)]
        down = [(j, i) for i, j in up]
        last = lax.slice_in_dim(array, length - width, length, axis=dim)
        leading = lax.slice_in_dim(array, 0, width, axis=dim)
        before = lax.ppermute(last, axis, up)
        after = lax.ppermute(leading, axis, down)
        array = jnp.concatenate([before, array, after], axis=dim)
    return array


def window(array_in, dim_index, offset):
    slicers = [slice(None)] * (array_in.ndim - 3)
    for which in range(3):
        shift_by = offset if which == dim_index else 0
        length_here = array_in.shape[array_in.ndim - 3 + which] - 2
        slicers.append(slice(1 + shift_by, 1 + shift_by + length_here))
    return array_in[tuple(slicers)]


def diffuse(vector, stiffness, fibre_weights):
    vector_pads = [(0, 0)] * (vector.ndim - 2) + [(1, 1), (1, 1)]
    stiff_pads = [(0, 0)] * (stiffness.ndim - 2) + [(1, 1), (1, 1)]
    padded_v = jnp.pad(vector, vector_pads)
    padded_c = jnp.pad(stiffness, stiff_pads)
    centre = window(padded_v, 0, 0)
    middle = window(padded_c, 0, 0)
    result = None
    for dim_index in range(3):
        upper = (
            0.5
            * (middle + window(padded_c, dim_index, 1))
            * (centre - window(padded_v, dim_index, 1))
        )
        lower = (
            0.5
            * (middle + window(padded_c, dim_index, -1))
            * (centre - window(padded_v, dim_index, -1))
        )
        column = fibre_weights[:, dim_index].reshape(3, 1, 1, 1)
        term = column * (upper + lower)
        result = term if result is None else result + term
    return result


def squares(vector):
    return lax.psum(jnp.sum(vector * vector), ("mode", "space"))


def row_table(both_rows, both_cols, both_vars, both_weights, base, mode_dev, slots):
    local_rows = both_rows - base
    valid_rows = (local_rows >= 0) & (local_rows < mode_dev)
    local_rows = jnp.where(valid_rows, local_rows, mode_dev)
    row_coupling = jnp.zeros((VARS, mode_dev, slots), jnp.float32)
    row_coupling = row_coupling.at[both_vars, local_rows, both_cols].add(both_weights, mode="drop")
    return row_coupling.reshape(VARS * mode_dev, slots)


def plain(right_side, mean_stiffness, ply_stiffness, fibre_weights, ply_map, coupling_table):
    mode_dev = right_side.shape[0]
    slots = mode_dev * lax.axis_size("mode")
    base = lax.axis_index("mode") * mode_dev
    first_mode = coupling_table[:, 0]
    second_mode = coupling_table[:, 1]
    variable = coupling_table[:, 2]
    entry_weight = jnp.sqrt(coupling_table[:, 3].astype(jnp.float32))
    both_rows = jnp.concatenate([first_mode, second_mode])
    both_cols = jnp.concatenate([second_mode, first_mode])
    both_vars = jnp.concatenate([variable, variable])
    both_weights = jnp.concatenate([entry_weight, entry_weight])
    plies = jnp.arange(VARS, dtype=jnp.int32).reshape(VARS, 1, 1, 1)
    ply_fields = (ply_map[None] == plies).astype(jnp.float32) * ply_stiffness.reshape(VARS, 1, 1, 1)
    stiff_stack = jnp.concatenate([mean_stiffness[None], ply_fields], axis=0)
    stiff_rims = extended(stiff_stack, (("space", 1),), 1)
    stiff_rims = stiff_rims[:, None]
    row_coupling = row_table(both_rows, both_cols, both_vars, both_weights, base, mode_dev, slots)
    solution_field = jnp.zeros_like(right_side)
    residual = right_side
    direction = right_side
    norm_now = squares(residual)
    for iteration in range(ITERS):
        shard_piece = lax.all_gather(direction, "mode", axis=0, tiled=True)
        mixed = jnp.dot(
            row_coupling,
            shard_piece.reshape(shard_piece.shape[0], -1),
            precision=lax.Precision.HIGHEST,
            preferred_element_type=jnp.float32,
        )
        stacked = jnp.concatenate(
            [direction[None], mixed.reshape((VARS,) + direction.shape)], axis=0
        )
        padded = extended(stacked, (("space", 3),), 1)
        terms = diffuse(padded, stiff_rims[:, None], fibre_weights)
        image = direction + jnp.sum(terms, axis=0)
        step_size = norm_now / lax.psum(jnp.sum(direction * image), ("mode", "space"))
        solution_field = solution_field + step_size * direction
        residual = residual - step_size * image
        norm_next = squares(residual)
        direction = residual + norm_next / norm_now * direction
        norm_now = norm_next
    return (solution_field, residual)


COMPS = 3
SLAB = 3
PARTS = 8
WIDE = 16
ROWS = 4
EVEN = 1 + VARS * (VARS + 1) // 2
SPAN = VARS * EVEN
FULL = 624
INNER = 6
TILES = 8
LANES = 128
VMEM = 56 * 1024 * 1024


def lane_id():
    return lax.broadcasted_iota(jnp.int32, (8, LANES), 1)


def swap_out(tile):
    block = lane_id() // WIDE
    tile = pltpu.roll(tile, 0, 1, stride=WIDE, stride_axis=0)
    for bit in (1, 2, 4):
        tile = jnp.where((block & bit) != 0, pltpu.roll(tile, 8 - bit, 0), tile)
    return tile


def swap_back(tile):
    block = lane_id() // WIDE
    row = lax.broadcasted_iota(jnp.int32, (8, LANES), 0)
    for bit in (1, 2, 4):
        tile = jnp.where((block & bit) != 0, pltpu.roll(tile, bit, 0), tile)
    for bit in (1, 2, 4):
        tile = jnp.where((row & bit) != 0, pltpu.roll(tile, LANES - WIDE * bit, 1), tile)
    return tile


def halo_row(planes):
    lane = lane_id()
    slot = lane % WIDE
    halo = jnp.zeros((8, LANES), jnp.float32)
    for x, plane in planes.items():
        places = [(-1, x + 1), (WIDE, x + 6)]
        if 0 <= x < SLAB:
            places += [(-2, x + 10), (WIDE + 1, x + 13)]
        for offset, place in places:
            inside = (lane >= WIDE) if offset < 0 else (lane < LANES - WIDE)
            moved = pltpu.roll(plane, (place - offset) % LANES, 1)
            halo = jnp.where((slot == place) & inside, moved, halo)
    return halo


UNROLL = 6


GROUP = PARTS // 2


def send_halves(half, block, scratch, keep, send, sems):
    copies = []
    for member in range(GROUP):
        to = pl.ds(member * block, block)
        for n, (goal, which) in enumerate(((keep, half), (send, 1 - half))):
            start = pl.multiple_of((2 * member + which) * block, 8)
            source = scratch.at[pl.ds(start, block), :]
            copies.append(pltpu.make_async_copy(source, goal.at[to, :], sems.at[2 * member + n]))
    for copy in copies:
        copy.start()
    for copy in copies:
        copy.wait()


def pack_kernel(half, field, *refs):
    modes = field.shape[0]
    keep, send, out, sems = refs[-4:]
    if len(refs) > 4:
        mean, ply, both = refs[:3]
        for x in range(SLAB):
            both[0, x] = mean[x]
            both[1, x] = (ply[x] + 1).astype(jnp.float32)

    def body(step, carry):
        for inner in range(UNROLL):
            mode = step * UNROLL + inner
            planes = [field[mode, 0, x] for x in range(SLAB)]
            halo = halo_row(dict(enumerate(planes)))
            for p, tile in enumerate(planes + [halo]):
                out[pl.ds(mode * ROWS + p, PARTS, stride=ROWS * modes), :] = swap_out(tile)
        return carry

    lax.fori_loop(0, modes // UNROLL, body, 0)
    send_halves(half[0], ROWS * modes, out, keep, send, sems)


def estimate(micros):
    return pl.CostEstimate(flops=int(micros * 1e9), bytes_accessed=int(micros * 3e6), transcendentals=0)


def pack(half, field, comp, *stiffness):
    modes = field.shape[0]
    block = (modes, 1) + field.shape[2:]
    vmem = pl.BlockSpec(memory_space=pltpu.VMEM)
    shapes = [jax.ShapeDtypeStruct((2,) + s.shape, jnp.float32) for s in stiffness[:1]]
    out_specs = [vmem] * len(shapes) + [pl.BlockSpec(memory_space=pl.ANY)] * 2
    shapes += [jax.ShapeDtypeStruct((GROUP * modes * ROWS, LANES), jnp.float32)] * 2
    return pl.pallas_call(
        pack_kernel,
        grid=(1,),
        out_shape=shapes,
        in_specs=[pl.BlockSpec(memory_space=pltpu.SMEM), pl.BlockSpec(block, lambda i: (0, comp, 0, 0, 0))]
        + [vmem] * len(stiffness),
        out_specs=out_specs,
        scratch_shapes=[
            pltpu.VMEM((PARTS * modes * ROWS, LANES), jnp.float32),
            pltpu.SemaphoreType.DMA((PARTS,)),
        ],
        compiler_params=pltpu.CompilerParams(vmem_limit_bytes=VMEM),
        cost_estimate=estimate(2.5),
        name="pack",
    )(half, field, *stiffness)


def stiffness_kernel(place, before, both, after, ply_stiffness, fields, wide):
    rows = []
    for kind in range(2):
        planes = {-2: before[kind, 1], -1: before[kind, 2], 3: after[kind, 0], 4: after[kind, 1]}
        planes.update({x: both[kind, x] for x in range(SLAB)})
        halo = halo_row({x: planes[x] for x in range(-1, 4)})
        ordered = [planes[0], planes[1], planes[2], planes[-1], planes[3], halo, planes[-2], planes[4]]
        for t, tile in enumerate(ordered):
            wide[...] = swap_out(tile)
            rows.append(wide[pl.ds(place[0], 1), :])
    for t in range(TILES):
        mean, ply = rows[t], rows[TILES + t]
        cols = slice(LANES * t, LANES * (t + 1))
        for k in range(VARS):
            fields[k : k + 1, cols] = jnp.where(ply == k + 1.0, ply_stiffness[k], 0.0)
        fields[VARS : VARS + 1, cols] = mean
        fields[VARS + 1 : VARS + 2, cols] = jnp.where(ply > 0.0, 1.0, 0.0)
        fields[VARS + 2 : 16, cols] = jnp.zeros((4, LANES), jnp.float32)


def stiffness_fields(place, before, both, after, ply_stiffness):
    vmem = pl.BlockSpec(memory_space=pltpu.VMEM)
    smem = pl.BlockSpec(memory_space=pltpu.SMEM)
    return pl.pallas_call(
        stiffness_kernel,
        out_shape=jax.ShapeDtypeStruct((16, TILES * LANES), jnp.float32),
        in_specs=[smem, vmem, vmem, vmem, smem],
        out_specs=vmem,
        scratch_shapes=[pltpu.VMEM((8, LANES), jnp.float32)],
        cost_estimate=estimate(2),
        name="stiffness_fields",
    )(place, before, both, after, ply_stiffness)


AT = {0: 0, 1: 1, 2: 2, -1: 3, 3: 4, -2: 6, 4: 7}
PLACE = {index: x for x, index in AT.items()}
HALO = 5


def neighbour(tiles, index, side, place, full=False):
    t = tiles[index]
    lane = lax.broadcasted_iota(jnp.int32, t.shape, 1)
    slot = lane % WIDE
    roll = lambda v, s: pltpu.roll(v, s % LANES, 1)
    if side in (2, 3):
        y = (place + lane // WIDE) & 7
        if side == 2:
            return jnp.where(y > 0, roll(t, WIDE), 0.0)
        return jnp.where(y < 7, roll(t, -WIDE), 0.0)
    if index == HALO:
        if side < 2:
            return roll(t, 1 if side == 0 else -1)
        result = roll(t, -9) if side == 4 else roll(t, -7)
        for x in range(-1, 4) if full else range(SLAB):
            goal, by = (x + 6, x - 9) if side == 4 else (x + 1, x + 1)
            result = jnp.where(slot == goal, roll(tiles[AT[x]], by), result)
        if full:
            result = jnp.where(slot >= 13, roll(t, 7), result) if side == 4 else jnp.where(
                (slot >= 10) & (slot < 13), roll(t, 9), result
            )
        return result
    x = PLACE[index]
    if side < 2:
        return tiles[AT[x - 1 if side == 0 else x + 1]]
    if side == 4:
        return jnp.where(slot == 0, roll(tiles[HALO], -(x + 1)), roll(t, 1))
    return jnp.where(slot == WIDE - 1, roll(tiles[HALO], 9 - x), roll(t, -1))


def sides_of(index, outer):
    if index < outer:
        return range(6)
    return {3: (1,), 4: (0,), HALO: (4, 5), 6: (1,), 7: (0,)}[index]


def split(array):
    high = array.astype(jnp.bfloat16)
    low = (array - high.astype(jnp.float32)).astype(jnp.bfloat16)
    return jnp.concatenate([high, low], axis=0)


STEP = 32
FACE = 16
EVEN_BLOCKS = ((0, 32), (32, EVEN))


def tile_cols(t):
    return slice(LANES * t, LANES * (t + 1))


def face_stiffness(fields, faces, weights, place):
    tiles = [fields[:, tile_cols(t)] for t in range(TILES)]
    for t in range(TILES):
        for side in sides_of(t, INNER):
            value = (0.5 * weights[side // 2]) * (tiles[t] + neighbour(tiles, t, side, place, True))
            faces[side * FACE : (side + 1) * FACE, tile_cols(t)] = value


def apply_operator(src, dst, mixed, flux, scaled, acc, faces, inside, to_even, to_all, place, inner, outer):
    slots = src.shape[0]
    for start in range(0, inner * LANES, 512):
        cols = slice(start, min(start + 512, inner * LANES))
        mixed[:, cols] = jnp.dot(to_even[...], split(src[:, cols]), preferred_element_type=jnp.float32)

    def face(side, k, t):
        return faces[side * FACE + k : side * FACE + k + 1, tile_cols(t)]

    for low, high in EVEN_BLOCKS:
        flows = {}
        for t in range(inner):
            sides = sides_of(t, outer)
            total = {}
            for k in range(VARS):
                value = mixed[k * EVEN + low : k * EVEN + high, tile_cols(t)]
                for side in sides:
                    term = face(side, k, t) * value
                    total[side] = term if k == 0 else total[side] + term
            for side in sides:
                flux[side, low:high, tile_cols(t)] = total[side]
        even = [mixed[SPAN + low : SPAN + high, tile_cols(t)] for t in range(inner)]
        for t in range(outer):
            steps = [even[t] - neighbour(even, t, side, place) for side in range(6)]
            for k in range(VARS):
                total = face(0, k, t) * steps[0]
                for side in range(1, 6):
                    total = total + face(side, k, t) * steps[side]
                scaled[k * EVEN + low : k * EVEN + high, tile_cols(t)] = total
        for t in range(outer):
            total = None
            for side in range(6):
                opposite = FluxTiles(flux, side ^ 1, low, high)
                term = flux[side, low:high, tile_cols(t)] - neighbour(opposite, t, side, place)
                total = term if total is None else total + term
            scaled[SPAN + low : SPAN + high, tile_cols(t)] = total
    scaled[SPAN + EVEN : FULL, : outer * LANES] = jnp.zeros((FULL - SPAN - EVEN, outer * LANES), jnp.float32)
    for start in range(0, outer * LANES, 512):
        cols = slice(start, min(start + 512, outer * LANES))
        acc[:, cols] = jnp.dot(to_all[...], split(scaled[:, cols]), preferred_element_type=jnp.float32)

    def last(step, carry):
        rows = pl.ds(pl.multiple_of(step * STEP, STEP), STEP)
        tiles = [src[rows, tile_cols(t)] for t in range(inner)]
        for t in range(outer):
            result = tiles[t] + acc[rows, tile_cols(t)]
            for side in range(6):
                result = result + face(side, VARS, t) * (tiles[t] - neighbour(tiles, t, side, place))
            if t >= SLAB:
                result = inside[t] * result
            dst[rows, tile_cols(t)] = result
        return carry

    lax.fori_loop(0, slots // STEP, last, 0)


class FluxTiles:
    def __init__(self, flux, side, low, high):
        self.flux, self.side, self.low, self.high = flux, side, low, high

    def __getitem__(self, t):
        return self.flux[self.side, self.low : self.high, tile_cols(t)]


def apply_kernel(
    place, half, own, before, after, scale, unscale, to_even, to_all, fields, fibre, so_far,
    keep, send, partial, out, field, first, second, mixed, flux, scaled, acc, faces, sems, *, comp,
):
    slots = scale.shape[0]
    here = place[0]
    face_stiffness(fields, faces, [fibre[comp, d] for d in range(3)], here)
    lane = lax.broadcasted_iota(jnp.int32, (slots, LANES), 1)
    slot = lane % WIDE
    load = lambda ref, p: ref[pl.ds(p, slots, stride=ROWS), :]
    left = pltpu.roll(load(before, 3), LANES - 3, 1)
    right = pltpu.roll(load(after, 3), 3, 1)
    halo = jnp.where((slot == 0) | (slot == 5), left, load(own, 3))
    halo = jnp.where((slot == 4) | (slot == 9), right, halo)
    ordered = [
        load(own, 0), load(own, 1), load(own, 2), load(before, 2), load(after, 0), halo,
        load(before, 1), load(after, 1),
    ]
    for t, tile in enumerate(ordered):
        field[:, tile_cols(t)] = tile * scale[...]
    inside = {t: fields[VARS + 1 : VARS + 2, tile_cols(t)] for t in range(SLAB, INNER)}
    slot = lax.broadcasted_iota(jnp.int32, (1, LANES), 1) % WIDE
    used = ((slot >= 1) & (slot <= 3)) | ((slot >= 6) & (slot <= 8))
    inside[HALO] = jnp.where(used, inside[HALO], 0.0)
    scratch = (mixed, flux, scaled, acc, faces, inside, to_even, to_all, here)
    apply_operator(field, first, *scratch, TILES, INNER)
    apply_operator(first, second, *scratch, INNER, SLAB)
    for p in range(SLAB):
        out[pl.ds(p, slots, stride=2 * SLAB), :] = first[:, tile_cols(p)] * unscale[...]
        out[pl.ds(p + SLAB, slots, stride=2 * SLAB), :] = second[:, tile_cols(p)] * unscale[...]
    send_halves(half[0], slots // PARTS * 2 * SLAB, out, keep, send, sems)
    sums = [jnp.zeros((1, LANES), jnp.float32)] * 5
    for p in range(SLAB):
        b = load(own, p)
        q = first[:, tile_cols(p)] * unscale[...]
        w = second[:, tile_cols(p)] * unscale[...]
        for n, (one, two) in enumerate(((b, b), (b, q), (q, q), (b, w), (q, w))):
            sums[n] = sums[n] + jnp.sum(one * two, axis=0, keepdims=True)
    partial[...] = so_far[...] + jnp.concatenate(sums + [jnp.zeros((3, LANES), jnp.float32)], axis=0)


def apply_twice(comp, place, half, own, before, after, tables, fields, fibre, so_far):
    scale, unscale, to_even, to_all = tables
    slots = scale.shape[0]
    vmem = pl.BlockSpec(memory_space=pltpu.VMEM)
    smem = pl.BlockSpec(memory_space=pltpu.SMEM)
    f32 = lambda *shape: pltpu.VMEM(shape, jnp.float32)
    return pl.pallas_call(
        functools.partial(apply_kernel, comp=comp),
        out_shape=[jax.ShapeDtypeStruct((slots * SLAB, LANES), jnp.float32)] * 2
        + [jax.ShapeDtypeStruct((8, LANES), jnp.float32)],
        in_specs=[smem, smem] + [vmem] * 8 + [smem, vmem],
        out_specs=[pl.BlockSpec(memory_space=pl.ANY)] * 2 + [vmem],
        scratch_shapes=[
            f32(slots * 2 * SLAB, LANES),
            f32(slots, TILES * LANES),
            f32(slots, INNER * LANES),
            f32(slots, SLAB * LANES),
            f32(FULL, TILES * LANES),
            f32(6, EVEN, TILES * LANES),
            f32(FULL, INNER * LANES),
            f32(slots, INNER * LANES),
            f32(6 * FACE, TILES * LANES),
            pltpu.SemaphoreType.DMA((PARTS,)),
        ],
        compiler_params=pltpu.CompilerParams(vmem_limit_bytes=VMEM),
        cost_estimate=estimate(15),
        name="apply_twice",
    )(place, half, own, before, after, scale, unscale, to_even, to_all, fields, fibre, so_far)


def finish(field, images, coefs):
    modes = field.shape[0]
    per_part = modes * 2 * SLAB
    steps = 2

    def kernel(field, *refs):
        images, coefs, solution_field, residual = refs[:COMPS], refs[COMPS], refs[-2], refs[-1]
        first = pl.program_id(0) * (modes // steps)

        def body(step, carry):
            for inner in range(SLAB):
                mode = step * SLAB + inner
                base = (first + mode) * 2 * SLAB
                for comp in range(COMPS):
                    for p in range(SLAB):
                        b = field[mode, comp, p]
                        q = swap_back(images[comp][pl.ds(base + p, PARTS, stride=per_part), :])
                        w = swap_back(images[comp][pl.ds(base + p + SLAB, PARTS, stride=per_part), :])
                        solution_field[mode, comp, p] = coefs[0] * b + coefs[1] * q
                        residual[mode, comp, p] = b + coefs[2] * q + coefs[3] * w
            return carry

        lax.fori_loop(0, modes // steps // SLAB, body, 0)

    block = pl.BlockSpec((modes // steps,) + field.shape[1:], lambda i: (i, 0, 0, 0, 0))
    whole = pl.BlockSpec(memory_space=pltpu.VMEM)
    return pl.pallas_call(
        kernel,
        grid=(steps,),
        out_shape=[jax.ShapeDtypeStruct(field.shape, jnp.float32)] * 2,
        in_specs=[block] + [whole] * COMPS + [pl.BlockSpec(memory_space=pltpu.SMEM)],
        out_specs=[block, block],
        compiler_params=pltpu.CompilerParams(vmem_limit_bytes=VMEM),
        cost_estimate=estimate(6),
        name="finish",
    )(field, *images, coefs)


def mode_tables(coupling_table, slots):
    lower, upper, variable, code = (coupling_table[:, n] for n in range(4))
    order = jnp.arange(slots, dtype=jnp.int32).reshape(2, GROUP, slots // PARTS)
    slot = order.transpose(1, 0, 2).reshape(slots)
    is_lower = lower[:, None] == slot
    is_upper = upper[:, None] == slot
    degree = jnp.sum(jnp.where(is_upper, code[:, None], 0), axis=0)
    factor = jnp.where(code == 3, 6, code).astype(jnp.float32)[:, None]
    factorial = jnp.prod(jnp.where(is_upper, factor, 1.0), axis=0)
    root = (degree == 0) & jnp.any(is_lower, axis=0)
    even = (degree == 2) | root
    rank = jnp.sum(jnp.where(even[:, None] & (slot[:, None] < slot), 1, 0), axis=0)
    lower_even = jnp.any(is_lower & even, axis=1)
    is_even_end = jnp.where(lower_even[:, None], is_lower, is_upper)
    is_odd_end = jnp.where(lower_even[:, None], is_upper, is_lower)
    column = variable * EVEN + jnp.sum(jnp.where(is_even_end, rank, 0), axis=1)
    at_column = column[:, None] == jnp.arange(FULL, dtype=jnp.int32)
    down = code.astype(jnp.float32)[:, None]
    first = jnp.where(lower_even[:, None], 1.0, down)
    second = jnp.where(lower_even[:, None], down, 1.0)
    odd_ends = is_odd_end.astype(jnp.float32)
    columns = at_column.astype(jnp.float32)
    half = jnp.bfloat16
    to_even = jnp.dot(
        columns.astype(half).T, (odd_ends * first).astype(half), preferred_element_type=jnp.float32
    )
    to_odd = jnp.dot(
        odd_ends.astype(half).T, (columns * second).astype(half), preferred_element_type=jnp.float32
    )
    pick = (jnp.arange(FULL, dtype=jnp.int32)[:, None] - SPAN == rank) & even
    pick = pick.astype(jnp.float32)
    to_even = (to_even + pick).astype(half)
    to_all = (to_odd + pick.T).astype(half)
    scale = jnp.sqrt(factorial)
    wide = lambda v: jnp.broadcast_to(v[:, None], (slots, LANES))
    twice = lambda v: jnp.concatenate([v, v], axis=1)
    return wide(scale), wide(1.0 / scale), twice(to_even), twice(to_all)


def all_sum(value):
    for axis in ("space", "mode"):
        devices = lax.axis_size(axis)
        bit = 1
        while bit < devices:
            value = value + lax.ppermute(value, axis, [(i, i ^ bit) for i in range(devices)])
            bit *= 2
    return value


def transposed(right_side, mean_stiffness, ply_stiffness, fibre_weights, ply_map, coupling_table):
    slots = right_side.shape[0] * PARTS
    devices = lax.axis_size("space")
    up = [(i, i + 1) for i in range(devices - 1)]
    down = [(j, i) for i, j in up]
    index = lax.axis_index("mode").astype(jnp.int32)
    half = index // GROUP
    place = (2 * (index % GROUP) + half).reshape(1)
    groups = [list(range(GROUP)), list(range(GROUP, PARTS))]

    def exchange(keep, send):
        came = lax.ppermute(send, "mode", [(i, i ^ GROUP) for i in range(PARTS)])
        keep, came = (v.reshape(GROUP, -1, LANES) for v in (keep, came))
        both = jnp.where(
            half == 0, jnp.concatenate([keep, came], axis=1), jnp.concatenate([came, keep], axis=1)
        )
        both = lax.all_to_all(both, "mode", 0, 0, axis_index_groups=groups, tiled=True)
        return both.reshape(-1, LANES)

    half_row = half.reshape(1)
    first = pack(half_row, right_side, 0)
    both, *second = pack(half_row, right_side, 1, mean_stiffness, ply_map)
    third = pack(half_row, right_side, 2)
    own = [exchange(*p) for p in (first, second, third)]
    before = [lax.ppermute(p, "space", up) for p in own]
    after = [lax.ppermute(p, "space", down) for p in own]
    tables = mode_tables(coupling_table, slots)
    both_before = lax.ppermute(both, "space", up)
    both_after = lax.ppermute(both, "space", down)
    fields = stiffness_fields(place, both_before, both, both_after, ply_stiffness)
    partial = jnp.zeros((8, LANES), jnp.float32)
    images = []
    for comp in range(COMPS):
        keep, send, partial = apply_twice(
            comp, place, half_row, own[comp], before[comp], after[comp], tables, fields, fibre_weights,
            partial,
        )
        images.append(exchange(keep, send))
    bb, bq, qq, bw, qw = (jnp.sum(all_sum(partial)[n]) for n in range(5))
    step_one = bb / bq
    norm = bb - 2.0 * step_one * bq + step_one * step_one * qq
    beta = norm / bb
    grown = 1.0 + beta
    curve = grown * grown * bq - step_one * grown * (bw + qq) + step_one * step_one * qw
    step_two = norm / curve
    coefs = jnp.stack(
        [
            step_one + step_two * grown,
            -step_one * step_two,
            -step_one - step_two * grown,
            step_one * step_two,
        ]
    )
    return tuple(finish(right_side, images, coefs))


def on_device(right_side, mean_stiffness, ply_stiffness, fibre_weights, ply_map, coupling_table):
    args = (right_side, mean_stiffness, ply_stiffness, fibre_weights, ply_map, coupling_table)
    fits = right_side.shape[1:] == (COMPS, SLAB, 8, 128) and lax.axis_size("mode") == PARTS
    return transposed(*args) if fits else plain(*args)


def solution(mesh):
    return jax.shard_map(
        on_device,
        mesh=mesh,
        in_specs=(
            P("mode", None, "space", None, None),
            P("space", None, None),
            P(),
            P(),
            P("space", None, None),
            P(),
        ),
        out_specs=(P("mode", None, "space", None, None), P("mode", None, "space", None, None)),
        check_vma=False,
    )
```

```python
import functools

import jax
import jax.numpy as jnp
from jax import lax
from jax.experimental import pallas as pl
from jax.experimental.pallas import tpu as pltpu
from jax.sharding import PartitionSpec as P

VARS = 10
ITERS = 2


def extended(array, sides, width):
    for axis, dim in sides:
        devices, length = (lax.axis_size(axis), array.shape[dim])
        up = [(i, (i + 1) % devices) for i in range(devices - 1)]
        down = [(j, i) for i, j in up]
        last = lax.slice_in_dim(array, length - width, length, axis=dim)
        leading = lax.slice_in_dim(array, 0, width, axis=dim)
        before = lax.ppermute(last, axis, up)
        after = lax.ppermute(leading, axis, down)
        array = jnp.concatenate([before, array, after], axis=dim)
    return array


def window(array_in, dim_index, offset):
    slicers = [slice(None)] * (array_in.ndim - 3)
    for which in range(3):
        shift_by = offset if which == dim_index else 0
        length_here = array_in.shape[array_in.ndim - 3 + which] - 2
        slicers.append(slice(1 + shift_by, 1 + shift_by + length_here))
    return array_in[tuple(slicers)]


def diffuse(vector, stiffness, fibre_weights):
    vector_pads = [(0, 0)] * (vector.ndim - 2) + [(1, 1), (1, 1)]
    stiff_pads = [(0, 0)] * (stiffness.ndim - 2) + [(1, 1), (1, 1)]
    padded_v = jnp.pad(vector, vector_pads)
    padded_c = jnp.pad(stiffness, stiff_pads)
    centre = window(padded_v, 0, 0)
    middle = window(padded_c, 0, 0)
    result = None
    for dim_index in range(3):
        upper = (
            0.5
            * (middle + window(padded_c, dim_index, 1))
            * (centre - window(padded_v, dim_index, 1))
        )
        lower = (
            0.5
            * (middle + window(padded_c, dim_index, -1))
            * (centre - window(padded_v, dim_index, -1))
        )
        column = fibre_weights[:, dim_index].reshape(3, 1, 1, 1)
        term = column * (upper + lower)
        result = term if result is None else result + term
    return result


def squares(vector):
    return lax.psum(jnp.sum(vector * vector), ("mode", "space"))


def row_table(both_rows, both_cols, both_vars, both_weights, base, mode_dev, slots):
    local_rows = both_rows - base
    valid_rows = (local_rows >= 0) & (local_rows < mode_dev)
    local_rows = jnp.where(valid_rows, local_rows, mode_dev)
    row_coupling = jnp.zeros((VARS, mode_dev, slots), jnp.float32)
    row_coupling = row_coupling.at[both_vars, local_rows, both_cols].add(both_weights, mode="drop")
    return row_coupling.reshape(VARS * mode_dev, slots)


def plain(right_side, mean_stiffness, ply_stiffness, fibre_weights, ply_map, coupling_table):
    mode_dev = right_side.shape[0]
    slots = mode_dev * lax.axis_size("mode")
    base = lax.axis_index("mode") * mode_dev
    first_mode = coupling_table[:, 0]
    second_mode = coupling_table[:, 1]
    variable = coupling_table[:, 2]
    entry_weight = jnp.sqrt(coupling_table[:, 3].astype(jnp.float32))
    both_rows = jnp.concatenate([first_mode, second_mode])
    both_cols = jnp.concatenate([second_mode, first_mode])
    both_vars = jnp.concatenate([variable, variable])
    both_weights = jnp.concatenate([entry_weight, entry_weight])
    plies = jnp.arange(VARS, dtype=jnp.int32).reshape(VARS, 1, 1, 1)
    ply_fields = (ply_map[None] == plies).astype(jnp.float32) * ply_stiffness.reshape(VARS, 1, 1, 1)
    stiff_stack = jnp.concatenate([mean_stiffness[None], ply_fields], axis=0)
    stiff_rims = extended(stiff_stack, (("space", 1),), 1)
    stiff_rims = stiff_rims[:, None]
    row_coupling = row_table(both_rows, both_cols, both_vars, both_weights, base, mode_dev, slots)
    solution_field = jnp.zeros_like(right_side)
    residual = right_side
    direction = right_side
    norm_now = squares(residual)
    for iteration in range(ITERS):
        shard_piece = lax.all_gather(direction, "mode", axis=0, tiled=True)
        mixed = jnp.dot(
            row_coupling,
            shard_piece.reshape(shard_piece.shape[0], -1),
            precision=lax.Precision.HIGHEST,
            preferred_element_type=jnp.float32,
        )
        stacked = jnp.concatenate(
            [direction[None], mixed.reshape((VARS,) + direction.shape)], axis=0
        )
        padded = extended(stacked, (("space", 3),), 1)
        terms = diffuse(padded, stiff_rims[:, None], fibre_weights)
        image = direction + jnp.sum(terms, axis=0)
        step_size = norm_now / lax.psum(jnp.sum(direction * image), ("mode", "space"))
        solution_field = solution_field + step_size * direction
        residual = residual - step_size * image
        norm_next = squares(residual)
        direction = residual + norm_next / norm_now * direction
        norm_now = norm_next
    return (solution_field, residual)


COMPS = 3
SLAB = 3
PARTS = 8
WIDE = 16
ROWS = 4
EVEN = 1 + VARS * (VARS + 1) // 2
SPAN = VARS * EVEN
FULL = 624
INNER = 6
TILES = 8
LANES = 128
VMEM = 56 * 1024 * 1024


def lane_id():
    return lax.broadcasted_iota(jnp.int32, (8, LANES), 1)


def swap_out(tile):
    block = lane_id() // WIDE
    tile = pltpu.roll(tile, 0, 1, stride=WIDE, stride_axis=0)
    for bit in (1, 2, 4):
        tile = jnp.where((block & bit) != 0, pltpu.roll(tile, 8 - bit, 0), tile)
    return tile


def swap_back(tile):
    block = lane_id() // WIDE
    row = lax.broadcasted_iota(jnp.int32, (8, LANES), 0)
    for bit in (1, 2, 4):
        tile = jnp.where((block & bit) != 0, pltpu.roll(tile, bit, 0), tile)
    for bit in (1, 2, 4):
        tile = jnp.where((row & bit) != 0, pltpu.roll(tile, LANES - WIDE * bit, 1), tile)
    return tile


def halo_row(planes):
    lane = lane_id()
    slot = lane % WIDE
    halo = jnp.zeros((8, LANES), jnp.float32)
    for x, plane in planes.items():
        places = [(-1, x + 1), (WIDE, x + 6)]
        if 0 <= x < SLAB:
            places += [(-2, x + 10), (WIDE + 1, x + 13)]
        for offset, place in places:
            inside = (lane >= WIDE) if offset < 0 else (lane < LANES - WIDE)
            moved = pltpu.roll(plane, (place - offset) % LANES, 1)
            halo = jnp.where((slot == place) & inside, moved, halo)
    return halo


UNROLL = 6


ORDER = (0, 2, 4, 6, 1, 3, 5, 7)


def pack_kernel(field, *refs):
    modes = field.shape[0]
    out = refs[-1]
    if len(refs) == 4:
        mean, ply, both = refs[:3]
        for x in range(SLAB):
            both[0, x] = mean[x]
            both[1, x] = (ply[x] + 1).astype(jnp.float32)

    def body(step, carry):
        for inner in range(UNROLL):
            mode = step * UNROLL + inner
            planes = [field[mode, 0, x] for x in range(SLAB)]
            halo = halo_row(dict(enumerate(planes)))
            for p, tile in enumerate(planes + [halo]):
                out[pl.ds(mode * ROWS + p, PARTS, stride=ROWS * modes), :] = swap_out(tile)
        return carry

    lax.fori_loop(0, modes // UNROLL, body, 0)


def estimate(micros):
    return pl.CostEstimate(flops=int(micros * 1e9), bytes_accessed=int(micros * 3e6), transcendentals=0)


def pack(field, comp, stiffness=(), after=()):
    modes = field.shape[0]
    block = (modes, 1) + field.shape[2:]
    vmem = pl.BlockSpec(memory_space=pltpu.VMEM)
    shapes = [jax.ShapeDtypeStruct((2,) + s.shape, jnp.float32) for s in stiffness[:1]]
    shapes.append(jax.ShapeDtypeStruct((PARTS * modes * ROWS, LANES), jnp.float32))
    return pl.pallas_call(
        pack_kernel,
        grid=(1,),
        out_shape=shapes,
        in_specs=[pl.BlockSpec(block, lambda i: (0, comp, 0, 0, 0))]
        + [vmem] * len(stiffness)
        + [pl.BlockSpec(memory_space=pl.ANY)] * len(after),
        out_specs=[vmem] * len(shapes),
        compiler_params=pltpu.CompilerParams(vmem_limit_bytes=VMEM),
        cost_estimate=estimate(2.5),
        name="pack",
    )(field, *stiffness, *after)


def stiffness_kernel(place, before, both, after, ply_stiffness, fields, wide):
    rows = []
    for kind in range(2):
        planes = {-2: before[kind, 1], -1: before[kind, 2], 3: after[kind, 0], 4: after[kind, 1]}
        planes.update({x: both[kind, x] for x in range(SLAB)})
        halo = halo_row({x: planes[x] for x in range(-1, 4)})
        ordered = [planes[0], planes[1], planes[2], planes[-1], planes[3], halo, planes[-2], planes[4]]
        for t, tile in enumerate(ordered):
            wide[...] = swap_out(tile)
            rows.append(wide[pl.ds(place[0], 1), :])
    for t in range(TILES):
        mean, ply = rows[t], rows[TILES + t]
        cols = slice(LANES * t, LANES * (t + 1))
        for k in range(VARS):
            fields[k : k + 1, cols] = jnp.where(ply == k + 1.0, ply_stiffness[k], 0.0)
        fields[VARS : VARS + 1, cols] = mean
        fields[VARS + 1 : VARS + 2, cols] = jnp.where(ply > 0.0, 1.0, 0.0)
        fields[VARS + 2 : 16, cols] = jnp.zeros((4, LANES), jnp.float32)


def stiffness_fields(place, before, both, after, ply_stiffness):
    vmem = pl.BlockSpec(memory_space=pltpu.VMEM)
    smem = pl.BlockSpec(memory_space=pltpu.SMEM)
    return pl.pallas_call(
        stiffness_kernel,
        out_shape=jax.ShapeDtypeStruct((16, TILES * LANES), jnp.float32),
        in_specs=[smem, vmem, vmem, vmem, smem],
        out_specs=vmem,
        scratch_shapes=[pltpu.VMEM((8, LANES), jnp.float32)],
        cost_estimate=estimate(2),
        name="stiffness_fields",
    )(place, before, both, after, ply_stiffness)


AT = {0: 0, 1: 1, 2: 2, -1: 3, 3: 4, -2: 6, 4: 7}
PLACE = {index: x for x, index in AT.items()}
HALO = 5


def neighbour(tiles, index, side, place, full=False):
    t = tiles[index]
    lane = lax.broadcasted_iota(jnp.int32, t.shape, 1)
    slot = lane % WIDE
    roll = lambda v, s: pltpu.roll(v, s % LANES, 1)
    if side in (2, 3):
        y = (place + lane // WIDE) & 7
        if side == 2:
            return jnp.where(y > 0, roll(t, WIDE), 0.0)
        return jnp.where(y < 7, roll(t, -WIDE), 0.0)
    if index == HALO:
        if side < 2:
            return roll(t, 1 if side == 0 else -1)
        result = roll(t, -9) if side == 4 else roll(t, -7)
        for x in range(-1, 4) if full else range(SLAB):
            goal, by = (x + 6, x - 9) if side == 4 else (x + 1, x + 1)
            result = jnp.where(slot == goal, roll(tiles[AT[x]], by), result)
        if full:
            result = jnp.where(slot >= 13, roll(t, 7), result) if side == 4 else jnp.where(
                (slot >= 10) & (slot < 13), roll(t, 9), result
            )
        return result
    x = PLACE[index]
    if side < 2:
        return tiles[AT[x - 1 if side == 0 else x + 1]]
    if side == 4:
        return jnp.where(slot == 0, roll(tiles[HALO], -(x + 1)), roll(t, 1))
    return jnp.where(slot == WIDE - 1, roll(tiles[HALO], 9 - x), roll(t, -1))


def sides_of(index, outer):
    if index < outer:
        return range(6)
    return {3: (1,), 4: (0,), HALO: (4, 5), 6: (1,), 7: (0,)}[index]


def split(array):
    high = array.astype(jnp.bfloat16)
    low = (array - high.astype(jnp.float32)).astype(jnp.bfloat16)
    return jnp.concatenate([high, low], axis=0)


STEP = 32
FACE = 16
EVEN_BLOCKS = ((0, 32), (32, EVEN))


def tile_cols(t):
    return slice(LANES * t, LANES * (t + 1))


def face_stiffness(fields, faces, weights, place):
    tiles = [fields[:, tile_cols(t)] for t in range(TILES)]
    for t in range(TILES):
        for side in sides_of(t, INNER):
            value = (0.5 * weights[side // 2]) * (tiles[t] + neighbour(tiles, t, side, place, True))
            faces[side * FACE : (side + 1) * FACE, tile_cols(t)] = value


def apply_operator(src, dst, mixed, flux, scaled, acc, faces, inside, to_even, to_all, place, inner, outer):
    slots = src.shape[0]
    for start in range(0, inner * LANES, 512):
        cols = slice(start, min(start + 512, inner * LANES))
        mixed[:, cols] = jnp.dot(to_even[...], split(src[:, cols]), preferred_element_type=jnp.float32)

    def face(side, k, t):
        return faces[side * FACE + k : side * FACE + k + 1, tile_cols(t)]

    for low, high in EVEN_BLOCKS:
        flows = {}
        for t in range(inner):
            sides = sides_of(t, outer)
            total = {}
            for k in range(VARS):
                value = mixed[k * EVEN + low : k * EVEN + high, tile_cols(t)]
                for side in sides:
                    term = face(side, k, t) * value
                    total[side] = term if k == 0 else total[side] + term
            for side in sides:
                flux[side, low:high, tile_cols(t)] = total[side]
        even = [mixed[SPAN + low : SPAN + high, tile_cols(t)] for t in range(inner)]
        for t in range(outer):
            steps = [even[t] - neighbour(even, t, side, place) for side in range(6)]
            for k in range(VARS):
                total = face(0, k, t) * steps[0]
                for side in range(1, 6):
                    total = total + face(side, k, t) * steps[side]
                scaled[k * EVEN + low : k * EVEN + high, tile_cols(t)] = total
        for t in range(outer):
            total = None
            for side in range(6):
                opposite = FluxTiles(flux, side ^ 1, low, high)
                term = flux[side, low:high, tile_cols(t)] - neighbour(opposite, t, side, place)
                total = term if total is None else total + term
            scaled[SPAN + low : SPAN + high, tile_cols(t)] = total
    scaled[SPAN + EVEN : FULL, : outer * LANES] = jnp.zeros((FULL - SPAN - EVEN, outer * LANES), jnp.float32)
    for start in range(0, outer * LANES, 512):
        cols = slice(start, min(start + 512, outer * LANES))
        acc[:, cols] = jnp.dot(to_all[...], split(scaled[:, cols]), preferred_element_type=jnp.float32)

    def last(step, carry):
        rows = pl.ds(pl.multiple_of(step * STEP, STEP), STEP)
        tiles = [src[rows, tile_cols(t)] for t in range(inner)]
        for t in range(outer):
            result = tiles[t] + acc[rows, tile_cols(t)]
            for side in range(6):
                result = result + face(side, VARS, t) * (tiles[t] - neighbour(tiles, t, side, place))
            if t >= SLAB:
                result = inside[t] * result
            dst[rows, tile_cols(t)] = result
        return carry

    lax.fori_loop(0, slots // STEP, last, 0)


class FluxTiles:
    def __init__(self, flux, side, low, high):
        self.flux, self.side, self.low, self.high = flux, side, low, high

    def __getitem__(self, t):
        return self.flux[self.side, self.low : self.high, tile_cols(t)]


def apply_kernel(
    place, own, before, after, scale, unscale, to_even, to_all, fields, fibre, so_far,
    out, partial, field, first, second, mixed, flux, scaled, acc, faces, *, comp,
):
    slots = scale.shape[0]
    here = place[0]
    face_stiffness(fields, faces, [fibre[comp, d] for d in range(3)], here)
    lane = lax.broadcasted_iota(jnp.int32, (slots, LANES), 1)
    slot = lane % WIDE
    load = lambda ref, p: ref[pl.ds(p, slots, stride=ROWS), :]
    left = pltpu.roll(load(before, 3), LANES - 3, 1)
    right = pltpu.roll(load(after, 3), 3, 1)
    halo = jnp.where((slot == 0) | (slot == 5), left, load(own, 3))
    halo = jnp.where((slot == 4) | (slot == 9), right, halo)
    ordered = [
        load(own, 0), load(own, 1), load(own, 2), load(before, 2), load(after, 0), halo,
        load(before, 1), load(after, 1),
    ]
    for t, tile in enumerate(ordered):
        field[:, tile_cols(t)] = tile * scale[...]
    inside = {t: fields[VARS + 1 : VARS + 2, tile_cols(t)] for t in range(SLAB, INNER)}
    slot = lax.broadcasted_iota(jnp.int32, (1, LANES), 1) % WIDE
    used = ((slot >= 1) & (slot <= 3)) | ((slot >= 6) & (slot <= 8))
    inside[HALO] = jnp.where(used, inside[HALO], 0.0)
    scratch = (mixed, flux, scaled, acc, faces, inside, to_even, to_all, here)
    apply_operator(field, first, *scratch, TILES, INNER)
    apply_operator(first, second, *scratch, INNER, SLAB)
    sums = [jnp.zeros((1, LANES), jnp.float32)] * 5
    for p in range(SLAB):
        b = load(own, p)
        q = first[:, tile_cols(p)] * unscale[...]
        w = second[:, tile_cols(p)] * unscale[...]
        out[pl.ds(p, slots, stride=2 * SLAB), :] = q
        out[pl.ds(p + SLAB, slots, stride=2 * SLAB), :] = w
        for n, (one, two) in enumerate(((b, b), (b, q), (q, q), (b, w), (q, w))):
            sums[n] = sums[n] + jnp.sum(one * two, axis=0, keepdims=True)
    partial[...] = so_far[...] + jnp.concatenate(sums + [jnp.zeros((3, LANES), jnp.float32)], axis=0)


def apply_twice(comp, place, own, before, after, tables, fields, fibre, so_far):
    scale, unscale, to_even, to_all = tables
    slots = scale.shape[0]
    vmem = pl.BlockSpec(memory_space=pltpu.VMEM)
    smem = pl.BlockSpec(memory_space=pltpu.SMEM)
    f32 = lambda *shape: pltpu.VMEM(shape, jnp.float32)
    return pl.pallas_call(
        functools.partial(apply_kernel, comp=comp),
        out_shape=[
            jax.ShapeDtypeStruct((slots * 2 * SLAB, LANES), jnp.float32),
            jax.ShapeDtypeStruct((8, LANES), jnp.float32),
        ],
        in_specs=[smem] + [vmem] * 8 + [smem, vmem],
        out_specs=[vmem, vmem],
        scratch_shapes=[
            f32(slots, TILES * LANES),
            f32(slots, INNER * LANES),
            f32(slots, SLAB * LANES),
            f32(FULL, TILES * LANES),
            f32(6, EVEN, TILES * LANES),
            f32(FULL, INNER * LANES),
            f32(slots, INNER * LANES),
            f32(6 * FACE, TILES * LANES),
        ],
        compiler_params=pltpu.CompilerParams(vmem_limit_bytes=VMEM),
        cost_estimate=estimate(15),
        name="apply_twice",
    )(place, own, before, after, scale, unscale, to_even, to_all, fields, fibre, so_far)


def finish_kernel(field, image, coefs, *refs):
    modes = field.shape[0]
    solution_field, residual = refs[-2:]
    per_part = modes * 2 * SLAB

    def body(step, carry):
        for inner in range(UNROLL):
            mode = step * UNROLL + inner
            for p in range(SLAB):
                row = mode * 2 * SLAB + p
                b = field[mode, 0, p]
                q = swap_back(image[pl.ds(row, PARTS, stride=per_part), :])
                w = swap_back(image[pl.ds(row + SLAB, PARTS, stride=per_part), :])
                solution_field[mode, 0, p] = coefs[0] * b + coefs[1] * q
                residual[mode, 0, p] = b + coefs[2] * q + coefs[3] * w
        return carry

    lax.fori_loop(0, modes // UNROLL, body, 0)


def finish(field, comp, image, coefs, so_far):
    block = pl.BlockSpec((field.shape[0], 1) + field.shape[2:], lambda i: (0, comp, 0, 0, 0))
    vmem = pl.BlockSpec(memory_space=pltpu.VMEM)
    return pl.pallas_call(
        finish_kernel,
        grid=(1,),
        out_shape=[jax.ShapeDtypeStruct(field.shape, jnp.float32)] * 2,
        in_specs=[block, vmem, pl.BlockSpec(memory_space=pltpu.SMEM)]
        + [pl.BlockSpec(memory_space=pl.ANY)] * len(so_far),
        out_specs=[block, block],
        input_output_aliases={3 + n: n for n in range(len(so_far))},
        compiler_params=pltpu.CompilerParams(vmem_limit_bytes=VMEM),
        cost_estimate=estimate(2.5),
        name="finish",
    )(field, image, coefs, *so_far)


def mode_tables(coupling_table, slots):
    lower, upper, variable, code = (coupling_table[:, n] for n in range(4))
    within = jnp.arange(slots // PARTS, dtype=jnp.int32)
    first_modes = jnp.array(ORDER, jnp.int32) * (slots // PARTS)
    slot = (first_modes[:, None] + within).reshape(slots)
    is_lower = lower[:, None] == slot
    is_upper = upper[:, None] == slot
    degree = jnp.sum(jnp.where(is_upper, code[:, None], 0), axis=0)
    factor = jnp.where(code == 3, 6, code).astype(jnp.float32)[:, None]
    factorial = jnp.prod(jnp.where(is_upper, factor, 1.0), axis=0)
    root = (degree == 0) & jnp.any(is_lower, axis=0)
    even = (degree == 2) | root
    rank = jnp.sum(jnp.where(even[:, None] & (slot[:, None] < slot), 1, 0), axis=0)
    lower_even = jnp.any(is_lower & even, axis=1)
    is_even_end = jnp.where(lower_even[:, None], is_lower, is_upper)
    is_odd_end = jnp.where(lower_even[:, None], is_upper, is_lower)
    column = variable * EVEN + jnp.sum(jnp.where(is_even_end, rank, 0), axis=1)
    at_column = column[:, None] == jnp.arange(FULL, dtype=jnp.int32)
    down = code.astype(jnp.float32)[:, None]
    first = jnp.where(lower_even[:, None], 1.0, down)
    second = jnp.where(lower_even[:, None], down, 1.0)
    odd_ends = is_odd_end.astype(jnp.float32)
    columns = at_column.astype(jnp.float32)
    half = jnp.bfloat16
    to_even = jnp.dot(
        columns.astype(half).T, (odd_ends * first).astype(half), preferred_element_type=jnp.float32
    )
    to_odd = jnp.dot(
        odd_ends.astype(half).T, (columns * second).astype(half), preferred_element_type=jnp.float32
    )
    pick = (jnp.arange(FULL, dtype=jnp.int32)[:, None] - SPAN == rank) & even
    pick = pick.astype(jnp.float32)
    to_even = (to_even + pick).astype(half)
    to_all = (to_odd + pick.T).astype(half)
    scale = jnp.sqrt(factorial)
    wide = lambda v: jnp.broadcast_to(v[:, None], (slots, LANES))
    twice = lambda v: jnp.concatenate([v, v], axis=1)
    return wide(scale), wide(1.0 / scale), twice(to_even), twice(to_all)


def all_sum(value):
    for axis in ("space", "mode"):
        devices = lax.axis_size(axis)
        bit = 1
        while bit < devices:
            value = value + lax.ppermute(value, axis, [(i, i ^ bit) for i in range(devices)])
            bit *= 2
    return value


def transposed(right_side, mean_stiffness, ply_stiffness, fibre_weights, ply_map, coupling_table):
    slots = right_side.shape[0] * PARTS
    devices = lax.axis_size("space")
    up = [(i, i + 1) for i in range(devices - 1)]
    down = [(j, i) for i, j in up]
    index = lax.axis_index("mode").astype(jnp.int32)
    place = jnp.sum(jnp.where(jnp.array(ORDER) == index, jnp.arange(PARTS, dtype=jnp.int32), 0)).reshape(1)

    def swap(rows):
        return lax.all_to_all(rows, "mode", 0, 0, axis_index_groups=[list(ORDER)], tiled=True)

    def halo(rows):
        return lax.ppermute(rows, "space", up), lax.ppermute(rows, "space", down)

    (first,) = pack(right_side, 0)
    both, second = pack(right_side, 1, (mean_stiffness, ply_map))
    own = [swap(first), swap(second)]
    halos = [halo(rows) for rows in own]
    (third,) = pack(right_side, 2, (), halos[0])
    own.append(swap(third))
    halos.append(halo(own[2]))
    tables = mode_tables(coupling_table, slots)
    both_before = lax.ppermute(both, "space", up)
    both_after = lax.ppermute(both, "space", down)
    fields = stiffness_fields(place, both_before, both, both_after, ply_stiffness)
    partial = jnp.zeros((8, LANES), jnp.float32)
    images = []
    for comp in range(COMPS):
        out, partial = apply_twice(
            comp, place, own[comp], *halos[comp], tables, fields, fibre_weights, partial
        )
        images.append(swap(out))
    bb, bq, qq, bw, qw = (jnp.sum(all_sum(partial)[n]) for n in range(5))
    step_one = bb / bq
    norm = bb - 2.0 * step_one * bq + step_one * step_one * qq
    beta = norm / bb
    grown = 1.0 + beta
    curve = grown * grown * bq - step_one * grown * (bw + qq) + step_one * step_one * qw
    step_two = norm / curve
    coefs = jnp.stack(
        [
            step_one + step_two * grown,
            -step_one * step_two,
            -step_one - step_two * grown,
            step_one * step_two,
        ]
    )
    outputs = ()
    for comp in range(COMPS):
        outputs = finish(right_side, comp, images[comp], coefs, outputs)
    return tuple(outputs)


def on_device(right_side, mean_stiffness, ply_stiffness, fibre_weights, ply_map, coupling_table):
    args = (right_side, mean_stiffness, ply_stiffness, fibre_weights, ply_map, coupling_table)
    fits = right_side.shape[1:] == (COMPS, SLAB, 8, 128) and lax.axis_size("mode") == PARTS
    return transposed(*args) if fits else plain(*args)


def solution(mesh):
    return jax.shard_map(
        on_device,
        mesh=mesh,
        in_specs=(
            P("mode", None, "space", None, None),
            P("space", None, None),
            P(),
            P(),
            P("space", None, None),
            P(),
        ),
        out_specs=(P("mode", None, "space", None, None), P("mode", None, "space", None, None)),
        check_vma=False,
    )
```

```python
import functools

import jax
import jax.numpy as jnp
from jax import lax
from jax.experimental import pallas as pl
from jax.experimental.pallas import tpu as pltpu
from jax.sharding import PartitionSpec as P

VARS = 10
ITERS = 2


def extended(array, sides, width):
    for axis, dim in sides:
        devices, length = (lax.axis_size(axis), array.shape[dim])
        up = [(i, (i + 1) % devices) for i in range(devices - 1)]
        down = [(j, i) for i, j in up]
        last = lax.slice_in_dim(array, length - width, length, axis=dim)
        leading = lax.slice_in_dim(array, 0, width, axis=dim)
        before = lax.ppermute(last, axis, up)
        after = lax.ppermute(leading, axis, down)
        array = jnp.concatenate([before, array, after], axis=dim)
    return array


def window(array_in, dim_index, offset):
    slicers = [slice(None)] * (array_in.ndim - 3)
    for which in range(3):
        shift_by = offset if which == dim_index else 0
        length_here = array_in.shape[array_in.ndim - 3 + which] - 2
        slicers.append(slice(1 + shift_by, 1 + shift_by + length_here))
    return array_in[tuple(slicers)]


def diffuse(vector, stiffness, fibre_weights):
    vector_pads = [(0, 0)] * (vector.ndim - 2) + [(1, 1), (1, 1)]
    stiff_pads = [(0, 0)] * (stiffness.ndim - 2) + [(1, 1), (1, 1)]
    padded_v = jnp.pad(vector, vector_pads)
    padded_c = jnp.pad(stiffness, stiff_pads)
    centre = window(padded_v, 0, 0)
    middle = window(padded_c, 0, 0)
    result = None
    for dim_index in range(3):
        upper = (
            0.5
            * (middle + window(padded_c, dim_index, 1))
            * (centre - window(padded_v, dim_index, 1))
        )
        lower = (
            0.5
            * (middle + window(padded_c, dim_index, -1))
            * (centre - window(padded_v, dim_index, -1))
        )
        column = fibre_weights[:, dim_index].reshape(3, 1, 1, 1)
        term = column * (upper + lower)
        result = term if result is None else result + term
    return result


def squares(vector):
    return lax.psum(jnp.sum(vector * vector), ("mode", "space"))


def row_table(both_rows, both_cols, both_vars, both_weights, base, mode_dev, slots):
    local_rows = both_rows - base
    valid_rows = (local_rows >= 0) & (local_rows < mode_dev)
    local_rows = jnp.where(valid_rows, local_rows, mode_dev)
    row_coupling = jnp.zeros((VARS, mode_dev, slots), jnp.float32)
    row_coupling = row_coupling.at[both_vars, local_rows, both_cols].add(both_weights, mode="drop")
    return row_coupling.reshape(VARS * mode_dev, slots)


def plain(right_side, mean_stiffness, ply_stiffness, fibre_weights, ply_map, coupling_table):
    mode_dev = right_side.shape[0]
    slots = mode_dev * lax.axis_size("mode")
    base = lax.axis_index("mode") * mode_dev
    first_mode = coupling_table[:, 0]
    second_mode = coupling_table[:, 1]
    variable = coupling_table[:, 2]
    entry_weight = jnp.sqrt(coupling_table[:, 3].astype(jnp.float32))
    both_rows = jnp.concatenate([first_mode, second_mode])
    both_cols = jnp.concatenate([second_mode, first_mode])
    both_vars = jnp.concatenate([variable, variable])
    both_weights = jnp.concatenate([entry_weight, entry_weight])
    plies = jnp.arange(VARS, dtype=jnp.int32).reshape(VARS, 1, 1, 1)
    ply_fields = (ply_map[None] == plies).astype(jnp.float32) * ply_stiffness.reshape(VARS, 1, 1, 1)
    stiff_stack = jnp.concatenate([mean_stiffness[None], ply_fields], axis=0)
    stiff_rims = extended(stiff_stack, (("space", 1),), 1)
    stiff_rims = stiff_rims[:, None]
    row_coupling = row_table(both_rows, both_cols, both_vars, both_weights, base, mode_dev, slots)
    solution_field = jnp.zeros_like(right_side)
    residual = right_side
    direction = right_side
    norm_now = squares(residual)
    for iteration in range(ITERS):
        shard_piece = lax.all_gather(direction, "mode", axis=0, tiled=True)
        mixed = jnp.dot(
            row_coupling,
            shard_piece.reshape(shard_piece.shape[0], -1),
            precision=lax.Precision.HIGHEST,
            preferred_element_type=jnp.float32,
        )
        stacked = jnp.concatenate(
            [direction[None], mixed.reshape((VARS,) + direction.shape)], axis=0
        )
        padded = extended(stacked, (("space", 3),), 1)
        terms = diffuse(padded, stiff_rims[:, None], fibre_weights)
        image = direction + jnp.sum(terms, axis=0)
        step_size = norm_now / lax.psum(jnp.sum(direction * image), ("mode", "space"))
        solution_field = solution_field + step_size * direction
        residual = residual - step_size * image
        norm_next = squares(residual)
        direction = residual + norm_next / norm_now * direction
        norm_now = norm_next
    return (solution_field, residual)


COMPS = 3
SLAB = 3
PARTS = 8
WIDE = 16
ROWS = 4
EVEN = 1 + VARS * (VARS + 1) // 2
SPAN = VARS * EVEN
FULL = 624
INNER = 6
TILES = 8
LANES = 128
VMEM = 56 * 1024 * 1024


def lane_id():
    return lax.broadcasted_iota(jnp.int32, (8, LANES), 1)


def swap_out(tile):
    block = lane_id() // WIDE
    tile = pltpu.roll(tile, 0, 1, stride=WIDE, stride_axis=0)
    for bit in (1, 2, 4):
        tile = jnp.where((block & bit) != 0, pltpu.roll(tile, 8 - bit, 0), tile)
    return tile


def swap_back(tile):
    block = lane_id() // WIDE
    row = lax.broadcasted_iota(jnp.int32, (8, LANES), 0)
    for bit in (1, 2, 4):
        tile = jnp.where((block & bit) != 0, pltpu.roll(tile, bit, 0), tile)
    for bit in (1, 2, 4):
        tile = jnp.where((row & bit) != 0, pltpu.roll(tile, LANES - WIDE * bit, 1), tile)
    return tile


def halo_row(planes):
    lane = lane_id()
    slot = lane % WIDE
    halo = jnp.zeros((8, LANES), jnp.float32)
    for x, plane in planes.items():
        places = [(-1, x + 1), (WIDE, x + 6)]
        if 0 <= x < SLAB:
            places += [(-2, x + 10), (WIDE + 1, x + 13)]
        for offset, place in places:
            inside = (lane >= WIDE) if offset < 0 else (lane < LANES - WIDE)
            moved = pltpu.roll(plane, (place - offset) % LANES, 1)
            halo = jnp.where((slot == place) & inside, moved, halo)
    return halo


UNROLL = 6


ORDER = tuple(range(PARTS))


def pack_kernel(field, *refs):
    modes = field.shape[0]
    out = refs[-1]
    if len(refs) > 1:
        mean, ply, both = refs[0], refs[1], refs[-2]
        for x in range(SLAB):
            both[0, x] = mean[x]
            both[1, x] = (ply[x] + 1).astype(jnp.float32)

    def body(step, carry):
        for inner in range(UNROLL):
            mode = step * UNROLL + inner
            planes = [field[mode, 0, x] for x in range(SLAB)]
            halo = halo_row(dict(enumerate(planes)))
            for p, tile in enumerate(planes + [halo]):
                out[pl.ds(mode * ROWS + p, PARTS, stride=ROWS * modes), :] = swap_out(tile)
        return carry

    lax.fori_loop(0, modes // UNROLL, body, 0)


def estimate(micros):
    return pl.CostEstimate(flops=int(micros * 1e9), bytes_accessed=int(micros * 3e6), transcendentals=0)


def pack(field, comp, stiffness=(), after=()):
    modes = field.shape[0]
    block = (modes, 1) + field.shape[2:]
    vmem = pl.BlockSpec(memory_space=pltpu.VMEM)
    shapes = [jax.ShapeDtypeStruct((2,) + s.shape, jnp.float32) for s in stiffness[:1]]
    shapes.append(jax.ShapeDtypeStruct((PARTS * modes * ROWS, LANES), jnp.float32))
    return pl.pallas_call(
        pack_kernel,
        grid=(1,),
        out_shape=shapes,
        in_specs=[pl.BlockSpec(block, lambda i: (0, comp, 0, 0, 0))]
        + [vmem] * len(stiffness)
        + [pl.BlockSpec(memory_space=pl.ANY)] * len(after),
        out_specs=[vmem] * len(shapes),
        compiler_params=pltpu.CompilerParams(vmem_limit_bytes=VMEM),
        cost_estimate=estimate(2.5),
        name="pack",
    )(field, *stiffness, *after)


def stiffness_kernel(place, before, both, after, ply_stiffness, fields, wide):
    rows = []
    for kind in range(2):
        planes = {-2: before[kind, 1], -1: before[kind, 2], 3: after[kind, 0], 4: after[kind, 1]}
        planes.update({x: both[kind, x] for x in range(SLAB)})
        halo = halo_row({x: planes[x] for x in range(-1, 4)})
        ordered = [planes[0], planes[1], planes[2], planes[-1], planes[3], halo, planes[-2], planes[4]]
        for t, tile in enumerate(ordered):
            wide[...] = swap_out(tile)
            rows.append(wide[pl.ds(place[0], 1), :])
    for t in range(TILES):
        mean, ply = rows[t], rows[TILES + t]
        cols = slice(LANES * t, LANES * (t + 1))
        for k in range(VARS):
            fields[k : k + 1, cols] = jnp.where(ply == k + 1.0, ply_stiffness[k], 0.0)
        fields[VARS : VARS + 1, cols] = mean
        fields[VARS + 1 : VARS + 2, cols] = jnp.where(ply > 0.0, 1.0, 0.0)
        fields[VARS + 2 : 16, cols] = jnp.zeros((4, LANES), jnp.float32)


def stiffness_fields(place, before, both, after, ply_stiffness):
    vmem = pl.BlockSpec(memory_space=pltpu.VMEM)
    smem = pl.BlockSpec(memory_space=pltpu.SMEM)
    return pl.pallas_call(
        stiffness_kernel,
        out_shape=jax.ShapeDtypeStruct((16, TILES * LANES), jnp.float32),
        in_specs=[smem, vmem, vmem, vmem, smem],
        out_specs=vmem,
        scratch_shapes=[pltpu.VMEM((8, LANES), jnp.float32)],
        cost_estimate=estimate(2),
        name="stiffness_fields",
    )(place, before, both, after, ply_stiffness)


AT = {0: 0, 1: 1, 2: 2, -1: 3, 3: 4, -2: 6, 4: 7}
PLACE = {index: x for x, index in AT.items()}
HALO = 5


def neighbour(tiles, index, side, place, full=False, wrap=False):
    t = tiles[index]
    lane = lax.broadcasted_iota(jnp.int32, t.shape, 1)
    slot = lane % WIDE
    roll = lambda v, s: pltpu.roll(v, s % LANES, 1)
    if side in (2, 3) and wrap:
        return roll(t, WIDE if side == 2 else -WIDE)
    if side in (2, 3):
        y = (place + lane // WIDE) & 7
        if side == 2:
            return jnp.where(y > 0, roll(t, WIDE), 0.0)
        return jnp.where(y < 7, roll(t, -WIDE), 0.0)
    if index == HALO:
        if side < 2:
            return roll(t, 1 if side == 0 else -1)
        result = roll(t, -9) if side == 4 else roll(t, -7)
        for x in range(-1, 4) if full else range(SLAB):
            goal, by = (x + 6, x - 9) if side == 4 else (x + 1, x + 1)
            result = jnp.where(slot == goal, roll(tiles[AT[x]], by), result)
        if full:
            result = jnp.where(slot >= 13, roll(t, 7), result) if side == 4 else jnp.where(
                (slot >= 10) & (slot < 13), roll(t, 9), result
            )
        return result
    x = PLACE[index]
    if side < 2:
        return tiles[AT[x - 1 if side == 0 else x + 1]]
    if side == 4:
        return jnp.where(slot == 0, roll(tiles[HALO], -(x + 1)), roll(t, 1))
    return jnp.where(slot == WIDE - 1, roll(tiles[HALO], 9 - x), roll(t, -1))


def sides_of(index, outer):
    if index < outer:
        return range(6)
    return {3: (1,), 4: (0,), HALO: (4, 5), 6: (1,), 7: (0,)}[index]


def split(array):
    high = array.astype(jnp.bfloat16)
    low = (array - high.astype(jnp.float32)).astype(jnp.bfloat16)
    return jnp.concatenate([high, low], axis=0)


STEP = 16
FACE = 16
CENTRE = 6 * FACE
EVEN_BLOCKS = ((0, 32), (32, EVEN))


def tile_cols(t):
    return slice(LANES * t, LANES * (t + 1))


def face_stiffness(fields, faces, weights, place):
    tiles = [fields[:, tile_cols(t)] for t in range(TILES)]
    for t in range(TILES):
        for side in sides_of(t, INNER):
            value = (0.5 * weights[side // 2]) * (tiles[t] + neighbour(tiles, t, side, place, True))
            faces[side * FACE : (side + 1) * FACE, tile_cols(t)] = value
        if t < INNER:
            centre = 1.0 + sum(faces[side * FACE + VARS : side * FACE + VARS + 1, tile_cols(t)] for side in range(6))
            faces[CENTRE : CENTRE + 1, tile_cols(t)] = centre
            lane = lax.broadcasted_iota(jnp.int32, (1, LANES), 1)
            y = (place + lane // WIDE) & 7
            for side, edge in ((2, 0), (3, 7)):
                row = side * FACE + VARS
                faces[row + 1 : row + 2, tile_cols(t)] = jnp.where(
                    y == edge, 0.0, faces[row : row + 1, tile_cols(t)]
                )


def apply_operator(src, dst, mixed, flux, scaled, acc, faces, inside, to_even, to_all, place, inner, outer):
    slots = src.shape[0]
    for start in range(0, inner * LANES, 512):
        cols = slice(start, min(start + 512, inner * LANES))
        mixed[:, cols] = jnp.dot(to_even[...], split(src[:, cols]), preferred_element_type=jnp.float32)

    def face(side, k, t):
        return faces[side * FACE + k : side * FACE + k + 1, tile_cols(t)]

    for low, high in EVEN_BLOCKS:
        flows = {}
        for t in range(inner):
            sides = sides_of(t, outer)
            total = {}
            for k in range(VARS):
                value = mixed[k * EVEN + low : k * EVEN + high, tile_cols(t)]
                for side in sides:
                    term = face(side, k, t) * value
                    total[side] = term if k == 0 else total[side] + term
            for side in sides:
                flux[side, low:high, tile_cols(t)] = total[side]
        even = [mixed[SPAN + low : SPAN + high, tile_cols(t)] for t in range(inner)]
        for t in range(outer):
            steps = [even[t] - neighbour(even, t, side, place) for side in range(6)]
            for k in range(VARS):
                total = face(0, k, t) * steps[0]
                for side in range(1, 6):
                    total = total + face(side, k, t) * steps[side]
                scaled[k * EVEN + low : k * EVEN + high, tile_cols(t)] = total
        for t in range(outer):
            total = None
            for side in range(6):
                opposite = FluxTiles(flux, side ^ 1, low, high)
                term = flux[side, low:high, tile_cols(t)] - neighbour(opposite, t, side, place)
                total = term if total is None else total + term
            scaled[SPAN + low : SPAN + high, tile_cols(t)] = total
    scaled[SPAN + EVEN : FULL, : outer * LANES] = jnp.zeros((FULL - SPAN - EVEN, outer * LANES), jnp.float32)
    for start in range(0, outer * LANES, 512):
        cols = slice(start, min(start + 512, outer * LANES))
        acc[:, cols] = jnp.dot(to_all[...], split(scaled[:, cols]), preferred_element_type=jnp.float32)

    def last(step, carry):
        rows = pl.ds(pl.multiple_of(step * STEP, STEP), STEP)
        tiles = [src[rows, tile_cols(t)] for t in range(inner)]
        for t in range(outer):
            result = acc[rows, tile_cols(t)] + faces[CENTRE : CENTRE + 1, tile_cols(t)] * tiles[t]
            for side in range(6):
                row = VARS + 1 if side in (2, 3) else VARS
                result = result - face(side, row, t) * neighbour(tiles, t, side, place, wrap=True)
            if t >= SLAB:
                result = inside[t] * result
            dst[rows, tile_cols(t)] = result
        return carry

    lax.fori_loop(0, slots // STEP, last, 0)


class FluxTiles:
    def __init__(self, flux, side, low, high):
        self.flux, self.side, self.low, self.high = flux, side, low, high

    def __getitem__(self, t):
        return self.flux[self.side, self.low : self.high, tile_cols(t)]


def apply_kernel(
    place, own, before, after, scale, unscale, to_even, to_all, fields, fibre, so_far, *refs, comp, block, offset,
):
    rows_out, partial, out, field, first, second, mixed, flux, scaled, acc, faces, sems = refs[-12:]
    slots = scale.shape[0]
    here = place[0]
    face_stiffness(fields, faces, [fibre[comp, d] for d in range(3)], here)
    lane = lax.broadcasted_iota(jnp.int32, (slots, LANES), 1)
    slot = lane % WIDE
    load = lambda ref, p: ref[pl.ds(p, slots, stride=ROWS), :]
    left = pltpu.roll(load(before, 3), LANES - 3, 1)
    right = pltpu.roll(load(after, 3), 3, 1)
    halo = jnp.where((slot == 0) | (slot == 5), left, load(own, 3))
    halo = jnp.where((slot == 4) | (slot == 9), right, halo)
    ordered = [
        load(own, 0), load(own, 1), load(own, 2), load(before, 2), load(after, 0), halo,
        load(before, 1), load(after, 1),
    ]
    for t, tile in enumerate(ordered):
        field[:, tile_cols(t)] = tile * scale[...]
    inside = {t: fields[VARS + 1 : VARS + 2, tile_cols(t)] for t in range(SLAB, INNER)}
    slot = lax.broadcasted_iota(jnp.int32, (1, LANES), 1) % WIDE
    used = ((slot >= 1) & (slot <= 3)) | ((slot >= 6) & (slot <= 8))
    inside[HALO] = jnp.where(used, inside[HALO], 0.0)
    scratch = (mixed, flux, scaled, acc, faces, inside, to_even, to_all, here)
    apply_operator(field, first, *scratch, TILES, INNER)
    apply_operator(first, second, *scratch, INNER, SLAB)
    for p in range(SLAB):
        out[pl.ds(p, slots, stride=2 * SLAB), :] = first[:, tile_cols(p)] * unscale[...]
        out[pl.ds(p + SLAB, slots, stride=2 * SLAB), :] = second[:, tile_cols(p)] * unscale[...]
    part = slots // PARTS * 2 * SLAB
    copies = [
        pltpu.make_async_copy(
            out.at[pl.ds(n * part, part), :], rows_out.at[pl.ds(n * block + offset, part), :], sems.at[n]
        )
        for n in range(PARTS)
    ]
    for copy in copies:
        copy.start()
    sums = [jnp.zeros((1, LANES), jnp.float32)] * 5
    for p in range(SLAB):
        b = load(own, p)
        q = first[:, tile_cols(p)] * unscale[...]
        w = second[:, tile_cols(p)] * unscale[...]
        for n, (one, two) in enumerate(((b, b), (b, q), (q, q), (b, w), (q, w))):
            sums[n] = sums[n] + jnp.sum(one * two, axis=0, keepdims=True)
    partial[...] = so_far[...] + jnp.concatenate(sums + [jnp.zeros((3, LANES), jnp.float32)], axis=0)
    for copy in copies:
        copy.wait()


def apply_twice(comp, place, own, before, after, tables, fields, fibre, so_far, block, offset, rows_out=()):
    scale, unscale, to_even, to_all = tables
    slots = scale.shape[0]
    vmem = pl.BlockSpec(memory_space=pltpu.VMEM)
    smem = pl.BlockSpec(memory_space=pltpu.SMEM)
    whole = pl.BlockSpec(memory_space=pl.ANY)
    f32 = lambda *shape: pltpu.VMEM(shape, jnp.float32)
    return pl.pallas_call(
        functools.partial(apply_kernel, comp=comp, block=block, offset=offset),
        out_shape=[
            jax.ShapeDtypeStruct((PARTS * block, LANES), jnp.float32),
            jax.ShapeDtypeStruct((8, LANES), jnp.float32),
        ],
        in_specs=[smem] + [vmem] * 8 + [smem, vmem] + [whole] * len(rows_out),
        out_specs=[whole, vmem],
        input_output_aliases={11: 0} if rows_out else {},
        scratch_shapes=[
            f32(slots * 2 * SLAB, LANES),
            f32(slots, TILES * LANES),
            f32(slots, INNER * LANES),
            f32(slots, SLAB * LANES),
            f32(FULL, TILES * LANES),
            f32(6, EVEN, TILES * LANES),
            f32(FULL, INNER * LANES),
            f32(slots, INNER * LANES),
            f32(6 * FACE + 8, TILES * LANES),
            pltpu.SemaphoreType.DMA((PARTS,)),
        ],
        compiler_params=pltpu.CompilerParams(vmem_limit_bytes=VMEM),
        cost_estimate=estimate(15),
        name="apply_twice",
    )(place, own, before, after, scale, unscale, to_even, to_all, fields, fibre, so_far, *rows_out)


def combination(total):
    bb, bq, qq, bw, qw = (jnp.sum(total[n : n + 1, :], axis=1, keepdims=True) for n in range(5))
    step_one = bb / bq
    norm = bb - 2.0 * step_one * bq + step_one * step_one * qq
    grown = 1.0 + norm / bb
    curve = grown * grown * bq - step_one * grown * (bw + qq) + step_one * step_one * qw
    step_two = norm / curve
    spread = lambda v: jnp.broadcast_to(v, (8, LANES))
    sole = spread(step_one + step_two * grown)
    cross = spread(step_one * step_two)
    return sole, cross


STEPS = 3


def finish_kernel(field, image, images, total, solution_field, residual):
    modes = field.shape[0]
    part = STEPS * modes * 2 * SLAB
    sole, cross = combination(total)

    def body(step, carry):
        for inner in range(SLAB):
            mode = step * SLAB + inner
            for comp in range(COMPS):
                source, block, offset = (image, part, 0) if comp == 0 else (images, 2 * part, (comp - 1) * part)
                for p in range(SLAB):
                    row = offset + (pl.program_id(0) * modes + mode) * 2 * SLAB + p
                    b = field[mode, comp, p]
                    q = swap_back(source[pl.ds(row, PARTS, stride=block), :])
                    w = swap_back(source[pl.ds(row + SLAB, PARTS, stride=block), :])
                    solution_field[mode, comp, p] = sole * b - cross * q
                    residual[mode, comp, p] = b - sole * q + cross * w
        return carry

    lax.fori_loop(0, modes // SLAB, body, 0)


def finish(field, image, images, total):
    block = pl.BlockSpec((field.shape[0] // STEPS,) + field.shape[1:], lambda i: (i, 0, 0, 0, 0))
    vmem = pl.BlockSpec(memory_space=pltpu.VMEM)
    return pl.pallas_call(
        finish_kernel,
        grid=(STEPS,),
        out_shape=[jax.ShapeDtypeStruct(field.shape, jnp.float32)] * 2,
        in_specs=[block, vmem, vmem, vmem],
        out_specs=[block, block],
        compiler_params=pltpu.CompilerParams(vmem_limit_bytes=VMEM),
        cost_estimate=estimate(6),
        name="finish",
    )(field, image, images, total)


def mode_tables(coupling_table, slots):
    lower, upper, variable, code = (coupling_table[:, n] for n in range(4))
    within = jnp.arange(slots // PARTS, dtype=jnp.int32)
    first_modes = jnp.array(ORDER, jnp.int32) * (slots // PARTS)
    slot = (first_modes[:, None] + within).reshape(slots)
    is_lower = lower[:, None] == slot
    is_upper = upper[:, None] == slot
    degree = jnp.sum(jnp.where(is_upper, code[:, None], 0), axis=0)
    factor = jnp.where(code == 3, 6, code).astype(jnp.float32)[:, None]
    factorial = jnp.prod(jnp.where(is_upper, factor, 1.0), axis=0)
    root = (degree == 0) & jnp.any(is_lower, axis=0)
    even = (degree == 2) | root
    rank = jnp.sum(jnp.where(even[:, None] & (slot[:, None] < slot), 1, 0), axis=0)
    lower_even = jnp.any(is_lower & even, axis=1)
    is_even_end = jnp.where(lower_even[:, None], is_lower, is_upper)
    is_odd_end = jnp.where(lower_even[:, None], is_upper, is_lower)
    column = variable * EVEN + jnp.sum(jnp.where(is_even_end, rank, 0), axis=1)
    at_column = column[:, None] == jnp.arange(FULL, dtype=jnp.int32)
    down = code.astype(jnp.float32)[:, None]
    first = jnp.where(lower_even[:, None], 1.0, down)
    second = jnp.where(lower_even[:, None], down, 1.0)
    odd_ends = is_odd_end.astype(jnp.float32)
    columns = at_column.astype(jnp.float32)
    half = jnp.bfloat16
    to_even = jnp.dot(
        columns.astype(half).T, (odd_ends * first).astype(half), preferred_element_type=jnp.float32
    )
    to_odd = jnp.dot(
        odd_ends.astype(half).T, (columns * second).astype(half), preferred_element_type=jnp.float32
    )
    pick = (jnp.arange(FULL, dtype=jnp.int32)[:, None] - SPAN == rank) & even
    pick = pick.astype(jnp.float32)
    to_even = (to_even + pick).astype(half)
    to_all = (to_odd + pick.T).astype(half)
    scale = jnp.sqrt(factorial)
    wide = lambda v: jnp.broadcast_to(v[:, None], (slots, LANES))
    twice = lambda v: jnp.concatenate([v, v], axis=1)
    return wide(scale), wide(1.0 / scale), twice(to_even), twice(to_all)


def all_sum(value):
    for axis in ("space", "mode"):
        devices = lax.axis_size(axis)
        bit = 1
        while bit < devices:
            value = value + lax.ppermute(value, axis, [(i, i ^ bit) for i in range(devices)])
            bit *= 2
    return value


def transposed(right_side, mean_stiffness, ply_stiffness, fibre_weights, ply_map, coupling_table):
    slots = right_side.shape[0] * PARTS
    devices = lax.axis_size("space")
    up = [(i, i + 1) for i in range(devices - 1)]
    down = [(j, i) for i, j in up]
    index = lax.axis_index("mode").astype(jnp.int32)
    place = jnp.sum(jnp.where(jnp.array(ORDER) == index, jnp.arange(PARTS, dtype=jnp.int32), 0)).reshape(1)

    def swap(rows):
        return lax.all_to_all(rows, "mode", 0, 0, axis_index_groups=[list(ORDER)], tiled=True)

    def halo(rows):
        return lax.ppermute(rows, "space", up), lax.ppermute(rows, "space", down)

    (first,) = pack(right_side, 0)
    (second,) = pack(right_side, 1)
    own = [swap(first), swap(second)]
    both, third = pack(right_side, 2, (mean_stiffness, ply_map), own[:1])
    own.append(swap(third))
    halos = [halo(rows) for rows in own]
    tables = mode_tables(coupling_table, slots)
    both_before = lax.ppermute(both, "space", up)
    both_after = lax.ppermute(both, "space", down)
    fields = stiffness_fields(place, both_before, both, both_after, ply_stiffness)
    partial = jnp.zeros((8, LANES), jnp.float32)
    part = slots // PARTS * 2 * SLAB
    tables_and_fields = (tables, fields, fibre_weights)
    image, partial = apply_twice(0, place, own[0], *halos[0], *tables_and_fields, partial, part, 0)
    image = swap(image)
    images, partial = apply_twice(1, place, own[1], *halos[1], *tables_and_fields, partial, 2 * part, 0)
    images, partial = apply_twice(
        2, place, own[2], *halos[2], *tables_and_fields, partial, 2 * part, part, (images,)
    )
    return tuple(finish(right_side, image, swap(images), all_sum(partial)))


def on_device(right_side, mean_stiffness, ply_stiffness, fibre_weights, ply_map, coupling_table):
    args = (right_side, mean_stiffness, ply_stiffness, fibre_weights, ply_map, coupling_table)
    fits = right_side.shape[1:] == (COMPS, SLAB, 8, 128) and lax.axis_size("mode") == PARTS
    return transposed(*args) if fits else plain(*args)


def solution(mesh):
    return jax.shard_map(
        on_device,
        mesh=mesh,
        in_specs=(
            P("mode", None, "space", None, None),
            P("space", None, None),
            P(),
            P(),
            P("space", None, None),
            P(),
        ),
        out_specs=(P("mode", None, "space", None, None), P("mode", None, "space", None, None)),
        check_vma=False,
    )
```

```python
import functools

import jax
import jax.numpy as jnp
from jax import lax
from jax.experimental import pallas as pl
from jax.experimental.pallas import tpu as pltpu
from jax.sharding import PartitionSpec as P

VARS = 10
ITERS = 2


def extended(array, sides, width):
    for axis, dim in sides:
        devices, length = (lax.axis_size(axis), array.shape[dim])
        up = [(i, (i + 1) % devices) for i in range(devices - 1)]
        down = [(j, i) for i, j in up]
        last = lax.slice_in_dim(array, length - width, length, axis=dim)
        leading = lax.slice_in_dim(array, 0, width, axis=dim)
        before = lax.ppermute(last, axis, up)
        after = lax.ppermute(leading, axis, down)
        array = jnp.concatenate([before, array, after], axis=dim)
    return array


def window(array_in, dim_index, offset):
    slicers = [slice(None)] * (array_in.ndim - 3)
    for which in range(3):
        shift_by = offset if which == dim_index else 0
        length_here = array_in.shape[array_in.ndim - 3 + which] - 2
        slicers.append(slice(1 + shift_by, 1 + shift_by + length_here))
    return array_in[tuple(slicers)]


def diffuse(vector, stiffness, fibre_weights):
    vector_pads = [(0, 0)] * (vector.ndim - 2) + [(1, 1), (1, 1)]
    stiff_pads = [(0, 0)] * (stiffness.ndim - 2) + [(1, 1), (1, 1)]
    padded_v = jnp.pad(vector, vector_pads)
    padded_c = jnp.pad(stiffness, stiff_pads)
    centre = window(padded_v, 0, 0)
    middle = window(padded_c, 0, 0)
    result = None
    for dim_index in range(3):
        upper = (
            0.5
            * (middle + window(padded_c, dim_index, 1))
            * (centre - window(padded_v, dim_index, 1))
        )
        lower = (
            0.5
            * (middle + window(padded_c, dim_index, -1))
            * (centre - window(padded_v, dim_index, -1))
        )
        column = fibre_weights[:, dim_index].reshape(3, 1, 1, 1)
        term = column * (upper + lower)
        result = term if result is None else result + term
    return result


def squares(vector):
    return lax.psum(jnp.sum(vector * vector), ("mode", "space"))


def row_table(both_rows, both_cols, both_vars, both_weights, base, mode_dev, slots):
    local_rows = both_rows - base
    valid_rows = (local_rows >= 0) & (local_rows < mode_dev)
    local_rows = jnp.where(valid_rows, local_rows, mode_dev)
    row_coupling = jnp.zeros((VARS, mode_dev, slots), jnp.float32)
    row_coupling = row_coupling.at[both_vars, local_rows, both_cols].add(both_weights, mode="drop")
    return row_coupling.reshape(VARS * mode_dev, slots)


def plain(right_side, mean_stiffness, ply_stiffness, fibre_weights, ply_map, coupling_table):
    mode_dev = right_side.shape[0]
    slots = mode_dev * lax.axis_size("mode")
    base = lax.axis_index("mode") * mode_dev
    first_mode = coupling_table[:, 0]
    second_mode = coupling_table[:, 1]
    variable = coupling_table[:, 2]
    entry_weight = jnp.sqrt(coupling_table[:, 3].astype(jnp.float32))
    both_rows = jnp.concatenate([first_mode, second_mode])
    both_cols = jnp.concatenate([second_mode, first_mode])
    both_vars = jnp.concatenate([variable, variable])
    both_weights = jnp.concatenate([entry_weight, entry_weight])
    plies = jnp.arange(VARS, dtype=jnp.int32).reshape(VARS, 1, 1, 1)
    ply_fields = (ply_map[None] == plies).astype(jnp.float32) * ply_stiffness.reshape(VARS, 1, 1, 1)
    stiff_stack = jnp.concatenate([mean_stiffness[None], ply_fields], axis=0)
    stiff_rims = extended(stiff_stack, (("space", 1),), 1)
    stiff_rims = stiff_rims[:, None]
    row_coupling = row_table(both_rows, both_cols, both_vars, both_weights, base, mode_dev, slots)
    solution_field = jnp.zeros_like(right_side)
    residual = right_side
    direction = right_side
    norm_now = squares(residual)
    for iteration in range(ITERS):
        shard_piece = lax.all_gather(direction, "mode", axis=0, tiled=True)
        mixed = jnp.dot(
            row_coupling,
            shard_piece.reshape(shard_piece.shape[0], -1),
            precision=lax.Precision.HIGHEST,
            preferred_element_type=jnp.float32,
        )
        stacked = jnp.concatenate(
            [direction[None], mixed.reshape((VARS,) + direction.shape)], axis=0
        )
        padded = extended(stacked, (("space", 3),), 1)
        terms = diffuse(padded, stiff_rims[:, None], fibre_weights)
        image = direction + jnp.sum(terms, axis=0)
        step_size = norm_now / lax.psum(jnp.sum(direction * image), ("mode", "space"))
        solution_field = solution_field + step_size * direction
        residual = residual - step_size * image
        norm_next = squares(residual)
        direction = residual + norm_next / norm_now * direction
        norm_now = norm_next
    return (solution_field, residual)


COMPS = 3
SLAB = 3
PARTS = 8
WIDE = 16
ROWS = 4
EVEN = 1 + VARS * (VARS + 1) // 2
SPAN = VARS * EVEN
FULL = 624
INNER = 6
TILES = 8
LANES = 128
VMEM = 56 * 1024 * 1024


def lane_id():
    return lax.broadcasted_iota(jnp.int32, (8, LANES), 1)


def swap_out(tile):
    block = lane_id() // WIDE
    tile = pltpu.roll(tile, 0, 1, stride=WIDE, stride_axis=0)
    for bit in (1, 2, 4):
        tile = jnp.where((block & bit) != 0, pltpu.roll(tile, 8 - bit, 0), tile)
    return tile


def swap_back(tile):
    block = lane_id() // WIDE
    row = lax.broadcasted_iota(jnp.int32, (8, LANES), 0)
    for bit in (1, 2, 4):
        tile = jnp.where((block & bit) != 0, pltpu.roll(tile, bit, 0), tile)
    for bit in (1, 2, 4):
        tile = jnp.where((row & bit) != 0, pltpu.roll(tile, LANES - WIDE * bit, 1), tile)
    return tile


def halo_row(planes):
    lane = lane_id()
    slot = lane % WIDE
    halo = jnp.zeros((8, LANES), jnp.float32)
    for x, plane in planes.items():
        places = [(-1, x + 1), (WIDE, x + 6)]
        if 0 <= x < SLAB:
            places += [(-2, x + 10), (WIDE + 1, x + 13)]
        for offset, place in places:
            inside = (lane >= WIDE) if offset < 0 else (lane < LANES - WIDE)
            moved = pltpu.roll(plane, (place - offset) % LANES, 1)
            halo = jnp.where((slot == place) & inside, moved, halo)
    return halo


UNROLL = 3


def pack_kernel(field, *refs, comps):
    modes = field.shape[0]
    out = refs[-1]
    if len(refs) > 1:
        mean, ply, both = refs[0], refs[1], refs[-2]
        for x in range(SLAB):
            both[0, x] = mean[x]
            both[1, x] = (ply[x] + 1).astype(jnp.float32)
    rows = ROWS * len(comps)
    unroll = 2 * UNROLL // len(comps)

    def body(step, carry):
        for inner in range(unroll):
            mode = step * unroll + inner
            for n, comp in enumerate(comps):
                planes = [field[mode, comp, x] for x in range(SLAB)]
                halo = halo_row(dict(enumerate(planes)))
                for p, tile in enumerate(planes + [halo]):
                    out[pl.ds(mode * rows + n * ROWS + p, PARTS, stride=rows * modes), :] = swap_out(tile)
        return carry

    lax.fori_loop(0, modes // unroll, body, 0)


def estimate(micros):
    return pl.CostEstimate(flops=int(micros * 1e9), bytes_accessed=int(micros * 3e6), transcendentals=0)


def pack(field, comps, stiffness=(), after=()):
    modes = field.shape[0]
    vmem = pl.BlockSpec(memory_space=pltpu.VMEM)
    shapes = [jax.ShapeDtypeStruct((2,) + s.shape, jnp.float32) for s in stiffness[:1]]
    shapes.append(jax.ShapeDtypeStruct((PARTS * modes * ROWS * len(comps), LANES), jnp.float32))
    return pl.pallas_call(
        functools.partial(pack_kernel, comps=comps),
        grid=(1,),
        out_shape=shapes,
        in_specs=[pl.BlockSpec((modes, max(comps) + 1) + field.shape[2:], lambda i: (0, 0, 0, 0, 0))]
        + [vmem] * len(stiffness)
        + [pl.BlockSpec(memory_space=pl.ANY)] * len(after),
        out_specs=[vmem] * len(shapes),
        compiler_params=pltpu.CompilerParams(vmem_limit_bytes=VMEM),
        cost_estimate=estimate(2.5 * len(comps)),
        name="pack",
    )(field, *stiffness, *after)


def stiffness_kernel(place, before, both, after, ply_stiffness, fields, wide):
    rows = []
    for kind in range(2):
        planes = {-2: before[kind, 1], -1: before[kind, 2], 3: after[kind, 0], 4: after[kind, 1]}
        planes.update({x: both[kind, x] for x in range(SLAB)})
        halo = halo_row({x: planes[x] for x in range(-1, 4)})
        ordered = [planes[0], planes[1], planes[2], planes[-1], planes[3], halo, planes[-2], planes[4]]
        for t, tile in enumerate(ordered):
            wide[...] = swap_out(tile)
            rows.append(wide[pl.ds(place[0], 1), :])
    for t in range(TILES):
        mean, ply = rows[t], rows[TILES + t]
        cols = slice(LANES * t, LANES * (t + 1))
        for k in range(VARS):
            fields[k : k + 1, cols] = jnp.where(ply == k + 1.0, ply_stiffness[k], 0.0)
        fields[VARS : VARS + 1, cols] = mean
        fields[VARS + 1 : VARS + 2, cols] = jnp.where(ply > 0.0, 1.0, 0.0)
        fields[VARS + 2 : 16, cols] = jnp.zeros((4, LANES), jnp.float32)


def stiffness_fields(place, before, both, after, ply_stiffness):
    vmem = pl.BlockSpec(memory_space=pltpu.VMEM)
    smem = pl.BlockSpec(memory_space=pltpu.SMEM)
    return pl.pallas_call(
        stiffness_kernel,
        out_shape=jax.ShapeDtypeStruct((16, TILES * LANES), jnp.float32),
        in_specs=[smem, vmem, vmem, vmem, smem],
        out_specs=vmem,
        scratch_shapes=[pltpu.VMEM((8, LANES), jnp.float32)],
        cost_estimate=estimate(2),
        name="stiffness_fields",
    )(place, before, both, after, ply_stiffness)


AT = {0: 0, 1: 1, 2: 2, -1: 3, 3: 4, -2: 6, 4: 7}
PLACE = {index: x for x, index in AT.items()}
HALO = 5


def neighbour(tiles, index, side, place, full=False, wrap=False):
    t = tiles[index]
    lane = lax.broadcasted_iota(jnp.int32, t.shape, 1)
    slot = lane % WIDE
    roll = lambda v, s: pltpu.roll(v, s % LANES, 1)
    if side in (2, 3) and wrap:
        return roll(t, WIDE if side == 2 else -WIDE)
    if side in (2, 3):
        y = (place + lane // WIDE) & 7
        if side == 2:
            return jnp.where(y > 0, roll(t, WIDE), 0.0)
        return jnp.where(y < 7, roll(t, -WIDE), 0.0)
    if index == HALO:
        if side < 2:
            return roll(t, 1 if side == 0 else -1)
        result = roll(t, -9) if side == 4 else roll(t, -7)
        for x in range(-1, 4) if full else range(SLAB):
            goal, by = (x + 6, x - 9) if side == 4 else (x + 1, x + 1)
            result = jnp.where(slot == goal, roll(tiles[AT[x]], by), result)
        if full:
            result = jnp.where(slot >= 13, roll(t, 7), result) if side == 4 else jnp.where(
                (slot >= 10) & (slot < 13), roll(t, 9), result
            )
        return result
    x = PLACE[index]
    if side < 2:
        return tiles[AT[x - 1 if side == 0 else x + 1]]
    if side == 4:
        return jnp.where(slot == 0, roll(tiles[HALO], -(x + 1)), roll(t, 1))
    return jnp.where(slot == WIDE - 1, roll(tiles[HALO], 9 - x), roll(t, -1))


def sides_of(index, outer):
    if index < outer:
        return range(6)
    return {3: (1,), 4: (0,), HALO: (4, 5), 6: (1,), 7: (0,)}[index]


def split(array):
    high = array.astype(jnp.bfloat16)
    low = (array - high.astype(jnp.float32)).astype(jnp.bfloat16)
    return jnp.concatenate([high, low], axis=0)


STEP = 32
FACE = 16
CENTRE = 6 * FACE
EVEN_BLOCKS = ((0, 32), (32, EVEN))


def tile_cols(t):
    return slice(LANES * t, LANES * (t + 1))


def face_stiffness(fields, faces, weights, place):
    tiles = [fields[:, tile_cols(t)] for t in range(TILES)]
    for t in range(TILES):
        for side in sides_of(t, INNER):
            value = (0.5 * weights[side // 2]) * (tiles[t] + neighbour(tiles, t, side, place, True))
            faces[side * FACE : (side + 1) * FACE, tile_cols(t)] = value
        if t < INNER:
            centre = 1.0 + sum(faces[side * FACE + VARS : side * FACE + VARS + 1, tile_cols(t)] for side in range(6))
            faces[CENTRE : CENTRE + 1, tile_cols(t)] = centre
            lane = lax.broadcasted_iota(jnp.int32, (1, LANES), 1)
            y = (place + lane // WIDE) & 7
            for side, edge in ((2, 0), (3, 7)):
                row = side * FACE + VARS
                faces[row + 1 : row + 2, tile_cols(t)] = jnp.where(
                    y == edge, 0.0, faces[row : row + 1, tile_cols(t)]
                )


CHUNK = 2


def chunks(count):
    return [range(start, min(start + CHUNK, count)) for start in range(0, count, CHUNK)]


def chunk_cols(tiles):
    return slice(LANES * tiles[0], LANES * (tiles[-1] + 1))


def apply_operator(src, dst, mixed, flux, scaled, acc, faces, inside, to_even, to_all, place, inner, outer):
    slots = src.shape[0]

    def face(side, k, t):
        return faces[side * FACE + k : side * FACE + k + 1, tile_cols(t)]

    def mix(tiles):
        cols = chunk_cols(tiles)
        mixed[:, cols] = jnp.dot(to_even[...], split(src[:, cols]), preferred_element_type=jnp.float32)

    def flows(t):
        for low, high in EVEN_BLOCKS:
            total = {}
            for k in range(VARS):
                value = mixed[k * EVEN + low : k * EVEN + high, tile_cols(t)]
                for side in sides_of(t, outer):
                    term = face(side, k, t) * value
                    total[side] = term if k == 0 else total[side] + term
            for side, value in total.items():
                flux[side, low:high, tile_cols(t)] = value

    def scale_even(t):
        for low, high in EVEN_BLOCKS:
            even = EvenTiles(mixed, low, high)
            steps = [even[t] - neighbour(even, t, side, place) for side in range(6)]
            for k in range(VARS):
                total = face(0, k, t) * steps[0]
                for side in range(1, 6):
                    total = total + face(side, k, t) * steps[side]
                scaled[k * EVEN + low : k * EVEN + high, tile_cols(t)] = total
            total = None
            for side in range(6):
                opposite = FluxTiles(flux, side ^ 1, low, high)
                term = flux[side, low:high, tile_cols(t)] - neighbour(opposite, t, side, place)
                total = term if total is None else total + term
            scaled[SPAN + low : SPAN + high, tile_cols(t)] = total
        scaled[SPAN + EVEN : FULL, tile_cols(t)] = jnp.zeros((FULL - SPAN - EVEN, LANES), jnp.float32)

    def spread(tiles):
        cols = chunk_cols(tiles)
        acc[:, cols] = jnp.dot(to_all[...], split(scaled[:, cols]), preferred_element_type=jnp.float32)

    before = ()
    for tiles in chunks(inner):
        mix(tiles)
        for t in before:
            flows(t)
        before = tiles
    for t in before:
        flows(t)
    before = ()
    for tiles in chunks(outer):
        for t in tiles:
            scale_even(t)
        if before:
            spread(before)
        before = tiles
    spread(before)

    def last(step, carry):
        rows = pl.ds(pl.multiple_of(step * STEP, STEP), STEP)
        tiles = [src[rows, tile_cols(t)] for t in range(inner)]
        for t in range(outer):
            result = acc[rows, tile_cols(t)] + faces[CENTRE : CENTRE + 1, tile_cols(t)] * tiles[t]
            for side in range(6):
                row = VARS + 1 if side in (2, 3) else VARS
                result = result - face(side, row, t) * neighbour(tiles, t, side, place, wrap=True)
            if t >= SLAB:
                result = inside[t] * result
            dst[rows, tile_cols(t)] = result
        return carry

    lax.fori_loop(0, slots // STEP, last, 0)


class EvenTiles:
    def __init__(self, mixed, low, high):
        self.mixed, self.low, self.high = mixed, low, high

    def __getitem__(self, t):
        return self.mixed[SPAN + self.low : SPAN + self.high, tile_cols(t)]


class FluxTiles:
    def __init__(self, flux, side, low, high):
        self.flux, self.side, self.low, self.high = flux, side, low, high

    def __getitem__(self, t):
        return self.flux[self.side, self.low : self.high, tile_cols(t)]


def apply_kernel(
    place, own, before, after, scale, to_even, to_all, fields, fibre, *refs, comp, row, rows, block, offset,
):
    out_rows, partial, out, field, first, second, mixed, flux, scaled, acc, faces, sems = refs[-12:]
    slots = scale.shape[0]
    here = place[0]
    face_stiffness(fields, faces, [fibre[comp, d] for d in range(3)], here)
    lane = lax.broadcasted_iota(jnp.int32, (slots, LANES), 1)
    slot = lane % WIDE
    load = lambda ref, p: ref[pl.ds(row + p, slots, stride=rows), :]
    left = pltpu.roll(load(before, 3), LANES - 3, 1)
    right = pltpu.roll(load(after, 3), 3, 1)
    halo = jnp.where((slot == 0) | (slot == 5), left, load(own, 3))
    halo = jnp.where((slot == 4) | (slot == 9), right, halo)
    ordered = [
        load(own, 0), load(own, 1), load(own, 2), load(before, 2), load(after, 0), halo,
        load(before, 1), load(after, 1),
    ]
    for t, tile in enumerate(ordered):
        field[:, tile_cols(t)] = tile * scale[...]
    inside = {t: fields[VARS + 1 : VARS + 2, tile_cols(t)] for t in range(SLAB, INNER)}
    slot = lax.broadcasted_iota(jnp.int32, (1, LANES), 1) % WIDE
    used = ((slot >= 1) & (slot <= 3)) | ((slot >= 6) & (slot <= 8))
    inside[HALO] = jnp.where(used, inside[HALO], 0.0)
    scratch = (mixed, flux, scaled, acc, faces, inside, to_even, to_all, here)
    apply_operator(field, first, *scratch, TILES, INNER)
    apply_operator(first, second, *scratch, INNER, SLAB)
    sums = [jnp.zeros((1, LANES), jnp.float32)] * 5
    unscale = 1.0 / scale[...]
    for p in range(SLAB):
        b = load(own, p)
        q = first[:, tile_cols(p)] * unscale
        w = second[:, tile_cols(p)] * unscale
        out[pl.ds(p, slots, stride=2 * SLAB), :] = q
        out[pl.ds(p + SLAB, slots, stride=2 * SLAB), :] = w
        for n, (one, two) in enumerate(((b, b), (b, q), (q, q), (b, w), (q, w))):
            sums[n] = sums[n] + jnp.sum(one * two, axis=0, keepdims=True)
    part = slots // PARTS * 2 * SLAB
    copies = [
        pltpu.make_async_copy(
            out.at[pl.ds(n * part, part), :], out_rows.at[pl.ds(n * block + offset, part), :], sems.at[n]
        )
        for n in range(PARTS)
    ]
    for copy in copies:
        copy.start()
    total = jnp.concatenate(sums + [jnp.zeros((3, LANES), jnp.float32)], axis=0)
    partial[...] = total + refs[0][...] if comp > 0 else total
    for copy in copies:
        copy.wait()


def apply_twice(comp, place, own, before, after, tables, fields, fibre, so_far=None, out_rows=None):
    scale, to_even, to_all = tables
    slots = scale.shape[0]
    part = slots // PARTS * 2 * SLAB
    vmem = pl.BlockSpec(memory_space=pltpu.VMEM)
    smem = pl.BlockSpec(memory_space=pltpu.SMEM)
    whole = pl.BlockSpec(memory_space=pl.ANY)
    f32 = lambda *shape: pltpu.VMEM(shape, jnp.float32)
    alone = comp == 0
    block = part if alone else 2 * part
    extra = [v for v in (so_far, out_rows) if v is not None]
    kernel = functools.partial(
        apply_kernel, comp=comp, row=0 if alone else ROWS * (comp - 1), rows=ROWS if alone else 2 * ROWS,
        block=block, offset=part if comp == 2 else 0,
    )
    return pl.pallas_call(
        kernel,
        out_shape=[
            jax.ShapeDtypeStruct((PARTS * block, LANES), jnp.float32),
            jax.ShapeDtypeStruct((8, LANES), jnp.float32),
        ],
        in_specs=[smem] + [vmem] * 7 + [smem] + [vmem, whole][: len(extra)],
        out_specs=[whole, vmem],
        input_output_aliases={10: 0} if comp == 2 else {},
        scratch_shapes=[
            f32(slots * 2 * SLAB, LANES),
            f32(slots, TILES * LANES),
            f32(slots, INNER * LANES),
            f32(slots, SLAB * LANES),
            f32(FULL, TILES * LANES),
            f32(6, EVEN, TILES * LANES),
            f32(FULL, INNER * LANES),
            f32(slots, INNER * LANES),
            f32(6 * FACE + 8, TILES * LANES),
            pltpu.SemaphoreType.DMA((PARTS,)),
        ],
        compiler_params=pltpu.CompilerParams(vmem_limit_bytes=VMEM),
        cost_estimate=estimate(15),
        name="apply_twice",
    )(place, own, before, after, scale, to_even, to_all, fields, fibre, *extra)


def combination(total):
    bb, bq, qq, bw, qw = (jnp.sum(total[n : n + 1, :], axis=1, keepdims=True) for n in range(5))
    step_one = bb / bq
    norm = bb - 2.0 * step_one * bq + step_one * step_one * qq
    grown = 1.0 + norm / bb
    curve = grown * grown * bq - step_one * grown * (bw + qq) + step_one * step_one * qw
    step_two = norm / curve
    spread = lambda v: jnp.broadcast_to(v, (8, LANES))
    sole = spread(step_one + step_two * grown)
    cross = spread(step_one * step_two)
    return sole, cross


STEPS = 3


def finish_kernel(field, image, total, *refs, comps):
    solution_field, residual = refs[-2:]
    modes = field.shape[0]
    part = STEPS * modes * 2 * SLAB
    block = part * len(comps)
    sole, cross = combination(total)

    def body(step, carry):
        for inner in range(SLAB):
            mode = step * SLAB + inner
            for n in range(len(comps)):
                for p in range(SLAB):
                    row = n * part + (pl.program_id(0) * modes + mode) * 2 * SLAB + p
                    b = field[mode, comps[n], p]
                    q = swap_back(image[pl.ds(row, PARTS, stride=block), :])
                    w = swap_back(image[pl.ds(row + SLAB, PARTS, stride=block), :])
                    solution_field[mode, comps[n], p] = sole * b - cross * q
                    residual[mode, comps[n], p] = b - sole * q + cross * w
        if len(refs) > 2:
            for inner in range(SLAB):
                mode = step * SLAB + inner
                solution_field[mode, 0] = refs[0][mode, 0]
                residual[mode, 0] = refs[1][mode, 0]
        return carry

    lax.fori_loop(0, modes // SLAB, body, 0)


def finish(field, comps, image, total, so_far=()):
    whole = field.shape[2:]
    rows = field.shape[0] // STEPS
    index = lambda i: (i, 0, 0, 0, 0)
    block = pl.BlockSpec((rows, max(comps) + 1) + whole, index)
    vmem = pl.BlockSpec(memory_space=pltpu.VMEM)
    count = 1 if max(comps) == 0 else COMPS
    return pl.pallas_call(
        functools.partial(finish_kernel, comps=comps),
        grid=(STEPS,),
        out_shape=[jax.ShapeDtypeStruct((field.shape[0], count) + whole, jnp.float32)] * 2,
        in_specs=[block, vmem, vmem] + [pl.BlockSpec((rows, 1) + whole, index)] * len(so_far),
        out_specs=[block, block],
        compiler_params=pltpu.CompilerParams(vmem_limit_bytes=VMEM),
        cost_estimate=estimate(2.5 * len(comps)),
        name="finish",
    )(field, image, total, *so_far)


def mode_tables(coupling_table, slots):
    lower, upper, variable, code = (coupling_table[:, n] for n in range(4))
    slot = jnp.arange(slots, dtype=jnp.int32)
    is_lower = lower[:, None] == slot
    is_upper = upper[:, None] == slot
    degree = jnp.sum(jnp.where(is_upper, code[:, None], 0), axis=0)
    factor = jnp.where(code == 3, 6, code).astype(jnp.float32)[:, None]
    factorial = jnp.prod(jnp.where(is_upper, factor, 1.0), axis=0)
    root = (degree == 0) & jnp.any(is_lower, axis=0)
    even = (degree == 2) | root
    rank = jnp.sum(jnp.where(even[:, None] & (slot[:, None] < slot), 1, 0), axis=0)
    lower_even = jnp.any(is_lower & even, axis=1)
    is_even_end = jnp.where(lower_even[:, None], is_lower, is_upper)
    is_odd_end = jnp.where(lower_even[:, None], is_upper, is_lower)
    column = variable * EVEN + jnp.sum(jnp.where(is_even_end, rank, 0), axis=1)
    at_column = column[:, None] == jnp.arange(FULL, dtype=jnp.int32)
    down = code.astype(jnp.float32)[:, None]
    first = jnp.where(lower_even[:, None], 1.0, down)
    second = jnp.where(lower_even[:, None], down, 1.0)
    odd_ends = is_odd_end.astype(jnp.float32)
    columns = at_column.astype(jnp.float32)
    half = jnp.bfloat16
    to_even = jnp.dot(
        columns.astype(half).T, (odd_ends * first).astype(half), preferred_element_type=jnp.float32
    )
    to_odd = jnp.dot(
        odd_ends.astype(half).T, (columns * second).astype(half), preferred_element_type=jnp.float32
    )
    pick = (jnp.arange(FULL, dtype=jnp.int32)[:, None] - SPAN == rank) & even
    pick = pick.astype(jnp.float32)
    to_even = (to_even + pick).astype(half)
    to_all = (to_odd + pick.T).astype(half)
    scale = jnp.sqrt(factorial)
    wide = lambda v: jnp.broadcast_to(v[:, None], (slots, LANES))
    twice = lambda v: jnp.concatenate([v, v], axis=1)
    return wide(scale), twice(to_even), twice(to_all)


def all_sum(value):
    for axis, bit in (("space", 1), ("space", 2), ("mode", 1)):
        devices = lax.axis_size(axis)
        value = value + lax.ppermute(value, axis, [(i, i ^ bit) for i in range(devices)])
    others = [
        lax.ppermute(value, "mode", [(i, i ^ bit) for i in range(PARTS)]) for bit in range(2, PARTS, 2)
    ]
    return (value + others[0]) + (others[1] + others[2])


def transposed(right_side, mean_stiffness, ply_stiffness, fibre_weights, ply_map, coupling_table):
    slots = right_side.shape[0] * PARTS
    devices = lax.axis_size("space")
    up = [(i, i + 1) for i in range(devices - 1)]
    down = [(j, i) for i, j in up]
    place = lax.axis_index("mode").astype(jnp.int32).reshape(1)

    def swap(rows):
        return lax.all_to_all(rows, "mode", 0, 0, tiled=True)

    def halo(rows):
        return rows, lax.ppermute(rows, "space", up), lax.ppermute(rows, "space", down)

    (first,) = pack(right_side, (0,))
    both, others = pack(right_side, (1, 2), (mean_stiffness, ply_map), (first,))
    first, others = halo(swap(first)), halo(swap(others))
    tables = mode_tables(coupling_table, slots)
    both_before = lax.ppermute(both, "space", up)
    both_after = lax.ppermute(both, "space", down)
    fields = stiffness_fields(place, both_before, both, both_after, ply_stiffness)
    image, partial = apply_twice(0, place, *first, tables, fields, fibre_weights)
    image = swap(image)
    images, partial = apply_twice(1, place, *others, tables, fields, fibre_weights, partial)
    images, partial = apply_twice(2, place, *others, tables, fields, fibre_weights, partial, images)
    total = all_sum(partial)
    done = finish(right_side, (0,), image, total)
    return tuple(finish(right_side, (1, 2), swap(images), total, tuple(done)))


def on_device(right_side, mean_stiffness, ply_stiffness, fibre_weights, ply_map, coupling_table):
    args = (right_side, mean_stiffness, ply_stiffness, fibre_weights, ply_map, coupling_table)
    fits = right_side.shape[1:] == (COMPS, SLAB, 8, 128) and (lax.axis_size("mode"), lax.axis_size("space")) == (PARTS, 4)
    return transposed(*args) if fits else plain(*args)


def solution(mesh):
    return jax.shard_map(
        on_device,
        mesh=mesh,
        in_specs=(
            P("mode", None, "space", None, None),
            P("space", None, None),
            P(),
            P(),
            P("space", None, None),
            P(),
        ),
        out_specs=(P("mode", None, "space", None, None), P("mode", None, "space", None, None)),
        check_vma=False,
    )
```

```python
import functools

import jax
import jax.numpy as jnp
from jax import lax
from jax.experimental import pallas as pl
from jax.experimental.pallas import tpu as pltpu
from jax.sharding import PartitionSpec as P

VARS = 10
ITERS = 2


def extended(array, sides, width):
    for axis, dim in sides:
        devices, length = (lax.axis_size(axis), array.shape[dim])
        up = [(i, (i + 1) % devices) for i in range(devices - 1)]
        down = [(j, i) for i, j in up]
        last = lax.slice_in_dim(array, length - width, length, axis=dim)
        leading = lax.slice_in_dim(array, 0, width, axis=dim)
        before = lax.ppermute(last, axis, up)
        after = lax.ppermute(leading, axis, down)
        array = jnp.concatenate([before, array, after], axis=dim)
    return array


def window(array_in, dim_index, offset):
    slicers = [slice(None)] * (array_in.ndim - 3)
    for which in range(3):
        shift_by = offset if which == dim_index else 0
        length_here = array_in.shape[array_in.ndim - 3 + which] - 2
        slicers.append(slice(1 + shift_by, 1 + shift_by + length_here))
    return array_in[tuple(slicers)]


def diffuse(vector, stiffness, fibre_weights):
    vector_pads = [(0, 0)] * (vector.ndim - 2) + [(1, 1), (1, 1)]
    stiff_pads = [(0, 0)] * (stiffness.ndim - 2) + [(1, 1), (1, 1)]
    padded_v = jnp.pad(vector, vector_pads)
    padded_c = jnp.pad(stiffness, stiff_pads)
    centre = window(padded_v, 0, 0)
    middle = window(padded_c, 0, 0)
    result = None
    for dim_index in range(3):
        upper = (
            0.5
            * (middle + window(padded_c, dim_index, 1))
            * (centre - window(padded_v, dim_index, 1))
        )
        lower = (
            0.5
            * (middle + window(padded_c, dim_index, -1))
            * (centre - window(padded_v, dim_index, -1))
        )
        column = fibre_weights[:, dim_index].reshape(3, 1, 1, 1)
        term = column * (upper + lower)
        result = term if result is None else result + term
    return result


def squares(vector):
    return lax.psum(jnp.sum(vector * vector), ("mode", "space"))


def row_table(both_rows, both_cols, both_vars, both_weights, base, mode_dev, slots):
    local_rows = both_rows - base
    valid_rows = (local_rows >= 0) & (local_rows < mode_dev)
    local_rows = jnp.where(valid_rows, local_rows, mode_dev)
    row_coupling = jnp.zeros((VARS, mode_dev, slots), jnp.float32)
    row_coupling = row_coupling.at[both_vars, local_rows, both_cols].add(both_weights, mode="drop")
    return row_coupling.reshape(VARS * mode_dev, slots)


def plain(right_side, mean_stiffness, ply_stiffness, fibre_weights, ply_map, coupling_table):
    mode_dev = right_side.shape[0]
    slots = mode_dev * lax.axis_size("mode")
    base = lax.axis_index("mode") * mode_dev
    first_mode = coupling_table[:, 0]
    second_mode = coupling_table[:, 1]
    variable = coupling_table[:, 2]
    entry_weight = jnp.sqrt(coupling_table[:, 3].astype(jnp.float32))
    both_rows = jnp.concatenate([first_mode, second_mode])
    both_cols = jnp.concatenate([second_mode, first_mode])
    both_vars = jnp.concatenate([variable, variable])
    both_weights = jnp.concatenate([entry_weight, entry_weight])
    plies = jnp.arange(VARS, dtype=jnp.int32).reshape(VARS, 1, 1, 1)
    ply_fields = (ply_map[None] == plies).astype(jnp.float32) * ply_stiffness.reshape(VARS, 1, 1, 1)
    stiff_stack = jnp.concatenate([mean_stiffness[None], ply_fields], axis=0)
    stiff_rims = extended(stiff_stack, (("space", 1),), 1)
    stiff_rims = stiff_rims[:, None]
    row_coupling = row_table(both_rows, both_cols, both_vars, both_weights, base, mode_dev, slots)
    solution_field = jnp.zeros_like(right_side)
    residual = right_side
    direction = right_side
    norm_now = squares(residual)
    for iteration in range(ITERS):
        shard_piece = lax.all_gather(direction, "mode", axis=0, tiled=True)
        mixed = jnp.dot(
            row_coupling,
            shard_piece.reshape(shard_piece.shape[0], -1),
            precision=lax.Precision.HIGHEST,
            preferred_element_type=jnp.float32,
        )
        stacked = jnp.concatenate(
            [direction[None], mixed.reshape((VARS,) + direction.shape)], axis=0
        )
        padded = extended(stacked, (("space", 3),), 1)
        terms = diffuse(padded, stiff_rims[:, None], fibre_weights)
        image = direction + jnp.sum(terms, axis=0)
        step_size = norm_now / lax.psum(jnp.sum(direction * image), ("mode", "space"))
        solution_field = solution_field + step_size * direction
        residual = residual - step_size * image
        norm_next = squares(residual)
        direction = residual + norm_next / norm_now * direction
        norm_now = norm_next
    return (solution_field, residual)


COMPS = 3
SLAB = 3
PARTS = 8
WIDE = 16
ROWS = 4
EVEN = 1 + VARS * (VARS + 1) // 2
SPAN = VARS * EVEN
FULL = 624
INNER = 6
TILES = 8
LANES = 128
VMEM = 56 * 1024 * 1024


def lane_id():
    return lax.broadcasted_iota(jnp.int32, (8, LANES), 1)


def swap_out(tile):
    block = lane_id() // WIDE
    tile = pltpu.roll(tile, 0, 1, stride=WIDE, stride_axis=0)
    for bit in (1, 2, 4):
        tile = jnp.where((block & bit) != 0, pltpu.roll(tile, 8 - bit, 0), tile)
    return tile


def swap_back(tile):
    block = lane_id() // WIDE
    row = lax.broadcasted_iota(jnp.int32, (8, LANES), 0)
    for bit in (1, 2, 4):
        tile = jnp.where((block & bit) != 0, pltpu.roll(tile, bit, 0), tile)
    for bit in (1, 2, 4):
        tile = jnp.where((row & bit) != 0, pltpu.roll(tile, LANES - WIDE * bit, 1), tile)
    return tile


def halo_row(planes):
    lane = lane_id()
    slot = lane % WIDE
    halo = jnp.zeros((8, LANES), jnp.float32)
    for x, plane in planes.items():
        places = [(-1, x + 1), (WIDE, x + 6)]
        if 0 <= x < SLAB:
            places += [(-2, x + 10), (WIDE + 1, x + 13)]
        for offset, place in places:
            inside = (lane >= WIDE) if offset < 0 else (lane < LANES - WIDE)
            moved = pltpu.roll(plane, (place - offset) % LANES, 1)
            halo = jnp.where((slot == place) & inside, moved, halo)
    return halo


UNROLL = 3


def pack_kernel(field, *refs, comps):
    modes = field.shape[0]
    out = refs[-1]
    if len(refs) > 1:
        mean, ply, both = refs[0], refs[1], refs[-2]
        for x in range(SLAB):
            both[0, x] = mean[x]
            both[1, x] = (ply[x] + 1).astype(jnp.float32)
    rows = ROWS * len(comps)
    unroll = 2 * UNROLL // len(comps)

    def body(step, carry):
        for inner in range(unroll):
            mode = step * unroll + inner
            for n, comp in enumerate(comps):
                planes = [field[mode, comp, x] for x in range(SLAB)]
                halo = halo_row(dict(enumerate(planes)))
                for p, tile in enumerate(planes + [halo]):
                    out[pl.ds((n * modes + mode) * ROWS + p, PARTS, stride=rows * modes), :] = swap_out(tile)
        return carry

    lax.fori_loop(0, modes // unroll, body, 0)


def estimate(micros):
    return pl.CostEstimate(flops=int(micros * 1e9), bytes_accessed=int(micros * 3e6), transcendentals=0)


def pack(field, comps, stiffness=(), after=()):
    modes = field.shape[0]
    vmem = pl.BlockSpec(memory_space=pltpu.VMEM)
    shapes = [jax.ShapeDtypeStruct((2,) + s.shape, jnp.float32) for s in stiffness[:1]]
    shapes.append(jax.ShapeDtypeStruct((PARTS * modes * ROWS * len(comps), LANES), jnp.float32))
    return pl.pallas_call(
        functools.partial(pack_kernel, comps=comps),
        grid=(1,),
        out_shape=shapes,
        in_specs=[pl.BlockSpec((modes, max(comps) + 1) + field.shape[2:], lambda i: (0, 0, 0, 0, 0))]
        + [vmem] * len(stiffness)
        + [pl.BlockSpec(memory_space=pl.ANY)] * len(after),
        out_specs=[vmem] * len(shapes),
        compiler_params=pltpu.CompilerParams(vmem_limit_bytes=VMEM),
        cost_estimate=estimate(2.5 * len(comps)),
        name="pack",
    )(field, *stiffness, *after)


def part_kernel(rows, ready, *refs):
    *outs, sems = refs
    size = outs[0].shape[0] // PARTS
    copies = []
    for n, out in enumerate(outs):
        for device in range(PARTS):
            source = rows.at[pl.ds((device * len(outs) + n) * size, size), :]
            goal = out.at[pl.ds(device * size, size), :]
            copies.append(pltpu.make_async_copy(source, goal, sems.at[n * PARTS + device]))
    for copy in copies:
        copy.start()
    for copy in copies:
        copy.wait()


def part_components(rows, ready, count):
    whole = pl.BlockSpec(memory_space=pl.ANY)
    return pl.pallas_call(
        part_kernel,
        out_shape=[jax.ShapeDtypeStruct((rows.shape[0] // count, LANES), jnp.float32)] * count,
        in_specs=[whole, whole],
        out_specs=[whole] * count,
        scratch_shapes=[pltpu.SemaphoreType.DMA((count * PARTS,))],
        cost_estimate=estimate(1),
        name="part_components",
    )(rows, ready)


def stiffness_kernel(place, before, both, after, ply_stiffness, fields, wide):
    rows = []
    for kind in range(2):
        planes = {-2: before[kind, 1], -1: before[kind, 2], 3: after[kind, 0], 4: after[kind, 1]}
        planes.update({x: both[kind, x] for x in range(SLAB)})
        halo = halo_row({x: planes[x] for x in range(-1, 4)})
        ordered = [planes[0], planes[1], planes[2], planes[-1], planes[3], halo, planes[-2], planes[4]]
        for t, tile in enumerate(ordered):
            wide[...] = swap_out(tile)
            rows.append(wide[pl.ds(place[0], 1), :])
    for t in range(TILES):
        mean, ply = rows[t], rows[TILES + t]
        cols = slice(LANES * t, LANES * (t + 1))
        for k in range(VARS):
            fields[k : k + 1, cols] = jnp.where(ply == k + 1.0, ply_stiffness[k], 0.0)
        fields[VARS : VARS + 1, cols] = mean
        fields[VARS + 1 : VARS + 2, cols] = jnp.where(ply > 0.0, 1.0, 0.0)
        fields[VARS + 2 : 16, cols] = jnp.zeros((4, LANES), jnp.float32)


def stiffness_fields(place, before, both, after, ply_stiffness):
    vmem = pl.BlockSpec(memory_space=pltpu.VMEM)
    smem = pl.BlockSpec(memory_space=pltpu.SMEM)
    return pl.pallas_call(
        stiffness_kernel,
        out_shape=jax.ShapeDtypeStruct((16, TILES * LANES), jnp.float32),
        in_specs=[smem, vmem, vmem, vmem, smem],
        out_specs=vmem,
        scratch_shapes=[pltpu.VMEM((8, LANES), jnp.float32)],
        cost_estimate=estimate(2),
        name="stiffness_fields",
    )(place, before, both, after, ply_stiffness)


AT = {0: 0, 1: 1, 2: 2, -1: 3, 3: 4, -2: 6, 4: 7}
PLACE = {index: x for x, index in AT.items()}
HALO = 5


def neighbour(tiles, index, side, place, full=False, wrap=False):
    t = tiles[index]
    lane = lax.broadcasted_iota(jnp.int32, t.shape, 1)
    slot = lane % WIDE
    roll = lambda v, s: pltpu.roll(v, s % LANES, 1)
    if side in (2, 3) and wrap:
        return roll(t, WIDE if side == 2 else -WIDE)
    if side in (2, 3):
        y = (place + lane // WIDE) & 7
        if side == 2:
            return jnp.where(y > 0, roll(t, WIDE), 0.0)
        return jnp.where(y < 7, roll(t, -WIDE), 0.0)
    if index == HALO:
        if side < 2:
            return roll(t, 1 if side == 0 else -1)
        result = roll(t, -9) if side == 4 else roll(t, -7)
        for x in range(-1, 4) if full else range(SLAB):
            goal, by = (x + 6, x - 9) if side == 4 else (x + 1, x + 1)
            result = jnp.where(slot == goal, roll(tiles[AT[x]], by), result)
        if full:
            result = jnp.where(slot >= 13, roll(t, 7), result) if side == 4 else jnp.where(
                (slot >= 10) & (slot < 13), roll(t, 9), result
            )
        return result
    x = PLACE[index]
    if side < 2:
        return tiles[AT[x - 1 if side == 0 else x + 1]]
    if side == 4:
        return jnp.where(slot == 0, roll(tiles[HALO], -(x + 1)), roll(t, 1))
    return jnp.where(slot == WIDE - 1, roll(tiles[HALO], 9 - x), roll(t, -1))


def sides_of(index, outer):
    if index < outer:
        return range(6)
    return {3: (1,), 4: (0,), HALO: (4, 5), 6: (1,), 7: (0,)}[index]


def split(array):
    high = array.astype(jnp.bfloat16)
    low = (array - high.astype(jnp.float32)).astype(jnp.bfloat16)
    return jnp.concatenate([high, low], axis=0)


STEP = 32
FACE = 16
CENTRE = 6 * FACE
EVEN_BLOCKS = ((0, 32), (32, EVEN))


def tile_cols(t):
    return slice(LANES * t, LANES * (t + 1))


def face_stiffness(fields, faces, weights, place):
    tiles = [fields[:, tile_cols(t)] for t in range(TILES)]
    for t in range(TILES):
        for side in sides_of(t, INNER):
            value = (0.5 * weights[side // 2]) * (tiles[t] + neighbour(tiles, t, side, place, True))
            faces[side * FACE : (side + 1) * FACE, tile_cols(t)] = value
        if t < INNER:
            centre = 1.0 + sum(faces[side * FACE + VARS : side * FACE + VARS + 1, tile_cols(t)] for side in range(6))
            faces[CENTRE : CENTRE + 1, tile_cols(t)] = centre
            lane = lax.broadcasted_iota(jnp.int32, (1, LANES), 1)
            y = (place + lane // WIDE) & 7
            for side, edge in ((2, 0), (3, 7)):
                row = side * FACE + VARS
                faces[row + 1 : row + 2, tile_cols(t)] = jnp.where(
                    y == edge, 0.0, faces[row : row + 1, tile_cols(t)]
                )


CHUNK = 4


def chunks(count):
    return [range(start, min(start + CHUNK, count)) for start in range(0, count, CHUNK)]


def chunk_cols(tiles):
    return slice(LANES * tiles[0], LANES * (tiles[-1] + 1))


def apply_operator(src, dst, mixed, flux, scaled, acc, faces, inside, to_even, to_all, place, inner, outer):
    slots = src.shape[0]

    def face(side, k, t):
        return faces[side * FACE + k : side * FACE + k + 1, tile_cols(t)]

    def mix(tiles):
        cols = chunk_cols(tiles)
        mixed[:, cols] = jnp.dot(to_even[...], split(src[:, cols]), preferred_element_type=jnp.float32)

    def flows(t):
        for low, high in EVEN_BLOCKS:
            total = {}
            for k in range(VARS):
                value = mixed[k * EVEN + low : k * EVEN + high, tile_cols(t)]
                for side in sides_of(t, outer):
                    term = face(side, k, t) * value
                    total[side] = term if k == 0 else total[side] + term
            for side, value in total.items():
                flux[side, low:high, tile_cols(t)] = value

    def scale_even(t):
        for low, high in EVEN_BLOCKS:
            even = EvenTiles(mixed, low, high)
            steps = [even[t] - neighbour(even, t, side, place) for side in range(6)]
            for k in range(VARS):
                total = face(0, k, t) * steps[0]
                for side in range(1, 6):
                    total = total + face(side, k, t) * steps[side]
                scaled[k * EVEN + low : k * EVEN + high, tile_cols(t)] = total
            total = None
            for side in range(6):
                opposite = FluxTiles(flux, side ^ 1, low, high)
                term = flux[side, low:high, tile_cols(t)] - neighbour(opposite, t, side, place)
                total = term if total is None else total + term
            scaled[SPAN + low : SPAN + high, tile_cols(t)] = total
        scaled[SPAN + EVEN : FULL, tile_cols(t)] = jnp.zeros((FULL - SPAN - EVEN, LANES), jnp.float32)

    def spread(tiles):
        cols = chunk_cols(tiles)
        acc[:, cols] = jnp.dot(to_all[...], split(scaled[:, cols]), preferred_element_type=jnp.float32)

    before = ()
    for tiles in chunks(inner):
        mix(tiles)
        for t in before:
            flows(t)
        before = tiles
    for t in before:
        flows(t)
    before = ()
    for tiles in chunks(outer):
        for t in tiles:
            scale_even(t)
        if before:
            spread(before)
        before = tiles
    spread(before)

    def last(step, carry):
        rows = pl.ds(pl.multiple_of(step * STEP, STEP), STEP)
        tiles = [src[rows, tile_cols(t)] for t in range(inner)]
        for t in range(outer):
            result = acc[rows, tile_cols(t)] + faces[CENTRE : CENTRE + 1, tile_cols(t)] * tiles[t]
            for side in range(6):
                row = VARS + 1 if side in (2, 3) else VARS
                result = result - face(side, row, t) * neighbour(tiles, t, side, place, wrap=True)
            if t >= SLAB:
                result = inside[t] * result
            dst[rows, tile_cols(t)] = result
        return carry

    lax.fori_loop(0, slots // STEP, last, 0)


class EvenTiles:
    def __init__(self, mixed, low, high):
        self.mixed, self.low, self.high = mixed, low, high

    def __getitem__(self, t):
        return self.mixed[SPAN + self.low : SPAN + self.high, tile_cols(t)]


class FluxTiles:
    def __init__(self, flux, side, low, high):
        self.flux, self.side, self.low, self.high = flux, side, low, high

    def __getitem__(self, t):
        return self.flux[self.side, self.low : self.high, tile_cols(t)]


def apply_kernel(
    place, own, before, after, scale, to_even, to_all, fields, fibre, *refs, comp,
):
    out, partial, field, first, second, mixed, flux, scaled, acc, faces = refs[-10:]
    slots = scale.shape[0]
    here = place[0]
    face_stiffness(fields, faces, [fibre[comp, d] for d in range(3)], here)
    lane = lax.broadcasted_iota(jnp.int32, (slots, LANES), 1)
    slot = lane % WIDE
    load = lambda ref, p: ref[pl.ds(p, slots, stride=ROWS), :]
    left = pltpu.roll(load(before, 3), LANES - 3, 1)
    right = pltpu.roll(load(after, 3), 3, 1)
    halo = jnp.where((slot == 0) | (slot == 5), left, load(own, 3))
    halo = jnp.where((slot == 4) | (slot == 9), right, halo)
    ordered = [
        load(own, 0), load(own, 1), load(own, 2), load(before, 2), load(after, 0), halo,
        load(before, 1), load(after, 1),
    ]
    for t, tile in enumerate(ordered):
        field[:, tile_cols(t)] = tile * scale[...]
    inside = {t: fields[VARS + 1 : VARS + 2, tile_cols(t)] for t in range(SLAB, INNER)}
    slot = lax.broadcasted_iota(jnp.int32, (1, LANES), 1) % WIDE
    used = ((slot >= 1) & (slot <= 3)) | ((slot >= 6) & (slot <= 8))
    inside[HALO] = jnp.where(used, inside[HALO], 0.0)
    scratch = (mixed, flux, scaled, acc, faces, inside, to_even, to_all, here)
    apply_operator(field, first, *scratch, TILES, INNER)
    apply_operator(first, second, *scratch, INNER, SLAB)
    sums = [jnp.zeros((1, LANES), jnp.float32)] * 5
    unscale = 1.0 / scale[...]
    for p in range(SLAB):
        b = load(own, p)
        q = first[:, tile_cols(p)] * unscale
        w = second[:, tile_cols(p)] * unscale
        out[pl.ds(p, slots, stride=2 * SLAB), :] = q
        out[pl.ds(p + SLAB, slots, stride=2 * SLAB), :] = w
        for n, (one, two) in enumerate(((b, b), (b, q), (q, q), (b, w), (q, w))):
            sums[n] = sums[n] + jnp.sum(one * two, axis=0, keepdims=True)
    total = jnp.concatenate(sums + [jnp.zeros((3, LANES), jnp.float32)], axis=0)
    partial[...] = total + refs[0][...] if comp > 0 else total


def apply_twice(comp, place, own, before, after, tables, fields, fibre, *so_far):
    scale, to_even, to_all = tables
    slots = scale.shape[0]
    vmem = pl.BlockSpec(memory_space=pltpu.VMEM)
    smem = pl.BlockSpec(memory_space=pltpu.SMEM)
    f32 = lambda *shape: pltpu.VMEM(shape, jnp.float32)
    return pl.pallas_call(
        functools.partial(apply_kernel, comp=comp),
        out_shape=[
            jax.ShapeDtypeStruct((slots * 2 * SLAB, LANES), jnp.float32),
            jax.ShapeDtypeStruct((8, LANES), jnp.float32),
        ],
        in_specs=[smem] + [vmem] * 7 + [smem] + [vmem] * len(so_far),
        out_specs=[vmem, vmem],
        scratch_shapes=[
            f32(slots, TILES * LANES),
            f32(slots, INNER * LANES),
            f32(slots, SLAB * LANES),
            f32(FULL, TILES * LANES),
            f32(6, EVEN, TILES * LANES),
            f32(FULL, INNER * LANES),
            f32(slots, INNER * LANES),
            f32(6 * FACE + 8, TILES * LANES),
        ],
        compiler_params=pltpu.CompilerParams(vmem_limit_bytes=VMEM),
        cost_estimate=estimate(15),
        name="apply_twice",
    )(place, own, before, after, scale, to_even, to_all, fields, fibre, *so_far)


def factor_kernel(total, factors):
    bb, bq, qq, bw, qw = (jnp.sum(total[n : n + 1, :], axis=1, keepdims=True) for n in range(5))
    step_one = bb / bq
    norm = bb - 2.0 * step_one * bq + step_one * step_one * qq
    grown = 1.0 + norm / bb
    curve = grown * grown * bq - step_one * grown * (bw + qq) + step_one * step_one * qw
    step_two = norm / curve
    factors[0:8, :] = jnp.broadcast_to(step_one + step_two * grown, (8, LANES))
    factors[8:16, :] = jnp.broadcast_to(step_one * step_two, (8, LANES))


def combination(total):
    return pl.pallas_call(
        factor_kernel,
        out_shape=jax.ShapeDtypeStruct((16, LANES), jnp.float32),
        cost_estimate=estimate(1),
        name="combination",
    )(total)


def finish_kernel(field, image, factors, *refs):
    modes = field.shape[0]
    solution_field, residual = refs[-2:]
    per_part = modes * 2 * SLAB
    sole, cross = factors[0:8, :], factors[8:16, :]

    def body(step, carry):
        for inner in range(2 * UNROLL):
            mode = step * 2 * UNROLL + inner
            for p in range(SLAB):
                row = mode * 2 * SLAB + p
                b = field[mode, 0, p]
                q = swap_back(image[pl.ds(row, PARTS, stride=per_part), :])
                w = swap_back(image[pl.ds(row + SLAB, PARTS, stride=per_part), :])
                solution_field[mode, 0, p] = sole * b - cross * q
                residual[mode, 0, p] = b - sole * q + cross * w
        return carry

    lax.fori_loop(0, modes // (2 * UNROLL), body, 0)


def finish(field, comp, image, factors, so_far):
    block = pl.BlockSpec((field.shape[0], 1) + field.shape[2:], lambda i: (0, comp, 0, 0, 0))
    vmem = pl.BlockSpec(memory_space=pltpu.VMEM)
    return pl.pallas_call(
        finish_kernel,
        grid=(1,),
        out_shape=[jax.ShapeDtypeStruct(field.shape, jnp.float32)] * 2,
        in_specs=[block, vmem, vmem] + [pl.BlockSpec(memory_space=pl.ANY)] * len(so_far),
        out_specs=[block, block],
        input_output_aliases={3 + n: n for n in range(len(so_far))},
        compiler_params=pltpu.CompilerParams(vmem_limit_bytes=VMEM),
        cost_estimate=estimate(3),
        name="finish",
    )(field, image, factors, *so_far)


def mode_tables(coupling_table, slots):
    lower, upper, variable, code = (coupling_table[:, n] for n in range(4))
    slot = jnp.arange(slots, dtype=jnp.int32)
    is_lower = lower[:, None] == slot
    is_upper = upper[:, None] == slot
    degree = jnp.sum(jnp.where(is_upper, code[:, None], 0), axis=0)
    factor = jnp.where(code == 3, 6, code).astype(jnp.float32)[:, None]
    factorial = jnp.prod(jnp.where(is_upper, factor, 1.0), axis=0)
    root = (degree == 0) & jnp.any(is_lower, axis=0)
    even = (degree == 2) | root
    rank = jnp.sum(jnp.where(even[:, None] & (slot[:, None] < slot), 1, 0), axis=0)
    lower_even = jnp.any(is_lower & even, axis=1)
    is_even_end = jnp.where(lower_even[:, None], is_lower, is_upper)
    is_odd_end = jnp.where(lower_even[:, None], is_upper, is_lower)
    column = variable * EVEN + jnp.sum(jnp.where(is_even_end, rank, 0), axis=1)
    at_column = column[:, None] == jnp.arange(FULL, dtype=jnp.int32)
    down = code.astype(jnp.float32)[:, None]
    first = jnp.where(lower_even[:, None], 1.0, down)
    second = jnp.where(lower_even[:, None], down, 1.0)
    odd_ends = is_odd_end.astype(jnp.float32)
    columns = at_column.astype(jnp.float32)
    half = jnp.bfloat16
    to_even = jnp.dot(
        columns.astype(half).T, (odd_ends * first).astype(half), preferred_element_type=jnp.float32
    )
    to_odd = jnp.dot(
        odd_ends.astype(half).T, (columns * second).astype(half), preferred_element_type=jnp.float32
    )
    pick = (jnp.arange(FULL, dtype=jnp.int32)[:, None] - SPAN == rank) & even
    pick = pick.astype(jnp.float32)
    to_even = (to_even + pick).astype(half)
    to_all = (to_odd + pick.T).astype(half)
    scale = jnp.sqrt(factorial)
    wide = lambda v: jnp.broadcast_to(v[:, None], (slots, LANES))
    twice = lambda v: jnp.concatenate([v, v], axis=1)
    return wide(scale), twice(to_even), twice(to_all)


def all_sum(value):
    for axis, bit in (("space", 1), ("space", 2), ("mode", 1)):
        devices = lax.axis_size(axis)
        value = value + lax.ppermute(value, axis, [(i, i ^ bit) for i in range(devices)])
    others = [
        lax.ppermute(value, "mode", [(i, i ^ bit) for i in range(PARTS)]) for bit in range(2, PARTS, 2)
    ]
    return (value + others[0]) + (others[1] + others[2])


def transposed(right_side, mean_stiffness, ply_stiffness, fibre_weights, ply_map, coupling_table):
    slots = right_side.shape[0] * PARTS
    devices = lax.axis_size("space")
    up = [(i, i + 1) for i in range(devices - 1)]
    down = [(j, i) for i, j in up]
    place = lax.axis_index("mode").astype(jnp.int32).reshape(1)

    def swap(rows):
        return lax.all_to_all(rows, "mode", 0, 0, tiled=True)

    def halo(rows):
        return rows, lax.ppermute(rows, "space", up), lax.ppermute(rows, "space", down)

    (first,) = pack(right_side, (0,))
    both, others = pack(right_side, (1, 2), (mean_stiffness, ply_map), (first,))
    first = halo(swap(first))
    others = swap(others)
    tables = mode_tables(coupling_table, slots)
    both_before = lax.ppermute(both, "space", up)
    both_after = lax.ppermute(both, "space", down)
    fields = stiffness_fields(place, both_before, both, both_after, ply_stiffness)
    image, partial = apply_twice(0, place, *first, tables, fields, fibre_weights)
    images = [swap(image)]
    parts = part_components(others, partial, COMPS - 1)
    for comp, rows in enumerate(parts, 1):
        image, partial = apply_twice(comp, place, *halo(rows), tables, fields, fibre_weights, partial)
        images.append(swap(image))
    factors = combination(all_sum(partial))
    outputs = ()
    for comp in range(COMPS):
        outputs = finish(right_side, comp, images[comp], factors, outputs)
    return tuple(outputs)


def on_device(right_side, mean_stiffness, ply_stiffness, fibre_weights, ply_map, coupling_table):
    args = (right_side, mean_stiffness, ply_stiffness, fibre_weights, ply_map, coupling_table)
    fits = right_side.shape[1:] == (COMPS, SLAB, 8, 128) and (lax.axis_size("mode"), lax.axis_size("space")) == (PARTS, 4)
    return transposed(*args) if fits else plain(*args)


def solution(mesh):
    return jax.shard_map(
        on_device,
        mesh=mesh,
        in_specs=(
            P("mode", None, "space", None, None),
            P("space", None, None),
            P(),
            P(),
            P("space", None, None),
            P(),
        ),
        out_specs=(P("mode", None, "space", None, None), P("mode", None, "space", None, None)),
        check_vma=False,
    )
```

```python
import functools

import jax
import jax.numpy as jnp
from jax import lax
from jax.experimental import pallas as pl
from jax.experimental.pallas import tpu as pltpu
from jax.sharding import PartitionSpec as P

VARS = 10
ITERS = 2


def extended(array, sides, width):
    for axis, dim in sides:
        devices, length = (lax.axis_size(axis), array.shape[dim])
        up = [(i, (i + 1) % devices) for i in range(devices - 1)]
        down = [(j, i) for i, j in up]
        last = lax.slice_in_dim(array, length - width, length, axis=dim)
        leading = lax.slice_in_dim(array, 0, width, axis=dim)
        before = lax.ppermute(last, axis, up)
        after = lax.ppermute(leading, axis, down)
        array = jnp.concatenate([before, array, after], axis=dim)
    return array


def window(array_in, dim_index, offset):
    slicers = [slice(None)] * (array_in.ndim - 3)
    for which in range(3):
        shift_by = offset if which == dim_index else 0
        length_here = array_in.shape[array_in.ndim - 3 + which] - 2
        slicers.append(slice(1 + shift_by, 1 + shift_by + length_here))
    return array_in[tuple(slicers)]


def diffuse(vector, stiffness, fibre_weights):
    vector_pads = [(0, 0)] * (vector.ndim - 2) + [(1, 1), (1, 1)]
    stiff_pads = [(0, 0)] * (stiffness.ndim - 2) + [(1, 1), (1, 1)]
    padded_v = jnp.pad(vector, vector_pads)
    padded_c = jnp.pad(stiffness, stiff_pads)
    centre = window(padded_v, 0, 0)
    middle = window(padded_c, 0, 0)
    result = None
    for dim_index in range(3):
        upper = (
            0.5
            * (middle + window(padded_c, dim_index, 1))
            * (centre - window(padded_v, dim_index, 1))
        )
        lower = (
            0.5
            * (middle + window(padded_c, dim_index, -1))
            * (centre - window(padded_v, dim_index, -1))
        )
        column = fibre_weights[:, dim_index].reshape(3, 1, 1, 1)
        term = column * (upper + lower)
        result = term if result is None else result + term
    return result


def squares(vector):
    return lax.psum(jnp.sum(vector * vector), ("mode", "space"))


def row_table(both_rows, both_cols, both_vars, both_weights, base, mode_dev, slots):
    local_rows = both_rows - base
    valid_rows = (local_rows >= 0) & (local_rows < mode_dev)
    local_rows = jnp.where(valid_rows, local_rows, mode_dev)
    row_coupling = jnp.zeros((VARS, mode_dev, slots), jnp.float32)
    row_coupling = row_coupling.at[both_vars, local_rows, both_cols].add(both_weights, mode="drop")
    return row_coupling.reshape(VARS * mode_dev, slots)


def plain(right_side, mean_stiffness, ply_stiffness, fibre_weights, ply_map, coupling_table):
    mode_dev = right_side.shape[0]
    slots = mode_dev * lax.axis_size("mode")
    base = lax.axis_index("mode") * mode_dev
    first_mode = coupling_table[:, 0]
    second_mode = coupling_table[:, 1]
    variable = coupling_table[:, 2]
    entry_weight = jnp.sqrt(coupling_table[:, 3].astype(jnp.float32))
    both_rows = jnp.concatenate([first_mode, second_mode])
    both_cols = jnp.concatenate([second_mode, first_mode])
    both_vars = jnp.concatenate([variable, variable])
    both_weights = jnp.concatenate([entry_weight, entry_weight])
    plies = jnp.arange(VARS, dtype=jnp.int32).reshape(VARS, 1, 1, 1)
    ply_fields = (ply_map[None] == plies).astype(jnp.float32) * ply_stiffness.reshape(VARS, 1, 1, 1)
    stiff_stack = jnp.concatenate([mean_stiffness[None], ply_fields], axis=0)
    stiff_rims = extended(stiff_stack, (("space", 1),), 1)
    stiff_rims = stiff_rims[:, None]
    row_coupling = row_table(both_rows, both_cols, both_vars, both_weights, base, mode_dev, slots)
    solution_field = jnp.zeros_like(right_side)
    residual = right_side
    direction = right_side
    norm_now = squares(residual)
    for iteration in range(ITERS):
        shard_piece = lax.all_gather(direction, "mode", axis=0, tiled=True)
        mixed = jnp.dot(
            row_coupling,
            shard_piece.reshape(shard_piece.shape[0], -1),
            precision=lax.Precision.HIGHEST,
            preferred_element_type=jnp.float32,
        )
        stacked = jnp.concatenate(
            [direction[None], mixed.reshape((VARS,) + direction.shape)], axis=0
        )
        padded = extended(stacked, (("space", 3),), 1)
        terms = diffuse(padded, stiff_rims[:, None], fibre_weights)
        image = direction + jnp.sum(terms, axis=0)
        step_size = norm_now / lax.psum(jnp.sum(direction * image), ("mode", "space"))
        solution_field = solution_field + step_size * direction
        residual = residual - step_size * image
        norm_next = squares(residual)
        direction = residual + norm_next / norm_now * direction
        norm_now = norm_next
    return (solution_field, residual)


COMPS = 3
SLAB = 3
PARTS = 8
WIDE = 16
ROWS = 4
EVEN = 1 + VARS * (VARS + 1) // 2
SPAN = VARS * EVEN
FULL = 624
INNER = 6
TILES = 8
LANES = 128
VMEM = 56 * 1024 * 1024


def lane_id():
    return lax.broadcasted_iota(jnp.int32, (8, LANES), 1)


def swap_out(tile):
    block = lane_id() // WIDE
    tile = pltpu.roll(tile, 0, 1, stride=WIDE, stride_axis=0)
    for bit in (1, 2, 4):
        tile = jnp.where((block & bit) != 0, pltpu.roll(tile, 8 - bit, 0), tile)
    return tile


def swap_back(tile):
    block = lane_id() // WIDE
    row = lax.broadcasted_iota(jnp.int32, (8, LANES), 0)
    for bit in (1, 2, 4):
        tile = jnp.where((block & bit) != 0, pltpu.roll(tile, bit, 0), tile)
    for bit in (1, 2, 4):
        tile = jnp.where((row & bit) != 0, pltpu.roll(tile, LANES - WIDE * bit, 1), tile)
    return tile


def halo_row(planes):
    lane = lane_id()
    slot = lane % WIDE
    halo = jnp.zeros((8, LANES), jnp.float32)
    for x, plane in planes.items():
        places = [(-1, x + 1), (WIDE, x + 6)]
        if 0 <= x < SLAB:
            places += [(-2, x + 10), (WIDE + 1, x + 13)]
        for offset, place in places:
            inside = (lane >= WIDE) if offset < 0 else (lane < LANES - WIDE)
            moved = pltpu.roll(plane, (place - offset) % LANES, 1)
            halo = jnp.where((slot == place) & inside, moved, halo)
    return halo


UNROLL = 3


def pack_kernel(field, *refs, comps):
    modes = field.shape[0]
    out = refs[-1]
    if len(refs) > 1:
        mean, ply, both = refs[0], refs[1], refs[-2]
        for x in range(SLAB):
            both[0, x] = mean[x]
            both[1, x] = (ply[x] + 1).astype(jnp.float32)
    rows = ROWS * len(comps)
    unroll = 2 * UNROLL // len(comps)

    def body(step, carry):
        for inner in range(unroll):
            mode = step * unroll + inner
            for n, comp in enumerate(comps):
                planes = [field[mode, comp, x] for x in range(SLAB)]
                halo = halo_row(dict(enumerate(planes)))
                for p, tile in enumerate(planes + [halo]):
                    out[pl.ds((n * modes + mode) * ROWS + p, PARTS, stride=rows * modes), :] = swap_out(tile)
        return carry

    lax.fori_loop(0, modes // unroll, body, 0)


def estimate(micros):
    return pl.CostEstimate(flops=int(micros * 1e9), bytes_accessed=int(micros * 3e6), transcendentals=0)


def pack(field, comps, stiffness=(), after=()):
    modes = field.shape[0]
    vmem = pl.BlockSpec(memory_space=pltpu.VMEM)
    shapes = [jax.ShapeDtypeStruct((2,) + s.shape, jnp.float32) for s in stiffness[:1]]
    shapes.append(jax.ShapeDtypeStruct((PARTS * modes * ROWS * len(comps), LANES), jnp.float32))
    return pl.pallas_call(
        functools.partial(pack_kernel, comps=comps),
        grid=(1,),
        out_shape=shapes,
        in_specs=[pl.BlockSpec((modes, max(comps) + 1) + field.shape[2:], lambda i: (0, 0, 0, 0, 0))]
        + [vmem] * len(stiffness)
        + [pl.BlockSpec(memory_space=pl.ANY)] * len(after),
        out_specs=[vmem] * len(shapes),
        compiler_params=pltpu.CompilerParams(vmem_limit_bytes=VMEM),
        cost_estimate=estimate(0.5),
        name="pack",
    )(field, *stiffness, *after)


def copy_kernel(source, ready, goal):
    goal[...] = source[...]


def part_component(rows, n, ready):
    blocks = rows.reshape(PARTS, -1, LANES)
    part = (PARTS, blocks.shape[1] // (COMPS - 1), LANES)
    whole = pl.BlockSpec(memory_space=pl.ANY)
    return pl.pallas_call(
        copy_kernel,
        grid=(1,),
        out_shape=jax.ShapeDtypeStruct(part, jnp.float32),
        in_specs=[pl.BlockSpec(part, lambda i: (0, n, 0)), whole],
        out_specs=pl.BlockSpec(part, lambda i: (0, 0, 0)),
        compiler_params=pltpu.CompilerParams(vmem_limit_bytes=VMEM),
        cost_estimate=estimate(0.5),
        name="part_component",
    )(blocks, ready).reshape(-1, LANES)


def after_rows(table, ready):
    vmem = pl.BlockSpec(memory_space=pltpu.VMEM)
    return pl.pallas_call(
        copy_kernel,
        out_shape=jax.ShapeDtypeStruct(table.shape, table.dtype),
        in_specs=[vmem, pl.BlockSpec(memory_space=pl.ANY)],
        out_specs=vmem,
        cost_estimate=estimate(0.5),
        name="after_rows",
    )(table, ready)


def stiffness_kernel(place, before, both, after, ply_stiffness, fields, wide):
    rows = []
    for kind in range(2):
        planes = {-2: before[kind, 1], -1: before[kind, 2], 3: after[kind, 0], 4: after[kind, 1]}
        planes.update({x: both[kind, x] for x in range(SLAB)})
        halo = halo_row({x: planes[x] for x in range(-1, 4)})
        ordered = [planes[0], planes[1], planes[2], planes[-1], planes[3], halo, planes[-2], planes[4]]
        for t, tile in enumerate(ordered):
            wide[...] = swap_out(tile)
            rows.append(wide[pl.ds(place[0], 1), :])
    for t in range(TILES):
        mean, ply = rows[t], rows[TILES + t]
        cols = slice(LANES * t, LANES * (t + 1))
        for k in range(VARS):
            fields[k : k + 1, cols] = jnp.where(ply == k + 1.0, ply_stiffness[k], 0.0)
        fields[VARS : VARS + 1, cols] = mean
        fields[VARS + 1 : VARS + 2, cols] = jnp.where(ply > 0.0, 1.0, 0.0)
        fields[VARS + 2 : 16, cols] = jnp.zeros((4, LANES), jnp.float32)


def stiffness_fields(place, before, both, after, ply_stiffness):
    vmem = pl.BlockSpec(memory_space=pltpu.VMEM)
    smem = pl.BlockSpec(memory_space=pltpu.SMEM)
    return pl.pallas_call(
        stiffness_kernel,
        out_shape=jax.ShapeDtypeStruct((16, TILES * LANES), jnp.float32),
        in_specs=[smem, vmem, vmem, vmem, smem],
        out_specs=vmem,
        scratch_shapes=[pltpu.VMEM((8, LANES), jnp.float32)],
        cost_estimate=estimate(0.5),
        name="stiffness_fields",
    )(place, before, both, after, ply_stiffness)


AT = {0: 0, 1: 1, 2: 2, -1: 3, 3: 4, -2: 6, 4: 7}
PLACE = {index: x for x, index in AT.items()}
HALO = 5


def neighbour(tiles, index, side, place, full=False, wrap=False):
    t = tiles[index]
    lane = lax.broadcasted_iota(jnp.int32, t.shape, 1)
    slot = lane % WIDE
    roll = lambda v, s: pltpu.roll(v, s % LANES, 1)
    if side in (2, 3) and wrap:
        return roll(t, WIDE if side == 2 else -WIDE)
    if side in (2, 3):
        y = (place + lane // WIDE) & 7
        if side == 2:
            return jnp.where(y > 0, roll(t, WIDE), 0.0)
        return jnp.where(y < 7, roll(t, -WIDE), 0.0)
    if index == HALO:
        if side < 2:
            return roll(t, 1 if side == 0 else -1)
        result = roll(t, -9) if side == 4 else roll(t, -7)
        for x in range(-1, 4) if full else range(SLAB):
            goal, by = (x + 6, x - 9) if side == 4 else (x + 1, x + 1)
            result = jnp.where(slot == goal, roll(tiles[AT[x]], by), result)
        if full:
            result = jnp.where(slot >= 13, roll(t, 7), result) if side == 4 else jnp.where(
                (slot >= 10) & (slot < 13), roll(t, 9), result
            )
        return result
    x = PLACE[index]
    if side < 2:
        return tiles[AT[x - 1 if side == 0 else x + 1]]
    if side == 4:
        return jnp.where(slot == 0, roll(tiles[HALO], -(x + 1)), roll(t, 1))
    return jnp.where(slot == WIDE - 1, roll(tiles[HALO], 9 - x), roll(t, -1))


def sides_of(index, outer):
    if index < outer:
        return range(6)
    return {3: (1,), 4: (0,), HALO: (4, 5), 6: (1,), 7: (0,)}[index]


def split(array):
    high = array.astype(jnp.bfloat16)
    low = (array - high.astype(jnp.float32)).astype(jnp.bfloat16)
    return jnp.concatenate([high, low], axis=0)


STEP = 32
FACE = 16
CENTRE = 6 * FACE
EVEN_BLOCKS = ((0, 32), (32, EVEN))


def tile_cols(t):
    return slice(LANES * t, LANES * (t + 1))


def face_stiffness(fields, faces, weights, place):
    tiles = [fields[:, tile_cols(t)] for t in range(TILES)]
    for t in range(TILES):
        for side in sides_of(t, INNER):
            value = (0.5 * weights[side // 2]) * (tiles[t] + neighbour(tiles, t, side, place, True))
            faces[side * FACE : (side + 1) * FACE, tile_cols(t)] = value
        if t < INNER:
            centre = 1.0 + sum(faces[side * FACE + VARS : side * FACE + VARS + 1, tile_cols(t)] for side in range(6))
            faces[CENTRE : CENTRE + 1, tile_cols(t)] = centre
            lane = lax.broadcasted_iota(jnp.int32, (1, LANES), 1)
            y = (place + lane // WIDE) & 7
            for side, edge in ((2, 0), (3, 7)):
                row = side * FACE + VARS
                faces[row + 1 : row + 2, tile_cols(t)] = jnp.where(
                    y == edge, 0.0, faces[row : row + 1, tile_cols(t)]
                )


CHUNK = 4


def chunks(count):
    return [range(start, min(start + CHUNK, count)) for start in range(0, count, CHUNK)]


def chunk_cols(tiles):
    return slice(LANES * tiles[0], LANES * (tiles[-1] + 1))


def apply_operator(src, dst, mixed, flux, scaled, acc, faces, inside, to_even, to_all, place, inner, outer):
    slots = src.shape[0]

    def face(side, k, t):
        return faces[side * FACE + k : side * FACE + k + 1, tile_cols(t)]

    def mix(tiles):
        cols = chunk_cols(tiles)
        mixed[:, cols] = jnp.dot(to_even[...], split(src[:, cols]), preferred_element_type=jnp.float32)

    def flows(t):
        for low, high in EVEN_BLOCKS:
            total = {}
            for k in range(VARS):
                value = mixed[k * EVEN + low : k * EVEN + high, tile_cols(t)]
                for side in sides_of(t, outer):
                    term = face(side, k, t) * value
                    total[side] = term if k == 0 else total[side] + term
            for side, value in total.items():
                flux[side, low:high, tile_cols(t)] = value

    def scale_even(t):
        for low, high in EVEN_BLOCKS:
            even = EvenTiles(mixed, low, high)
            steps = [even[t] - neighbour(even, t, side, place) for side in range(6)]
            for k in range(VARS):
                total = face(0, k, t) * steps[0]
                for side in range(1, 6):
                    total = total + face(side, k, t) * steps[side]
                scaled[k * EVEN + low : k * EVEN + high, tile_cols(t)] = total
            total = None
            for side in range(6):
                opposite = FluxTiles(flux, side ^ 1, low, high)
                term = flux[side, low:high, tile_cols(t)] - neighbour(opposite, t, side, place)
                total = term if total is None else total + term
            scaled[SPAN + low : SPAN + high, tile_cols(t)] = total
        scaled[SPAN + EVEN : FULL, tile_cols(t)] = jnp.zeros((FULL - SPAN - EVEN, LANES), jnp.float32)

    def spread(tiles):
        cols = chunk_cols(tiles)
        acc[:, cols] = jnp.dot(to_all[...], split(scaled[:, cols]), preferred_element_type=jnp.float32)

    before = ()
    for tiles in chunks(inner):
        mix(tiles)
        for t in before:
            flows(t)
        before = tiles
    for t in before:
        flows(t)
    before = ()
    for tiles in chunks(outer):
        for t in tiles:
            scale_even(t)
        if before:
            spread(before)
        before = tiles
    spread(before)

    def last(step, carry):
        rows = pl.ds(pl.multiple_of(step * STEP, STEP), STEP)
        tiles = [src[rows, tile_cols(t)] for t in range(inner)]
        for t in range(outer):
            result = acc[rows, tile_cols(t)] + faces[CENTRE : CENTRE + 1, tile_cols(t)] * tiles[t]
            for side in range(6):
                row = VARS + 1 if side in (2, 3) else VARS
                result = result - face(side, row, t) * neighbour(tiles, t, side, place, wrap=True)
            if t >= SLAB:
                result = inside[t] * result
            dst[rows, tile_cols(t)] = result
        return carry

    lax.fori_loop(0, slots // STEP, last, 0)


class EvenTiles:
    def __init__(self, mixed, low, high):
        self.mixed, self.low, self.high = mixed, low, high

    def __getitem__(self, t):
        return self.mixed[SPAN + self.low : SPAN + self.high, tile_cols(t)]


class FluxTiles:
    def __init__(self, flux, side, low, high):
        self.flux, self.side, self.low, self.high = flux, side, low, high

    def __getitem__(self, t):
        return self.flux[self.side, self.low : self.high, tile_cols(t)]


def apply_kernel(
    place, own, before, after, scale, to_even, to_all, fields, fibre, *refs, comp,
):
    out, partial, field, first, second, mixed, flux, scaled, acc, faces = refs[-10:]
    slots = scale.shape[0]
    here = place[0]
    face_stiffness(fields, faces, [fibre[comp, d] for d in range(3)], here)
    lane = lax.broadcasted_iota(jnp.int32, (slots, LANES), 1)
    slot = lane % WIDE
    load = lambda ref, p: ref[pl.ds(p, slots, stride=ROWS), :]
    left = pltpu.roll(load(before, 3), LANES - 3, 1)
    right = pltpu.roll(load(after, 3), 3, 1)
    halo = jnp.where((slot == 0) | (slot == 5), left, load(own, 3))
    halo = jnp.where((slot == 4) | (slot == 9), right, halo)
    ordered = [
        load(own, 0), load(own, 1), load(own, 2), load(before, 2), load(after, 0), halo,
        load(before, 1), load(after, 1),
    ]
    for t, tile in enumerate(ordered):
        field[:, tile_cols(t)] = tile * scale[...]
    inside = {t: fields[VARS + 1 : VARS + 2, tile_cols(t)] for t in range(SLAB, INNER)}
    slot = lax.broadcasted_iota(jnp.int32, (1, LANES), 1) % WIDE
    used = ((slot >= 1) & (slot <= 3)) | ((slot >= 6) & (slot <= 8))
    inside[HALO] = jnp.where(used, inside[HALO], 0.0)
    scratch = (mixed, flux, scaled, acc, faces, inside, to_even, to_all, here)
    apply_operator(field, first, *scratch, TILES, INNER)
    apply_operator(first, second, *scratch, INNER, SLAB)
    sums = [jnp.zeros((1, LANES), jnp.float32)] * 5
    unscale = 1.0 / scale[...]
    for p in range(SLAB):
        b = load(own, p)
        q = first[:, tile_cols(p)] * unscale
        w = second[:, tile_cols(p)] * unscale
        out[pl.ds(p, slots, stride=2 * SLAB), :] = q
        out[pl.ds(p + SLAB, slots, stride=2 * SLAB), :] = w
        for n, (one, two) in enumerate(((b, b), (b, q), (q, q), (b, w), (q, w))):
            sums[n] = sums[n] + jnp.sum(one * two, axis=0, keepdims=True)
    total = jnp.concatenate(sums + [jnp.zeros((3, LANES), jnp.float32)], axis=0)
    partial[...] = total + refs[0][...] if comp > 0 else total


def apply_twice(comp, place, own, before, after, tables, fields, fibre, *so_far):
    scale, to_even, to_all = tables
    slots = scale.shape[0]
    vmem = pl.BlockSpec(memory_space=pltpu.VMEM)
    smem = pl.BlockSpec(memory_space=pltpu.SMEM)
    f32 = lambda *shape: pltpu.VMEM(shape, jnp.float32)
    return pl.pallas_call(
        functools.partial(apply_kernel, comp=comp),
        out_shape=[
            jax.ShapeDtypeStruct((slots * 2 * SLAB, LANES), jnp.float32),
            jax.ShapeDtypeStruct((8, LANES), jnp.float32),
        ],
        in_specs=[smem] + [vmem] * 7 + [smem] + [vmem] * len(so_far),
        out_specs=[vmem, vmem],
        scratch_shapes=[
            f32(slots, TILES * LANES),
            f32(slots, INNER * LANES),
            f32(slots, SLAB * LANES),
            f32(FULL, TILES * LANES),
            f32(6, EVEN, TILES * LANES),
            f32(FULL, INNER * LANES),
            f32(slots, INNER * LANES),
            f32(6 * FACE + 8, TILES * LANES),
        ],
        compiler_params=pltpu.CompilerParams(vmem_limit_bytes=VMEM),
        cost_estimate=estimate(15),
        name="apply_twice",
    )(place, own, before, after, scale, to_even, to_all, fields, fibre, *so_far)


def factor_kernel(total, factors):
    bb, bq, qq, bw, qw = (jnp.sum(total[n : n + 1, :], axis=1, keepdims=True) for n in range(5))
    step_one = bb / bq
    norm = bb - 2.0 * step_one * bq + step_one * step_one * qq
    grown = 1.0 + norm / bb
    curve = grown * grown * bq - step_one * grown * (bw + qq) + step_one * step_one * qw
    step_two = norm / curve
    factors[0:8, :] = jnp.broadcast_to(step_one + step_two * grown, (8, LANES))
    factors[8:16, :] = jnp.broadcast_to(step_one * step_two, (8, LANES))


def combination(total):
    return pl.pallas_call(
        factor_kernel,
        out_shape=jax.ShapeDtypeStruct((16, LANES), jnp.float32),
        cost_estimate=estimate(1),
        name="combination",
    )(total)


def finish_kernel(field, image, factors, *refs):
    modes = field.shape[0]
    solution_field, residual = refs[-2:]
    per_part = modes * 2 * SLAB
    sole, cross = factors[0:8, :], factors[8:16, :]

    def body(step, carry):
        for inner in range(2 * UNROLL):
            mode = step * 2 * UNROLL + inner
            for p in range(SLAB):
                row = mode * 2 * SLAB + p
                b = field[mode, 0, p]
                q = swap_back(image[pl.ds(row, PARTS, stride=per_part), :])
                w = swap_back(image[pl.ds(row + SLAB, PARTS, stride=per_part), :])
                solution_field[mode, 0, p] = sole * b - cross * q
                residual[mode, 0, p] = b - sole * q + cross * w
        return carry

    lax.fori_loop(0, modes // (2 * UNROLL), body, 0)


def finish(field, comp, image, factors, so_far):
    block = pl.BlockSpec((field.shape[0], 1) + field.shape[2:], lambda i: (0, comp, 0, 0, 0))
    vmem = pl.BlockSpec(memory_space=pltpu.VMEM)
    return pl.pallas_call(
        finish_kernel,
        grid=(1,),
        out_shape=[jax.ShapeDtypeStruct(field.shape, jnp.float32)] * 2,
        in_specs=[block, vmem, vmem] + [pl.BlockSpec(memory_space=pl.ANY)] * len(so_far),
        out_specs=[block, block],
        input_output_aliases={3 + n: n for n in range(len(so_far))},
        compiler_params=pltpu.CompilerParams(vmem_limit_bytes=VMEM),
        cost_estimate=estimate(3),
        name="finish",
    )(field, image, factors, *so_far)


def mode_tables(coupling_table, slots):
    lower, upper, variable, code = (coupling_table[:, n] for n in range(4))
    slot = jnp.arange(slots, dtype=jnp.int32)
    is_lower = lower[:, None] == slot
    is_upper = upper[:, None] == slot
    degree = jnp.sum(jnp.where(is_upper, code[:, None], 0), axis=0)
    factor = jnp.where(code == 3, 6, code).astype(jnp.float32)[:, None]
    factorial = jnp.prod(jnp.where(is_upper, factor, 1.0), axis=0)
    root = (degree == 0) & jnp.any(is_lower, axis=0)
    even = (degree == 2) | root
    rank = jnp.sum(jnp.where(even[:, None] & (slot[:, None] < slot), 1, 0), axis=0)
    lower_even = jnp.any(is_lower & even, axis=1)
    is_even_end = jnp.where(lower_even[:, None], is_lower, is_upper)
    is_odd_end = jnp.where(lower_even[:, None], is_upper, is_lower)
    column = variable * EVEN + jnp.sum(jnp.where(is_even_end, rank, 0), axis=1)
    at_column = column[:, None] == jnp.arange(FULL, dtype=jnp.int32)
    down = code.astype(jnp.float32)[:, None]
    first = jnp.where(lower_even[:, None], 1.0, down)
    second = jnp.where(lower_even[:, None], down, 1.0)
    odd_ends = is_odd_end.astype(jnp.float32)
    columns = at_column.astype(jnp.float32)
    half = jnp.bfloat16
    to_even = jnp.dot(
        columns.astype(half).T, (odd_ends * first).astype(half), preferred_element_type=jnp.float32
    )
    to_odd = jnp.dot(
        odd_ends.astype(half).T, (columns * second).astype(half), preferred_element_type=jnp.float32
    )
    pick = (jnp.arange(FULL, dtype=jnp.int32)[:, None] - SPAN == rank) & even
    pick = pick.astype(jnp.float32)
    to_even = (to_even + pick).astype(half)
    to_all = (to_odd + pick.T).astype(half)
    scale = jnp.sqrt(factorial)
    wide = lambda v: jnp.broadcast_to(v[:, None], (slots, LANES))
    twice = lambda v: jnp.concatenate([v, v], axis=1)
    return wide(scale), twice(to_even), twice(to_all)


def all_sum(value):
    for axis, bit in (("space", 1), ("space", 2), ("mode", 1)):
        devices = lax.axis_size(axis)
        value = value + lax.ppermute(value, axis, [(i, i ^ bit) for i in range(devices)])
    others = [
        lax.ppermute(value, "mode", [(i, i ^ bit) for i in range(PARTS)]) for bit in range(2, PARTS, 2)
    ]
    return (value + others[0]) + (others[1] + others[2])


def transposed(right_side, mean_stiffness, ply_stiffness, fibre_weights, ply_map, coupling_table):
    slots = right_side.shape[0] * PARTS
    devices = lax.axis_size("space")
    up = [(i, i + 1) for i in range(devices - 1)]
    down = [(j, i) for i, j in up]
    place = lax.axis_index("mode").astype(jnp.int32).reshape(1)

    def swap(rows):
        return lax.all_to_all(rows, "mode", 0, 0, tiled=True)

    def halo(rows):
        return rows, lax.ppermute(rows, "space", up), lax.ppermute(rows, "space", down)

    (first,) = pack(right_side, (0,))
    both, others = pack(right_side, (1, 2), (mean_stiffness, ply_map), (first,))
    first = halo(swap(first))
    others = swap(others)
    tables = mode_tables(after_rows(coupling_table, first[0]), slots)
    both_before = lax.ppermute(both, "space", up)
    both_after = lax.ppermute(both, "space", down)
    fields = stiffness_fields(place, both_before, both, both_after, ply_stiffness)
    image, partial = apply_twice(0, place, *first, tables, fields, fibre_weights)
    images = [swap(image)]
    for comp in range(1, COMPS):
        rows = halo(part_component(others, comp - 1, partial))
        image, partial = apply_twice(comp, place, *rows, tables, fields, fibre_weights, partial)
        images.append(swap(image))
    factors = combination(all_sum(partial))
    outputs = ()
    for comp in range(COMPS):
        outputs = finish(right_side, comp, images[comp], factors, outputs)
    return tuple(outputs)


def on_device(right_side, mean_stiffness, ply_stiffness, fibre_weights, ply_map, coupling_table):
    args = (right_side, mean_stiffness, ply_stiffness, fibre_weights, ply_map, coupling_table)
    fits = right_side.shape[1:] == (COMPS, SLAB, 8, 128) and (lax.axis_size("mode"), lax.axis_size("space")) == (PARTS, 4)
    return transposed(*args) if fits else plain(*args)


def solution(mesh):
    return jax.shard_map(
        on_device,
        mesh=mesh,
        in_specs=(
            P("mode", None, "space", None, None),
            P("space", None, None),
            P(),
            P(),
            P("space", None, None),
            P(),
        ),
        out_specs=(P("mode", None, "space", None, None), P("mode", None, "space", None, None)),
        check_vma=False,
    )
```

```python
import functools

import jax
import jax.numpy as jnp
from jax import lax
from jax.experimental import pallas as pl
from jax.experimental.pallas import tpu as pltpu
from jax.sharding import PartitionSpec as P

VARS = 10
ITERS = 2


def extended(array, sides, width):
    for axis, dim in sides:
        devices, length = (lax.axis_size(axis), array.shape[dim])
        up = [(i, (i + 1) % devices) for i in range(devices - 1)]
        down = [(j, i) for i, j in up]
        last = lax.slice_in_dim(array, length - width, length, axis=dim)
        leading = lax.slice_in_dim(array, 0, width, axis=dim)
        before = lax.ppermute(last, axis, up)
        after = lax.ppermute(leading, axis, down)
        array = jnp.concatenate([before, array, after], axis=dim)
    return array


def window(array_in, dim_index, offset):
    slicers = [slice(None)] * (array_in.ndim - 3)
    for which in range(3):
        shift_by = offset if which == dim_index else 0
        length_here = array_in.shape[array_in.ndim - 3 + which] - 2
        slicers.append(slice(1 + shift_by, 1 + shift_by + length_here))
    return array_in[tuple(slicers)]


def diffuse(vector, stiffness, fibre_weights):
    vector_pads = [(0, 0)] * (vector.ndim - 2) + [(1, 1), (1, 1)]
    stiff_pads = [(0, 0)] * (stiffness.ndim - 2) + [(1, 1), (1, 1)]
    padded_v = jnp.pad(vector, vector_pads)
    padded_c = jnp.pad(stiffness, stiff_pads)
    centre = window(padded_v, 0, 0)
    middle = window(padded_c, 0, 0)
    result = None
    for dim_index in range(3):
        upper = (
            0.5
            * (middle + window(padded_c, dim_index, 1))
            * (centre - window(padded_v, dim_index, 1))
        )
        lower = (
            0.5
            * (middle + window(padded_c, dim_index, -1))
            * (centre - window(padded_v, dim_index, -1))
        )
        column = fibre_weights[:, dim_index].reshape(3, 1, 1, 1)
        term = column * (upper + lower)
        result = term if result is None else result + term
    return result


def squares(vector):
    return lax.psum(jnp.sum(vector * vector), ("mode", "space"))


def row_table(both_rows, both_cols, both_vars, both_weights, base, mode_dev, slots):
    local_rows = both_rows - base
    valid_rows = (local_rows >= 0) & (local_rows < mode_dev)
    local_rows = jnp.where(valid_rows, local_rows, mode_dev)
    row_coupling = jnp.zeros((VARS, mode_dev, slots), jnp.float32)
    row_coupling = row_coupling.at[both_vars, local_rows, both_cols].add(both_weights, mode="drop")
    return row_coupling.reshape(VARS * mode_dev, slots)


def plain(right_side, mean_stiffness, ply_stiffness, fibre_weights, ply_map, coupling_table):
    mode_dev = right_side.shape[0]
    slots = mode_dev * lax.axis_size("mode")
    base = lax.axis_index("mode") * mode_dev
    first_mode = coupling_table[:, 0]
    second_mode = coupling_table[:, 1]
    variable = coupling_table[:, 2]
    entry_weight = jnp.sqrt(coupling_table[:, 3].astype(jnp.float32))
    both_rows = jnp.concatenate([first_mode, second_mode])
    both_cols = jnp.concatenate([second_mode, first_mode])
    both_vars = jnp.concatenate([variable, variable])
    both_weights = jnp.concatenate([entry_weight, entry_weight])
    plies = jnp.arange(VARS, dtype=jnp.int32).reshape(VARS, 1, 1, 1)
    ply_fields = (ply_map[None] == plies).astype(jnp.float32) * ply_stiffness.reshape(VARS, 1, 1, 1)
    stiff_stack = jnp.concatenate([mean_stiffness[None], ply_fields], axis=0)
    stiff_rims = extended(stiff_stack, (("space", 1),), 1)
    stiff_rims = stiff_rims[:, None]
    row_coupling = row_table(both_rows, both_cols, both_vars, both_weights, base, mode_dev, slots)
    solution_field = jnp.zeros_like(right_side)
    residual = right_side
    direction = right_side
    norm_now = squares(residual)
    for iteration in range(ITERS):
        shard_piece = lax.all_gather(direction, "mode", axis=0, tiled=True)
        mixed = jnp.dot(
            row_coupling,
            shard_piece.reshape(shard_piece.shape[0], -1),
            precision=lax.Precision.HIGHEST,
            preferred_element_type=jnp.float32,
        )
        stacked = jnp.concatenate(
            [direction[None], mixed.reshape((VARS,) + direction.shape)], axis=0
        )
        padded = extended(stacked, (("space", 3),), 1)
        terms = diffuse(padded, stiff_rims[:, None], fibre_weights)
        image = direction + jnp.sum(terms, axis=0)
        step_size = norm_now / lax.psum(jnp.sum(direction * image), ("mode", "space"))
        solution_field = solution_field + step_size * direction
        residual = residual - step_size * image
        norm_next = squares(residual)
        direction = residual + norm_next / norm_now * direction
        norm_now = norm_next
    return (solution_field, residual)


COMPS = 3
SLAB = 3
PARTS = 8
WIDE = 16
ROWS = 4
EVEN = 1 + VARS * (VARS + 1) // 2
SPAN = VARS * EVEN
FULL = 624
INNER = 6
TILES = 8
LANES = 128
VMEM = 56 * 1024 * 1024


def lane_id():
    return lax.broadcasted_iota(jnp.int32, (8, LANES), 1)


def swap_out(tile):
    block = lane_id() // WIDE
    tile = pltpu.roll(tile, 0, 1, stride=WIDE, stride_axis=0)
    for bit in (1, 2, 4):
        tile = jnp.where((block & bit) != 0, pltpu.roll(tile, 8 - bit, 0), tile)
    return tile


def swap_back(tile):
    block = lane_id() // WIDE
    row = lax.broadcasted_iota(jnp.int32, (8, LANES), 0)
    for bit in (1, 2, 4):
        tile = jnp.where((block & bit) != 0, pltpu.roll(tile, bit, 0), tile)
    for bit in (1, 2, 4):
        tile = jnp.where((row & bit) != 0, pltpu.roll(tile, LANES - WIDE * bit, 1), tile)
    return tile


def halo_row(planes):
    lane = lane_id()
    slot = lane % WIDE
    halo = jnp.zeros((8, LANES), jnp.float32)
    for x, plane in planes.items():
        places = [(-1, x + 1), (WIDE, x + 6)]
        if 0 <= x < SLAB:
            places += [(-2, x + 10), (WIDE + 1, x + 13)]
        for offset, place in places:
            inside = (lane >= WIDE) if offset < 0 else (lane < LANES - WIDE)
            moved = pltpu.roll(plane, (place - offset) % LANES, 1)
            halo = jnp.where((slot == place) & inside, moved, halo)
    return halo


UNROLL = 3


def pack_kernel(field, *refs, comps):
    modes = field.shape[0]
    out = refs[-1]
    if len(refs) > 1:
        mean, ply, both = refs[0], refs[1], refs[-2]
        for x in range(SLAB):
            both[0, x] = mean[x]
            both[1, x] = (ply[x] + 1).astype(jnp.float32)
    rows = ROWS * len(comps)
    unroll = 2 * UNROLL // len(comps)

    def body(step, carry):
        for inner in range(unroll):
            mode = step * unroll + inner
            for n, comp in enumerate(comps):
                planes = [field[mode, comp, x] for x in range(SLAB)]
                halo = halo_row(dict(enumerate(planes)))
                for p, tile in enumerate(planes + [halo]):
                    out[pl.ds((n * modes + mode) * ROWS + p, PARTS, stride=rows * modes), :] = swap_out(tile)
        return carry

    lax.fori_loop(0, modes // unroll, body, 0)


def estimate(micros):
    return pl.CostEstimate(flops=int(micros * 1e9), bytes_accessed=int(micros * 3e6), transcendentals=0)


def pack(field, comps, stiffness=(), after=()):
    modes = field.shape[0]
    vmem = pl.BlockSpec(memory_space=pltpu.VMEM)
    shapes = [jax.ShapeDtypeStruct((2,) + s.shape, jnp.float32) for s in stiffness[:1]]
    shapes.append(jax.ShapeDtypeStruct((PARTS * modes * ROWS * len(comps), LANES), jnp.float32))
    return pl.pallas_call(
        functools.partial(pack_kernel, comps=comps),
        grid=(1,),
        out_shape=shapes,
        in_specs=[pl.BlockSpec((modes, max(comps) + 1) + field.shape[2:], lambda i: (0, 0, 0, 0, 0))]
        + [vmem] * len(stiffness)
        + [pl.BlockSpec(memory_space=pl.ANY)] * len(after),
        out_specs=[vmem] * len(shapes),
        compiler_params=pltpu.CompilerParams(vmem_limit_bytes=VMEM),
        cost_estimate=estimate(0.5),
        name="pack",
    )(field, *stiffness, *after)


def copy_kernel(source, ready, goal):
    goal[...] = source[...]


def part_component(rows, n, ready):
    blocks = rows.reshape(PARTS, -1, LANES)
    part = (PARTS, blocks.shape[1] // (COMPS - 1), LANES)
    whole = pl.BlockSpec(memory_space=pl.ANY)
    return pl.pallas_call(
        copy_kernel,
        grid=(1,),
        out_shape=jax.ShapeDtypeStruct(part, jnp.float32),
        in_specs=[pl.BlockSpec(part, lambda i: (0, n, 0)), whole],
        out_specs=pl.BlockSpec(part, lambda i: (0, 0, 0)),
        compiler_params=pltpu.CompilerParams(vmem_limit_bytes=VMEM),
        cost_estimate=estimate(0.5),
        name="part_component",
    )(blocks, ready).reshape(-1, LANES)


def after_rows(table, ready):
    vmem = pl.BlockSpec(memory_space=pltpu.VMEM)
    return pl.pallas_call(
        copy_kernel,
        out_shape=jax.ShapeDtypeStruct(table.shape, table.dtype),
        in_specs=[vmem, pl.BlockSpec(memory_space=pl.ANY)],
        out_specs=vmem,
        cost_estimate=estimate(0.5),
        name="after_rows",
    )(table, ready)


def stiffness_kernel(place, before, both, after, ply_stiffness, fields, wide):
    rows = []
    for kind in range(2):
        planes = {-2: before[kind, 1], -1: before[kind, 2], 3: after[kind, 0], 4: after[kind, 1]}
        planes.update({x: both[kind, x] for x in range(SLAB)})
        halo = halo_row({x: planes[x] for x in range(-1, 4)})
        ordered = [planes[0], planes[1], planes[2], planes[-1], planes[3], halo, planes[-2], planes[4]]
        for t, tile in enumerate(ordered):
            wide[...] = swap_out(tile)
            rows.append(wide[pl.ds(place[0], 1), :])
    for t in range(TILES):
        mean, ply = rows[t], rows[TILES + t]
        cols = slice(LANES * t, LANES * (t + 1))
        for k in range(VARS):
            fields[k : k + 1, cols] = jnp.where(ply == k + 1.0, ply_stiffness[k], 0.0)
        fields[VARS : VARS + 1, cols] = mean
        fields[VARS + 1 : VARS + 2, cols] = jnp.where(ply > 0.0, 1.0, 0.0)
        fields[VARS + 2 : 16, cols] = jnp.zeros((4, LANES), jnp.float32)


def stiffness_fields(place, before, both, after, ply_stiffness):
    vmem = pl.BlockSpec(memory_space=pltpu.VMEM)
    smem = pl.BlockSpec(memory_space=pltpu.SMEM)
    return pl.pallas_call(
        stiffness_kernel,
        out_shape=jax.ShapeDtypeStruct((16, TILES * LANES), jnp.float32),
        in_specs=[smem, vmem, vmem, vmem, smem],
        out_specs=vmem,
        scratch_shapes=[pltpu.VMEM((8, LANES), jnp.float32)],
        cost_estimate=estimate(0.5),
        name="stiffness_fields",
    )(place, before, both, after, ply_stiffness)


AT = {0: 0, 1: 1, 2: 2, -1: 3, 3: 4, -2: 6, 4: 7}
PLACE = {index: x for x, index in AT.items()}
HALO = 5


def neighbour(tiles, index, side, place, full=False, wrap=False):
    t = tiles[index]
    lane = lax.broadcasted_iota(jnp.int32, t.shape, 1)
    slot = lane % WIDE
    roll = lambda v, s: pltpu.roll(v, s % LANES, 1)
    if side in (2, 3) and wrap:
        return roll(t, WIDE if side == 2 else -WIDE)
    if side in (2, 3):
        y = (place + lane // WIDE) & 7
        if side == 2:
            return jnp.where(y > 0, roll(t, WIDE), 0.0)
        return jnp.where(y < 7, roll(t, -WIDE), 0.0)
    if index == HALO:
        if side < 2:
            return roll(t, 1 if side == 0 else -1)
        result = roll(t, -9) if side == 4 else roll(t, -7)
        for x in range(-1, 4) if full else range(SLAB):
            goal, by = (x + 6, x - 9) if side == 4 else (x + 1, x + 1)
            result = jnp.where(slot == goal, roll(tiles[AT[x]], by), result)
        if full:
            result = jnp.where(slot >= 13, roll(t, 7), result) if side == 4 else jnp.where(
                (slot >= 10) & (slot < 13), roll(t, 9), result
            )
        return result
    x = PLACE[index]
    if side < 2:
        return tiles[AT[x - 1 if side == 0 else x + 1]]
    if side == 4:
        return jnp.where(slot == 0, roll(tiles[HALO], -(x + 1)), roll(t, 1))
    return jnp.where(slot == WIDE - 1, roll(tiles[HALO], 9 - x), roll(t, -1))


def sides_of(index, outer):
    if index < outer:
        return range(6)
    return {3: (1,), 4: (0,), HALO: (4, 5), 6: (1,), 7: (0,)}[index]


def split(array):
    high = array.astype(jnp.bfloat16)
    low = (array - high.astype(jnp.float32)).astype(jnp.bfloat16)
    return jnp.concatenate([high, low], axis=0)


STEP = 32
FACE = 16
CENTRE = 6 * FACE
EVEN_BLOCKS = ((0, 32), (32, EVEN))


def tile_cols(t):
    return slice(LANES * t, LANES * (t + 1))


def face_stiffness(fields, faces, weights, place):
    tiles = [fields[:, tile_cols(t)] for t in range(TILES)]
    for t in range(TILES):
        for side in sides_of(t, INNER):
            value = (0.5 * weights[side // 2]) * (tiles[t] + neighbour(tiles, t, side, place, True))
            faces[side * FACE : (side + 1) * FACE, tile_cols(t)] = value
        if t < INNER:
            centre = 1.0 + sum(faces[side * FACE + VARS : side * FACE + VARS + 1, tile_cols(t)] for side in range(6))
            faces[CENTRE : CENTRE + 1, tile_cols(t)] = centre
            lane = lax.broadcasted_iota(jnp.int32, (1, LANES), 1)
            y = (place + lane // WIDE) & 7
            for side, edge in ((2, 0), (3, 7)):
                row = side * FACE + VARS
                faces[row + 1 : row + 2, tile_cols(t)] = jnp.where(
                    y == edge, 0.0, faces[row : row + 1, tile_cols(t)]
                )


CHUNK = 4


def chunks(count):
    return [range(start, min(start + CHUNK, count)) for start in range(0, count, CHUNK)]


def chunk_cols(tiles):
    return slice(LANES * tiles[0], LANES * (tiles[-1] + 1))


def apply_operator(src, dst, mixed, flux, scaled, acc, faces, inside, to_even, to_all, place, inner, outer):
    slots = src.shape[0]

    def face(side, k, t):
        return faces[side * FACE + k : side * FACE + k + 1, tile_cols(t)]

    def mix(tiles):
        cols = chunk_cols(tiles)
        mixed[:, cols] = jnp.dot(to_even[...], split(src[:, cols]), preferred_element_type=jnp.float32)

    def flows(t):
        for low, high in EVEN_BLOCKS:
            total = {}
            for k in range(VARS):
                value = mixed[k * EVEN + low : k * EVEN + high, tile_cols(t)]
                for side in sides_of(t, outer):
                    term = face(side, k, t) * value
                    total[side] = term if k == 0 else total[side] + term
            for side, value in total.items():
                flux[side, low:high, tile_cols(t)] = value

    def scale_even(t):
        for low, high in EVEN_BLOCKS:
            even = EvenTiles(mixed, low, high)
            steps = [even[t] - neighbour(even, t, side, place) for side in range(6)]
            for k in range(VARS):
                total = face(0, k, t) * steps[0]
                for side in range(1, 6):
                    total = total + face(side, k, t) * steps[side]
                scaled[k * EVEN + low : k * EVEN + high, tile_cols(t)] = total
            total = None
            for side in range(6):
                opposite = FluxTiles(flux, side ^ 1, low, high)
                term = flux[side, low:high, tile_cols(t)] - neighbour(opposite, t, side, place)
                total = term if total is None else total + term
            scaled[SPAN + low : SPAN + high, tile_cols(t)] = total
        scaled[SPAN + EVEN : FULL, tile_cols(t)] = jnp.zeros((FULL - SPAN - EVEN, LANES), jnp.float32)

    def spread(tiles):
        cols = chunk_cols(tiles)
        acc[:, cols] = jnp.dot(to_all[...], split(scaled[:, cols]), preferred_element_type=jnp.float32)

    before = ()
    for tiles in chunks(inner):
        mix(tiles)
        for t in before:
            flows(t)
        before = tiles
    for t in before:
        flows(t)
    before = ()
    for tiles in chunks(outer):
        for t in tiles:
            scale_even(t)
        if before:
            spread(before)
        before = tiles
    spread(before)

    def last(step, carry):
        rows = pl.ds(pl.multiple_of(step * STEP, STEP), STEP)
        tiles = [src[rows, tile_cols(t)] for t in range(inner)]
        for t in range(outer):
            result = acc[rows, tile_cols(t)] + faces[CENTRE : CENTRE + 1, tile_cols(t)] * tiles[t]
            for side in range(6):
                row = VARS + 1 if side in (2, 3) else VARS
                result = result - face(side, row, t) * neighbour(tiles, t, side, place, wrap=True)
            if t >= SLAB:
                result = inside[t] * result
            dst[rows, tile_cols(t)] = result
        return carry

    lax.fori_loop(0, slots // STEP, last, 0)


class EvenTiles:
    def __init__(self, mixed, low, high):
        self.mixed, self.low, self.high = mixed, low, high

    def __getitem__(self, t):
        return self.mixed[SPAN + self.low : SPAN + self.high, tile_cols(t)]


class FluxTiles:
    def __init__(self, flux, side, low, high):
        self.flux, self.side, self.low, self.high = flux, side, low, high

    def __getitem__(self, t):
        return self.flux[self.side, self.low : self.high, tile_cols(t)]


def apply_kernel(
    place, own, before, after, scale, to_even, to_all, fields, fibre, *refs, comp,
):
    out, partial, field, first, second, mixed, flux, scaled, acc, faces = refs[-10:]
    slots = scale.shape[0]
    here = place[0]
    face_stiffness(fields, faces, [fibre[comp, d] for d in range(3)], here)
    lane = lax.broadcasted_iota(jnp.int32, (slots, LANES), 1)
    slot = lane % WIDE
    load = lambda ref, p: ref[pl.ds(p, slots, stride=ROWS), :]
    left = pltpu.roll(load(before, 3), LANES - 3, 1)
    right = pltpu.roll(load(after, 3), 3, 1)
    halo = jnp.where((slot == 0) | (slot == 5), left, load(own, 3))
    halo = jnp.where((slot == 4) | (slot == 9), right, halo)
    ordered = [
        load(own, 0), load(own, 1), load(own, 2), load(before, 2), load(after, 0), halo,
        load(before, 1), load(after, 1),
    ]
    for t, tile in enumerate(ordered):
        field[:, tile_cols(t)] = tile * scale[...]
    inside = {t: fields[VARS + 1 : VARS + 2, tile_cols(t)] for t in range(SLAB, INNER)}
    slot = lax.broadcasted_iota(jnp.int32, (1, LANES), 1) % WIDE
    used = ((slot >= 1) & (slot <= 3)) | ((slot >= 6) & (slot <= 8))
    inside[HALO] = jnp.where(used, inside[HALO], 0.0)
    scratch = (mixed, flux, scaled, acc, faces, inside, to_even, to_all, here)
    apply_operator(field, first, *scratch, TILES, INNER)
    apply_operator(first, second, *scratch, INNER, SLAB)
    sums = [jnp.zeros((1, LANES), jnp.float32)] * 5
    unscale = 1.0 / scale[...]
    for p in range(SLAB):
        b = load(own, p)
        q = first[:, tile_cols(p)] * unscale
        w = second[:, tile_cols(p)] * unscale
        out[pl.ds(p, slots, stride=2 * SLAB), :] = q
        out[pl.ds(p + SLAB, slots, stride=2 * SLAB), :] = w
        for n, (one, two) in enumerate(((b, b), (b, q), (q, q), (b, w), (q, w))):
            sums[n] = sums[n] + jnp.sum(one * two, axis=0, keepdims=True)
    total = jnp.concatenate(sums + [jnp.zeros((3, LANES), jnp.float32)], axis=0)
    partial[...] = total + refs[0][...] if comp > 0 else total


def apply_twice(comp, place, own, before, after, tables, fields, fibre, *so_far):
    scale, to_even, to_all = tables
    slots = scale.shape[0]
    vmem = pl.BlockSpec(memory_space=pltpu.VMEM)
    smem = pl.BlockSpec(memory_space=pltpu.SMEM)
    f32 = lambda *shape: pltpu.VMEM(shape, jnp.float32)
    return pl.pallas_call(
        functools.partial(apply_kernel, comp=comp),
        out_shape=[
            jax.ShapeDtypeStruct((slots * 2 * SLAB, LANES), jnp.float32),
            jax.ShapeDtypeStruct((8, LANES), jnp.float32),
        ],
        in_specs=[smem] + [vmem] * 7 + [smem] + [vmem] * len(so_far),
        out_specs=[vmem, vmem],
        scratch_shapes=[
            f32(slots, TILES * LANES),
            f32(slots, INNER * LANES),
            f32(slots, SLAB * LANES),
            f32(FULL, TILES * LANES),
            f32(6, EVEN, TILES * LANES),
            f32(FULL, INNER * LANES),
            f32(slots, INNER * LANES),
            f32(6 * FACE + 8, TILES * LANES),
        ],
        compiler_params=pltpu.CompilerParams(vmem_limit_bytes=VMEM),
        cost_estimate=estimate(2),
        name="apply_twice",
    )(place, own, before, after, scale, to_even, to_all, fields, fibre, *so_far)


def combination(total):
    bb, bq, qq, bw, qw = (jnp.sum(total[n : n + 1, :], axis=1, keepdims=True) for n in range(5))
    step_one = bb / bq
    norm = bb - 2.0 * step_one * bq + step_one * step_one * qq
    grown = 1.0 + norm / bb
    curve = grown * grown * bq - step_one * grown * (bw + qq) + step_one * step_one * qw
    step_two = norm / curve
    return step_one + step_two * grown, step_one * step_two


def unpack_kernel(image, natural):
    modes = natural.shape[1]
    per_part = modes * 2 * SLAB

    def body(step, carry):
        for inner in range(2 * UNROLL):
            mode = step * 2 * UNROLL + inner
            for power in range(2):
                for p in range(SLAB):
                    row = (mode * 2 + power) * SLAB + p
                    natural[power, mode, p] = swap_back(image[pl.ds(row, PARTS, stride=per_part), :])
        return carry

    lax.fori_loop(0, modes // (2 * UNROLL), body, 0)


def unpack(image, modes):
    vmem = pl.BlockSpec(memory_space=pltpu.VMEM)
    return pl.pallas_call(
        unpack_kernel,
        out_shape=jax.ShapeDtypeStruct((2, modes, SLAB, 8, LANES), jnp.float32),
        in_specs=[vmem],
        out_specs=vmem,
        compiler_params=pltpu.CompilerParams(vmem_limit_bytes=VMEM),
        cost_estimate=estimate(3),
        name="unpack",
    )(image)


STEPS = 2


def finish_kernel(field, total, image, *refs):
    *natural, solution_field, residual, factors = refs
    modes = field.shape[0]
    per_part = STEPS * modes * 2 * SLAB

    @pl.when(pl.program_id(0) == 0)
    def _():
        sole, cross = combination(total)
        factors[0:8, :] = jnp.broadcast_to(sole, (8, LANES))
        factors[8:16, :] = jnp.broadcast_to(cross, (8, LANES))

    sole, cross = factors[0:8, :], factors[8:16, :]
    first = pl.program_id(0) * modes

    def body(step, carry):
        for inner in range(2 * UNROLL):
            mode = step * 2 * UNROLL + inner
            for comp in range(COMPS):
                for p in range(SLAB):
                    b = field[mode, comp, p]
                    if comp < len(natural):
                        q, w = natural[comp][0, mode, p], natural[comp][1, mode, p]
                    else:
                        row = (first + mode) * 2 * SLAB + p
                        q = swap_back(image[pl.ds(row, PARTS, stride=per_part), :])
                        w = swap_back(image[pl.ds(row + SLAB, PARTS, stride=per_part), :])
                    solution_field[mode, comp, p] = sole * b - cross * q
                    residual[mode, comp, p] = b - sole * q + cross * w
        return carry

    lax.fori_loop(0, modes // (2 * UNROLL), body, 0)


def finish(field, total, image, *natural):
    rows = field.shape[0] // STEPS
    block = pl.BlockSpec((rows,) + field.shape[1:], lambda i: (i, 0, 0, 0, 0))
    vmem = pl.BlockSpec(memory_space=pltpu.VMEM)
    return pl.pallas_call(
        finish_kernel,
        grid=(STEPS,),
        out_shape=[jax.ShapeDtypeStruct(field.shape, jnp.float32)] * 2,
        in_specs=[block, vmem, vmem]
        + [pl.BlockSpec((2, rows) + field.shape[2:], lambda i: (0, i, 0, 0, 0))] * len(natural),
        out_specs=[block, block],
        scratch_shapes=[pltpu.VMEM((16, LANES), jnp.float32)],
        compiler_params=pltpu.CompilerParams(vmem_limit_bytes=VMEM),
        cost_estimate=estimate(6),
        name="finish",
    )(field, total, image, *natural)


def mode_tables(coupling_table, slots):
    lower, upper, variable, code = (coupling_table[:, n] for n in range(4))
    slot = jnp.arange(slots, dtype=jnp.int32)
    is_lower = lower[:, None] == slot
    is_upper = upper[:, None] == slot
    degree = jnp.sum(jnp.where(is_upper, code[:, None], 0), axis=0)
    factor = jnp.where(code == 3, 6, code).astype(jnp.float32)[:, None]
    factorial = jnp.prod(jnp.where(is_upper, factor, 1.0), axis=0)
    root = (degree == 0) & jnp.any(is_lower, axis=0)
    even = (degree == 2) | root
    rank = jnp.sum(jnp.where(even[:, None] & (slot[:, None] < slot), 1, 0), axis=0)
    lower_even = jnp.any(is_lower & even, axis=1)
    is_even_end = jnp.where(lower_even[:, None], is_lower, is_upper)
    is_odd_end = jnp.where(lower_even[:, None], is_upper, is_lower)
    column = variable * EVEN + jnp.sum(jnp.where(is_even_end, rank, 0), axis=1)
    at_column = column[:, None] == jnp.arange(FULL, dtype=jnp.int32)
    down = code.astype(jnp.float32)[:, None]
    first = jnp.where(lower_even[:, None], 1.0, down)
    second = jnp.where(lower_even[:, None], down, 1.0)
    odd_ends = is_odd_end.astype(jnp.float32)
    columns = at_column.astype(jnp.float32)
    half = jnp.bfloat16
    to_even = jnp.dot(
        columns.astype(half).T, (odd_ends * first).astype(half), preferred_element_type=jnp.float32
    )
    to_odd = jnp.dot(
        odd_ends.astype(half).T, (columns * second).astype(half), preferred_element_type=jnp.float32
    )
    pick = (jnp.arange(FULL, dtype=jnp.int32)[:, None] - SPAN == rank) & even
    pick = pick.astype(jnp.float32)
    to_even = (to_even + pick).astype(half)
    to_all = (to_odd + pick.T).astype(half)
    scale = jnp.sqrt(factorial)
    wide = lambda v: jnp.broadcast_to(v[:, None], (slots, LANES))
    twice = lambda v: jnp.concatenate([v, v], axis=1)
    return wide(scale), twice(to_even), twice(to_all)


def all_sum(value):
    for axis, bit in (("space", 1), ("space", 2), ("mode", 1)):
        devices = lax.axis_size(axis)
        value = value + lax.ppermute(value, axis, [(i, i ^ bit) for i in range(devices)])
    others = [
        lax.ppermute(value, "mode", [(i, i ^ bit) for i in range(PARTS)]) for bit in range(2, PARTS, 2)
    ]
    return (value + others[0]) + (others[1] + others[2])


def transposed(right_side, mean_stiffness, ply_stiffness, fibre_weights, ply_map, coupling_table):
    slots = right_side.shape[0] * PARTS
    devices = lax.axis_size("space")
    up = [(i, i + 1) for i in range(devices - 1)]
    down = [(j, i) for i, j in up]
    place = lax.axis_index("mode").astype(jnp.int32).reshape(1)

    def swap(rows):
        return lax.all_to_all(rows, "mode", 0, 0, tiled=True)

    def halo(rows):
        return rows, lax.ppermute(rows, "space", up), lax.ppermute(rows, "space", down)

    (first,) = pack(right_side, (0,))
    both, others = pack(right_side, (1, 2), (mean_stiffness, ply_map), (first,))
    first = halo(swap(first))
    others = swap(others)
    tables = mode_tables(after_rows(coupling_table, first[0]), slots)
    both_before = lax.ppermute(both, "space", up)
    both_after = lax.ppermute(both, "space", down)
    fields = stiffness_fields(place, both_before, both, both_after, ply_stiffness)
    image, partial = apply_twice(0, place, *first, tables, fields, fibre_weights)
    images = [swap(image)]
    for comp in range(1, COMPS):
        rows = halo(part_component(others, comp - 1, partial))
        image, partial = apply_twice(comp, place, *rows, tables, fields, fibre_weights, partial)
        images.append(swap(image))
    natural = [unpack(image, right_side.shape[0]) for image in images[:-1]]
    return tuple(finish(right_side, all_sum(partial), images[-1], *natural))


def on_device(right_side, mean_stiffness, ply_stiffness, fibre_weights, ply_map, coupling_table):
    args = (right_side, mean_stiffness, ply_stiffness, fibre_weights, ply_map, coupling_table)
    fits = right_side.shape[1:] == (COMPS, SLAB, 8, 128) and (lax.axis_size("mode"), lax.axis_size("space")) == (PARTS, 4)
    return transposed(*args) if fits else plain(*args)


def solution(mesh):
    return jax.shard_map(
        on_device,
        mesh=mesh,
        in_specs=(
            P("mode", None, "space", None, None),
            P("space", None, None),
            P(),
            P(),
            P("space", None, None),
            P(),
        ),
        out_specs=(P("mode", None, "space", None, None), P("mode", None, "space", None, None)),
        check_vma=False,
    )
```

```python
import functools

import jax
import jax.numpy as jnp
from jax import lax
from jax.experimental import pallas as pl
from jax.experimental.pallas import tpu as pltpu
from jax.sharding import PartitionSpec as P

VARS = 10
ITERS = 2


def extended(array, sides, width):
    for axis, dim in sides:
        devices, length = (lax.axis_size(axis), array.shape[dim])
        up = [(i, (i + 1) % devices) for i in range(devices - 1)]
        down = [(j, i) for i, j in up]
        last = lax.slice_in_dim(array, length - width, length, axis=dim)
        leading = lax.slice_in_dim(array, 0, width, axis=dim)
        before = lax.ppermute(last, axis, up)
        after = lax.ppermute(leading, axis, down)
        array = jnp.concatenate([before, array, after], axis=dim)
    return array


def window(array_in, dim_index, offset):
    slicers = [slice(None)] * (array_in.ndim - 3)
    for which in range(3):
        shift_by = offset if which == dim_index else 0
        length_here = array_in.shape[array_in.ndim - 3 + which] - 2
        slicers.append(slice(1 + shift_by, 1 + shift_by + length_here))
    return array_in[tuple(slicers)]


def diffuse(vector, stiffness, fibre_weights):
    vector_pads = [(0, 0)] * (vector.ndim - 2) + [(1, 1), (1, 1)]
    stiff_pads = [(0, 0)] * (stiffness.ndim - 2) + [(1, 1), (1, 1)]
    padded_v = jnp.pad(vector, vector_pads)
    padded_c = jnp.pad(stiffness, stiff_pads)
    centre = window(padded_v, 0, 0)
    middle = window(padded_c, 0, 0)
    result = None
    for dim_index in range(3):
        upper = (
            0.5
            * (middle + window(padded_c, dim_index, 1))
            * (centre - window(padded_v, dim_index, 1))
        )
        lower = (
            0.5
            * (middle + window(padded_c, dim_index, -1))
            * (centre - window(padded_v, dim_index, -1))
        )
        column = fibre_weights[:, dim_index].reshape(3, 1, 1, 1)
        term = column * (upper + lower)
        result = term if result is None else result + term
    return result


def squares(vector):
    return lax.psum(jnp.sum(vector * vector), ("mode", "space"))


def row_table(both_rows, both_cols, both_vars, both_weights, base, mode_dev, slots):
    local_rows = both_rows - base
    valid_rows = (local_rows >= 0) & (local_rows < mode_dev)
    local_rows = jnp.where(valid_rows, local_rows, mode_dev)
    row_coupling = jnp.zeros((VARS, mode_dev, slots), jnp.float32)
    row_coupling = row_coupling.at[both_vars, local_rows, both_cols].add(both_weights, mode="drop")
    return row_coupling.reshape(VARS * mode_dev, slots)


def plain(right_side, mean_stiffness, ply_stiffness, fibre_weights, ply_map, coupling_table):
    mode_dev = right_side.shape[0]
    slots = mode_dev * lax.axis_size("mode")
    base = lax.axis_index("mode") * mode_dev
    first_mode = coupling_table[:, 0]
    second_mode = coupling_table[:, 1]
    variable = coupling_table[:, 2]
    entry_weight = jnp.sqrt(coupling_table[:, 3].astype(jnp.float32))
    both_rows = jnp.concatenate([first_mode, second_mode])
    both_cols = jnp.concatenate([second_mode, first_mode])
    both_vars = jnp.concatenate([variable, variable])
    both_weights = jnp.concatenate([entry_weight, entry_weight])
    plies = jnp.arange(VARS, dtype=jnp.int32).reshape(VARS, 1, 1, 1)
    ply_fields = (ply_map[None] == plies).astype(jnp.float32) * ply_stiffness.reshape(VARS, 1, 1, 1)
    stiff_stack = jnp.concatenate([mean_stiffness[None], ply_fields], axis=0)
    stiff_rims = extended(stiff_stack, (("space", 1),), 1)
    stiff_rims = stiff_rims[:, None]
    row_coupling = row_table(both_rows, both_cols, both_vars, both_weights, base, mode_dev, slots)
    solution_field = jnp.zeros_like(right_side)
    residual = right_side
    direction = right_side
    norm_now = squares(residual)
    for iteration in range(ITERS):
        shard_piece = lax.all_gather(direction, "mode", axis=0, tiled=True)
        mixed = jnp.dot(
            row_coupling,
            shard_piece.reshape(shard_piece.shape[0], -1),
            precision=lax.Precision.HIGHEST,
            preferred_element_type=jnp.float32,
        )
        stacked = jnp.concatenate(
            [direction[None], mixed.reshape((VARS,) + direction.shape)], axis=0
        )
        padded = extended(stacked, (("space", 3),), 1)
        terms = diffuse(padded, stiff_rims[:, None], fibre_weights)
        image = direction + jnp.sum(terms, axis=0)
        step_size = norm_now / lax.psum(jnp.sum(direction * image), ("mode", "space"))
        solution_field = solution_field + step_size * direction
        residual = residual - step_size * image
        norm_next = squares(residual)
        direction = residual + norm_next / norm_now * direction
        norm_now = norm_next
    return (solution_field, residual)


COMPS = 3
SLAB = 3
PARTS = 8
WIDE = 16
ROWS = 4
EVEN = 1 + VARS * (VARS + 1) // 2
SPAN = VARS * EVEN
FULL = 624
INNER = 6
TILES = 8
LANES = 128
VMEM = 56 * 1024 * 1024


def lane_id():
    return lax.broadcasted_iota(jnp.int32, (8, LANES), 1)


def swap_out(tile):
    block = lane_id() // WIDE
    tile = pltpu.roll(tile, 0, 1, stride=WIDE, stride_axis=0)
    for bit in (1, 2, 4):
        tile = jnp.where((block & bit) != 0, pltpu.roll(tile, 8 - bit, 0), tile)
    return tile


def swap_back(tile):
    block = lane_id() // WIDE
    row = lax.broadcasted_iota(jnp.int32, (8, LANES), 0)
    for bit in (1, 2, 4):
        tile = jnp.where((block & bit) != 0, pltpu.roll(tile, bit, 0), tile)
    for bit in (1, 2, 4):
        tile = jnp.where((row & bit) != 0, pltpu.roll(tile, LANES - WIDE * bit, 1), tile)
    return tile


def halo_row(planes):
    lane = lane_id()
    slot = lane % WIDE
    halo = jnp.zeros((8, LANES), jnp.float32)
    for x, plane in planes.items():
        places = [(-1, x + 1), (WIDE, x + 6)]
        if 0 <= x < SLAB:
            places += [(-2, x + 10), (WIDE + 1, x + 13)]
        for offset, place in places:
            inside = (lane >= WIDE) if offset < 0 else (lane < LANES - WIDE)
            moved = pltpu.roll(plane, (place - offset) % LANES, 1)
            halo = jnp.where((slot == place) & inside, moved, halo)
    return halo


UNROLL = 3


def pack_kernel(field, *refs, comps):
    modes = field.shape[0]
    out = refs[-1]
    if len(refs) > 1:
        mean, ply, both = refs[0], refs[1], refs[-2]
        for x in range(SLAB):
            both[0, x] = mean[x]
            both[1, x] = (ply[x] + 1).astype(jnp.float32)
    rows = ROWS * len(comps)
    unroll = 2 * UNROLL // len(comps)

    def body(step, carry):
        for inner in range(unroll):
            mode = step * unroll + inner
            for n, comp in enumerate(comps):
                planes = [field[mode, comp, x] for x in range(SLAB)]
                halo = halo_row(dict(enumerate(planes)))
                for p, tile in enumerate(planes + [halo]):
                    out[pl.ds((n * modes + mode) * ROWS + p, PARTS, stride=rows * modes), :] = swap_out(tile)
        return carry

    lax.fori_loop(0, modes // unroll, body, 0)


def estimate(micros):
    return pl.CostEstimate(flops=int(micros * 1e9), bytes_accessed=int(micros * 3e6), transcendentals=0)


def pack(field, comps, stiffness=(), after=()):
    modes = field.shape[0]
    vmem = pl.BlockSpec(memory_space=pltpu.VMEM)
    shapes = [jax.ShapeDtypeStruct((2,) + s.shape, jnp.float32) for s in stiffness[:1]]
    shapes.append(jax.ShapeDtypeStruct((PARTS * modes * ROWS * len(comps), LANES), jnp.float32))
    return pl.pallas_call(
        functools.partial(pack_kernel, comps=comps),
        grid=(1,),
        out_shape=shapes,
        in_specs=[pl.BlockSpec((modes, max(comps) + 1) + field.shape[2:], lambda i: (0, 0, 0, 0, 0))]
        + [vmem] * len(stiffness)
        + [pl.BlockSpec(memory_space=pl.ANY)] * len(after),
        out_specs=[vmem] * len(shapes),
        compiler_params=pltpu.CompilerParams(vmem_limit_bytes=VMEM),
        cost_estimate=estimate(0.5),
        name="pack",
    )(field, *stiffness, *after)


def copy_kernel(source, ready, goal):
    goal[...] = source[...]


def part_component(rows, n, ready):
    blocks = rows.reshape(PARTS, -1, LANES)
    part = (PARTS, blocks.shape[1] // (COMPS - 1), LANES)
    whole = pl.BlockSpec(memory_space=pl.ANY)
    return pl.pallas_call(
        copy_kernel,
        grid=(1,),
        out_shape=jax.ShapeDtypeStruct(part, jnp.float32),
        in_specs=[pl.BlockSpec(part, lambda i: (0, n, 0)), whole],
        out_specs=pl.BlockSpec(part, lambda i: (0, 0, 0)),
        compiler_params=pltpu.CompilerParams(vmem_limit_bytes=VMEM),
        cost_estimate=estimate(0.5),
        name="part_component",
    )(blocks, ready).reshape(-1, LANES)


def after_rows(table, ready):
    vmem = pl.BlockSpec(memory_space=pltpu.VMEM)
    return pl.pallas_call(
        copy_kernel,
        out_shape=jax.ShapeDtypeStruct(table.shape, table.dtype),
        in_specs=[vmem, pl.BlockSpec(memory_space=pl.ANY)],
        out_specs=vmem,
        cost_estimate=estimate(0.5),
        name="after_rows",
    )(table, ready)


def stiffness_kernel(place, before, both, after, ply_stiffness, fields, wide):
    rows = []
    for kind in range(2):
        planes = {-2: before[kind, 1], -1: before[kind, 2], 3: after[kind, 0], 4: after[kind, 1]}
        planes.update({x: both[kind, x] for x in range(SLAB)})
        halo = halo_row({x: planes[x] for x in range(-1, 4)})
        ordered = [planes[0], planes[1], planes[2], planes[-1], planes[3], halo, planes[-2], planes[4]]
        for t, tile in enumerate(ordered):
            wide[...] = swap_out(tile)
            rows.append(wide[pl.ds(place[0], 1), :])
    for t in range(TILES):
        mean, ply = rows[t], rows[TILES + t]
        cols = slice(LANES * t, LANES * (t + 1))
        for k in range(VARS):
            fields[k : k + 1, cols] = jnp.where(ply == k + 1.0, ply_stiffness[k], 0.0)
        fields[VARS : VARS + 1, cols] = mean
        fields[VARS + 1 : VARS + 2, cols] = jnp.where(ply > 0.0, 1.0, 0.0)
        fields[VARS + 2 : 16, cols] = jnp.zeros((4, LANES), jnp.float32)


def stiffness_fields(place, before, both, after, ply_stiffness):
    vmem = pl.BlockSpec(memory_space=pltpu.VMEM)
    smem = pl.BlockSpec(memory_space=pltpu.SMEM)
    return pl.pallas_call(
        stiffness_kernel,
        out_shape=jax.ShapeDtypeStruct((16, TILES * LANES), jnp.float32),
        in_specs=[smem, vmem, vmem, vmem, smem],
        out_specs=vmem,
        scratch_shapes=[pltpu.VMEM((8, LANES), jnp.float32)],
        cost_estimate=estimate(0.5),
        name="stiffness_fields",
    )(place, before, both, after, ply_stiffness)


AT = {0: 0, 1: 1, 2: 2, -1: 3, 3: 4, -2: 6, 4: 7}
PLACE = {index: x for x, index in AT.items()}
HALO = 5


def neighbour(tiles, index, side, place, full=False, wrap=False):
    t = tiles[index]
    lane = lax.broadcasted_iota(jnp.int32, t.shape, 1)
    slot = lane % WIDE
    roll = lambda v, s: pltpu.roll(v, s % LANES, 1)
    if side in (2, 3) and wrap:
        return roll(t, WIDE if side == 2 else -WIDE)
    if side in (2, 3):
        y = (place + lane // WIDE) & 7
        if side == 2:
            return jnp.where(y > 0, roll(t, WIDE), 0.0)
        return jnp.where(y < 7, roll(t, -WIDE), 0.0)
    if index == HALO:
        if side < 2:
            return roll(t, 1 if side == 0 else -1)
        result = roll(t, -9) if side == 4 else roll(t, -7)
        for x in range(-1, 4) if full else range(SLAB):
            goal, by = (x + 6, x - 9) if side == 4 else (x + 1, x + 1)
            result = jnp.where(slot == goal, roll(tiles[AT[x]], by), result)
        if full:
            result = jnp.where(slot >= 13, roll(t, 7), result) if side == 4 else jnp.where(
                (slot >= 10) & (slot < 13), roll(t, 9), result
            )
        return result
    x = PLACE[index]
    if side < 2:
        return tiles[AT[x - 1 if side == 0 else x + 1]]
    if side == 4:
        return jnp.where(slot == 0, roll(tiles[HALO], -(x + 1)), roll(t, 1))
    return jnp.where(slot == WIDE - 1, roll(tiles[HALO], 9 - x), roll(t, -1))


def sides_of(index, outer):
    if index < outer:
        return range(6)
    return {3: (1,), 4: (0,), HALO: (4, 5), 6: (1,), 7: (0,)}[index]


def split(array):
    high = array.astype(jnp.bfloat16)
    low = (array - high.astype(jnp.float32)).astype(jnp.bfloat16)
    return jnp.concatenate([high, low], axis=0)


STEP = 32
FACE = 16
CENTRE = 6 * FACE
EVEN_BLOCKS = ((0, 32), (32, EVEN))


def tile_cols(t):
    return slice(LANES * t, LANES * (t + 1))


def face_stiffness(fields, faces, weights, place):
    tiles = [fields[:, tile_cols(t)] for t in range(TILES)]
    for t in range(TILES):
        for side in sides_of(t, INNER):
            value = (0.5 * weights[side // 2]) * (tiles[t] + neighbour(tiles, t, side, place, True))
            faces[side * FACE : (side + 1) * FACE, tile_cols(t)] = value
        if t < INNER:
            centre = 1.0 + sum(faces[side * FACE + VARS : side * FACE + VARS + 1, tile_cols(t)] for side in range(6))
            faces[CENTRE : CENTRE + 1, tile_cols(t)] = centre
            lane = lax.broadcasted_iota(jnp.int32, (1, LANES), 1)
            y = (place + lane // WIDE) & 7
            for side, edge in ((2, 0), (3, 7)):
                row = side * FACE + VARS
                faces[row + 1 : row + 2, tile_cols(t)] = jnp.where(
                    y == edge, 0.0, faces[row : row + 1, tile_cols(t)]
                )


CHUNK = 4


def chunks(count):
    return [range(start, min(start + CHUNK, count)) for start in range(0, count, CHUNK)]


def chunk_cols(tiles):
    return slice(LANES * tiles[0], LANES * (tiles[-1] + 1))


def apply_operator(src, dst, mixed, flux, scaled, acc, faces, inside, to_even, to_all, place, inner, outer):
    slots = src.shape[0]

    def face(side, k, t):
        return faces[side * FACE + k : side * FACE + k + 1, tile_cols(t)]

    def mix(tiles):
        cols = chunk_cols(tiles)
        mixed[:, cols] = jnp.dot(to_even[...], split(src[:, cols]), preferred_element_type=jnp.float32)

    def flows(t):
        for low, high in EVEN_BLOCKS:
            total = {}
            for k in range(VARS):
                value = mixed[k * EVEN + low : k * EVEN + high, tile_cols(t)]
                for side in sides_of(t, outer):
                    term = face(side, k, t) * value
                    total[side] = term if k == 0 else total[side] + term
            for side, value in total.items():
                flux[side, low:high, tile_cols(t)] = value

    def scale_even(t):
        for low, high in EVEN_BLOCKS:
            even = EvenTiles(mixed, low, high)
            steps = [even[t] - neighbour(even, t, side, place) for side in range(6)]
            for k in range(VARS):
                total = face(0, k, t) * steps[0]
                for side in range(1, 6):
                    total = total + face(side, k, t) * steps[side]
                scaled[k * EVEN + low : k * EVEN + high, tile_cols(t)] = total
            total = None
            for side in range(6):
                opposite = FluxTiles(flux, side ^ 1, low, high)
                term = flux[side, low:high, tile_cols(t)] - neighbour(opposite, t, side, place)
                total = term if total is None else total + term
            scaled[SPAN + low : SPAN + high, tile_cols(t)] = total
        scaled[SPAN + EVEN : FULL, tile_cols(t)] = jnp.zeros((FULL - SPAN - EVEN, LANES), jnp.float32)

    def spread(tiles):
        cols = chunk_cols(tiles)
        acc[:, cols] = jnp.dot(to_all[...], split(scaled[:, cols]), preferred_element_type=jnp.float32)

    before = ()
    for tiles in chunks(inner):
        mix(tiles)
        for t in before:
            flows(t)
        before = tiles
    for t in before:
        flows(t)
    before = ()
    for tiles in chunks(outer):
        for t in tiles:
            scale_even(t)
        if before:
            spread(before)
        before = tiles
    spread(before)

    def last(step, carry):
        rows = pl.ds(pl.multiple_of(step * STEP, STEP), STEP)
        tiles = [src[rows, tile_cols(t)] for t in range(inner)]
        for t in range(outer):
            result = acc[rows, tile_cols(t)] + faces[CENTRE : CENTRE + 1, tile_cols(t)] * tiles[t]
            for side in range(6):
                row = VARS + 1 if side in (2, 3) else VARS
                result = result - face(side, row, t) * neighbour(tiles, t, side, place, wrap=True)
            if t >= SLAB:
                result = inside[t] * result
            dst[rows, tile_cols(t)] = result
        return carry

    lax.fori_loop(0, slots // STEP, last, 0)


class EvenTiles:
    def __init__(self, mixed, low, high):
        self.mixed, self.low, self.high = mixed, low, high

    def __getitem__(self, t):
        return self.mixed[SPAN + self.low : SPAN + self.high, tile_cols(t)]


class FluxTiles:
    def __init__(self, flux, side, low, high):
        self.flux, self.side, self.low, self.high = flux, side, low, high

    def __getitem__(self, t):
        return self.flux[self.side, self.low : self.high, tile_cols(t)]


def apply_kernel(
    place, own, before, after, scale, to_even, to_all, fields, fibre, *refs, comp,
):
    out, partial, field, first, second, mixed, flux, scaled, acc, faces = refs[-10:]
    slots = scale.shape[0]
    here = place[0]
    face_stiffness(fields, faces, [fibre[comp, d] for d in range(3)], here)
    lane = lax.broadcasted_iota(jnp.int32, (slots, LANES), 1)
    slot = lane % WIDE
    load = lambda ref, p: ref[pl.ds(p, slots, stride=ROWS), :]
    left = pltpu.roll(load(before, 3), LANES - 3, 1)
    right = pltpu.roll(load(after, 3), 3, 1)
    halo = jnp.where((slot == 0) | (slot == 5), left, load(own, 3))
    halo = jnp.where((slot == 4) | (slot == 9), right, halo)
    ordered = [
        load(own, 0), load(own, 1), load(own, 2), load(before, 2), load(after, 0), halo,
        load(before, 1), load(after, 1),
    ]
    for t, tile in enumerate(ordered):
        field[:, tile_cols(t)] = tile * scale[...]
    inside = {t: fields[VARS + 1 : VARS + 2, tile_cols(t)] for t in range(SLAB, INNER)}
    slot = lax.broadcasted_iota(jnp.int32, (1, LANES), 1) % WIDE
    used = ((slot >= 1) & (slot <= 3)) | ((slot >= 6) & (slot <= 8))
    inside[HALO] = jnp.where(used, inside[HALO], 0.0)
    scratch = (mixed, flux, scaled, acc, faces, inside, to_even, to_all, here)
    apply_operator(field, first, *scratch, TILES, INNER)
    apply_operator(first, second, *scratch, INNER, SLAB)
    sums = [jnp.zeros((1, LANES), jnp.float32)] * 5
    unscale = 1.0 / scale[...]
    for p in range(SLAB):
        b = load(own, p)
        q = first[:, tile_cols(p)] * unscale
        w = second[:, tile_cols(p)] * unscale
        out[pl.ds(p, slots, stride=2 * SLAB), :] = q
        out[pl.ds(p + SLAB, slots, stride=2 * SLAB), :] = w
        for n, (one, two) in enumerate(((b, b), (b, q), (q, q), (b, w), (q, w))):
            sums[n] = sums[n] + jnp.sum(one * two, axis=0, keepdims=True)
    total = jnp.concatenate(sums + [jnp.zeros((3, LANES), jnp.float32)], axis=0)
    partial[...] = total + refs[0][...] if comp > 0 else total


def apply_twice(comp, place, own, before, after, tables, fields, fibre, *so_far):
    scale, to_even, to_all = tables
    slots = scale.shape[0]
    vmem = pl.BlockSpec(memory_space=pltpu.VMEM)
    smem = pl.BlockSpec(memory_space=pltpu.SMEM)
    f32 = lambda *shape: pltpu.VMEM(shape, jnp.float32)
    return pl.pallas_call(
        functools.partial(apply_kernel, comp=comp),
        out_shape=[
            jax.ShapeDtypeStruct((slots * 2 * SLAB, LANES), jnp.float32),
            jax.ShapeDtypeStruct((8, LANES), jnp.float32),
        ],
        in_specs=[smem] + [vmem] * 7 + [smem] + [vmem] * len(so_far),
        out_specs=[vmem, vmem],
        scratch_shapes=[
            f32(slots, TILES * LANES),
            f32(slots, INNER * LANES),
            f32(slots, SLAB * LANES),
            f32(FULL, TILES * LANES),
            f32(6, EVEN, TILES * LANES),
            f32(FULL, INNER * LANES),
            f32(slots, INNER * LANES),
            f32(6 * FACE + 8, TILES * LANES),
        ],
        compiler_params=pltpu.CompilerParams(vmem_limit_bytes=VMEM),
        cost_estimate=estimate(2),
        name="apply_twice",
    )(place, own, before, after, scale, to_even, to_all, fields, fibre, *so_far)


def combination(total):
    bb, bq, qq, bw, qw = (jnp.sum(total[n : n + 1, :], axis=1, keepdims=True) for n in range(5))
    step_one = bb / bq
    norm = bb - 2.0 * step_one * bq + step_one * step_one * qq
    grown = 1.0 + norm / bb
    curve = grown * grown * bq - step_one * grown * (bw + qq) + step_one * step_one * qw
    step_two = norm / curve
    return step_one + step_two * grown, step_one * step_two


def unpack_kernel(image, natural):
    modes = natural.shape[1]
    per_part = modes * 2 * SLAB

    def body(step, carry):
        for inner in range(2 * UNROLL):
            mode = step * 2 * UNROLL + inner
            for power in range(2):
                for p in range(SLAB):
                    row = (mode * 2 + power) * SLAB + p
                    natural[power, mode, p] = swap_back(image[pl.ds(row, PARTS, stride=per_part), :])
        return carry

    lax.fori_loop(0, modes // (2 * UNROLL), body, 0)


def unpack(image, modes):
    vmem = pl.BlockSpec(memory_space=pltpu.VMEM)
    return pl.pallas_call(
        unpack_kernel,
        out_shape=jax.ShapeDtypeStruct((2, modes, SLAB, 8, LANES), jnp.float32),
        in_specs=[vmem],
        out_specs=vmem,
        compiler_params=pltpu.CompilerParams(vmem_limit_bytes=VMEM),
        cost_estimate=estimate(3),
        name="unpack",
    )(image)


STEPS = 2


def finish_kernel(field, total, image, *refs):
    *natural, solution_field, residual, factors = refs
    modes = field.shape[0]
    per_part = STEPS * modes * 2 * SLAB

    @pl.when(pl.program_id(0) == 0)
    def _():
        sole, cross = combination(total)
        factors[0:8, :] = jnp.broadcast_to(sole, (8, LANES))
        factors[8:16, :] = jnp.broadcast_to(cross, (8, LANES))

    sole, cross = factors[0:8, :], factors[8:16, :]
    first = pl.program_id(0) * modes

    def body(step, carry):
        for inner in range(2 * UNROLL):
            mode = step * 2 * UNROLL + inner
            for comp in range(COMPS):
                for p in range(SLAB):
                    b = field[mode, comp, p]
                    if comp < len(natural):
                        q, w = natural[comp][0, mode, p], natural[comp][1, mode, p]
                    else:
                        row = (first + mode) * 2 * SLAB + p
                        q = swap_back(image[pl.ds(row, PARTS, stride=per_part), :])
                        w = swap_back(image[pl.ds(row + SLAB, PARTS, stride=per_part), :])
                    solution_field[mode, comp, p] = sole * b - cross * q
                    residual[mode, comp, p] = b - sole * q + cross * w
        return carry

    lax.fori_loop(0, modes // (2 * UNROLL), body, 0)


def finish(field, total, image, *natural):
    rows = field.shape[0] // STEPS
    block = pl.BlockSpec((rows,) + field.shape[1:], lambda i: (i, 0, 0, 0, 0))
    vmem = pl.BlockSpec(memory_space=pltpu.VMEM)
    return pl.pallas_call(
        finish_kernel,
        grid=(STEPS,),
        out_shape=[jax.ShapeDtypeStruct(field.shape, jnp.float32)] * 2,
        in_specs=[block, vmem, vmem]
        + [pl.BlockSpec((2, rows) + field.shape[2:], lambda i: (0, i, 0, 0, 0))] * len(natural),
        out_specs=[block, block],
        scratch_shapes=[pltpu.VMEM((16, LANES), jnp.float32)],
        compiler_params=pltpu.CompilerParams(vmem_limit_bytes=VMEM),
        cost_estimate=estimate(6),
        name="finish",
    )(field, total, image, *natural)


def mode_tables(coupling_table, slots):
    lower, upper, variable, code = (coupling_table[:, n] for n in range(4))
    slot = jnp.arange(slots, dtype=jnp.int32)
    is_lower = lower[:, None] == slot
    is_upper = upper[:, None] == slot
    degree = jnp.sum(jnp.where(is_upper, code[:, None], 0), axis=0)
    factor = jnp.where(code == 3, 6, code).astype(jnp.float32)[:, None]
    factorial = jnp.prod(jnp.where(is_upper, factor, 1.0), axis=0)
    root = (degree == 0) & jnp.any(is_lower, axis=0)
    even = (degree == 2) | root
    rank = jnp.sum(jnp.where(even[:, None] & (slot[:, None] < slot), 1, 0), axis=0)
    lower_even = jnp.any(is_lower & even, axis=1)
    is_even_end = jnp.where(lower_even[:, None], is_lower, is_upper)
    is_odd_end = jnp.where(lower_even[:, None], is_upper, is_lower)
    column = variable * EVEN + jnp.sum(jnp.where(is_even_end, rank, 0), axis=1)
    at_column = column[:, None] == jnp.arange(FULL, dtype=jnp.int32)
    down = code.astype(jnp.float32)[:, None]
    first = jnp.where(lower_even[:, None], 1.0, down)
    second = jnp.where(lower_even[:, None], down, 1.0)
    odd_ends = is_odd_end.astype(jnp.float32)
    columns = at_column.astype(jnp.float32)
    half = jnp.bfloat16
    to_even = jnp.dot(
        columns.astype(half).T, (odd_ends * first).astype(half), preferred_element_type=jnp.float32
    )
    to_odd = jnp.dot(
        odd_ends.astype(half).T, (columns * second).astype(half), preferred_element_type=jnp.float32
    )
    pick = (jnp.arange(FULL, dtype=jnp.int32)[:, None] - SPAN == rank) & even
    pick = pick.astype(jnp.float32)
    to_even = (to_even + pick).astype(half)
    to_all = (to_odd + pick.T).astype(half)
    scale = jnp.sqrt(factorial)
    wide = lambda v: jnp.broadcast_to(v[:, None], (slots, LANES))
    twice = lambda v: jnp.concatenate([v, v], axis=1)
    return wide(scale), twice(to_even), twice(to_all)


def all_sum(value):
    for axis, bit in (("space", 1), ("space", 2), ("mode", 1)):
        devices = lax.axis_size(axis)
        value = value + lax.ppermute(value, axis, [(i, i ^ bit) for i in range(devices)])
    others = [
        lax.ppermute(value, "mode", [(i, i ^ bit) for i in range(PARTS)]) for bit in range(2, PARTS, 2)
    ]
    return (value + others[0]) + (others[1] + others[2])


def transposed(right_side, mean_stiffness, ply_stiffness, fibre_weights, ply_map, coupling_table):
    slots = right_side.shape[0] * PARTS
    devices = lax.axis_size("space")
    up = [(i, i + 1) for i in range(devices - 1)]
    down = [(j, i) for i, j in up]
    place = lax.axis_index("mode").astype(jnp.int32).reshape(1)

    def swap(rows):
        return lax.all_to_all(rows, "mode", 0, 0, tiled=True)

    def halo(rows):
        return rows, lax.ppermute(rows, "space", up), lax.ppermute(rows, "space", down)

    (first,) = pack(right_side, (0,))
    both, others = pack(right_side, (1, 2), (mean_stiffness, ply_map), (first,))
    first = halo(swap(first))
    others = swap(others)
    tables = mode_tables(after_rows(coupling_table, first[0]), slots)
    both_before = lax.ppermute(both, "space", up)
    both_after = lax.ppermute(both, "space", down)
    fields = stiffness_fields(place, both_before, both, both_after, ply_stiffness)
    image, partial = apply_twice(0, place, *first, tables, fields, fibre_weights)
    images = [swap(image)]
    parts = [halo(part_component(others, n, partial)) for n in range(COMPS - 1)]
    for comp in range(1, COMPS):
        image, partial = apply_twice(comp, place, *parts[comp - 1], tables, fields, fibre_weights, partial)
        images.append(swap(image))
    natural = [unpack(image, right_side.shape[0]) for image in images[:-1]]
    return tuple(finish(right_side, all_sum(partial), images[-1], *natural))


def on_device(right_side, mean_stiffness, ply_stiffness, fibre_weights, ply_map, coupling_table):
    args = (right_side, mean_stiffness, ply_stiffness, fibre_weights, ply_map, coupling_table)
    fits = right_side.shape[1:] == (COMPS, SLAB, 8, 128) and (lax.axis_size("mode"), lax.axis_size("space")) == (PARTS, 4)
    return transposed(*args) if fits else plain(*args)


def solution(mesh):
    return jax.shard_map(
        on_device,
        mesh=mesh,
        in_specs=(
            P("mode", None, "space", None, None),
            P("space", None, None),
            P(),
            P(),
            P("space", None, None),
            P(),
        ),
        out_specs=(P("mode", None, "space", None, None), P("mode", None, "space", None, None)),
        check_vma=False,
    )
```

```python
import functools

import jax
import jax.numpy as jnp
from jax import lax
from jax.experimental import pallas as pl
from jax.experimental.pallas import tpu as pltpu
from jax.sharding import PartitionSpec as P

VARS = 10
ITERS = 2


def extended(array, sides, width):
    for axis, dim in sides:
        devices, length = (lax.axis_size(axis), array.shape[dim])
        up = [(i, (i + 1) % devices) for i in range(devices - 1)]
        down = [(j, i) for i, j in up]
        last = lax.slice_in_dim(array, length - width, length, axis=dim)
        leading = lax.slice_in_dim(array, 0, width, axis=dim)
        before = lax.ppermute(last, axis, up)
        after = lax.ppermute(leading, axis, down)
        array = jnp.concatenate([before, array, after], axis=dim)
    return array


def window(array_in, dim_index, offset):
    slicers = [slice(None)] * (array_in.ndim - 3)
    for which in range(3):
        shift_by = offset if which == dim_index else 0
        length_here = array_in.shape[array_in.ndim - 3 + which] - 2
        slicers.append(slice(1 + shift_by, 1 + shift_by + length_here))
    return array_in[tuple(slicers)]


def diffuse(vector, stiffness, fibre_weights):
    vector_pads = [(0, 0)] * (vector.ndim - 2) + [(1, 1), (1, 1)]
    stiff_pads = [(0, 0)] * (stiffness.ndim - 2) + [(1, 1), (1, 1)]
    padded_v = jnp.pad(vector, vector_pads)
    padded_c = jnp.pad(stiffness, stiff_pads)
    centre = window(padded_v, 0, 0)
    middle = window(padded_c, 0, 0)
    result = None
    for dim_index in range(3):
        upper = (
            0.5
            * (middle + window(padded_c, dim_index, 1))
            * (centre - window(padded_v, dim_index, 1))
        )
        lower = (
            0.5
            * (middle + window(padded_c, dim_index, -1))
            * (centre - window(padded_v, dim_index, -1))
        )
        column = fibre_weights[:, dim_index].reshape(3, 1, 1, 1)
        term = column * (upper + lower)
        result = term if result is None else result + term
    return result


def squares(vector):
    return lax.psum(jnp.sum(vector * vector), ("mode", "space"))


def row_table(both_rows, both_cols, both_vars, both_weights, base, mode_dev, slots):
    local_rows = both_rows - base
    valid_rows = (local_rows >= 0) & (local_rows < mode_dev)
    local_rows = jnp.where(valid_rows, local_rows, mode_dev)
    row_coupling = jnp.zeros((VARS, mode_dev, slots), jnp.float32)
    row_coupling = row_coupling.at[both_vars, local_rows, both_cols].add(both_weights, mode="drop")
    return row_coupling.reshape(VARS * mode_dev, slots)


def plain(right_side, mean_stiffness, ply_stiffness, fibre_weights, ply_map, coupling_table):
    mode_dev = right_side.shape[0]
    slots = mode_dev * lax.axis_size("mode")
    base = lax.axis_index("mode") * mode_dev
    first_mode = coupling_table[:, 0]
    second_mode = coupling_table[:, 1]
    variable = coupling_table[:, 2]
    entry_weight = jnp.sqrt(coupling_table[:, 3].astype(jnp.float32))
    both_rows = jnp.concatenate([first_mode, second_mode])
    both_cols = jnp.concatenate([second_mode, first_mode])
    both_vars = jnp.concatenate([variable, variable])
    both_weights = jnp.concatenate([entry_weight, entry_weight])
    plies = jnp.arange(VARS, dtype=jnp.int32).reshape(VARS, 1, 1, 1)
    ply_fields = (ply_map[None] == plies).astype(jnp.float32) * ply_stiffness.reshape(VARS, 1, 1, 1)
    stiff_stack = jnp.concatenate([mean_stiffness[None], ply_fields], axis=0)
    stiff_rims = extended(stiff_stack, (("space", 1),), 1)
    stiff_rims = stiff_rims[:, None]
    row_coupling = row_table(both_rows, both_cols, both_vars, both_weights, base, mode_dev, slots)
    solution_field = jnp.zeros_like(right_side)
    residual = right_side
    direction = right_side
    norm_now = squares(residual)
    for iteration in range(ITERS):
        shard_piece = lax.all_gather(direction, "mode", axis=0, tiled=True)
        mixed = jnp.dot(
            row_coupling,
            shard_piece.reshape(shard_piece.shape[0], -1),
            precision=lax.Precision.HIGHEST,
            preferred_element_type=jnp.float32,
        )
        stacked = jnp.concatenate(
            [direction[None], mixed.reshape((VARS,) + direction.shape)], axis=0
        )
        padded = extended(stacked, (("space", 3),), 1)
        terms = diffuse(padded, stiff_rims[:, None], fibre_weights)
        image = direction + jnp.sum(terms, axis=0)
        step_size = norm_now / lax.psum(jnp.sum(direction * image), ("mode", "space"))
        solution_field = solution_field + step_size * direction
        residual = residual - step_size * image
        norm_next = squares(residual)
        direction = residual + norm_next / norm_now * direction
        norm_now = norm_next
    return (solution_field, residual)


COMPS = 3
SLAB = 3
PARTS = 8
WIDE = 16
ROWS = 4
EVEN = 1 + VARS * (VARS + 1) // 2
SPAN = VARS * EVEN
FULL = 624
INNER = 6
TILES = 8
LANES = 128
VMEM = 56 * 1024 * 1024


def lane_id():
    return lax.broadcasted_iota(jnp.int32, (8, LANES), 1)


def swap_out(tile):
    block = lane_id() // WIDE
    tile = pltpu.roll(tile, 0, 1, stride=WIDE, stride_axis=0)
    for bit in (1, 2, 4):
        tile = jnp.where((block & bit) != 0, pltpu.roll(tile, 8 - bit, 0), tile)
    return tile


def swap_back(tile):
    block = lane_id() // WIDE
    row = lax.broadcasted_iota(jnp.int32, (8, LANES), 0)
    for bit in (1, 2, 4):
        tile = jnp.where((block & bit) != 0, pltpu.roll(tile, bit, 0), tile)
    for bit in (1, 2, 4):
        tile = jnp.where((row & bit) != 0, pltpu.roll(tile, LANES - WIDE * bit, 1), tile)
    return tile


def halo_row(planes):
    lane = lane_id()
    slot = lane % WIDE
    halo = jnp.zeros((8, LANES), jnp.float32)
    for x, plane in planes.items():
        places = [(-1, x + 1), (WIDE, x + 6)]
        if 0 <= x < SLAB:
            places += [(-2, x + 10), (WIDE + 1, x + 13)]
        for offset, place in places:
            inside = (lane >= WIDE) if offset < 0 else (lane < LANES - WIDE)
            moved = pltpu.roll(plane, (place - offset) % LANES, 1)
            halo = jnp.where((slot == place) & inside, moved, halo)
    return halo


UNROLL = 3


def pack_kernel(field, *refs, comps):
    modes = field.shape[0]
    out = refs[-1]
    if len(refs) > 1:
        mean, ply, both = refs[0], refs[1], refs[-2]
        for x in range(SLAB):
            both[0, x] = mean[x]
            both[1, x] = (ply[x] + 1).astype(jnp.float32)
    rows = ROWS * len(comps)
    unroll = 2 * UNROLL // len(comps)

    def body(step, carry):
        for inner in range(unroll):
            mode = step * unroll + inner
            for n, comp in enumerate(comps):
                planes = [field[mode, comp, x] for x in range(SLAB)]
                halo = halo_row(dict(enumerate(planes)))
                for p, tile in enumerate(planes + [halo]):
                    out[pl.ds((n * modes + mode) * ROWS + p, PARTS, stride=rows * modes), :] = swap_out(tile)
        return carry

    lax.fori_loop(0, modes // unroll, body, 0)


def estimate(micros):
    return pl.CostEstimate(flops=int(micros * 1e9), bytes_accessed=int(micros * 3e6), transcendentals=0)


def pack(field, comps, stiffness=(), after=()):
    modes = field.shape[0]
    vmem = pl.BlockSpec(memory_space=pltpu.VMEM)
    shapes = [jax.ShapeDtypeStruct((2,) + s.shape, jnp.float32) for s in stiffness[:1]]
    shapes.append(jax.ShapeDtypeStruct((PARTS * modes * ROWS * len(comps), LANES), jnp.float32))
    return pl.pallas_call(
        functools.partial(pack_kernel, comps=comps),
        grid=(1,),
        out_shape=shapes,
        in_specs=[pl.BlockSpec((modes, max(comps) + 1) + field.shape[2:], lambda i: (0, 0, 0, 0, 0))]
        + [vmem] * len(stiffness)
        + [pl.BlockSpec(memory_space=pl.ANY)] * len(after),
        out_specs=[vmem] * len(shapes),
        compiler_params=pltpu.CompilerParams(vmem_limit_bytes=VMEM),
        cost_estimate=estimate(0.5),
        name="pack",
    )(field, *stiffness, *after)


def copy_kernel(source, ready, goal):
    goal[...] = source[...]


def part_component(rows, n, ready):
    blocks = rows.reshape(PARTS, -1, LANES)
    part = (PARTS, blocks.shape[1] // (COMPS - 1), LANES)
    whole = pl.BlockSpec(memory_space=pl.ANY)
    return pl.pallas_call(
        copy_kernel,
        grid=(1,),
        out_shape=jax.ShapeDtypeStruct(part, jnp.float32),
        in_specs=[pl.BlockSpec(part, lambda i: (0, n, 0)), whole],
        out_specs=pl.BlockSpec(part, lambda i: (0, 0, 0)),
        compiler_params=pltpu.CompilerParams(vmem_limit_bytes=VMEM),
        cost_estimate=estimate(0.5),
        name="part_component",
    )(blocks, ready).reshape(-1, LANES)


def after_rows(table, ready):
    vmem = pl.BlockSpec(memory_space=pltpu.VMEM)
    return pl.pallas_call(
        copy_kernel,
        out_shape=jax.ShapeDtypeStruct(table.shape, table.dtype),
        in_specs=[vmem, pl.BlockSpec(memory_space=pl.ANY)],
        out_specs=vmem,
        cost_estimate=estimate(0.5),
        name="after_rows",
    )(table, ready)


def stiffness_kernel(place, before, both, after, ply_stiffness, fields, wide):
    rows = []
    for kind in range(2):
        planes = {-2: before[kind, 1], -1: before[kind, 2], 3: after[kind, 0], 4: after[kind, 1]}
        planes.update({x: both[kind, x] for x in range(SLAB)})
        halo = halo_row({x: planes[x] for x in range(-1, 4)})
        ordered = [planes[0], planes[1], planes[2], planes[-1], planes[3], halo, planes[-2], planes[4]]
        for t, tile in enumerate(ordered):
            wide[...] = swap_out(tile)
            rows.append(wide[pl.ds(place[0], 1), :])
    for t in range(TILES):
        mean, ply = rows[t], rows[TILES + t]
        cols = slice(LANES * t, LANES * (t + 1))
        for k in range(VARS):
            fields[k : k + 1, cols] = jnp.where(ply == k + 1.0, ply_stiffness[k], 0.0)
        fields[VARS : VARS + 1, cols] = mean
        fields[VARS + 1 : VARS + 2, cols] = jnp.where(ply > 0.0, 1.0, 0.0)
        fields[VARS + 2 : 16, cols] = jnp.zeros((4, LANES), jnp.float32)


def stiffness_fields(place, before, both, after, ply_stiffness):
    vmem = pl.BlockSpec(memory_space=pltpu.VMEM)
    smem = pl.BlockSpec(memory_space=pltpu.SMEM)
    return pl.pallas_call(
        stiffness_kernel,
        out_shape=jax.ShapeDtypeStruct((16, TILES * LANES), jnp.float32),
        in_specs=[smem, vmem, vmem, vmem, smem],
        out_specs=vmem,
        scratch_shapes=[pltpu.VMEM((8, LANES), jnp.float32)],
        cost_estimate=estimate(0.5),
        name="stiffness_fields",
    )(place, before, both, after, ply_stiffness)


AT = {0: 0, 1: 1, 2: 2, -1: 3, 3: 4, -2: 6, 4: 7}
PLACE = {index: x for x, index in AT.items()}
HALO = 5


def neighbour(tiles, index, side, place, full=False, wrap=False):
    t = tiles[index]
    lane = lax.broadcasted_iota(jnp.int32, t.shape, 1)
    slot = lane % WIDE
    roll = lambda v, s: pltpu.roll(v, s % LANES, 1)
    if side in (2, 3) and wrap:
        return roll(t, WIDE if side == 2 else -WIDE)
    if side in (2, 3):
        y = (place + lane // WIDE) & 7
        if side == 2:
            return jnp.where(y > 0, roll(t, WIDE), 0.0)
        return jnp.where(y < 7, roll(t, -WIDE), 0.0)
    if index == HALO:
        if side < 2:
            return roll(t, 1 if side == 0 else -1)
        result = roll(t, -9) if side == 4 else roll(t, -7)
        for x in range(-1, 4) if full else range(SLAB):
            goal, by = (x + 6, x - 9) if side == 4 else (x + 1, x + 1)
            result = jnp.where(slot == goal, roll(tiles[AT[x]], by), result)
        if full:
            result = jnp.where(slot >= 13, roll(t, 7), result) if side == 4 else jnp.where(
                (slot >= 10) & (slot < 13), roll(t, 9), result
            )
        return result
    x = PLACE[index]
    if side < 2:
        return tiles[AT[x - 1 if side == 0 else x + 1]]
    if side == 4:
        return jnp.where(slot == 0, roll(tiles[HALO], -(x + 1)), roll(t, 1))
    return jnp.where(slot == WIDE - 1, roll(tiles[HALO], 9 - x), roll(t, -1))


def sides_of(index, outer):
    if index < outer:
        return range(6)
    return {3: (1,), 4: (0,), HALO: (4, 5), 6: (1,), 7: (0,)}[index]


def split(array):
    high = array.astype(jnp.bfloat16)
    low = (array - high.astype(jnp.float32)).astype(jnp.bfloat16)
    return jnp.concatenate([high, low], axis=0)


STEP = 32
FACE = 16
CENTRE = 6 * FACE
EVEN_BLOCKS = ((0, 32), (32, EVEN))


def tile_cols(t):
    return slice(LANES * t, LANES * (t + 1))


def face_stiffness(fields, faces, weights, place):
    tiles = [fields[:, tile_cols(t)] for t in range(TILES)]
    for t in range(TILES):
        for side in sides_of(t, INNER):
            value = (0.5 * weights[side // 2]) * (tiles[t] + neighbour(tiles, t, side, place, True))
            faces[side * FACE : (side + 1) * FACE, tile_cols(t)] = value
        if t < INNER:
            centre = 1.0 + sum(faces[side * FACE + VARS : side * FACE + VARS + 1, tile_cols(t)] for side in range(6))
            faces[CENTRE : CENTRE + 1, tile_cols(t)] = centre
            lane = lax.broadcasted_iota(jnp.int32, (1, LANES), 1)
            y = (place + lane // WIDE) & 7
            for side, edge in ((2, 0), (3, 7)):
                row = side * FACE + VARS
                faces[row + 1 : row + 2, tile_cols(t)] = jnp.where(
                    y == edge, 0.0, faces[row : row + 1, tile_cols(t)]
                )


CHUNK = 4


def chunks(count):
    return [range(start, min(start + CHUNK, count)) for start in range(0, count, CHUNK)]


def chunk_cols(tiles):
    return slice(LANES * tiles[0], LANES * (tiles[-1] + 1))


def apply_operator(src, dst, mixed, flux, scaled, acc, faces, inside, to_even, to_all, place, inner, outer):
    slots = src.shape[0]

    def face(side, k, t):
        return faces[side * FACE + k : side * FACE + k + 1, tile_cols(t)]

    def mix(tiles):
        cols = chunk_cols(tiles)
        mixed[:, cols] = jnp.dot(to_even[...], split(src[:, cols]), preferred_element_type=jnp.float32)

    def flows(t):
        for low, high in EVEN_BLOCKS:
            total = {}
            for k in range(VARS):
                value = mixed[k * EVEN + low : k * EVEN + high, tile_cols(t)]
                for side in sides_of(t, outer):
                    term = face(side, k, t) * value
                    total[side] = term if k == 0 else total[side] + term
            for side, value in total.items():
                flux[side, low:high, tile_cols(t)] = value

    def scale_even(t):
        for low, high in EVEN_BLOCKS:
            even = EvenTiles(mixed, low, high)
            steps = [even[t] - neighbour(even, t, side, place) for side in range(6)]
            for k in range(VARS):
                total = face(0, k, t) * steps[0]
                for side in range(1, 6):
                    total = total + face(side, k, t) * steps[side]
                scaled[k * EVEN + low : k * EVEN + high, tile_cols(t)] = total
            total = None
            for side in range(6):
                opposite = FluxTiles(flux, side ^ 1, low, high)
                term = flux[side, low:high, tile_cols(t)] - neighbour(opposite, t, side, place)
                total = term if total is None else total + term
            scaled[SPAN + low : SPAN + high, tile_cols(t)] = total
        scaled[SPAN + EVEN : FULL, tile_cols(t)] = jnp.zeros((FULL - SPAN - EVEN, LANES), jnp.float32)

    def spread(tiles):
        cols = chunk_cols(tiles)
        acc[:, cols] = jnp.dot(to_all[...], split(scaled[:, cols]), preferred_element_type=jnp.float32)

    before = ()
    for tiles in chunks(inner):
        mix(tiles)
        for t in before:
            flows(t)
        before = tiles
    for t in before:
        flows(t)
    before = ()
    for tiles in chunks(outer):
        for t in tiles:
            scale_even(t)
        if before:
            spread(before)
        before = tiles
    spread(before)

    def last(step, carry):
        rows = pl.ds(pl.multiple_of(step * STEP, STEP), STEP)
        tiles = [src[rows, tile_cols(t)] for t in range(inner)]
        for t in range(outer):
            result = acc[rows, tile_cols(t)] + faces[CENTRE : CENTRE + 1, tile_cols(t)] * tiles[t]
            for side in range(6):
                row = VARS + 1 if side in (2, 3) else VARS
                result = result - face(side, row, t) * neighbour(tiles, t, side, place, wrap=True)
            if t >= SLAB:
                result = inside[t] * result
            dst[rows, tile_cols(t)] = result
        return carry

    lax.fori_loop(0, slots // STEP, last, 0)


class EvenTiles:
    def __init__(self, mixed, low, high):
        self.mixed, self.low, self.high = mixed, low, high

    def __getitem__(self, t):
        return self.mixed[SPAN + self.low : SPAN + self.high, tile_cols(t)]


class FluxTiles:
    def __init__(self, flux, side, low, high):
        self.flux, self.side, self.low, self.high = flux, side, low, high

    def __getitem__(self, t):
        return self.flux[self.side, self.low : self.high, tile_cols(t)]


def apply_kernel(
    place, own, before, after, scale, to_even, to_all, fields, fibre, *refs, comp,
):
    out, partial, field, first, second, mixed, flux, scaled, acc, faces = refs[-10:]
    slots = scale.shape[0]
    here = place[0]
    face_stiffness(fields, faces, [fibre[comp, d] for d in range(3)], here)
    lane = lax.broadcasted_iota(jnp.int32, (slots, LANES), 1)
    slot = lane % WIDE
    load = lambda ref, p: ref[pl.ds(p, slots, stride=ROWS), :]
    left = pltpu.roll(load(before, 3), LANES - 3, 1)
    right = pltpu.roll(load(after, 3), 3, 1)
    halo = jnp.where((slot == 0) | (slot == 5), left, load(own, 3))
    halo = jnp.where((slot == 4) | (slot == 9), right, halo)
    ordered = [
        load(own, 0), load(own, 1), load(own, 2), load(before, 2), load(after, 0), halo,
        load(before, 1), load(after, 1),
    ]
    for t, tile in enumerate(ordered):
        field[:, tile_cols(t)] = tile * scale[...]
    inside = {t: fields[VARS + 1 : VARS + 2, tile_cols(t)] for t in range(SLAB, INNER)}
    slot = lax.broadcasted_iota(jnp.int32, (1, LANES), 1) % WIDE
    used = ((slot >= 1) & (slot <= 3)) | ((slot >= 6) & (slot <= 8))
    inside[HALO] = jnp.where(used, inside[HALO], 0.0)
    scratch = (mixed, flux, scaled, acc, faces, inside, to_even, to_all, here)
    apply_operator(field, first, *scratch, TILES, INNER)
    apply_operator(first, second, *scratch, INNER, SLAB)
    sums = [jnp.zeros((1, LANES), jnp.float32)] * 5
    unscale = 1.0 / scale[...]
    for p in range(SLAB):
        b = load(own, p)
        q = first[:, tile_cols(p)] * unscale
        w = second[:, tile_cols(p)] * unscale
        out[pl.ds(p, slots, stride=2 * SLAB), :] = q
        out[pl.ds(p + SLAB, slots, stride=2 * SLAB), :] = w
        for n, (one, two) in enumerate(((b, b), (b, q), (q, q), (b, w), (q, w))):
            sums[n] = sums[n] + jnp.sum(one * two, axis=0, keepdims=True)
    total = jnp.concatenate(sums + [jnp.zeros((3, LANES), jnp.float32)], axis=0)
    partial[...] = total + refs[0][...] if comp > 0 else total


def apply_twice(comp, place, own, before, after, tables, fields, fibre, so_far=(), ready=()):
    scale, to_even, to_all = tables
    slots = scale.shape[0]
    vmem = pl.BlockSpec(memory_space=pltpu.VMEM)
    smem = pl.BlockSpec(memory_space=pltpu.SMEM)
    f32 = lambda *shape: pltpu.VMEM(shape, jnp.float32)
    return pl.pallas_call(
        functools.partial(apply_kernel, comp=comp),
        out_shape=[
            jax.ShapeDtypeStruct((slots * 2 * SLAB, LANES), jnp.float32),
            jax.ShapeDtypeStruct((8, LANES), jnp.float32),
        ],
        in_specs=[smem] + [vmem] * 7 + [smem] + [vmem] * len(so_far) + [pl.BlockSpec(memory_space=pl.ANY)] * len(ready),
        out_specs=[vmem, vmem],
        scratch_shapes=[
            f32(slots, TILES * LANES),
            f32(slots, INNER * LANES),
            f32(slots, SLAB * LANES),
            f32(FULL, TILES * LANES),
            f32(6, EVEN, TILES * LANES),
            f32(FULL, INNER * LANES),
            f32(slots, INNER * LANES),
            f32(6 * FACE + 8, TILES * LANES),
        ],
        compiler_params=pltpu.CompilerParams(vmem_limit_bytes=VMEM),
        cost_estimate=estimate(2),
        name="apply_twice",
    )(place, own, before, after, scale, to_even, to_all, fields, fibre, *so_far, *ready)


def combination(total):
    bb, bq, qq, bw, qw = (jnp.sum(total[n : n + 1, :], axis=1, keepdims=True) for n in range(5))
    step_one = bb / bq
    norm = bb - 2.0 * step_one * bq + step_one * step_one * qq
    grown = 1.0 + norm / bb
    curve = grown * grown * bq - step_one * grown * (bw + qq) + step_one * step_one * qw
    step_two = norm / curve
    return step_one + step_two * grown, step_one * step_two


def unpack_kernel(image, natural):
    modes = natural.shape[1]
    per_part = modes * 2 * SLAB

    def body(step, carry):
        for inner in range(2 * UNROLL):
            mode = step * 2 * UNROLL + inner
            for power in range(2):
                for p in range(SLAB):
                    row = (mode * 2 + power) * SLAB + p
                    natural[power, mode, p] = swap_back(image[pl.ds(row, PARTS, stride=per_part), :])
        return carry

    lax.fori_loop(0, modes // (2 * UNROLL), body, 0)


def unpack(image, modes):
    vmem = pl.BlockSpec(memory_space=pltpu.VMEM)
    return pl.pallas_call(
        unpack_kernel,
        out_shape=jax.ShapeDtypeStruct((2, modes, SLAB, 8, LANES), jnp.float32),
        in_specs=[vmem],
        out_specs=vmem,
        compiler_params=pltpu.CompilerParams(vmem_limit_bytes=VMEM),
        cost_estimate=estimate(3),
        name="unpack",
    )(image)


STEPS = 2


def finish_kernel(field, total, image, *refs):
    *natural, solution_field, residual, factors = refs
    modes = field.shape[0]
    per_part = STEPS * modes * 2 * SLAB

    @pl.when(pl.program_id(0) == 0)
    def _():
        sole, cross = combination(total)
        factors[0:8, :] = jnp.broadcast_to(sole, (8, LANES))
        factors[8:16, :] = jnp.broadcast_to(cross, (8, LANES))

    sole, cross = factors[0:8, :], factors[8:16, :]
    first = pl.program_id(0) * modes

    def body(step, carry):
        for inner in range(2 * UNROLL):
            mode = step * 2 * UNROLL + inner
            for comp in range(COMPS):
                for p in range(SLAB):
                    b = field[mode, comp, p]
                    if comp < len(natural):
                        q, w = natural[comp][0, mode, p], natural[comp][1, mode, p]
                    else:
                        row = (first + mode) * 2 * SLAB + p
                        q = swap_back(image[pl.ds(row, PARTS, stride=per_part), :])
                        w = swap_back(image[pl.ds(row + SLAB, PARTS, stride=per_part), :])
                    solution_field[mode, comp, p] = sole * b - cross * q
                    residual[mode, comp, p] = b - sole * q + cross * w
        return carry

    lax.fori_loop(0, modes // (2 * UNROLL), body, 0)


def finish(field, total, image, *natural):
    rows = field.shape[0] // STEPS
    block = pl.BlockSpec((rows,) + field.shape[1:], lambda i: (i, 0, 0, 0, 0))
    vmem = pl.BlockSpec(memory_space=pltpu.VMEM)
    return pl.pallas_call(
        finish_kernel,
        grid=(STEPS,),
        out_shape=[jax.ShapeDtypeStruct(field.shape, jnp.float32)] * 2,
        in_specs=[block, vmem, vmem]
        + [pl.BlockSpec((2, rows) + field.shape[2:], lambda i: (0, i, 0, 0, 0))] * len(natural),
        out_specs=[block, block],
        scratch_shapes=[pltpu.VMEM((16, LANES), jnp.float32)],
        compiler_params=pltpu.CompilerParams(vmem_limit_bytes=VMEM),
        cost_estimate=estimate(6),
        name="finish",
    )(field, total, image, *natural)


def mode_tables(coupling_table, slots):
    lower, upper, variable, code = (coupling_table[:, n] for n in range(4))
    slot = jnp.arange(slots, dtype=jnp.int32)
    is_lower = lower[:, None] == slot
    is_upper = upper[:, None] == slot
    degree = jnp.sum(jnp.where(is_upper, code[:, None], 0), axis=0)
    factor = jnp.where(code == 3, 6, code).astype(jnp.float32)[:, None]
    factorial = jnp.prod(jnp.where(is_upper, factor, 1.0), axis=0)
    root = (degree == 0) & jnp.any(is_lower, axis=0)
    even = (degree == 2) | root
    rank = jnp.sum(jnp.where(even[:, None] & (slot[:, None] < slot), 1, 0), axis=0)
    lower_even = jnp.any(is_lower & even, axis=1)
    is_even_end = jnp.where(lower_even[:, None], is_lower, is_upper)
    is_odd_end = jnp.where(lower_even[:, None], is_upper, is_lower)
    column = variable * EVEN + jnp.sum(jnp.where(is_even_end, rank, 0), axis=1)
    at_column = column[:, None] == jnp.arange(FULL, dtype=jnp.int32)
    down = code.astype(jnp.float32)[:, None]
    first = jnp.where(lower_even[:, None], 1.0, down)
    second = jnp.where(lower_even[:, None], down, 1.0)
    odd_ends = is_odd_end.astype(jnp.float32)
    columns = at_column.astype(jnp.float32)
    half = jnp.bfloat16
    to_even = jnp.dot(
        columns.astype(half).T, (odd_ends * first).astype(half), preferred_element_type=jnp.float32
    )
    to_odd = jnp.dot(
        odd_ends.astype(half).T, (columns * second).astype(half), preferred_element_type=jnp.float32
    )
    pick = (jnp.arange(FULL, dtype=jnp.int32)[:, None] - SPAN == rank) & even
    pick = pick.astype(jnp.float32)
    to_even = (to_even + pick).astype(half)
    to_all = (to_odd + pick.T).astype(half)
    scale = jnp.sqrt(factorial)
    wide = lambda v: jnp.broadcast_to(v[:, None], (slots, LANES))
    twice = lambda v: jnp.concatenate([v, v], axis=1)
    return wide(scale), twice(to_even), twice(to_all)


def all_sum(value):
    for axis, bit in (("space", 1), ("space", 2), ("mode", 1)):
        devices = lax.axis_size(axis)
        value = value + lax.ppermute(value, axis, [(i, i ^ bit) for i in range(devices)])
    others = [
        lax.ppermute(value, "mode", [(i, i ^ bit) for i in range(PARTS)]) for bit in range(2, PARTS, 2)
    ]
    return (value + others[0]) + (others[1] + others[2])


def transposed(right_side, mean_stiffness, ply_stiffness, fibre_weights, ply_map, coupling_table):
    slots = right_side.shape[0] * PARTS
    devices = lax.axis_size("space")
    up = [(i, i + 1) for i in range(devices - 1)]
    down = [(j, i) for i, j in up]
    place = lax.axis_index("mode").astype(jnp.int32).reshape(1)

    def swap(rows):
        return lax.all_to_all(rows, "mode", 0, 0, tiled=True)

    def halo(rows):
        return rows, lax.ppermute(rows, "space", up), lax.ppermute(rows, "space", down)

    (first,) = pack(right_side, (0,))
    both, others = pack(right_side, (1, 2), (mean_stiffness, ply_map), (first,))
    first = halo(swap(first))
    others = swap(others)
    tables = mode_tables(after_rows(coupling_table, first[0]), slots)
    both_before = lax.ppermute(both, "space", up)
    both_after = lax.ppermute(both, "space", down)
    fields = stiffness_fields(place, both_before, both, both_after, ply_stiffness)
    image, partial = apply_twice(0, place, *first, tables, fields, fibre_weights)
    images = [swap(image)]
    parts = [part_component(others, n, partial) for n in range(COMPS - 1)]
    halos = [halo(rows) for rows in parts]
    modes = right_side.shape[0]
    image, partial = apply_twice(1, place, *halos[0], tables, fields, fibre_weights, (partial,), parts[1:])
    images.append(swap(image))
    natural = [unpack(images[0], modes)]
    image, partial = apply_twice(2, place, *halos[1], tables, fields, fibre_weights, (partial,), natural)
    images.append(swap(image))
    natural.append(unpack(images[1], modes))
    return tuple(finish(right_side, all_sum(partial), images[2], *natural))


def on_device(right_side, mean_stiffness, ply_stiffness, fibre_weights, ply_map, coupling_table):
    args = (right_side, mean_stiffness, ply_stiffness, fibre_weights, ply_map, coupling_table)
    fits = right_side.shape[1:] == (COMPS, SLAB, 8, 128) and (lax.axis_size("mode"), lax.axis_size("space")) == (PARTS, 4)
    return transposed(*args) if fits else plain(*args)


def solution(mesh):
    return jax.shard_map(
        on_device,
        mesh=mesh,
        in_specs=(
            P("mode", None, "space", None, None),
            P("space", None, None),
            P(),
            P(),
            P("space", None, None),
            P(),
        ),
        out_specs=(P("mode", None, "space", None, None), P("mode", None, "space", None, None)),
        check_vma=False,
    )
```

```python
import functools

import jax
import jax.numpy as jnp
from jax import lax
from jax.experimental import pallas as pl
from jax.experimental.pallas import tpu as pltpu
from jax.sharding import PartitionSpec as P

VARS = 10
ITERS = 2


def extended(array, sides, width):
    for axis, dim in sides:
        devices, length = (lax.axis_size(axis), array.shape[dim])
        up = [(i, (i + 1) % devices) for i in range(devices - 1)]
        down = [(j, i) for i, j in up]
        last = lax.slice_in_dim(array, length - width, length, axis=dim)
        leading = lax.slice_in_dim(array, 0, width, axis=dim)
        before = lax.ppermute(last, axis, up)
        after = lax.ppermute(leading, axis, down)
        array = jnp.concatenate([before, array, after], axis=dim)
    return array


def window(array_in, dim_index, offset):
    slicers = [slice(None)] * (array_in.ndim - 3)
    for which in range(3):
        shift_by = offset if which == dim_index else 0
        length_here = array_in.shape[array_in.ndim - 3 + which] - 2
        slicers.append(slice(1 + shift_by, 1 + shift_by + length_here))
    return array_in[tuple(slicers)]


def diffuse(vector, stiffness, fibre_weights):
    vector_pads = [(0, 0)] * (vector.ndim - 2) + [(1, 1), (1, 1)]
    stiff_pads = [(0, 0)] * (stiffness.ndim - 2) + [(1, 1), (1, 1)]
    padded_v = jnp.pad(vector, vector_pads)
    padded_c = jnp.pad(stiffness, stiff_pads)
    centre = window(padded_v, 0, 0)
    middle = window(padded_c, 0, 0)
    result = None
    for dim_index in range(3):
        upper = (
            0.5
            * (middle + window(padded_c, dim_index, 1))
            * (centre - window(padded_v, dim_index, 1))
        )
        lower = (
            0.5
            * (middle + window(padded_c, dim_index, -1))
            * (centre - window(padded_v, dim_index, -1))
        )
        column = fibre_weights[:, dim_index].reshape(3, 1, 1, 1)
        term = column * (upper + lower)
        result = term if result is None else result + term
    return result


def squares(vector):
    return lax.psum(jnp.sum(vector * vector), ("mode", "space"))


def row_table(both_rows, both_cols, both_vars, both_weights, base, mode_dev, slots):
    local_rows = both_rows - base
    valid_rows = (local_rows >= 0) & (local_rows < mode_dev)
    local_rows = jnp.where(valid_rows, local_rows, mode_dev)
    row_coupling = jnp.zeros((VARS, mode_dev, slots), jnp.float32)
    row_coupling = row_coupling.at[both_vars, local_rows, both_cols].add(both_weights, mode="drop")
    return row_coupling.reshape(VARS * mode_dev, slots)


def plain(right_side, mean_stiffness, ply_stiffness, fibre_weights, ply_map, coupling_table):
    mode_dev = right_side.shape[0]
    slots = mode_dev * lax.axis_size("mode")
    base = lax.axis_index("mode") * mode_dev
    first_mode = coupling_table[:, 0]
    second_mode = coupling_table[:, 1]
    variable = coupling_table[:, 2]
    entry_weight = jnp.sqrt(coupling_table[:, 3].astype(jnp.float32))
    both_rows = jnp.concatenate([first_mode, second_mode])
    both_cols = jnp.concatenate([second_mode, first_mode])
    both_vars = jnp.concatenate([variable, variable])
    both_weights = jnp.concatenate([entry_weight, entry_weight])
    plies = jnp.arange(VARS, dtype=jnp.int32).reshape(VARS, 1, 1, 1)
    ply_fields = (ply_map[None] == plies).astype(jnp.float32) * ply_stiffness.reshape(VARS, 1, 1, 1)
    stiff_stack = jnp.concatenate([mean_stiffness[None], ply_fields], axis=0)
    stiff_rims = extended(stiff_stack, (("space", 1),), 1)
    stiff_rims = stiff_rims[:, None]
    row_coupling = row_table(both_rows, both_cols, both_vars, both_weights, base, mode_dev, slots)
    solution_field = jnp.zeros_like(right_side)
    residual = right_side
    direction = right_side
    norm_now = squares(residual)
    for iteration in range(ITERS):
        shard_piece = lax.all_gather(direction, "mode", axis=0, tiled=True)
        mixed = jnp.dot(
            row_coupling,
            shard_piece.reshape(shard_piece.shape[0], -1),
            precision=lax.Precision.HIGHEST,
            preferred_element_type=jnp.float32,
        )
        stacked = jnp.concatenate(
            [direction[None], mixed.reshape((VARS,) + direction.shape)], axis=0
        )
        padded = extended(stacked, (("space", 3),), 1)
        terms = diffuse(padded, stiff_rims[:, None], fibre_weights)
        image = direction + jnp.sum(terms, axis=0)
        step_size = norm_now / lax.psum(jnp.sum(direction * image), ("mode", "space"))
        solution_field = solution_field + step_size * direction
        residual = residual - step_size * image
        norm_next = squares(residual)
        direction = residual + norm_next / norm_now * direction
        norm_now = norm_next
    return (solution_field, residual)


COMPS = 3
SLAB = 3
PARTS = 8
WIDE = 16
ROWS = 4
UPWARD = (1, 2, 3)
DOWNWARD = (0, 1, 3)
EVEN = 1 + VARS * (VARS + 1) // 2
SPAN = VARS * EVEN
FULL = 624
INNER = 6
TILES = 8
LANES = 128
VMEM = 56 * 1024 * 1024


def lane_id():
    return lax.broadcasted_iota(jnp.int32, (8, LANES), 1)


def swap_out(tile):
    block = lane_id() // WIDE
    tile = pltpu.roll(tile, 0, 1, stride=WIDE, stride_axis=0)
    for bit in (1, 2, 4):
        tile = jnp.where((block & bit) != 0, pltpu.roll(tile, 8 - bit, 0), tile)
    return tile


def swap_back(tile):
    block = lane_id() // WIDE
    row = lax.broadcasted_iota(jnp.int32, (8, LANES), 0)
    for bit in (1, 2, 4):
        tile = jnp.where((block & bit) != 0, pltpu.roll(tile, bit, 0), tile)
    for bit in (1, 2, 4):
        tile = jnp.where((row & bit) != 0, pltpu.roll(tile, LANES - WIDE * bit, 1), tile)
    return tile


def halo_row(planes):
    lane = lane_id()
    slot = lane % WIDE
    halo = jnp.zeros((8, LANES), jnp.float32)
    for x, plane in planes.items():
        places = [(-1, x + 1), (WIDE, x + 6)]
        if 0 <= x < SLAB:
            places += [(-2, x + 10), (WIDE + 1, x + 13)]
        for offset, place in places:
            inside = (lane >= WIDE) if offset < 0 else (lane < LANES - WIDE)
            moved = pltpu.roll(plane, (place - offset) % LANES, 1)
            halo = jnp.where((slot == place) & inside, moved, halo)
    return halo


UNROLL = 3


def pack_kernel(field, *refs, comps):
    modes = field.shape[0]
    out = refs[-1]
    if len(refs) > 1:
        mean, ply, both = refs[0], refs[1], refs[-2]
        for x in range(SLAB):
            both[0, x] = mean[x]
            both[1, x] = (ply[x] + 1).astype(jnp.float32)
    rows = ROWS * len(comps)
    unroll = 2 * UNROLL // len(comps)

    def body(step, carry):
        for inner in range(unroll):
            mode = step * unroll + inner
            for n, comp in enumerate(comps):
                planes = [field[mode, comp, x] for x in range(SLAB)]
                halo = halo_row(dict(enumerate(planes)))
                for p, tile in enumerate(planes + [halo]):
                    out[pl.ds((n * modes + mode) * ROWS + p, PARTS, stride=rows * modes), :] = swap_out(tile)
        return carry

    lax.fori_loop(0, modes // unroll, body, 0)


def estimate(micros):
    return pl.CostEstimate(flops=int(micros * 1e9), bytes_accessed=int(micros * 3e6), transcendentals=0)


def pack(field, comps, stiffness=(), after=()):
    modes = field.shape[0]
    vmem = pl.BlockSpec(memory_space=pltpu.VMEM)
    shapes = [jax.ShapeDtypeStruct((2,) + s.shape, jnp.float32) for s in stiffness[:1]]
    shapes.append(jax.ShapeDtypeStruct((PARTS * modes * ROWS * len(comps), LANES), jnp.float32))
    return pl.pallas_call(
        functools.partial(pack_kernel, comps=comps),
        grid=(1,),
        out_shape=shapes,
        in_specs=[pl.BlockSpec((modes, max(comps) + 1) + field.shape[2:], lambda i: (0, 0, 0, 0, 0))]
        + [vmem] * len(stiffness)
        + [pl.BlockSpec(memory_space=pl.ANY)] * len(after),
        out_specs=[vmem] * len(shapes),
        compiler_params=pltpu.CompilerParams(vmem_limit_bytes=VMEM),
        cost_estimate=estimate(0.5),
        name="pack",
    )(field, *stiffness, *after)


def copy_kernel(source, ready, goal):
    goal[...] = source[...]


def part_kernel(source, ready, own, upward, downward):
    rows = own.shape[0]
    slots = rows // ROWS
    own[...] = source[...].reshape(rows, LANES)
    for goal, planes in ((upward, UPWARD), (downward, DOWNWARD)):
        for n, p in enumerate(planes):
            goal[n * slots : (n + 1) * slots, :] = own[pl.ds(p, slots, stride=ROWS), :]


def part_component(rows, n, ready):
    blocks = rows.reshape(PARTS, -1, LANES)
    part = (PARTS, blocks.shape[1] // (COMPS - 1), LANES)
    count = part[0] * part[1]
    vmem = pl.BlockSpec(memory_space=pltpu.VMEM)
    return pl.pallas_call(
        part_kernel,
        grid=(1,),
        out_shape=[
            jax.ShapeDtypeStruct((size, LANES), jnp.float32)
            for size in (count, count * len(UPWARD) // ROWS, count * len(DOWNWARD) // ROWS)
        ],
        in_specs=[pl.BlockSpec(part, lambda i: (0, n, 0)), pl.BlockSpec(memory_space=pl.ANY)],
        out_specs=[vmem] * 3,
        compiler_params=pltpu.CompilerParams(vmem_limit_bytes=VMEM),
        cost_estimate=estimate(0.5),
        name="part_component",
    )(blocks, ready)


def after_rows(table, ready):
    vmem = pl.BlockSpec(memory_space=pltpu.VMEM)
    return pl.pallas_call(
        copy_kernel,
        out_shape=jax.ShapeDtypeStruct(table.shape, table.dtype),
        in_specs=[vmem, pl.BlockSpec(memory_space=pl.ANY)],
        out_specs=vmem,
        cost_estimate=estimate(0.5),
        name="after_rows",
    )(table, ready)


def stiffness_kernel(place, before, both, after, ply_stiffness, fields, wide):
    rows = []
    for kind in range(2):
        planes = {-2: before[kind, 1], -1: before[kind, 2], 3: after[kind, 0], 4: after[kind, 1]}
        planes.update({x: both[kind, x] for x in range(SLAB)})
        halo = halo_row({x: planes[x] for x in range(-1, 4)})
        ordered = [planes[0], planes[1], planes[2], planes[-1], planes[3], halo, planes[-2], planes[4]]
        for t, tile in enumerate(ordered):
            wide[...] = swap_out(tile)
            rows.append(wide[pl.ds(place[0], 1), :])
    for t in range(TILES):
        mean, ply = rows[t], rows[TILES + t]
        cols = slice(LANES * t, LANES * (t + 1))
        for k in range(VARS):
            fields[k : k + 1, cols] = jnp.where(ply == k + 1.0, ply_stiffness[k], 0.0)
        fields[VARS : VARS + 1, cols] = mean
        fields[VARS + 1 : VARS + 2, cols] = jnp.where(ply > 0.0, 1.0, 0.0)
        fields[VARS + 2 : 16, cols] = jnp.zeros((4, LANES), jnp.float32)


def stiffness_fields(place, before, both, after, ply_stiffness):
    vmem = pl.BlockSpec(memory_space=pltpu.VMEM)
    smem = pl.BlockSpec(memory_space=pltpu.SMEM)
    return pl.pallas_call(
        stiffness_kernel,
        out_shape=jax.ShapeDtypeStruct((16, TILES * LANES), jnp.float32),
        in_specs=[smem, vmem, vmem, vmem, smem],
        out_specs=vmem,
        scratch_shapes=[pltpu.VMEM((8, LANES), jnp.float32)],
        cost_estimate=estimate(0.5),
        name="stiffness_fields",
    )(place, before, both, after, ply_stiffness)


AT = {0: 0, 1: 1, 2: 2, -1: 3, 3: 4, -2: 6, 4: 7}
PLACE = {index: x for x, index in AT.items()}
HALO = 5


def neighbour(tiles, index, side, place, full=False, wrap=False):
    t = tiles[index]
    lane = lax.broadcasted_iota(jnp.int32, t.shape, 1)
    slot = lane % WIDE
    roll = lambda v, s: pltpu.roll(v, s % LANES, 1)
    if side in (2, 3) and wrap:
        return roll(t, WIDE if side == 2 else -WIDE)
    if side in (2, 3):
        y = (place + lane // WIDE) & 7
        if side == 2:
            return jnp.where(y > 0, roll(t, WIDE), 0.0)
        return jnp.where(y < 7, roll(t, -WIDE), 0.0)
    if index == HALO:
        if side < 2:
            return roll(t, 1 if side == 0 else -1)
        result = roll(t, -9) if side == 4 else roll(t, -7)
        for x in range(-1, 4) if full else range(SLAB):
            goal, by = (x + 6, x - 9) if side == 4 else (x + 1, x + 1)
            result = jnp.where(slot == goal, roll(tiles[AT[x]], by), result)
        if full:
            result = jnp.where(slot >= 13, roll(t, 7), result) if side == 4 else jnp.where(
                (slot >= 10) & (slot < 13), roll(t, 9), result
            )
        return result
    x = PLACE[index]
    if side < 2:
        return tiles[AT[x - 1 if side == 0 else x + 1]]
    if side == 4:
        return jnp.where(slot == 0, roll(tiles[HALO], -(x + 1)), roll(t, 1))
    return jnp.where(slot == WIDE - 1, roll(tiles[HALO], 9 - x), roll(t, -1))


def sides_of(index, outer):
    if index < outer:
        return range(6)
    return {3: (1,), 4: (0,), HALO: (4, 5), 6: (1,), 7: (0,)}[index]


def split(array):
    high = array.astype(jnp.bfloat16)
    low = (array - high.astype(jnp.float32)).astype(jnp.bfloat16)
    return jnp.concatenate([high, low], axis=0)


STEP = 48
FACE = 16
CENTRE = 6 * FACE
EVEN_BLOCKS = ((0, 32), (32, EVEN))


def tile_cols(t):
    return slice(LANES * t, LANES * (t + 1))


def face_stiffness(fields, faces, weights, place):
    tiles = [fields[:, tile_cols(t)] for t in range(TILES)]
    for t in range(TILES):
        for side in sides_of(t, INNER):
            value = (0.5 * weights[side // 2]) * (tiles[t] + neighbour(tiles, t, side, place, True))
            faces[side * FACE : (side + 1) * FACE, tile_cols(t)] = value
        if t < INNER:
            centre = 1.0 + sum(faces[side * FACE + VARS : side * FACE + VARS + 1, tile_cols(t)] for side in range(6))
            faces[CENTRE : CENTRE + 1, tile_cols(t)] = centre
            lane = lax.broadcasted_iota(jnp.int32, (1, LANES), 1)
            y = (place + lane // WIDE) & 7
            for side, edge in ((2, 0), (3, 7)):
                row = side * FACE + VARS
                faces[row + 1 : row + 2, tile_cols(t)] = jnp.where(
                    y == edge, 0.0, faces[row : row + 1, tile_cols(t)]
                )


CHUNK = 8


def chunks(count):
    return [range(start, min(start + CHUNK, count)) for start in range(0, count, CHUNK)]


def chunk_cols(tiles):
    return slice(LANES * tiles[0], LANES * (tiles[-1] + 1))


def apply_operator(src, dst, mixed, flux, scaled, acc, faces, inside, to_even, to_all, place, inner, outer):
    slots = src.shape[0]

    def face(side, k, t):
        return faces[side * FACE + k : side * FACE + k + 1, tile_cols(t)]

    def mix(tiles):
        cols = chunk_cols(tiles)
        mixed[:, cols] = jnp.dot(to_even[...], split(src[:, cols]), preferred_element_type=jnp.float32)

    def flows(t):
        for low, high in EVEN_BLOCKS:
            total = {}
            for k in range(VARS):
                value = mixed[k * EVEN + low : k * EVEN + high, tile_cols(t)]
                for side in sides_of(t, outer):
                    term = face(side, k, t) * value
                    total[side] = term if k == 0 else total[side] + term
            for side, value in total.items():
                flux[side, low:high, tile_cols(t)] = value

    def scale_even(t):
        for low, high in EVEN_BLOCKS:
            even = EvenTiles(mixed, low, high)
            steps = [even[t] - neighbour(even, t, side, place) for side in range(6)]
            for k in range(VARS):
                total = face(0, k, t) * steps[0]
                for side in range(1, 6):
                    total = total + face(side, k, t) * steps[side]
                scaled[k * EVEN + low : k * EVEN + high, tile_cols(t)] = total
            total = None
            for side in range(6):
                opposite = FluxTiles(flux, side ^ 1, low, high)
                term = flux[side, low:high, tile_cols(t)] - neighbour(opposite, t, side, place)
                total = term if total is None else total + term
            scaled[SPAN + low : SPAN + high, tile_cols(t)] = total
        scaled[SPAN + EVEN : FULL, tile_cols(t)] = jnp.zeros((FULL - SPAN - EVEN, LANES), jnp.float32)

    def spread(tiles):
        cols = chunk_cols(tiles)
        acc[:, cols] = jnp.dot(to_all[...], split(scaled[:, cols]), preferred_element_type=jnp.float32)

    before = ()
    for tiles in chunks(inner):
        mix(tiles)
        for t in before:
            flows(t)
        before = tiles
    for t in before:
        flows(t)
    before = ()
    for tiles in chunks(outer):
        for t in tiles:
            scale_even(t)
        if before:
            spread(before)
        before = tiles
    spread(before)

    def last(step, carry):
        rows = pl.ds(pl.multiple_of(step * STEP, STEP), STEP)
        tiles = [src[rows, tile_cols(t)] for t in range(inner)]
        for t in range(outer):
            result = acc[rows, tile_cols(t)] + faces[CENTRE : CENTRE + 1, tile_cols(t)] * tiles[t]
            for side in range(6):
                row = VARS + 1 if side in (2, 3) else VARS
                result = result - face(side, row, t) * neighbour(tiles, t, side, place, wrap=True)
            if t >= SLAB:
                result = inside[t] * result
            dst[rows, tile_cols(t)] = result
        return carry

    lax.fori_loop(0, slots // STEP, last, 0)


class EvenTiles:
    def __init__(self, mixed, low, high):
        self.mixed, self.low, self.high = mixed, low, high

    def __getitem__(self, t):
        return self.mixed[SPAN + self.low : SPAN + self.high, tile_cols(t)]


class FluxTiles:
    def __init__(self, flux, side, low, high):
        self.flux, self.side, self.low, self.high = flux, side, low, high

    def __getitem__(self, t):
        return self.flux[self.side, self.low : self.high, tile_cols(t)]


def apply_kernel(
    place, own, before, after, scale, to_even, to_all, fields, fibre, *refs, comp,
):
    out, partial, field, first, second, mixed, flux, scaled, acc, faces = refs[-10:]
    slots = scale.shape[0]
    here = place[0]
    face_stiffness(fields, faces, [fibre[comp, d] for d in range(3)], here)
    lane = lax.broadcasted_iota(jnp.int32, (slots, LANES), 1)
    slot = lane % WIDE
    load = lambda ref, p: ref[pl.ds(p, slots, stride=ROWS), :]
    whole = before.shape[0] == own.shape[0]
    below = lambda p: load(before, p) if whole else before[pl.ds(UPWARD.index(p) * slots, slots), :]
    above = lambda p: load(after, p) if whole else after[pl.ds(DOWNWARD.index(p) * slots, slots), :]
    left = pltpu.roll(below(3), LANES - 3, 1)
    right = pltpu.roll(above(3), 3, 1)
    halo = jnp.where((slot == 0) | (slot == 5), left, load(own, 3))
    halo = jnp.where((slot == 4) | (slot == 9), right, halo)
    ordered = [
        load(own, 0), load(own, 1), load(own, 2), below(2), above(0), halo,
        below(1), above(1),
    ]
    for t, tile in enumerate(ordered):
        field[:, tile_cols(t)] = tile * scale[...]
    inside = {t: fields[VARS + 1 : VARS + 2, tile_cols(t)] for t in range(SLAB, INNER)}
    slot = lax.broadcasted_iota(jnp.int32, (1, LANES), 1) % WIDE
    used = ((slot >= 1) & (slot <= 3)) | ((slot >= 6) & (slot <= 8))
    inside[HALO] = jnp.where(used, inside[HALO], 0.0)
    scratch = (mixed, flux, scaled, acc, faces, inside, to_even, to_all, here)
    apply_operator(field, first, *scratch, TILES, INNER)
    apply_operator(first, second, *scratch, INNER, SLAB)
    sums = [jnp.zeros((1, LANES), jnp.float32)] * 5
    unscale = 1.0 / scale[...]
    for p in range(SLAB):
        b = load(own, p)
        q = first[:, tile_cols(p)] * unscale
        w = second[:, tile_cols(p)] * unscale
        out[pl.ds(p, slots, stride=2 * SLAB), :] = q
        out[pl.ds(p + SLAB, slots, stride=2 * SLAB), :] = w
        for n, (one, two) in enumerate(((b, b), (b, q), (q, q), (b, w), (q, w))):
            sums[n] = sums[n] + jnp.sum(one * two, axis=0, keepdims=True)
    total = jnp.concatenate(sums + [jnp.zeros((3, LANES), jnp.float32)], axis=0)
    partial[...] = total + refs[0][...] if comp > 0 else total


def apply_twice(comp, place, own, before, after, tables, fields, fibre, so_far=(), ready=()):
    scale, to_even, to_all = tables
    slots = scale.shape[0]
    vmem = pl.BlockSpec(memory_space=pltpu.VMEM)
    smem = pl.BlockSpec(memory_space=pltpu.SMEM)
    f32 = lambda *shape: pltpu.VMEM(shape, jnp.float32)
    return pl.pallas_call(
        functools.partial(apply_kernel, comp=comp),
        out_shape=[
            jax.ShapeDtypeStruct((slots * 2 * SLAB, LANES), jnp.float32),
            jax.ShapeDtypeStruct((8, LANES), jnp.float32),
        ],
        in_specs=[smem] + [vmem] * 7 + [smem] + [vmem] * len(so_far) + [pl.BlockSpec(memory_space=pl.ANY)] * len(ready),
        out_specs=[vmem, vmem],
        scratch_shapes=[
            f32(slots, TILES * LANES),
            f32(slots, INNER * LANES),
            f32(slots, SLAB * LANES),
            f32(FULL, TILES * LANES),
            f32(6, EVEN, TILES * LANES),
            f32(FULL, INNER * LANES),
            f32(slots, INNER * LANES),
            f32(6 * FACE + 8, TILES * LANES),
        ],
        compiler_params=pltpu.CompilerParams(vmem_limit_bytes=VMEM),
        cost_estimate=estimate(2),
        name="apply_twice",
    )(place, own, before, after, scale, to_even, to_all, fields, fibre, *so_far, *ready)


def combination(total):
    bb, bq, qq, bw, qw = (jnp.sum(total[n : n + 1, :], axis=1, keepdims=True) for n in range(5))
    step_one = bb / bq
    norm = bb - 2.0 * step_one * bq + step_one * step_one * qq
    grown = 1.0 + norm / bb
    curve = grown * grown * bq - step_one * grown * (bw + qq) + step_one * step_one * qw
    step_two = norm / curve
    return step_one + step_two * grown, step_one * step_two


def unpack_kernel(image, natural):
    modes = natural.shape[1]
    per_part = modes * 2 * SLAB

    def body(step, carry):
        for inner in range(2 * UNROLL):
            mode = step * 2 * UNROLL + inner
            for power in range(2):
                for p in range(SLAB):
                    row = (mode * 2 + power) * SLAB + p
                    natural[power, mode, p] = swap_back(image[pl.ds(row, PARTS, stride=per_part), :])
        return carry

    lax.fori_loop(0, modes // (2 * UNROLL), body, 0)


def unpack(image, modes):
    vmem = pl.BlockSpec(memory_space=pltpu.VMEM)
    return pl.pallas_call(
        unpack_kernel,
        out_shape=jax.ShapeDtypeStruct((2, modes, SLAB, 8, LANES), jnp.float32),
        in_specs=[vmem],
        out_specs=vmem,
        compiler_params=pltpu.CompilerParams(vmem_limit_bytes=VMEM),
        cost_estimate=estimate(3),
        name="unpack",
    )(image)


STEPS = 2


def finish_kernel(field, total, image, *refs):
    *natural, solution_field, residual, factors = refs
    modes = field.shape[0]
    per_part = STEPS * modes * 2 * SLAB

    @pl.when(pl.program_id(0) == 0)
    def _():
        sole, cross = combination(total)
        factors[0:8, :] = jnp.broadcast_to(sole, (8, LANES))
        factors[8:16, :] = jnp.broadcast_to(cross, (8, LANES))

    sole, cross = factors[0:8, :], factors[8:16, :]
    first = pl.program_id(0) * modes

    def body(step, carry):
        for inner in range(2 * UNROLL):
            mode = step * 2 * UNROLL + inner
            for comp in range(COMPS):
                for p in range(SLAB):
                    b = field[mode, comp, p]
                    if comp < len(natural):
                        q, w = natural[comp][0, mode, p], natural[comp][1, mode, p]
                    else:
                        row = (first + mode) * 2 * SLAB + p
                        q = swap_back(image[pl.ds(row, PARTS, stride=per_part), :])
                        w = swap_back(image[pl.ds(row + SLAB, PARTS, stride=per_part), :])
                    solution_field[mode, comp, p] = sole * b - cross * q
                    residual[mode, comp, p] = b - sole * q + cross * w
        return carry

    lax.fori_loop(0, modes // (2 * UNROLL), body, 0)


def finish(field, total, image, *natural):
    rows = field.shape[0] // STEPS
    block = pl.BlockSpec((rows,) + field.shape[1:], lambda i: (i, 0, 0, 0, 0))
    vmem = pl.BlockSpec(memory_space=pltpu.VMEM)
    return pl.pallas_call(
        finish_kernel,
        grid=(STEPS,),
        out_shape=[jax.ShapeDtypeStruct(field.shape, jnp.float32)] * 2,
        in_specs=[block, vmem, vmem]
        + [pl.BlockSpec((2, rows) + field.shape[2:], lambda i: (0, i, 0, 0, 0))] * len(natural),
        out_specs=[block, block],
        scratch_shapes=[pltpu.VMEM((16, LANES), jnp.float32)],
        compiler_params=pltpu.CompilerParams(vmem_limit_bytes=VMEM),
        cost_estimate=estimate(6),
        name="finish",
    )(field, total, image, *natural)


def mode_tables(coupling_table, slots):
    lower, upper, variable, code = (coupling_table[:, n] for n in range(4))
    slot = jnp.arange(slots, dtype=jnp.int32)
    is_lower = lower[:, None] == slot
    is_upper = upper[:, None] == slot
    degree = jnp.sum(jnp.where(is_upper, code[:, None], 0), axis=0)
    factor = jnp.where(code == 3, 6, code).astype(jnp.float32)[:, None]
    factorial = jnp.prod(jnp.where(is_upper, factor, 1.0), axis=0)
    root = (degree == 0) & jnp.any(is_lower, axis=0)
    even = (degree == 2) | root
    rank = jnp.sum(jnp.where(even[:, None] & (slot[:, None] < slot), 1, 0), axis=0)
    lower_even = jnp.any(is_lower & even, axis=1)
    is_even_end = jnp.where(lower_even[:, None], is_lower, is_upper)
    is_odd_end = jnp.where(lower_even[:, None], is_upper, is_lower)
    column = variable * EVEN + jnp.sum(jnp.where(is_even_end, rank, 0), axis=1)
    at_column = column[:, None] == jnp.arange(FULL, dtype=jnp.int32)
    down = code.astype(jnp.float32)[:, None]
    first = jnp.where(lower_even[:, None], 1.0, down)
    second = jnp.where(lower_even[:, None], down, 1.0)
    odd_ends = is_odd_end.astype(jnp.float32)
    columns = at_column.astype(jnp.float32)
    half = jnp.bfloat16
    to_even = jnp.dot(
        columns.astype(half).T, (odd_ends * first).astype(half), preferred_element_type=jnp.float32
    )
    to_odd = jnp.dot(
        odd_ends.astype(half).T, (columns * second).astype(half), preferred_element_type=jnp.float32
    )
    pick = (jnp.arange(FULL, dtype=jnp.int32)[:, None] - SPAN == rank) & even
    pick = pick.astype(jnp.float32)
    to_even = (to_even + pick).astype(half)
    to_all = (to_odd + pick.T).astype(half)
    scale = jnp.sqrt(factorial)
    wide = lambda v: jnp.broadcast_to(v[:, None], (slots, LANES))
    twice = lambda v: jnp.concatenate([v, v], axis=1)
    return wide(scale), twice(to_even), twice(to_all)


def all_sum(value):
    for axis, bit in (("space", 1), ("space", 2), ("mode", 1)):
        devices = lax.axis_size(axis)
        value = value + lax.ppermute(value, axis, [(i, i ^ bit) for i in range(devices)])
    others = [
        lax.ppermute(value, "mode", [(i, i ^ bit) for i in range(PARTS)]) for bit in range(2, PARTS, 2)
    ]
    return (value + others[0]) + (others[1] + others[2])


def transposed(right_side, mean_stiffness, ply_stiffness, fibre_weights, ply_map, coupling_table):
    slots = right_side.shape[0] * PARTS
    devices = lax.axis_size("space")
    up = [(i, i + 1) for i in range(devices - 1)]
    down = [(j, i) for i, j in up]
    place = lax.axis_index("mode").astype(jnp.int32).reshape(1)

    def swap(rows):
        return lax.all_to_all(rows, "mode", 0, 0, tiled=True)

    def halo(rows, upward, downward):
        return rows, lax.ppermute(upward, "space", up), lax.ppermute(downward, "space", down)

    (first,) = pack(right_side, (0,))
    both, others = pack(right_side, (1, 2), (mean_stiffness, ply_map), (first,))
    first = swap(first)
    first = halo(first, first, first)
    others = swap(others)
    tables = mode_tables(after_rows(coupling_table, first[0]), slots)
    both_before = lax.ppermute(both, "space", up)
    both_after = lax.ppermute(both, "space", down)
    fields = stiffness_fields(place, both_before, both, both_after, ply_stiffness)
    image, partial = apply_twice(0, place, *first, tables, fields, fibre_weights)
    images = [swap(image)]
    parts = [part_component(others, n, partial) for n in range(COMPS - 1)]
    halos = [halo(*part) for part in parts]
    modes = right_side.shape[0]
    image, partial = apply_twice(1, place, *halos[0], tables, fields, fibre_weights, (partial,), parts[1][:1])
    images.append(swap(image))
    natural = [unpack(images[0], modes)]
    image, partial = apply_twice(2, place, *halos[1], tables, fields, fibre_weights, (partial,), natural)
    images.append(swap(image))
    natural.append(unpack(images[1], modes))
    return tuple(finish(right_side, all_sum(partial), images[2], *natural))


def on_device(right_side, mean_stiffness, ply_stiffness, fibre_weights, ply_map, coupling_table):
    args = (right_side, mean_stiffness, ply_stiffness, fibre_weights, ply_map, coupling_table)
    fits = right_side.shape[1:] == (COMPS, SLAB, 8, 128) and (lax.axis_size("mode"), lax.axis_size("space")) == (PARTS, 4)
    return transposed(*args) if fits else plain(*args)


def solution(mesh):
    return jax.shard_map(
        on_device,
        mesh=mesh,
        in_specs=(
            P("mode", None, "space", None, None),
            P("space", None, None),
            P(),
            P(),
            P("space", None, None),
            P(),
        ),
        out_specs=(P("mode", None, "space", None, None), P("mode", None, "space", None, None)),
        check_vma=False,
    )
```

```python
import functools

import jax
import jax.numpy as jnp
from jax import lax
from jax.experimental import pallas as pl
from jax.experimental.pallas import tpu as pltpu
from jax.sharding import PartitionSpec as P

VARS = 10
ITERS = 2


def extended(array, sides, width):
    for axis, dim in sides:
        devices, length = (lax.axis_size(axis), array.shape[dim])
        up = [(i, (i + 1) % devices) for i in range(devices - 1)]
        down = [(j, i) for i, j in up]
        last = lax.slice_in_dim(array, length - width, length, axis=dim)
        leading = lax.slice_in_dim(array, 0, width, axis=dim)
        before = lax.ppermute(last, axis, up)
        after = lax.ppermute(leading, axis, down)
        array = jnp.concatenate([before, array, after], axis=dim)
    return array


def window(array_in, dim_index, offset):
    slicers = [slice(None)] * (array_in.ndim - 3)
    for which in range(3):
        shift_by = offset if which == dim_index else 0
        length_here = array_in.shape[array_in.ndim - 3 + which] - 2
        slicers.append(slice(1 + shift_by, 1 + shift_by + length_here))
    return array_in[tuple(slicers)]


def diffuse(vector, stiffness, fibre_weights):
    vector_pads = [(0, 0)] * (vector.ndim - 2) + [(1, 1), (1, 1)]
    stiff_pads = [(0, 0)] * (stiffness.ndim - 2) + [(1, 1), (1, 1)]
    padded_v = jnp.pad(vector, vector_pads)
    padded_c = jnp.pad(stiffness, stiff_pads)
    centre = window(padded_v, 0, 0)
    middle = window(padded_c, 0, 0)
    result = None
    for dim_index in range(3):
        upper = (
            0.5
            * (middle + window(padded_c, dim_index, 1))
            * (centre - window(padded_v, dim_index, 1))
        )
        lower = (
            0.5
            * (middle + window(padded_c, dim_index, -1))
            * (centre - window(padded_v, dim_index, -1))
        )
        column = fibre_weights[:, dim_index].reshape(3, 1, 1, 1)
        term = column * (upper + lower)
        result = term if result is None else result + term
    return result


def squares(vector):
    return lax.psum(jnp.sum(vector * vector), ("mode", "space"))


def row_table(both_rows, both_cols, both_vars, both_weights, base, mode_dev, slots):
    local_rows = both_rows - base
    valid_rows = (local_rows >= 0) & (local_rows < mode_dev)
    local_rows = jnp.where(valid_rows, local_rows, mode_dev)
    row_coupling = jnp.zeros((VARS, mode_dev, slots), jnp.float32)
    row_coupling = row_coupling.at[both_vars, local_rows, both_cols].add(both_weights, mode="drop")
    return row_coupling.reshape(VARS * mode_dev, slots)


def plain(right_side, mean_stiffness, ply_stiffness, fibre_weights, ply_map, coupling_table):
    mode_dev = right_side.shape[0]
    slots = mode_dev * lax.axis_size("mode")
    base = lax.axis_index("mode") * mode_dev
    first_mode = coupling_table[:, 0]
    second_mode = coupling_table[:, 1]
    variable = coupling_table[:, 2]
    entry_weight = jnp.sqrt(coupling_table[:, 3].astype(jnp.float32))
    both_rows = jnp.concatenate([first_mode, second_mode])
    both_cols = jnp.concatenate([second_mode, first_mode])
    both_vars = jnp.concatenate([variable, variable])
    both_weights = jnp.concatenate([entry_weight, entry_weight])
    plies = jnp.arange(VARS, dtype=jnp.int32).reshape(VARS, 1, 1, 1)
    ply_fields = (ply_map[None] == plies).astype(jnp.float32) * ply_stiffness.reshape(VARS, 1, 1, 1)
    stiff_stack = jnp.concatenate([mean_stiffness[None], ply_fields], axis=0)
    stiff_rims = extended(stiff_stack, (("space", 1),), 1)
    stiff_rims = stiff_rims[:, None]
    row_coupling = row_table(both_rows, both_cols, both_vars, both_weights, base, mode_dev, slots)
    solution_field = jnp.zeros_like(right_side)
    residual = right_side
    direction = right_side
    norm_now = squares(residual)
    for iteration in range(ITERS):
        shard_piece = lax.all_gather(direction, "mode", axis=0, tiled=True)
        mixed = jnp.dot(
            row_coupling,
            shard_piece.reshape(shard_piece.shape[0], -1),
            precision=lax.Precision.HIGHEST,
            preferred_element_type=jnp.float32,
        )
        stacked = jnp.concatenate(
            [direction[None], mixed.reshape((VARS,) + direction.shape)], axis=0
        )
        padded = extended(stacked, (("space", 3),), 1)
        terms = diffuse(padded, stiff_rims[:, None], fibre_weights)
        image = direction + jnp.sum(terms, axis=0)
        step_size = norm_now / lax.psum(jnp.sum(direction * image), ("mode", "space"))
        solution_field = solution_field + step_size * direction
        residual = residual - step_size * image
        norm_next = squares(residual)
        direction = residual + norm_next / norm_now * direction
        norm_now = norm_next
    return (solution_field, residual)


COMPS = 3
SLAB = 3
PARTS = 8
WIDE = 16
ROWS = 4
UPWARD = (1, 2, 3)
DOWNWARD = (0, 1, 3)
EVEN = 1 + VARS * (VARS + 1) // 2
SPAN = VARS * EVEN
FULL = 624
INNER = 6
TILES = 8
LANES = 128
VMEM = 56 * 1024 * 1024


def lane_id():
    return lax.broadcasted_iota(jnp.int32, (8, LANES), 1)


def swap_out(tile):
    block = lane_id() // WIDE
    tile = pltpu.roll(tile, 0, 1, stride=WIDE, stride_axis=0)
    for bit in (1, 2, 4):
        tile = jnp.where((block & bit) != 0, pltpu.roll(tile, 8 - bit, 0), tile)
    return tile


def swap_back(tile):
    block = lane_id() // WIDE
    row = lax.broadcasted_iota(jnp.int32, (8, LANES), 0)
    for bit in (1, 2, 4):
        tile = jnp.where((block & bit) != 0, pltpu.roll(tile, bit, 0), tile)
    for bit in (1, 2, 4):
        tile = jnp.where((row & bit) != 0, pltpu.roll(tile, LANES - WIDE * bit, 1), tile)
    return tile


def halo_row(planes):
    lane = lane_id()
    slot = lane % WIDE
    halo = jnp.zeros((8, LANES), jnp.float32)
    for x, plane in planes.items():
        places = [(-1, x + 1), (WIDE, x + 6)]
        if 0 <= x < SLAB:
            places += [(-2, x + 10), (WIDE + 1, x + 13)]
        for offset, place in places:
            inside = (lane >= WIDE) if offset < 0 else (lane < LANES - WIDE)
            moved = pltpu.roll(plane, (place - offset) % LANES, 1)
            halo = jnp.where((slot == place) & inside, moved, halo)
    return halo


UNROLL = 3


def pack_kernel(field, *refs, comps):
    modes = field.shape[0]
    out = refs[-1]
    if len(refs) > 1:
        mean, ply, both = refs[0], refs[1], refs[-2]
        for x in range(SLAB):
            both[0, x] = mean[x]
            both[1, x] = (ply[x] + 1).astype(jnp.float32)
    rows = ROWS * len(comps)
    unroll = 2 * UNROLL // len(comps)

    def body(step, carry):
        for inner in range(unroll):
            mode = step * unroll + inner
            for n, comp in enumerate(comps):
                planes = [field[mode, comp, x] for x in range(SLAB)]
                halo = halo_row(dict(enumerate(planes)))
                for p, tile in enumerate(planes + [halo]):
                    out[pl.ds((n * modes + mode) * ROWS + p, PARTS, stride=rows * modes), :] = swap_out(tile)
        return carry

    lax.fori_loop(0, modes // unroll, body, 0)


def estimate(micros):
    return pl.CostEstimate(flops=int(micros * 1e9), bytes_accessed=int(micros * 3e6), transcendentals=0)


def pack(field, comps, stiffness=(), after=()):
    modes = field.shape[0]
    vmem = pl.BlockSpec(memory_space=pltpu.VMEM)
    shapes = [jax.ShapeDtypeStruct((2,) + s.shape, jnp.float32) for s in stiffness[:1]]
    shapes.append(jax.ShapeDtypeStruct((PARTS * modes * ROWS * len(comps), LANES), jnp.float32))
    return pl.pallas_call(
        functools.partial(pack_kernel, comps=comps),
        grid=(1,),
        out_shape=shapes,
        in_specs=[pl.BlockSpec((modes, max(comps) + 1) + field.shape[2:], lambda i: (0, 0, 0, 0, 0))]
        + [vmem] * len(stiffness)
        + [pl.BlockSpec(memory_space=pl.ANY)] * len(after),
        out_specs=[vmem] * len(shapes),
        compiler_params=pltpu.CompilerParams(vmem_limit_bytes=VMEM),
        cost_estimate=estimate(0.5),
        name="pack",
    )(field, *stiffness, *after)


def copy_kernel(source, ready, goal):
    goal[...] = source[...]


def part_kernel(turns, source, ready, own, across, beside):
    rows = own.shape[0]
    slots = rows // ROWS
    own[...] = source[...].reshape(rows, LANES)
    for n, goal in enumerate((across, beside)):
        for m in range(len(UPWARD) - 1):
            goal[m * slots : (m + 1) * slots, :] = own[pl.ds(m + turns[n], slots, stride=ROWS), :]
        goal[(len(UPWARD) - 1) * slots :, :] = own[pl.ds(UPWARD[-1], slots, stride=ROWS), :]


def part_component(turns, rows, n, ready):
    blocks = rows.reshape(PARTS, -1, LANES)
    part = (PARTS, blocks.shape[1] // (COMPS - 1), LANES)
    count = part[0] * part[1]
    vmem = pl.BlockSpec(memory_space=pltpu.VMEM)
    return pl.pallas_call(
        part_kernel,
        grid=(1,),
        out_shape=[
            jax.ShapeDtypeStruct((size, LANES), jnp.float32)
            for size in (count, count * len(UPWARD) // ROWS, count * len(DOWNWARD) // ROWS)
        ],
        in_specs=[
            pl.BlockSpec(memory_space=pltpu.SMEM),
            pl.BlockSpec(part, lambda i: (0, n, 0)),
            pl.BlockSpec(memory_space=pl.ANY),
        ],
        out_specs=[vmem] * 3,
        compiler_params=pltpu.CompilerParams(vmem_limit_bytes=VMEM),
        cost_estimate=estimate(0.5),
        name="part_component",
    )(turns, blocks, ready)


def after_rows(table, ready):
    vmem = pl.BlockSpec(memory_space=pltpu.VMEM)
    return pl.pallas_call(
        copy_kernel,
        out_shape=jax.ShapeDtypeStruct(table.shape, table.dtype),
        in_specs=[vmem, pl.BlockSpec(memory_space=pl.ANY)],
        out_specs=vmem,
        cost_estimate=estimate(0.5),
        name="after_rows",
    )(table, ready)


def stiffness_kernel(place, before, both, after, ply_stiffness, fields, wide):
    rows = []
    for kind in range(2):
        planes = {-2: before[kind, 1], -1: before[kind, 2], 3: after[kind, 0], 4: after[kind, 1]}
        planes.update({x: both[kind, x] for x in range(SLAB)})
        halo = halo_row({x: planes[x] for x in range(-1, 4)})
        ordered = [planes[0], planes[1], planes[2], planes[-1], planes[3], halo, planes[-2], planes[4]]
        for t, tile in enumerate(ordered):
            wide[...] = swap_out(tile)
            rows.append(wide[pl.ds(place[0], 1), :])
    for t in range(TILES):
        mean, ply = rows[t], rows[TILES + t]
        cols = slice(LANES * t, LANES * (t + 1))
        for k in range(VARS):
            fields[k : k + 1, cols] = jnp.where(ply == k + 1.0, ply_stiffness[k], 0.0)
        fields[VARS : VARS + 1, cols] = mean
        fields[VARS + 1 : VARS + 2, cols] = jnp.where(ply > 0.0, 1.0, 0.0)
        fields[VARS + 2 : 16, cols] = jnp.zeros((4, LANES), jnp.float32)


def stiffness_fields(place, before, both, after, ply_stiffness):
    vmem = pl.BlockSpec(memory_space=pltpu.VMEM)
    smem = pl.BlockSpec(memory_space=pltpu.SMEM)
    return pl.pallas_call(
        stiffness_kernel,
        out_shape=jax.ShapeDtypeStruct((16, TILES * LANES), jnp.float32),
        in_specs=[smem, vmem, vmem, vmem, smem],
        out_specs=vmem,
        scratch_shapes=[pltpu.VMEM((8, LANES), jnp.float32)],
        cost_estimate=estimate(0.5),
        name="stiffness_fields",
    )(place, before, both, after, ply_stiffness)


AT = {0: 0, 1: 1, 2: 2, -1: 3, 3: 4, -2: 6, 4: 7}
PLACE = {index: x for x, index in AT.items()}
HALO = 5


def neighbour(tiles, index, side, place, full=False, wrap=False):
    t = tiles[index]
    lane = lax.broadcasted_iota(jnp.int32, t.shape, 1)
    slot = lane % WIDE
    roll = lambda v, s: pltpu.roll(v, s % LANES, 1)
    if side in (2, 3) and wrap:
        return roll(t, WIDE if side == 2 else -WIDE)
    if side in (2, 3):
        y = (place + lane // WIDE) & 7
        if side == 2:
            return jnp.where(y > 0, roll(t, WIDE), 0.0)
        return jnp.where(y < 7, roll(t, -WIDE), 0.0)
    if index == HALO:
        if side < 2:
            return roll(t, 1 if side == 0 else -1)
        result = roll(t, -9) if side == 4 else roll(t, -7)
        for x in range(-1, 4) if full else range(SLAB):
            goal, by = (x + 6, x - 9) if side == 4 else (x + 1, x + 1)
            result = jnp.where(slot == goal, roll(tiles[AT[x]], by), result)
        if full:
            result = jnp.where(slot >= 13, roll(t, 7), result) if side == 4 else jnp.where(
                (slot >= 10) & (slot < 13), roll(t, 9), result
            )
        return result
    x = PLACE[index]
    if side < 2:
        return tiles[AT[x - 1 if side == 0 else x + 1]]
    if side == 4:
        return jnp.where(slot == 0, roll(tiles[HALO], -(x + 1)), roll(t, 1))
    return jnp.where(slot == WIDE - 1, roll(tiles[HALO], 9 - x), roll(t, -1))


def sides_of(index, outer):
    if index < outer:
        return range(6)
    return {3: (1,), 4: (0,), HALO: (4, 5), 6: (1,), 7: (0,)}[index]


def split(array):
    high = array.astype(jnp.bfloat16)
    low = (array - high.astype(jnp.float32)).astype(jnp.bfloat16)
    return jnp.concatenate([high, low], axis=0)


STEP = 48
FACE = 16
CENTRE = 6 * FACE
EVEN_BLOCKS = ((0, 32), (32, EVEN))


def tile_cols(t):
    return slice(LANES * t, LANES * (t + 1))


def face_stiffness(fields, faces, weights, place):
    tiles = [fields[:, tile_cols(t)] for t in range(TILES)]
    for t in range(TILES):
        for side in sides_of(t, INNER):
            value = (0.5 * weights[side // 2]) * (tiles[t] + neighbour(tiles, t, side, place, True))
            faces[side * FACE : (side + 1) * FACE, tile_cols(t)] = value
        if t < INNER:
            centre = 1.0 + sum(faces[side * FACE + VARS : side * FACE + VARS + 1, tile_cols(t)] for side in range(6))
            faces[CENTRE : CENTRE + 1, tile_cols(t)] = centre
            lane = lax.broadcasted_iota(jnp.int32, (1, LANES), 1)
            y = (place + lane // WIDE) & 7
            for side, edge in ((2, 0), (3, 7)):
                row = side * FACE + VARS
                faces[row + 1 : row + 2, tile_cols(t)] = jnp.where(
                    y == edge, 0.0, faces[row : row + 1, tile_cols(t)]
                )


CHUNK = 8


def chunks(count):
    return [range(start, min(start + CHUNK, count)) for start in range(0, count, CHUNK)]


def chunk_cols(tiles):
    return slice(LANES * tiles[0], LANES * (tiles[-1] + 1))


def apply_operator(src, dst, mixed, flux, scaled, acc, faces, inside, to_even, to_all, place, inner, outer):
    slots = src.shape[0]

    def face(side, k, t):
        return faces[side * FACE + k : side * FACE + k + 1, tile_cols(t)]

    def mix(tiles):
        cols = chunk_cols(tiles)
        mixed[:, cols] = jnp.dot(to_even[...], split(src[:, cols]), preferred_element_type=jnp.float32)

    def flows(t):
        for low, high in EVEN_BLOCKS:
            total = {}
            for k in range(VARS):
                value = mixed[k * EVEN + low : k * EVEN + high, tile_cols(t)]
                for side in sides_of(t, outer):
                    term = face(side, k, t) * value
                    total[side] = term if k == 0 else total[side] + term
            for side, value in total.items():
                flux[side, low:high, tile_cols(t)] = value

    def scale_even(t):
        for low, high in EVEN_BLOCKS:
            even = EvenTiles(mixed, low, high)
            steps = [even[t] - neighbour(even, t, side, place) for side in range(6)]
            for k in range(VARS):
                total = face(0, k, t) * steps[0]
                for side in range(1, 6):
                    total = total + face(side, k, t) * steps[side]
                scaled[k * EVEN + low : k * EVEN + high, tile_cols(t)] = total
            total = None
            for side in range(6):
                opposite = FluxTiles(flux, side ^ 1, low, high)
                term = flux[side, low:high, tile_cols(t)] - neighbour(opposite, t, side, place)
                total = term if total is None else total + term
            scaled[SPAN + low : SPAN + high, tile_cols(t)] = total
        scaled[SPAN + EVEN : FULL, tile_cols(t)] = jnp.zeros((FULL - SPAN - EVEN, LANES), jnp.float32)

    def spread(tiles):
        cols = chunk_cols(tiles)
        acc[:, cols] = jnp.dot(to_all[...], split(scaled[:, cols]), preferred_element_type=jnp.float32)

    before = ()
    for tiles in chunks(inner):
        mix(tiles)
        for t in before:
            flows(t)
        before = tiles
    for t in before:
        flows(t)
    before = ()
    for tiles in chunks(outer):
        for t in tiles:
            scale_even(t)
        if before:
            spread(before)
        before = tiles
    spread(before)

    def last(step, carry):
        rows = pl.ds(pl.multiple_of(step * STEP, STEP), STEP)
        tiles = [src[rows, tile_cols(t)] for t in range(inner)]
        for t in range(outer):
            result = acc[rows, tile_cols(t)] + faces[CENTRE : CENTRE + 1, tile_cols(t)] * tiles[t]
            for side in range(6):
                row = VARS + 1 if side in (2, 3) else VARS
                result = result - face(side, row, t) * neighbour(tiles, t, side, place, wrap=True)
            if t >= SLAB:
                result = inside[t] * result
            dst[rows, tile_cols(t)] = result
        return carry

    lax.fori_loop(0, slots // STEP, last, 0)


class EvenTiles:
    def __init__(self, mixed, low, high):
        self.mixed, self.low, self.high = mixed, low, high

    def __getitem__(self, t):
        return self.mixed[SPAN + self.low : SPAN + self.high, tile_cols(t)]


class FluxTiles:
    def __init__(self, flux, side, low, high):
        self.flux, self.side, self.low, self.high = flux, side, low, high

    def __getitem__(self, t):
        return self.flux[self.side, self.low : self.high, tile_cols(t)]


def apply_kernel(
    place, own, before, after, scale, to_even, to_all, fields, fibre, *refs, comp,
):
    out, partial, field, first, second, mixed, flux, scaled, acc, faces = refs[-10:]
    slots = scale.shape[0]
    here = place[0]
    face_stiffness(fields, faces, [fibre[comp, d] for d in range(3)], here)
    lane = lax.broadcasted_iota(jnp.int32, (slots, LANES), 1)
    slot = lane % WIDE
    load = lambda ref, p: ref[pl.ds(p, slots, stride=ROWS), :]
    whole = before.shape[0] == own.shape[0]
    odd = place[1] == 1
    pick = lambda one, two, n: jnp.where(odd, two[pl.ds(n * slots, slots), :], one[pl.ds(n * slots, slots), :])
    below = lambda p: load(before, p) if whole else pick(before, after, UPWARD.index(p))
    above = lambda p: load(after, p) if whole else pick(after, before, DOWNWARD.index(p))
    left = pltpu.roll(below(3), LANES - 3, 1)
    right = pltpu.roll(above(3), 3, 1)
    halo = jnp.where((slot == 0) | (slot == 5), left, load(own, 3))
    halo = jnp.where((slot == 4) | (slot == 9), right, halo)
    ordered = [
        load(own, 0), load(own, 1), load(own, 2), below(2), above(0), halo,
        below(1), above(1),
    ]
    for t, tile in enumerate(ordered):
        field[:, tile_cols(t)] = tile * scale[...]
    inside = {t: fields[VARS + 1 : VARS + 2, tile_cols(t)] for t in range(SLAB, INNER)}
    slot = lax.broadcasted_iota(jnp.int32, (1, LANES), 1) % WIDE
    used = ((slot >= 1) & (slot <= 3)) | ((slot >= 6) & (slot <= 8))
    inside[HALO] = jnp.where(used, inside[HALO], 0.0)
    scratch = (mixed, flux, scaled, acc, faces, inside, to_even, to_all, here)
    apply_operator(field, first, *scratch, TILES, INNER)
    apply_operator(first, second, *scratch, INNER, SLAB)
    sums = [jnp.zeros((1, LANES), jnp.float32)] * 5
    unscale = 1.0 / scale[...]
    for p in range(SLAB):
        b = load(own, p)
        q = first[:, tile_cols(p)] * unscale
        w = second[:, tile_cols(p)] * unscale
        out[pl.ds(p, slots, stride=2 * SLAB), :] = q
        out[pl.ds(p + SLAB, slots, stride=2 * SLAB), :] = w
        for n, (one, two) in enumerate(((b, b), (b, q), (q, q), (b, w), (q, w))):
            sums[n] = sums[n] + jnp.sum(one * two, axis=0, keepdims=True)
    total = jnp.concatenate(sums + [jnp.zeros((3, LANES), jnp.float32)], axis=0)
    partial[...] = total + refs[0][...] if comp > 0 else total


def apply_twice(comp, place, own, before, after, tables, fields, fibre, so_far=(), ready=()):
    scale, to_even, to_all = tables
    slots = scale.shape[0]
    vmem = pl.BlockSpec(memory_space=pltpu.VMEM)
    smem = pl.BlockSpec(memory_space=pltpu.SMEM)
    f32 = lambda *shape: pltpu.VMEM(shape, jnp.float32)
    return pl.pallas_call(
        functools.partial(apply_kernel, comp=comp),
        out_shape=[
            jax.ShapeDtypeStruct((slots * 2 * SLAB, LANES), jnp.float32),
            jax.ShapeDtypeStruct((8, LANES), jnp.float32),
        ],
        in_specs=[smem] + [vmem] * 7 + [smem] + [vmem] * len(so_far) + [pl.BlockSpec(memory_space=pl.ANY)] * len(ready),
        out_specs=[vmem, vmem],
        scratch_shapes=[
            f32(slots, TILES * LANES),
            f32(slots, INNER * LANES),
            f32(slots, SLAB * LANES),
            f32(FULL, TILES * LANES),
            f32(6, EVEN, TILES * LANES),
            f32(FULL, INNER * LANES),
            f32(slots, INNER * LANES),
            f32(6 * FACE + 8, TILES * LANES),
        ],
        compiler_params=pltpu.CompilerParams(vmem_limit_bytes=VMEM),
        cost_estimate=estimate(2),
        name="apply_twice",
    )(place, own, before, after, scale, to_even, to_all, fields, fibre, *so_far, *ready)


def combination(total):
    bb, bq, qq, bw, qw = (jnp.sum(total[n : n + 1, :], axis=1, keepdims=True) for n in range(5))
    step_one = bb / bq
    norm = bb - 2.0 * step_one * bq + step_one * step_one * qq
    grown = 1.0 + norm / bb
    curve = grown * grown * bq - step_one * grown * (bw + qq) + step_one * step_one * qw
    step_two = norm / curve
    return step_one + step_two * grown, step_one * step_two


def unpack_kernel(image, natural):
    modes = natural.shape[1]
    per_part = modes * 2 * SLAB

    def body(step, carry):
        for inner in range(2 * UNROLL):
            mode = step * 2 * UNROLL + inner
            for power in range(2):
                for p in range(SLAB):
                    row = (mode * 2 + power) * SLAB + p
                    natural[power, mode, p] = swap_back(image[pl.ds(row, PARTS, stride=per_part), :])
        return carry

    lax.fori_loop(0, modes // (2 * UNROLL), body, 0)


def unpack(image, modes):
    vmem = pl.BlockSpec(memory_space=pltpu.VMEM)
    return pl.pallas_call(
        unpack_kernel,
        out_shape=jax.ShapeDtypeStruct((2, modes, SLAB, 8, LANES), jnp.float32),
        in_specs=[vmem],
        out_specs=vmem,
        compiler_params=pltpu.CompilerParams(vmem_limit_bytes=VMEM),
        cost_estimate=estimate(3),
        name="unpack",
    )(image)


STEPS = 2


def finish_kernel(field, total, image, *refs):
    *natural, solution_field, residual, factors = refs
    modes = field.shape[0]
    per_part = STEPS * modes * 2 * SLAB

    @pl.when(pl.program_id(0) == 0)
    def _():
        sole, cross = combination(total)
        factors[0:8, :] = jnp.broadcast_to(sole, (8, LANES))
        factors[8:16, :] = jnp.broadcast_to(cross, (8, LANES))

    sole, cross = factors[0:8, :], factors[8:16, :]
    first = pl.program_id(0) * modes

    def body(step, carry):
        for inner in range(2 * UNROLL):
            mode = step * 2 * UNROLL + inner
            for comp in range(COMPS):
                for p in range(SLAB):
                    b = field[mode, comp, p]
                    if comp < len(natural):
                        q, w = natural[comp][0, mode, p], natural[comp][1, mode, p]
                    else:
                        row = (first + mode) * 2 * SLAB + p
                        q = swap_back(image[pl.ds(row, PARTS, stride=per_part), :])
                        w = swap_back(image[pl.ds(row + SLAB, PARTS, stride=per_part), :])
                    solution_field[mode, comp, p] = sole * b - cross * q
                    residual[mode, comp, p] = b - sole * q + cross * w
        return carry

    lax.fori_loop(0, modes // (2 * UNROLL), body, 0)


def finish(field, total, image, *natural):
    rows = field.shape[0] // STEPS
    block = pl.BlockSpec((rows,) + field.shape[1:], lambda i: (i, 0, 0, 0, 0))
    vmem = pl.BlockSpec(memory_space=pltpu.VMEM)
    return pl.pallas_call(
        finish_kernel,
        grid=(STEPS,),
        out_shape=[jax.ShapeDtypeStruct(field.shape, jnp.float32)] * 2,
        in_specs=[block, vmem, vmem]
        + [pl.BlockSpec((2, rows) + field.shape[2:], lambda i: (0, i, 0, 0, 0))] * len(natural),
        out_specs=[block, block],
        scratch_shapes=[pltpu.VMEM((16, LANES), jnp.float32)],
        compiler_params=pltpu.CompilerParams(vmem_limit_bytes=VMEM),
        cost_estimate=estimate(6),
        name="finish",
    )(field, total, image, *natural)


def mode_tables(coupling_table, slots):
    lower, upper, variable, code = (coupling_table[:, n] for n in range(4))
    slot = jnp.arange(slots, dtype=jnp.int32)
    is_lower = lower[:, None] == slot
    is_upper = upper[:, None] == slot
    degree = jnp.sum(jnp.where(is_upper, code[:, None], 0), axis=0)
    factor = jnp.where(code == 3, 6, code).astype(jnp.float32)[:, None]
    factorial = jnp.prod(jnp.where(is_upper, factor, 1.0), axis=0)
    root = (degree == 0) & jnp.any(is_lower, axis=0)
    even = (degree == 2) | root
    rank = jnp.sum(jnp.where(even[:, None] & (slot[:, None] < slot), 1, 0), axis=0)
    lower_even = jnp.any(is_lower & even, axis=1)
    is_even_end = jnp.where(lower_even[:, None], is_lower, is_upper)
    is_odd_end = jnp.where(lower_even[:, None], is_upper, is_lower)
    column = variable * EVEN + jnp.sum(jnp.where(is_even_end, rank, 0), axis=1)
    at_column = column[:, None] == jnp.arange(FULL, dtype=jnp.int32)
    down = code.astype(jnp.float32)[:, None]
    first = jnp.where(lower_even[:, None], 1.0, down)
    second = jnp.where(lower_even[:, None], down, 1.0)
    odd_ends = is_odd_end.astype(jnp.float32)
    columns = at_column.astype(jnp.float32)
    half = jnp.bfloat16
    to_even = jnp.dot(
        columns.astype(half).T, (odd_ends * first).astype(half), preferred_element_type=jnp.float32
    )
    to_odd = jnp.dot(
        odd_ends.astype(half).T, (columns * second).astype(half), preferred_element_type=jnp.float32
    )
    pick = (jnp.arange(FULL, dtype=jnp.int32)[:, None] - SPAN == rank) & even
    pick = pick.astype(jnp.float32)
    to_even = (to_even + pick).astype(half)
    to_all = (to_odd + pick.T).astype(half)
    scale = jnp.sqrt(factorial)
    wide = lambda v: jnp.broadcast_to(v[:, None], (slots, LANES))
    twice = lambda v: jnp.concatenate([v, v], axis=1)
    return wide(scale), twice(to_even), twice(to_all)


def all_sum(value):
    for axis, bit in (("space", 1), ("space", 2), ("mode", 1)):
        devices = lax.axis_size(axis)
        value = value + lax.ppermute(value, axis, [(i, i ^ bit) for i in range(devices)])
    others = [
        lax.ppermute(value, "mode", [(i, i ^ bit) for i in range(PARTS)]) for bit in range(2, PARTS, 2)
    ]
    return (value + others[0]) + (others[1] + others[2])


def transposed(right_side, mean_stiffness, ply_stiffness, fibre_weights, ply_map, coupling_table):
    slots = right_side.shape[0] * PARTS
    devices = lax.axis_size("space")
    up = [(i, i + 1) for i in range(devices - 1)]
    down = [(j, i) for i, j in up]
    slab = lax.axis_index("space").astype(jnp.int32)
    place = jnp.stack([lax.axis_index("mode").astype(jnp.int32), slab % 2])
    turns = jnp.stack([(slab == 1).astype(jnp.int32), 1 - slab % 2])

    def swap(rows):
        return lax.all_to_all(rows, "mode", 0, 0, tiled=True)

    def halo(rows, across, beside):
        across = lax.ppermute(across, "space", [(1, 2), (2, 1)])
        return rows, across, lax.ppermute(beside, "space", [(0, 1), (1, 0), (2, 3), (3, 2)])

    (first,) = pack(right_side, (0,))
    both, others = pack(right_side, (1, 2), (mean_stiffness, ply_map), (first,))
    first = swap(first)
    first = (first, lax.ppermute(first, "space", up), lax.ppermute(first, "space", down))
    others = swap(others)
    tables = mode_tables(after_rows(coupling_table, first[0]), slots)
    both_before = lax.ppermute(both, "space", up)
    both_after = lax.ppermute(both, "space", down)
    fields = stiffness_fields(place, both_before, both, both_after, ply_stiffness)
    image, partial = apply_twice(0, place, *first, tables, fields, fibre_weights)
    images = [swap(image)]
    parts = [part_component(turns, others, n, partial) for n in range(COMPS - 1)]
    halos = [halo(*part) for part in parts]
    modes = right_side.shape[0]
    image, partial = apply_twice(1, place, *halos[0], tables, fields, fibre_weights, (partial,), parts[1][:1])
    images.append(swap(image))
    natural = [unpack(images[0], modes)]
    image, partial = apply_twice(2, place, *halos[1], tables, fields, fibre_weights, (partial,), natural)
    images.append(swap(image))
    natural.append(unpack(images[1], modes))
    return tuple(finish(right_side, all_sum(partial), images[2], *natural))


def on_device(right_side, mean_stiffness, ply_stiffness, fibre_weights, ply_map, coupling_table):
    args = (right_side, mean_stiffness, ply_stiffness, fibre_weights, ply_map, coupling_table)
    fits = right_side.shape[1:] == (COMPS, SLAB, 8, 128) and (lax.axis_size("mode"), lax.axis_size("space")) == (PARTS, 4)
    return transposed(*args) if fits else plain(*args)


def solution(mesh):
    return jax.shard_map(
        on_device,
        mesh=mesh,
        in_specs=(
            P("mode", None, "space", None, None),
            P("space", None, None),
            P(),
            P(),
            P("space", None, None),
            P(),
        ),
        out_specs=(P("mode", None, "space", None, None), P("mode", None, "space", None, None)),
        check_vma=False,
    )
```

```python
import functools

import jax
import jax.numpy as jnp
from jax import lax
from jax.experimental import pallas as pl
from jax.experimental.pallas import tpu as pltpu
from jax.sharding import PartitionSpec as P

VARS = 10
ITERS = 2


def extended(array, sides, width):
    for axis, dim in sides:
        devices, length = (lax.axis_size(axis), array.shape[dim])
        up = [(i, (i + 1) % devices) for i in range(devices - 1)]
        down = [(j, i) for i, j in up]
        last = lax.slice_in_dim(array, length - width, length, axis=dim)
        leading = lax.slice_in_dim(array, 0, width, axis=dim)
        before = lax.ppermute(last, axis, up)
        after = lax.ppermute(leading, axis, down)
        array = jnp.concatenate([before, array, after], axis=dim)
    return array


def window(array_in, dim_index, offset):
    slicers = [slice(None)] * (array_in.ndim - 3)
    for which in range(3):
        shift_by = offset if which == dim_index else 0
        length_here = array_in.shape[array_in.ndim - 3 + which] - 2
        slicers.append(slice(1 + shift_by, 1 + shift_by + length_here))
    return array_in[tuple(slicers)]


def diffuse(vector, stiffness, fibre_weights):
    vector_pads = [(0, 0)] * (vector.ndim - 2) + [(1, 1), (1, 1)]
    stiff_pads = [(0, 0)] * (stiffness.ndim - 2) + [(1, 1), (1, 1)]
    padded_v = jnp.pad(vector, vector_pads)
    padded_c = jnp.pad(stiffness, stiff_pads)
    centre = window(padded_v, 0, 0)
    middle = window(padded_c, 0, 0)
    result = None
    for dim_index in range(3):
        upper = (
            0.5
            * (middle + window(padded_c, dim_index, 1))
            * (centre - window(padded_v, dim_index, 1))
        )
        lower = (
            0.5
            * (middle + window(padded_c, dim_index, -1))
            * (centre - window(padded_v, dim_index, -1))
        )
        column = fibre_weights[:, dim_index].reshape(3, 1, 1, 1)
        term = column * (upper + lower)
        result = term if result is None else result + term
    return result


def squares(vector):
    return lax.psum(jnp.sum(vector * vector), ("mode", "space"))


def row_table(both_rows, both_cols, both_vars, both_weights, base, mode_dev, slots):
    local_rows = both_rows - base
    valid_rows = (local_rows >= 0) & (local_rows < mode_dev)
    local_rows = jnp.where(valid_rows, local_rows, mode_dev)
    row_coupling = jnp.zeros((VARS, mode_dev, slots), jnp.float32)
    row_coupling = row_coupling.at[both_vars, local_rows, both_cols].add(both_weights, mode="drop")
    return row_coupling.reshape(VARS * mode_dev, slots)


def plain(right_side, mean_stiffness, ply_stiffness, fibre_weights, ply_map, coupling_table):
    mode_dev = right_side.shape[0]
    slots = mode_dev * lax.axis_size("mode")
    base = lax.axis_index("mode") * mode_dev
    first_mode = coupling_table[:, 0]
    second_mode = coupling_table[:, 1]
    variable = coupling_table[:, 2]
    entry_weight = jnp.sqrt(coupling_table[:, 3].astype(jnp.float32))
    both_rows = jnp.concatenate([first_mode, second_mode])
    both_cols = jnp.concatenate([second_mode, first_mode])
    both_vars = jnp.concatenate([variable, variable])
    both_weights = jnp.concatenate([entry_weight, entry_weight])
    plies = jnp.arange(VARS, dtype=jnp.int32).reshape(VARS, 1, 1, 1)
    ply_fields = (ply_map[None] == plies).astype(jnp.float32) * ply_stiffness.reshape(VARS, 1, 1, 1)
    stiff_stack = jnp.concatenate([mean_stiffness[None], ply_fields], axis=0)
    stiff_rims = extended(stiff_stack, (("space", 1),), 1)
    stiff_rims = stiff_rims[:, None]
    row_coupling = row_table(both_rows, both_cols, both_vars, both_weights, base, mode_dev, slots)
    solution_field = jnp.zeros_like(right_side)
    residual = right_side
    direction = right_side
    norm_now = squares(residual)
    for iteration in range(ITERS):
        shard_piece = lax.all_gather(direction, "mode", axis=0, tiled=True)
        mixed = jnp.dot(
            row_coupling,
            shard_piece.reshape(shard_piece.shape[0], -1),
            precision=lax.Precision.HIGHEST,
            preferred_element_type=jnp.float32,
        )
        stacked = jnp.concatenate(
            [direction[None], mixed.reshape((VARS,) + direction.shape)], axis=0
        )
        padded = extended(stacked, (("space", 3),), 1)
        terms = diffuse(padded, stiff_rims[:, None], fibre_weights)
        image = direction + jnp.sum(terms, axis=0)
        step_size = norm_now / lax.psum(jnp.sum(direction * image), ("mode", "space"))
        solution_field = solution_field + step_size * direction
        residual = residual - step_size * image
        norm_next = squares(residual)
        direction = residual + norm_next / norm_now * direction
        norm_now = norm_next
    return (solution_field, residual)


COMPS = 3
SLAB = 3
PARTS = 8
WIDE = 16
ROWS = 4
UPWARD = (1, 2, 3)
DOWNWARD = (0, 1, 3)
EVEN = 1 + VARS * (VARS + 1) // 2
SPAN = VARS * EVEN
FULL = 624
INNER = 6
TILES = 8
LANES = 128
VMEM = 56 * 1024 * 1024


def lane_id():
    return lax.broadcasted_iota(jnp.int32, (8, LANES), 1)


def swap_out(tile):
    block = lane_id() // WIDE
    tile = pltpu.roll(tile, 0, 1, stride=WIDE, stride_axis=0)
    for bit in (1, 2, 4):
        tile = jnp.where((block & bit) != 0, pltpu.roll(tile, 8 - bit, 0), tile)
    return tile


def swap_back(tile):
    block = lane_id() // WIDE
    row = lax.broadcasted_iota(jnp.int32, (8, LANES), 0)
    for bit in (1, 2, 4):
        tile = jnp.where((block & bit) != 0, pltpu.roll(tile, bit, 0), tile)
    for bit in (1, 2, 4):
        tile = jnp.where((row & bit) != 0, pltpu.roll(tile, LANES - WIDE * bit, 1), tile)
    return tile


def halo_row(planes):
    lane = lane_id()
    slot = lane % WIDE
    halo = jnp.zeros((8, LANES), jnp.float32)
    for x, plane in planes.items():
        places = [(-1, x + 1), (WIDE, x + 6)]
        if 0 <= x < SLAB:
            places += [(-2, x + 10), (WIDE + 1, x + 13)]
        for offset, place in places:
            inside = (lane >= WIDE) if offset < 0 else (lane < LANES - WIDE)
            moved = pltpu.roll(plane, (place - offset) % LANES, 1)
            halo = jnp.where((slot == place) & inside, moved, halo)
    return halo


UNROLL = 3


def pack_kernel(field, *refs, comps):
    modes = field.shape[0]
    out = refs[-1]
    if len(refs) > 1:
        mean, ply, both = refs[0], refs[1], refs[-2]
        for x in range(SLAB):
            both[0, x] = mean[x]
            both[1, x] = (ply[x] + 1).astype(jnp.float32)
    rows = ROWS * len(comps)
    unroll = 2 * UNROLL // len(comps)

    def body(step, carry):
        for inner in range(unroll):
            mode = step * unroll + inner
            for n, comp in enumerate(comps):
                planes = [field[mode, comp, x] for x in range(SLAB)]
                halo = halo_row(dict(enumerate(planes)))
                for p, tile in enumerate(planes + [halo]):
                    out[pl.ds((n * modes + mode) * ROWS + p, PARTS, stride=rows * modes), :] = swap_out(tile)
        return carry

    lax.fori_loop(0, modes // unroll, body, 0)


def estimate(micros):
    return pl.CostEstimate(flops=int(micros * 1e9), bytes_accessed=int(micros * 3e6), transcendentals=0)


def pack(field, comps, stiffness=(), after=()):
    modes = field.shape[0]
    vmem = pl.BlockSpec(memory_space=pltpu.VMEM)
    shapes = [jax.ShapeDtypeStruct((2,) + s.shape, jnp.float32) for s in stiffness[:1]]
    shapes.append(jax.ShapeDtypeStruct((PARTS * modes * ROWS * len(comps), LANES), jnp.float32))
    return pl.pallas_call(
        functools.partial(pack_kernel, comps=comps),
        grid=(1,),
        out_shape=shapes,
        in_specs=[pl.BlockSpec((modes, max(comps) + 1) + field.shape[2:], lambda i: (0, 0, 0, 0, 0))]
        + [vmem] * len(stiffness)
        + [pl.BlockSpec(memory_space=pl.ANY)] * len(after),
        out_specs=[vmem] * len(shapes),
        compiler_params=pltpu.CompilerParams(vmem_limit_bytes=VMEM),
        cost_estimate=estimate(0.5),
        name="pack",
    )(field, *stiffness, *after)


def copy_kernel(source, ready, goal):
    goal[...] = source[...]


def part_kernel(turns, source, ready, own, across, beside):
    rows = own.shape[0]
    slots = rows // ROWS
    own[...] = source[...].reshape(rows, LANES)
    for n, goal in enumerate((across, beside)):
        for m in range(len(UPWARD) - 1):
            goal[m * slots : (m + 1) * slots, :] = own[pl.ds(m + turns[n], slots, stride=ROWS), :]
        goal[(len(UPWARD) - 1) * slots :, :] = own[pl.ds(UPWARD[-1], slots, stride=ROWS), :]


def part_component(turns, rows, n, ready):
    blocks = rows.reshape(PARTS, -1, LANES)
    part = (PARTS, blocks.shape[1] // (COMPS - 1), LANES)
    count = part[0] * part[1]
    vmem = pl.BlockSpec(memory_space=pltpu.VMEM)
    return pl.pallas_call(
        part_kernel,
        grid=(1,),
        out_shape=[
            jax.ShapeDtypeStruct((size, LANES), jnp.float32)
            for size in (count, count * len(UPWARD) // ROWS, count * len(DOWNWARD) // ROWS)
        ],
        in_specs=[
            pl.BlockSpec(memory_space=pltpu.SMEM),
            pl.BlockSpec(part, lambda i: (0, n, 0)),
            pl.BlockSpec(memory_space=pl.ANY),
        ],
        out_specs=[vmem] * 3,
        compiler_params=pltpu.CompilerParams(vmem_limit_bytes=VMEM),
        cost_estimate=estimate(0.5),
        name="part_component",
    )(turns, blocks, ready)


def after_rows(table, ready):
    vmem = pl.BlockSpec(memory_space=pltpu.VMEM)
    return pl.pallas_call(
        copy_kernel,
        out_shape=jax.ShapeDtypeStruct(table.shape, table.dtype),
        in_specs=[vmem, pl.BlockSpec(memory_space=pl.ANY)],
        out_specs=vmem,
        cost_estimate=estimate(0.5),
        name="after_rows",
    )(table, ready)


def stiffness_kernel(place, before, both, after, ply_stiffness, fields, wide):
    rows = []
    for kind in range(2):
        planes = {-2: before[kind, 1], -1: before[kind, 2], 3: after[kind, 0], 4: after[kind, 1]}
        planes.update({x: both[kind, x] for x in range(SLAB)})
        halo = halo_row({x: planes[x] for x in range(-1, 4)})
        ordered = [planes[0], planes[1], planes[2], planes[-1], planes[3], halo, planes[-2], planes[4]]
        for t, tile in enumerate(ordered):
            wide[...] = swap_out(tile)
            rows.append(wide[pl.ds(place[0], 1), :])
    for t in range(TILES):
        mean, ply = rows[t], rows[TILES + t]
        cols = slice(LANES * t, LANES * (t + 1))
        for k in range(VARS):
            fields[k : k + 1, cols] = jnp.where(ply == k + 1.0, ply_stiffness[k], 0.0)
        fields[VARS : VARS + 1, cols] = mean
        fields[VARS + 1 : VARS + 2, cols] = jnp.where(ply > 0.0, 1.0, 0.0)
        fields[VARS + 2 : 16, cols] = jnp.zeros((4, LANES), jnp.float32)


def stiffness_fields(place, before, both, after, ply_stiffness):
    vmem = pl.BlockSpec(memory_space=pltpu.VMEM)
    smem = pl.BlockSpec(memory_space=pltpu.SMEM)
    return pl.pallas_call(
        stiffness_kernel,
        out_shape=jax.ShapeDtypeStruct((16, TILES * LANES), jnp.float32),
        in_specs=[smem, vmem, vmem, vmem, smem],
        out_specs=vmem,
        scratch_shapes=[pltpu.VMEM((8, LANES), jnp.float32)],
        cost_estimate=estimate(0.5),
        name="stiffness_fields",
    )(place, before, both, after, ply_stiffness)


AT = {0: 0, 1: 1, 2: 2, -1: 3, 3: 4, -2: 6, 4: 7}
PLACE = {index: x for x, index in AT.items()}
HALO = 5


def neighbour(tiles, index, side, place, full=False, wrap=False):
    t = tiles[index]
    lane = lax.broadcasted_iota(jnp.int32, t.shape, 1)
    slot = lane % WIDE
    roll = lambda v, s: pltpu.roll(v, s % LANES, 1)
    if side in (2, 3) and wrap:
        return roll(t, WIDE if side == 2 else -WIDE)
    if side in (2, 3):
        y = (place + lane // WIDE) & 7
        if side == 2:
            return jnp.where(y > 0, roll(t, WIDE), 0.0)
        return jnp.where(y < 7, roll(t, -WIDE), 0.0)
    if index == HALO:
        if side < 2:
            return roll(t, 1 if side == 0 else -1)
        result = roll(t, -9) if side == 4 else roll(t, -7)
        for x in range(-1, 4) if full else range(SLAB):
            goal, by = (x + 6, x - 9) if side == 4 else (x + 1, x + 1)
            result = jnp.where(slot == goal, roll(tiles[AT[x]], by), result)
        if full:
            result = jnp.where(slot >= 13, roll(t, 7), result) if side == 4 else jnp.where(
                (slot >= 10) & (slot < 13), roll(t, 9), result
            )
        return result
    x = PLACE[index]
    if side < 2:
        return tiles[AT[x - 1 if side == 0 else x + 1]]
    if side == 4:
        return jnp.where(slot == 0, roll(tiles[HALO], -(x + 1)), roll(t, 1))
    return jnp.where(slot == WIDE - 1, roll(tiles[HALO], 9 - x), roll(t, -1))


def sides_of(index, outer):
    if index < outer:
        return range(6)
    return {3: (1,), 4: (0,), HALO: (4, 5), 6: (1,), 7: (0,)}[index]


def split(array):
    high = array.astype(jnp.bfloat16)
    low = (array - high.astype(jnp.float32)).astype(jnp.bfloat16)
    return jnp.concatenate([high, low], axis=0)


STEP = 48
FACE = 16
CENTRE = 6 * FACE
EVEN_BLOCKS = ((0, 32), (32, EVEN))


def tile_cols(t):
    return slice(LANES * t, LANES * (t + 1))


def face_stiffness(fields, faces, weights, place):
    tiles = [fields[:, tile_cols(t)] for t in range(TILES)]
    for t in range(TILES):
        for side in sides_of(t, INNER):
            value = (0.5 * weights[side // 2]) * (tiles[t] + neighbour(tiles, t, side, place, True))
            faces[side * FACE : (side + 1) * FACE, tile_cols(t)] = value
        if t < INNER:
            centre = 1.0 + sum(faces[side * FACE + VARS : side * FACE + VARS + 1, tile_cols(t)] for side in range(6))
            faces[CENTRE : CENTRE + 1, tile_cols(t)] = centre
            lane = lax.broadcasted_iota(jnp.int32, (1, LANES), 1)
            y = (place + lane // WIDE) & 7
            for side, edge in ((2, 0), (3, 7)):
                row = side * FACE + VARS
                faces[row + 1 : row + 2, tile_cols(t)] = jnp.where(
                    y == edge, 0.0, faces[row : row + 1, tile_cols(t)]
                )


CHUNK = 8


def chunks(count):
    return [range(start, min(start + CHUNK, count)) for start in range(0, count, CHUNK)]


def chunk_cols(tiles):
    return slice(LANES * tiles[0], LANES * (tiles[-1] + 1))


def apply_operator(src, dst, mixed, flux, scaled, acc, faces, inside, to_even, to_all, place, inner, outer):
    slots = src.shape[0]

    def face(side, k, t):
        return faces[side * FACE + k : side * FACE + k + 1, tile_cols(t)]

    def mix(tiles):
        cols = chunk_cols(tiles)
        mixed[:, cols] = jnp.dot(to_even[...], split(src[:, cols]), preferred_element_type=jnp.float32)

    def flows(t):
        for low, high in EVEN_BLOCKS:
            total = {}
            for k in range(VARS):
                value = mixed[k * EVEN + low : k * EVEN + high, tile_cols(t)]
                for side in sides_of(t, outer):
                    term = face(side, k, t) * value
                    total[side] = term if k == 0 else total[side] + term
            for side, value in total.items():
                flux[side, low:high, tile_cols(t)] = value

    def scale_even(t):
        for low, high in EVEN_BLOCKS:
            even = EvenTiles(mixed, low, high)
            steps = [even[t] - neighbour(even, t, side, place) for side in range(6)]
            for k in range(VARS):
                total = face(0, k, t) * steps[0]
                for side in range(1, 6):
                    total = total + face(side, k, t) * steps[side]
                scaled[k * EVEN + low : k * EVEN + high, tile_cols(t)] = total
            total = None
            for side in range(6):
                opposite = FluxTiles(flux, side ^ 1, low, high)
                term = flux[side, low:high, tile_cols(t)] - neighbour(opposite, t, side, place)
                total = term if total is None else total + term
            scaled[SPAN + low : SPAN + high, tile_cols(t)] = total
        scaled[SPAN + EVEN : FULL, tile_cols(t)] = jnp.zeros((FULL - SPAN - EVEN, LANES), jnp.float32)

    def spread(tiles):
        cols = chunk_cols(tiles)
        acc[:, cols] = jnp.dot(to_all[...], split(scaled[:, cols]), preferred_element_type=jnp.float32)

    before = ()
    for tiles in chunks(inner):
        mix(tiles)
        for t in before:
            flows(t)
        before = tiles
    for t in before:
        flows(t)
    before = ()
    for tiles in chunks(outer):
        for t in tiles:
            scale_even(t)
        if before:
            spread(before)
        before = tiles
    spread(before)

    def last(step, carry):
        rows = pl.ds(pl.multiple_of(step * STEP, STEP), STEP)
        tiles = [src[rows, tile_cols(t)] for t in range(inner)]
        for t in range(outer):
            result = acc[rows, tile_cols(t)] + faces[CENTRE : CENTRE + 1, tile_cols(t)] * tiles[t]
            for side in range(6):
                row = VARS + 1 if side in (2, 3) else VARS
                result = result - face(side, row, t) * neighbour(tiles, t, side, place, wrap=True)
            if t >= SLAB:
                result = inside[t] * result
            dst[rows, tile_cols(t)] = result
        return carry

    lax.fori_loop(0, slots // STEP, last, 0)


class EvenTiles:
    def __init__(self, mixed, low, high):
        self.mixed, self.low, self.high = mixed, low, high

    def __getitem__(self, t):
        return self.mixed[SPAN + self.low : SPAN + self.high, tile_cols(t)]


class FluxTiles:
    def __init__(self, flux, side, low, high):
        self.flux, self.side, self.low, self.high = flux, side, low, high

    def __getitem__(self, t):
        return self.flux[self.side, self.low : self.high, tile_cols(t)]


def apply_kernel(
    place, own, before, after, scale, to_even, to_all, fields, fibre, *refs, comp,
):
    out, partial, field, first, second, mixed, flux, scaled, acc, faces = refs[-10:]
    slots = scale.shape[0]
    here = place[0]
    face_stiffness(fields, faces, [fibre[comp, d] for d in range(3)], here)
    lane = lax.broadcasted_iota(jnp.int32, (slots, LANES), 1)
    slot = lane % WIDE
    load = lambda ref, p: ref[pl.ds(p, slots, stride=ROWS), :]
    whole = before.shape[0] == own.shape[0]
    odd = place[1] == 1
    pick = lambda one, two, n: jnp.where(odd, two[pl.ds(n * slots, slots), :], one[pl.ds(n * slots, slots), :])
    below = lambda p: load(before, p) if whole else pick(before, after, UPWARD.index(p))
    above = lambda p: load(after, p) if whole else pick(after, before, DOWNWARD.index(p))
    left = pltpu.roll(below(3), LANES - 3, 1)
    right = pltpu.roll(above(3), 3, 1)
    halo = jnp.where((slot == 0) | (slot == 5), left, load(own, 3))
    halo = jnp.where((slot == 4) | (slot == 9), right, halo)
    ordered = [
        load(own, 0), load(own, 1), load(own, 2), below(2), above(0), halo,
        below(1), above(1),
    ]
    for t, tile in enumerate(ordered):
        field[:, tile_cols(t)] = tile * scale[...]
    inside = {t: fields[VARS + 1 : VARS + 2, tile_cols(t)] for t in range(SLAB, INNER)}
    slot = lax.broadcasted_iota(jnp.int32, (1, LANES), 1) % WIDE
    used = ((slot >= 1) & (slot <= 3)) | ((slot >= 6) & (slot <= 8))
    inside[HALO] = jnp.where(used, inside[HALO], 0.0)
    scratch = (mixed, flux, scaled, acc, faces, inside, to_even, to_all, here)
    apply_operator(field, first, *scratch, TILES, INNER)
    apply_operator(first, second, *scratch, INNER, SLAB)
    sums = [jnp.zeros((1, LANES), jnp.float32)] * 5
    unscale = 1.0 / scale[...]
    for p in range(SLAB):
        b = load(own, p)
        q = first[:, tile_cols(p)] * unscale
        w = second[:, tile_cols(p)] * unscale
        out[pl.ds(p, slots, stride=2 * SLAB), :] = q
        out[pl.ds(p + SLAB, slots, stride=2 * SLAB), :] = w
        for n, (one, two) in enumerate(((b, b), (b, q), (q, q), (b, w), (q, w))):
            sums[n] = sums[n] + jnp.sum(one * two, axis=0, keepdims=True)
    total = jnp.concatenate(sums + [jnp.zeros((3, LANES), jnp.float32)], axis=0)
    partial[...] = total + refs[0][...] if comp > 0 else total


def apply_twice(comp, place, own, before, after, tables, fields, fibre, so_far=(), ready=()):
    scale, to_even, to_all = tables
    slots = scale.shape[0]
    vmem = pl.BlockSpec(memory_space=pltpu.VMEM)
    smem = pl.BlockSpec(memory_space=pltpu.SMEM)
    f32 = lambda *shape: pltpu.VMEM(shape, jnp.float32)
    return pl.pallas_call(
        functools.partial(apply_kernel, comp=comp),
        out_shape=[
            jax.ShapeDtypeStruct((slots * 2 * SLAB, LANES), jnp.float32),
            jax.ShapeDtypeStruct((8, LANES), jnp.float32),
        ],
        in_specs=[smem] + [vmem] * 7 + [smem] + [vmem] * len(so_far) + [pl.BlockSpec(memory_space=pl.ANY)] * len(ready),
        out_specs=[vmem, vmem],
        scratch_shapes=[
            f32(slots, TILES * LANES),
            f32(slots, INNER * LANES),
            f32(slots, SLAB * LANES),
            f32(FULL, TILES * LANES),
            f32(6, EVEN, TILES * LANES),
            f32(FULL, INNER * LANES),
            f32(slots, INNER * LANES),
            f32(6 * FACE + 8, TILES * LANES),
        ],
        compiler_params=pltpu.CompilerParams(vmem_limit_bytes=VMEM),
        cost_estimate=estimate(2),
        name="apply_twice",
    )(place, own, before, after, scale, to_even, to_all, fields, fibre, *so_far, *ready)


def combination(total):
    bb, bq, qq, bw, qw = (jnp.sum(total[n : n + 1, :], axis=1, keepdims=True) for n in range(5))
    step_one = bb / bq
    norm = bb - 2.0 * step_one * bq + step_one * step_one * qq
    grown = 1.0 + norm / bb
    curve = grown * grown * bq - step_one * grown * (bw + qq) + step_one * step_one * qw
    step_two = norm / curve
    return step_one + step_two * grown, step_one * step_two


def unpack_kernel(image, natural):
    modes = natural.shape[1]
    per_part = modes * 2 * SLAB

    def body(step, carry):
        for inner in range(2 * UNROLL):
            mode = step * 2 * UNROLL + inner
            for power in range(2):
                for p in range(SLAB):
                    row = (mode * 2 + power) * SLAB + p
                    natural[power, mode, p] = swap_back(image[pl.ds(row, PARTS, stride=per_part), :])
        return carry

    lax.fori_loop(0, modes // (2 * UNROLL), body, 0)


def unpack(image, modes):
    vmem = pl.BlockSpec(memory_space=pltpu.VMEM)
    return pl.pallas_call(
        unpack_kernel,
        out_shape=jax.ShapeDtypeStruct((2, modes, SLAB, 8, LANES), jnp.float32),
        in_specs=[vmem],
        out_specs=vmem,
        compiler_params=pltpu.CompilerParams(vmem_limit_bytes=VMEM),
        cost_estimate=estimate(3),
        name="unpack",
    )(image)


STEPS = 2


def finish_kernel(field, total, natural, *refs):
    *images, solution_field, residual, factors = refs
    modes = field.shape[0]
    per_part = STEPS * modes * 2 * SLAB

    @pl.when(pl.program_id(0) == 0)
    def _():
        sole, cross = combination(total)
        factors[0:8, :] = jnp.broadcast_to(sole, (8, LANES))
        factors[8:16, :] = jnp.broadcast_to(cross, (8, LANES))

    sole, cross = factors[0:8, :], factors[8:16, :]
    first = pl.program_id(0) * modes

    def body(step, carry):
        for inner in range(2 * UNROLL):
            mode = step * 2 * UNROLL + inner
            for comp in range(COMPS):
                for p in range(SLAB):
                    b = field[mode, comp, p]
                    if comp == 0:
                        q, w = natural[0, mode, p], natural[1, mode, p]
                    else:
                        image = images[comp - 1]
                        row = (first + mode) * 2 * SLAB + p
                        q = swap_back(image[pl.ds(row, PARTS, stride=per_part), :])
                        w = swap_back(image[pl.ds(row + SLAB, PARTS, stride=per_part), :])
                    solution_field[mode, comp, p] = sole * b - cross * q
                    residual[mode, comp, p] = b - sole * q + cross * w
        return carry

    lax.fori_loop(0, modes // (2 * UNROLL), body, 0)


def finish(field, total, natural, *images):
    rows = field.shape[0] // STEPS
    block = pl.BlockSpec((rows,) + field.shape[1:], lambda i: (i, 0, 0, 0, 0))
    vmem = pl.BlockSpec(memory_space=pltpu.VMEM)
    return pl.pallas_call(
        finish_kernel,
        grid=(STEPS,),
        out_shape=[jax.ShapeDtypeStruct(field.shape, jnp.float32)] * 2,
        in_specs=[block, vmem, pl.BlockSpec((2, rows) + field.shape[2:], lambda i: (0, i, 0, 0, 0))]
        + [vmem] * len(images),
        out_specs=[block, block],
        scratch_shapes=[pltpu.VMEM((16, LANES), jnp.float32)],
        compiler_params=pltpu.CompilerParams(vmem_limit_bytes=VMEM),
        cost_estimate=estimate(6),
        name="finish",
    )(field, total, natural, *images)


def mode_tables(coupling_table, slots):
    lower, upper, variable, code = (coupling_table[:, n] for n in range(4))
    slot = jnp.arange(slots, dtype=jnp.int32)
    is_lower = lower[:, None] == slot
    is_upper = upper[:, None] == slot
    degree = jnp.sum(jnp.where(is_upper, code[:, None], 0), axis=0)
    factor = jnp.where(code == 3, 6, code).astype(jnp.float32)[:, None]
    factorial = jnp.prod(jnp.where(is_upper, factor, 1.0), axis=0)
    root = (degree == 0) & jnp.any(is_lower, axis=0)
    even = (degree == 2) | root
    rank = jnp.sum(jnp.where(even[:, None] & (slot[:, None] < slot), 1, 0), axis=0)
    lower_even = jnp.any(is_lower & even, axis=1)
    is_even_end = jnp.where(lower_even[:, None], is_lower, is_upper)
    is_odd_end = jnp.where(lower_even[:, None], is_upper, is_lower)
    column = variable * EVEN + jnp.sum(jnp.where(is_even_end, rank, 0), axis=1)
    at_column = column[:, None] == jnp.arange(FULL, dtype=jnp.int32)
    down = code.astype(jnp.float32)[:, None]
    first = jnp.where(lower_even[:, None], 1.0, down)
    second = jnp.where(lower_even[:, None], down, 1.0)
    odd_ends = is_odd_end.astype(jnp.float32)
    columns = at_column.astype(jnp.float32)
    half = jnp.bfloat16
    to_even = jnp.dot(
        columns.astype(half).T, (odd_ends * first).astype(half), preferred_element_type=jnp.float32
    )
    to_odd = jnp.dot(
        odd_ends.astype(half).T, (columns * second).astype(half), preferred_element_type=jnp.float32
    )
    pick = (jnp.arange(FULL, dtype=jnp.int32)[:, None] - SPAN == rank) & even
    pick = pick.astype(jnp.float32)
    to_even = (to_even + pick).astype(half)
    to_all = (to_odd + pick.T).astype(half)
    scale = jnp.sqrt(factorial)
    wide = lambda v: jnp.broadcast_to(v[:, None], (slots, LANES))
    twice = lambda v: jnp.concatenate([v, v], axis=1)
    return wide(scale), twice(to_even), twice(to_all)


def all_sum(value):
    for axis, bit in (("space", 1), ("space", 2), ("mode", 1)):
        devices = lax.axis_size(axis)
        value = value + lax.ppermute(value, axis, [(i, i ^ bit) for i in range(devices)])
    others = [
        lax.ppermute(value, "mode", [(i, i ^ bit) for i in range(PARTS)]) for bit in range(2, PARTS, 2)
    ]
    return (value + others[0]) + (others[1] + others[2])


def transposed(right_side, mean_stiffness, ply_stiffness, fibre_weights, ply_map, coupling_table):
    slots = right_side.shape[0] * PARTS
    devices = lax.axis_size("space")
    up = [(i, i + 1) for i in range(devices - 1)]
    down = [(j, i) for i, j in up]
    slab = lax.axis_index("space").astype(jnp.int32)
    place = jnp.stack([lax.axis_index("mode").astype(jnp.int32), slab % 2])
    turns = jnp.stack([(slab == 1).astype(jnp.int32), 1 - slab % 2])

    def swap(rows):
        return lax.all_to_all(rows, "mode", 0, 0, tiled=True)

    def halo(rows, across, beside):
        across = lax.ppermute(across, "space", [(1, 2), (2, 1)])
        return rows, across, lax.ppermute(beside, "space", [(0, 1), (1, 0), (2, 3), (3, 2)])

    (first,) = pack(right_side, (0,))
    both, others = pack(right_side, (1, 2), (mean_stiffness, ply_map), (first,))
    first = swap(first)
    first = (first, lax.ppermute(first, "space", up), lax.ppermute(first, "space", down))
    others = swap(others)
    tables = mode_tables(after_rows(coupling_table, first[0]), slots)
    both_before = lax.ppermute(both, "space", up)
    both_after = lax.ppermute(both, "space", down)
    fields = stiffness_fields(place, both_before, both, both_after, ply_stiffness)
    image, partial = apply_twice(0, place, *first, tables, fields, fibre_weights)
    images = [swap(image)]
    parts = [part_component(turns, others, n, partial) for n in range(COMPS - 1)]
    halos = [halo(*part) for part in parts]
    modes = right_side.shape[0]
    image, partial = apply_twice(1, place, *halos[0], tables, fields, fibre_weights, (partial,), parts[1][:1])
    images.append(swap(image))
    natural = unpack(images[0], modes)
    image, partial = apply_twice(2, place, *halos[1], tables, fields, fibre_weights, (partial,), (natural,))
    images.append(swap(image))
    return tuple(finish(right_side, all_sum(partial), natural, *images[1:]))


def on_device(right_side, mean_stiffness, ply_stiffness, fibre_weights, ply_map, coupling_table):
    args = (right_side, mean_stiffness, ply_stiffness, fibre_weights, ply_map, coupling_table)
    fits = right_side.shape[1:] == (COMPS, SLAB, 8, 128) and (lax.axis_size("mode"), lax.axis_size("space")) == (PARTS, 4)
    return transposed(*args) if fits else plain(*args)


def solution(mesh):
    return jax.shard_map(
        on_device,
        mesh=mesh,
        in_specs=(
            P("mode", None, "space", None, None),
            P("space", None, None),
            P(),
            P(),
            P("space", None, None),
            P(),
        ),
        out_specs=(P("mode", None, "space", None, None), P("mode", None, "space", None, None)),
        check_vma=False,
    )
```
